32 devices in a mesh: mode: 8 (over z, y), slab: 4 (over x, core).
Axes of the slice: x: 2, y: 2, z: 4, core: 2. Of those that a mesh axis runs over, the one named last changes fastest.
Arguments:
- guess: float32 [1024, 128, 128], P('mode', 'slab'), may hold values from -6 to 6
- right_side: float32 [1024, 128, 128], P('mode', 'slab'), may hold values from -6 to 6
- mean_coef: float32 [128, 128], P('slab'), may hold values from 0.5 to 2
- field_coef: float32 [3, 128, 128], P(None, 'slab'), may hold values from -2.5 to 2.5
- coupling: bfloat16 [8, 16, 128, 128], replicated, may hold values from -0.0625 to 0.0625
- coupling_list: int32 [8, 16], replicated, may hold values from 0 to 23, as said below
- pair_count: int32 [8], replicated, may hold values from 4 to 16, as said below
Outputs:
- solution: float32 [1024, 128, 128], P('mode', 'slab')
- residual: float32 [1024, 128, 128], P('mode', 'slab')
The draws below stay inside these ranges and needn't reach their ends.
Inputs may be any that keep to these rules, and one draw needn't show every extreme that they name: `coupling_list`: each row holds 16 distinct entries; entry e couples its row's mode block to mode block e // 3 through coefficient field e % 3. Only the first pair_count entries of a row are live. `pair_count`: number of live entries of each mode block's row.
All inputs are finite; a program needn't handle non-finite values.
Results may differ from the reference program's by a relative error of at most 0.0012.
Values may be sent and summed in bfloat16 or wider, within the bound.
No kernel may reach another device: no remote copies, remote signals or barrier semaphores. Data moves between devices by JAX's collectives and lax.ppermute only.
A program may use at most 256 MiB of HBM per device.

```python
import math
import jax
import jax.numpy as jnp
from jax import lax

BLK = 128
FIELDS = 3
MAXC = 16
NX = 128
NY = 128
ITERS = 2
BLOCKS = 8
MODES = 1024


def move_front(entries, value, slot):
    position = jnp.argmax(entries == value)
    displaced = entries[slot]
    return entries.at[slot].set(value).at[position].set(displaced)


def draw_coupling_list(key, part):
    pair_total = BLOCKS * FIELDS
    row_keys = jax.random.split(jax.random.fold_in(key, 11), BLOCKS)
    shuffled = jax.vmap(lambda single: jax.random.permutation(single, pair_total))(row_keys)
    chosen = jax.random.randint(jax.random.fold_in(key, 12), (), 0, BLOCKS)
    special = move_front(shuffled[chosen], pair_total - 1, 0)
    special = move_front(special, 0, 1)
    shuffled = shuffled.at[chosen].set(special)
    return shuffled[:, :MAXC].astype(jnp.int32)


def draw_pair_count(key, part):
    lowest = MAXC // 4
    counts = jax.random.randint(jax.random.fold_in(key, 21), (BLOCKS,), lowest, MAXC + 1)
    first = jax.random.randint(jax.random.fold_in(key, 22), (), 0, BLOCKS)
    offset = jax.random.randint(jax.random.fold_in(key, 23), (), 1, BLOCKS)
    second = (first + offset) % BLOCKS
    counts = counts.at[first].set(MAXC).at[second].set(lowest)
    return counts.astype(jnp.int32)


def level_of(rng, extent, pieces, low, largest):
    def one(dim, shards_of):
        draws = jax.random.uniform(jax.random.fold_in(jax.random.fold_in(rng, 6), dim), (shards_of,), jnp.float32, low / len(pieces), largest / len(pieces))
        return jnp.repeat(jnp.exp(draws), extent[dim] // shards_of).reshape((-1,) + (1,) * (len(extent) - dim - 1))

    gain = one(*pieces[0])
    for cut in pieces[1:]:
        gain = gain * one(*cut)
    return gain


def normal_values(rng, extent, width, bound, pieces=(), kind=jnp.bfloat16):
    gain = level_of(rng, extent, pieces, -0.22, 0.18) if pieces else 1.0
    values = jax.random.normal(rng, extent, jnp.float32) * width * gain
    return jnp.minimum(jnp.maximum(values, -bound), bound).astype(kind)


def setup_inputs(seed: int = 0) -> dict:
    splits = jax.random.split(jax.random.key(seed), 8)
    guess = normal_values(splits[0], (MODES, NX, NY), 1.0, 6.0, ((0, 8), (1, 4)), jnp.float32)
    right_side = normal_values(splits[1], (MODES, NX, NY), 1.0, 6.0, ((0, 8), (1, 4)), jnp.float32)
    mean_coef = jnp.clip(jnp.exp(math.log(2.0) - 1.3862944 * jax.random.uniform(splits[2], (NX, NY), jnp.float32) ** level_of(splits[2], (NX, NY), ((0, 4),), -0.2, 0.2)), 0.5, 2.0)
    field_coef = normal_values(splits[3], (FIELDS, NX, NY), 0.5, 2.5, ((1, 4),), jnp.float32)
    coupling = normal_values(splits[4], (BLOCKS, MAXC, BLK, BLK), (4 * BLK * MAXC) ** -0.5, 0.0625)
    coupling_list = draw_coupling_list(jax.random.fold_in(splits[7], 71), 0)
    pair_count = draw_pair_count(jax.random.fold_in(splits[7], 71), 0)
    return {"guess": guess, "right_side": right_side, "mean_coef": mean_coef, "field_coef": field_coef, "coupling": coupling, "coupling_list": coupling_list, "pair_count": pair_count}


relaxation = 0.6

def operate(padded, coef_pad):
    center = coef_pad[..., 1:-1, :]
    field = padded[..., 1:-1, :]
    result = 0.5 * (center + coef_pad[..., :-2, :]) * (field - padded[..., :-2, :])
    result = result + 0.5 * (center + coef_pad[..., 2:, :]) * (field - padded[..., 2:, :])
    side_coef = jnp.pad(center, [(0, 0)] * (center.ndim - 1) + [(1, 1)], mode='edge')
    side_field = jnp.pad(field, [(0, 0)] * (field.ndim - 1) + [(1, 1)])
    result = result + 0.5 * (center + side_coef[..., :-2]) * (field - side_field[..., :-2])
    result = result + 0.5 * (center + side_coef[..., 2:]) * (field - side_field[..., 2:])
    return result

def sine_table(length):
    counter = jnp.arange(length).astype(jnp.float32) + 1.0
    angle = math.pi * counter[:, None] * counter[None, :] / (length + 1)
    return math.sqrt(2.0 / (length + 1)) * jnp.sin(angle)

def eigen_table(first, second):
    along_first = 2.0 * jnp.cos(math.pi * (jnp.arange(first).astype(jnp.float32) + 1.0) / (first + 1))
    along_second = 2.0 * jnp.cos(math.pi * (jnp.arange(second).astype(jnp.float32) + 1.0) / (second + 1))
    return 4.0 - along_first[:, None] - along_second[None, :]

def mean_solve(resid):
    highest = lax.Precision.HIGHEST
    rows_table = sine_table(NX)
    cols_table = sine_table(NY)
    spectral = jnp.einsum('px,mxy->mpy', rows_table, resid, precision=highest)
    spectral = jnp.einsum('mpy,yq->mpq', spectral, cols_table, precision=highest)
    spectral = spectral / eigen_table(NX, NY)
    spatial = jnp.einsum('xp,mpq->mxq', rows_table, spectral, precision=highest)
    return jnp.einsum('mxq,qy->mxy', spatial, cols_table, precision=highest)

def reference(guess, right_side, mean_coef, field_coef, coupling, coupling_list, pair_count):
    highest = lax.Precision.HIGHEST
    coef_rows = jnp.pad(mean_coef, ((1, 1), (0, 0)), mode='edge')
    field_rows = jnp.pad(field_coef, ((0, 0), (1, 1), (0, 0)), mode='edge')
    solution = guess
    residual = right_side
    for sweep in range(ITERS):
        padded = jnp.pad(solution, ((0, 0), (1, 1), (0, 0)))
        mean_part = operate(padded, coef_rows)
        state = solution.astype(jnp.bfloat16).reshape(BLOCKS, BLK, NX * NY)

        def block_term(index):
            entries = coupling_list[index]
            partner = (entries // FIELDS).astype(jnp.int32)
            field_index = (entries % FIELDS).astype(jnp.int32)
            live_mask = jnp.arange(MAXC).astype(jnp.int32) < pair_count[index]
            onehot = ((field_index[:, None] == jnp.arange(FIELDS).astype(jnp.int32)[None, :]) & live_mask[:, None]).astype(jnp.float32)
            gathered = state[partner].astype(jnp.float32)
            products = jnp.einsum('kab,kbc->kac', coupling[index].astype(jnp.float32), gathered, precision=highest)
            grouped = jnp.einsum('kf,kac->fac', onehot, products, precision=highest).reshape(FIELDS, BLK, NX, NY)
            grouped_pad = jnp.pad(grouped, ((0, 0), (0, 0), (1, 1), (0, 0)))
            return lax.optimization_barrier(jnp.sum(operate(grouped_pad, field_rows[:, None]), axis=0))
        coupled = lax.map(block_term, jnp.arange(BLOCKS).astype(jnp.int32)).reshape(MODES, NX, NY)
        residual = right_side - mean_part - coupled
        solution = solution + relaxation * mean_solve(residual)
    return (solution, residual)
```

```python
import functools
import math

import jax
import jax.numpy as jnp
from jax import lax
from jax.experimental import pallas as pl
from jax.experimental.pallas import tpu as pltpu
from jax.sharding import PartitionSpec as P

ITERS = 2
RELAXATION = 0.6
MIB = 1 << 20


def sine_table(length):
    counter = jnp.arange(length).astype(jnp.float32) + 1.0
    angle = math.pi * counter[:, None] * counter[None, :] / (length + 1)
    return math.sqrt(2.0 / (length + 1)) * jnp.sin(angle)


def eigen_table(first, second):
    along_first = 2.0 * jnp.cos(
        math.pi * (jnp.arange(first).astype(jnp.float32) + 1.0) / (first + 1)
    )
    along_second = 2.0 * jnp.cos(
        math.pi * (jnp.arange(second).astype(jnp.float32) + 1.0) / (second + 1)
    )
    return 4.0 - along_first[:, None] - along_second[None, :]


def stencil_weights(coefs):
    padded = jnp.pad(coefs, [(0, 0), (1, 1), (1, 1)], mode="edge")
    up = 0.5 * (coefs + padded[:, :-2, 1:-1])
    down = 0.5 * (coefs + padded[:, 2:, 1:-1])
    left = 0.5 * (coefs + padded[:, 1:-1, :-2])
    right = 0.5 * (coefs + padded[:, 1:-1, 2:])
    nx, ny = coefs.shape[1:]
    row = lax.broadcasted_iota(jnp.int32, (nx, ny), 0)
    col = lax.broadcasted_iota(jnp.int32, (nx, ny), 1)
    centre = up + down + left + right
    return jnp.stack(
        [
            centre,
            jnp.where(row == 0, 0.0, up),
            jnp.where(row == nx - 1, 0.0, down),
            jnp.where(col == 0, 0.0, left),
            jnp.where(col == ny - 1, 0.0, right),
        ],
        axis=1,
    )


def split(value):
    high = value.astype(jnp.bfloat16)
    low = (value - high.astype(jnp.float32)).astype(jnp.bfloat16)
    return high, low


def split_table(value):
    high = lax.reduce_precision(value, 8, 7)
    return high.astype(jnp.bfloat16), (value - high).astype(jnp.bfloat16)


def pack_kernel(strips, rows, height, x_ref, low_ref, high_ref, out_ref):
    modes, cols = low_ref.shape
    for strip in range(strips):
        for r in range(height + 2):
            row = strip * height + r - 1
            if row < 0:
                value = low_ref[...]
            elif row >= rows:
                value = high_ref[...]
            else:
                value = x_ref[pl.ds(row, modes, stride=rows), :]
            out_ref[strip, :, r * cols : (r + 1) * cols] = value.astype(jnp.bfloat16)


def pack_strips(block, low, high, strips):
    modes, rows, cols = block.shape
    height = rows // strips
    return pl.pallas_call(
        functools.partial(pack_kernel, strips, rows, height),
        out_shape=jax.ShapeDtypeStruct((strips, modes, (height + 2) * cols), jnp.bfloat16),
        compiler_params=pltpu.CompilerParams(vmem_limit_bytes=32 * MIB),
    )(block.reshape(modes * rows, cols), low, high)


def dense_kernel(fields, entry_ref, count_ref, coupling_ref, out_ref):
    block = pl.program_id(0)
    width = coupling_ref.shape[-1]
    out_ref[...] = jnp.zeros_like(out_ref)

    def place(k, carry):
        entry = entry_ref[block, k]
        column = pl.multiple_of((entry // fields) * width, width)
        out_ref[0, entry % fields, :, pl.ds(column, width)] = coupling_ref[0, k]
        return carry

    lax.fori_loop(0, count_ref[block], place, 0)


def dense_coupling(coupling, coupling_list, pair_count, fields):
    blocks, entries, width, _ = coupling.shape
    return pl.pallas_call(
        functools.partial(dense_kernel, fields),
        grid_spec=pltpu.PrefetchScalarGridSpec(
            num_scalar_prefetch=2,
            grid=(blocks,),
            in_specs=[pl.BlockSpec((1, entries, width, width), lambda i, *_: (i, 0, 0, 0))],
            out_specs=pl.BlockSpec(
                (1, fields, width, blocks * width), lambda i, *_: (i, 0, 0, 0)
            ),
        ),
        out_shape=jax.ShapeDtypeStruct((blocks, fields, width, blocks * width), coupling.dtype),
        compiler_params=pltpu.CompilerParams(vmem_limit_bytes=32 * MIB),
    )(coupling_list, pair_count, coupling)


def coupled_kernel(height, cols, matrix_ref, state_ref, weight_ref, out_ref, sums_ref):
    fields, width, depth = matrix_ref.shape[1:]
    sums_ref[...] = jnp.dot(
        matrix_ref[0].reshape(fields * width, depth),
        state_ref[...],
        preferred_element_type=jnp.float32,
    )
    for r in range(height):
        total = None
        from_left = None
        from_right = None
        for f in range(fields):
            rows = slice(f * width, (f + 1) * width)
            above = sums_ref[rows, r * cols : (r + 1) * cols]
            here = sums_ref[rows, (r + 1) * cols : (r + 2) * cols]
            below = sums_ref[rows, (r + 2) * cols : (r + 3) * cols]

            def weight(which):
                at = (f * 5 + which) * height + r
                return weight_ref[at : at + 1, :]

            term = weight(0) * here - weight(1) * above - weight(2) * below
            total = term if total is None else total + term
            rightward = weight(4) * here
            leftward = weight(3) * here
            from_left = rightward if from_left is None else from_left + rightward
            from_right = leftward if from_right is None else from_right + leftward
        total = total - pltpu.roll(from_left, 1, 1) - pltpu.roll(from_right, cols - 1, 1)
        out_ref[:, r * cols : (r + 1) * cols] = total


def coupled_sums(matrix, state, weights):
    blocks, fields, width, depth = matrix.shape
    _, five, height, cols = weights.shape
    cells = state.shape[1]
    return pl.pallas_call(
        functools.partial(coupled_kernel, height, cols),
        grid=(blocks,),
        in_specs=[
            pl.BlockSpec((1, fields, width, depth), lambda i: (i, 0, 0, 0)),
            pl.BlockSpec((depth, cells), lambda i: (0, 0)),
            pl.BlockSpec((fields * five * height, cols), lambda i: (0, 0)),
        ],
        out_specs=pl.BlockSpec((width, height * cols), lambda i: (i, 0)),
        out_shape=jax.ShapeDtypeStruct((blocks * width, height * cols), jnp.float32),
        scratch_shapes=[pltpu.VMEM((fields * width, cells), jnp.float32)],
        compiler_params=pltpu.CompilerParams(vmem_limit_bytes=40 * MIB),
    )(matrix, state, weights.reshape(fields * five * height, cols))


TOGETHER = 4
GROUP = 16


def solve(resid, right_ref, left_ref, scale_ref):
    nx, ny = resid[0].shape

    def along_cols(fields):
        high, low = split(jnp.concatenate(fields, axis=0))
        both = jnp.dot(
            jnp.concatenate([high, low], axis=1),
            right_ref[...],
            preferred_element_type=jnp.float32,
        )
        both = both[:, :ny] + both[:, ny:]
        return [both[i * nx : (i + 1) * nx] for i in range(len(fields))]

    def along_rows(wide):
        high, low = split(wide)
        both = jnp.dot(
            left_ref[...],
            jnp.concatenate([high, low], axis=0),
            preferred_element_type=jnp.float32,
        )
        return both[:nx] + both[nx:]

    wide = jnp.concatenate(along_cols(resid), axis=1)
    wide = along_rows(wide)
    scale = scale_ref[...]
    wide = wide * jnp.concatenate([scale] * len(resid), axis=1)
    wide = along_rows(wide)
    return along_cols([wide[:, i * ny : (i + 1) * ny] for i in range(len(resid))])


def sweep_kernel(
    mode_count,
    slab_count,
    last,
    current_ref,
    right_side_ref,
    coupled_ref,
    weight_ref,
    right_ref,
    left_ref,
    scale_ref,
    *refs,
):
    if last:
        solution_ref, residual_ref, turned_ref = refs
    else:
        solution_ref, state_ref, turned_ref = refs
    nx, ny = scale_ref.shape
    group = coupled_ref.shape[1]
    height = nx // (mode_count * slab_count)

    for source in range(mode_count * slab_count):
        first = ((source % slab_count) * mode_count + source // slab_count) * height
        for r in range(height):
            turned_ref[(first + r) * group : (first + r + 1) * group, :] = coupled_ref[
                source, :, r * ny : (r + 1) * ny
            ]

    def several(step, carry):
        values = []
        resid = []
        for i in range(TOGETHER):
            mode = step * TOGETHER + i
            if last:
                here = current_ref[mode]
            else:
                here = current_ref[:, mode].reshape(nx, ny)
            mean = (
                weight_ref[0] * here
                - weight_ref[1] * pltpu.roll(here, 1, 0)
                - weight_ref[2] * pltpu.roll(here, nx - 1, 0)
                - pltpu.roll(weight_ref[4] * here, 1, 1)
                - pltpu.roll(weight_ref[3] * here, ny - 1, 1)
            )
            coupled = turned_ref[pl.ds(mode, nx, stride=group), :]
            value = right_side_ref[:, mode].reshape(nx, ny) - mean - coupled
            if last:
                residual_ref[:, mode] = value.reshape(slab_count, nx // slab_count, ny)
            values.append(here)
            resid.append(value)
        change = solve(resid, right_ref, left_ref, scale_ref)
        for i in range(TOGETHER):
            mode = step * TOGETHER + i
            value = values[i] + change[i]
            if last:
                solution_ref[:, mode] = value.reshape(slab_count, nx // slab_count, ny)
            else:
                solution_ref[mode] = value
                turned_ref[pl.ds(mode, nx, stride=group), :] = value
        return carry

    lax.fori_loop(0, group // TOGETHER, several, 0)

    if not last:
        for target in range(mode_count * slab_count):
            first = ((target % slab_count) * mode_count + target // slab_count) * height
            for r in range(height + 2):
                row = first + r - 1
                if 0 <= row < nx:
                    value = turned_ref[row * group : (row + 1) * group, :].astype(jnp.bfloat16)
                else:
                    value = jnp.zeros((group, ny), jnp.bfloat16)
                state_ref[target, :, r * ny : (r + 1) * ny] = value


def sweep(current, right_side, coupled, weights, tables, mode_count, slab_count, last):
    right, left, scale = tables
    nx, ny = scale.shape
    modes = right_side.shape[1]
    devices = mode_count * slab_count
    height = nx // devices
    whole = lambda a: pl.BlockSpec(a.shape, lambda g: (0,) * a.ndim)
    slabs = pl.BlockSpec((slab_count, GROUP, nx // slab_count, ny), lambda g: (0, g, 0, 0))
    fields = pl.BlockSpec((GROUP, nx, ny), lambda g: (g, 0, 0))
    strips = pl.BlockSpec((devices, GROUP, height * ny), lambda g: (0, g, 0))
    halo_strips = pl.BlockSpec((devices, GROUP, (height + 2) * ny), lambda g: (0, g, 0))
    slabs_shape = jax.ShapeDtypeStruct((slab_count, modes, nx // slab_count, ny), jnp.float32)
    if last:
        out_specs = [slabs, slabs]
        out_shape = [slabs_shape, slabs_shape]
    else:
        out_specs = [fields, halo_strips]
        out_shape = [
            jax.ShapeDtypeStruct((modes, nx, ny), jnp.float32),
            jax.ShapeDtypeStruct((devices, modes, (height + 2) * ny), jnp.bfloat16),
        ]
    return pl.pallas_call(
        functools.partial(sweep_kernel, mode_count, slab_count, last),
        grid=(modes // GROUP,),
        in_specs=[
            fields if last else slabs,
            slabs,
            strips,
            whole(weights),
            whole(right),
            whole(left),
            whole(scale),
        ],
        out_specs=out_specs,
        out_shape=out_shape,
        scratch_shapes=[pltpu.VMEM((nx * GROUP, ny), jnp.float32)],
        compiler_params=pltpu.CompilerParams(vmem_limit_bytes=48 * MIB),
    )(current, right_side, coupled, weights, right, left, scale)


def local(guess, right_side, mean_coef, field_coef, coupling, coupling_list, pair_count):
    mode_count = lax.axis_size("mode")
    slab_count = lax.axis_size("slab")
    both = ("mode", "slab")
    modes, rows, cols = guess.shape
    fields = field_coef.shape[0]
    nx = rows * slab_count
    devices = mode_count * slab_count
    height = nx // devices
    share = modes // slab_count

    forward = [(i, i + 1) for i in range(slab_count - 1)]
    backward = [(i + 1, i) for i in range(slab_count - 1)]
    low = lax.ppermute(guess[:, -1].astype(jnp.bfloat16), "slab", forward)
    high = lax.ppermute(guess[:, 0].astype(jnp.bfloat16), "slab", backward)
    strips = pack_strips(guess, low, high, mode_count)
    state = lax.all_to_all(strips, "mode", 0, 0, tiled=True)
    state = state.reshape(mode_count * modes, (height + 2) * cols)

    def to_fields(block):
        moved = lax.all_to_all(block, "slab", 0, 0, tiled=True)
        return moved.reshape(slab_count, share, rows, cols)

    def to_slabs(block):
        flat = block.reshape(modes, rows, cols)
        return lax.all_to_all(flat, "slab", 0, 0, tiled=True)

    current = to_fields(guess)
    right = to_fields(right_side)

    coefs = jnp.concatenate([mean_coef[None], field_coef], 0)
    coefs = lax.all_gather(coefs, "slab", axis=1, tiled=True)
    weights = stencil_weights(coefs)
    strip = lax.axis_index("slab") * mode_count + lax.axis_index("mode")
    strip_weights = lax.dynamic_slice_in_dim(weights[1:], strip * height, height, axis=2)
    matrix = dense_coupling(coupling, coupling_list, pair_count, fields)

    row_high, row_low = split_table(sine_table(nx))
    col_high, col_low = split_table(sine_table(cols))
    tables = (
        jnp.concatenate(
            [
                jnp.concatenate([col_high, col_low], 1),
                jnp.concatenate([col_high, jnp.zeros_like(col_low)], 1),
            ],
            0,
        ),
        jnp.concatenate(
            [
                jnp.concatenate([row_high, row_high], 1),
                jnp.concatenate([row_low, jnp.zeros_like(row_low)], 1),
            ],
            0,
        ),
        RELAXATION / eigen_table(nx, cols),
    )

    for number in range(ITERS):
        last = number == ITERS - 1
        sums = coupled_sums(matrix, state, strip_weights)
        sums = lax.all_to_all(sums, both, 0, 0, tiled=True)
        sums = sums.reshape(devices, share, height * cols)
        current, other = sweep(
            current, right, sums, weights[0], tables, mode_count, slab_count, last
        )
        if not last:
            state = other.reshape(devices * share, (height + 2) * cols)
            state = lax.all_to_all(state, both, 0, 0, tiled=True)
    return to_slabs(current), to_slabs(other)


def solution(mesh):
    placed = (
        P("mode", "slab", None),
        P("mode", "slab", None),
        P("slab", None),
        P(None, "slab", None),
        P(),
        P(),
        P(),
    )
    return jax.shard_map(
        local,
        mesh=mesh,
        in_specs=placed,
        out_specs=(P("mode", "slab", None), P("mode", "slab", None)),
        check_vma=False,
    )
```

```python
import functools
import math

import jax
import jax.numpy as jnp
from jax import lax
from jax.experimental import pallas as pl
from jax.experimental.pallas import tpu as pltpu
from jax.sharding import PartitionSpec as P

ITERS = 2
RELAXATION = 0.6
MIB = 1 << 20


def sine_table(length):
    counter = jnp.arange(length).astype(jnp.float32) + 1.0
    angle = math.pi * counter[:, None] * counter[None, :] / (length + 1)
    return math.sqrt(2.0 / (length + 1)) * jnp.sin(angle)


def eigen_table(first, second):
    along_first = 2.0 * jnp.cos(
        math.pi * (jnp.arange(first).astype(jnp.float32) + 1.0) / (first + 1)
    )
    along_second = 2.0 * jnp.cos(
        math.pi * (jnp.arange(second).astype(jnp.float32) + 1.0) / (second + 1)
    )
    return 4.0 - along_first[:, None] - along_second[None, :]


def stencil_weights(coefs):
    padded = jnp.pad(coefs, [(0, 0), (1, 1), (1, 1)], mode="edge")
    up = 0.5 * (coefs + padded[:, :-2, 1:-1])
    down = 0.5 * (coefs + padded[:, 2:, 1:-1])
    left = 0.5 * (coefs + padded[:, 1:-1, :-2])
    right = 0.5 * (coefs + padded[:, 1:-1, 2:])
    nx, ny = coefs.shape[1:]
    row = lax.broadcasted_iota(jnp.int32, (nx, ny), 0)
    col = lax.broadcasted_iota(jnp.int32, (nx, ny), 1)
    centre = up + down + left + right
    return jnp.stack(
        [
            centre,
            jnp.where(row == 0, 0.0, up),
            jnp.where(row == nx - 1, 0.0, down),
            jnp.where(col == 0, 0.0, left),
            jnp.where(col == ny - 1, 0.0, right),
        ],
        axis=1,
    )


def split(value):
    high = value.astype(jnp.bfloat16)
    low = (value - high.astype(jnp.float32)).astype(jnp.bfloat16)
    return high, low


def split_table(value):
    high = lax.reduce_precision(value, 8, 7)
    return high.astype(jnp.bfloat16), (value - high).astype(jnp.bfloat16)


def pack_kernel(strips, rows, height, x_ref, low_ref, high_ref, out_ref):
    modes, cols = low_ref.shape
    for strip in range(strips):
        for r in range(height + 2):
            row = strip * height + r - 1
            if row < 0:
                value = low_ref[...]
            elif row >= rows:
                value = high_ref[...]
            else:
                value = x_ref[pl.ds(row, modes, stride=rows), :]
            out_ref[strip, :, r * cols : (r + 1) * cols] = value.astype(jnp.bfloat16)


def pack_strips(block, low, high, strips):
    modes, rows, cols = block.shape
    height = rows // strips
    return pl.pallas_call(
        functools.partial(pack_kernel, strips, rows, height),
        out_shape=jax.ShapeDtypeStruct((strips, modes, (height + 2) * cols), jnp.bfloat16),
        compiler_params=pltpu.CompilerParams(vmem_limit_bytes=32 * MIB),
    )(block.reshape(modes * rows, cols), low, high)


def dense_kernel(fields, entry_ref, count_ref, coupling_ref, out_ref):
    block = pl.program_id(0)
    width = coupling_ref.shape[-1]
    out_ref[...] = jnp.zeros_like(out_ref)

    def place(k, carry):
        entry = entry_ref[block, k]
        column = pl.multiple_of((entry // fields) * width, width)
        out_ref[0, entry % fields, :, pl.ds(column, width)] = coupling_ref[0, k]
        return carry

    lax.fori_loop(0, count_ref[block], place, 0)


def dense_coupling(coupling, coupling_list, pair_count, fields):
    blocks, entries, width, _ = coupling.shape
    return pl.pallas_call(
        functools.partial(dense_kernel, fields),
        grid_spec=pltpu.PrefetchScalarGridSpec(
            num_scalar_prefetch=2,
            grid=(blocks,),
            in_specs=[pl.BlockSpec((1, entries, width, width), lambda i, *_: (i, 0, 0, 0))],
            out_specs=pl.BlockSpec(
                (1, fields, width, blocks * width), lambda i, *_: (i, 0, 0, 0)
            ),
        ),
        out_shape=jax.ShapeDtypeStruct((blocks, fields, width, blocks * width), coupling.dtype),
        compiler_params=pltpu.CompilerParams(vmem_limit_bytes=32 * MIB),
    )(coupling_list, pair_count, coupling)


def coupled_kernel(height, cols, matrix_ref, state_ref, weight_ref, out_ref, sums_ref):
    fields, width, depth = matrix_ref.shape[1:]
    sums_ref[...] = jnp.dot(
        matrix_ref[0].reshape(fields * width, depth),
        state_ref[...],
        preferred_element_type=jnp.float32,
    )
    for r in range(height):
        total = None
        from_left = None
        from_right = None
        for f in range(fields):
            rows = slice(f * width, (f + 1) * width)
            above = sums_ref[rows, r * cols : (r + 1) * cols]
            here = sums_ref[rows, (r + 1) * cols : (r + 2) * cols]
            below = sums_ref[rows, (r + 2) * cols : (r + 3) * cols]

            def weight(which):
                at = (f * 5 + which) * height + r
                return weight_ref[at : at + 1, :]

            term = weight(0) * here - weight(1) * above - weight(2) * below
            total = term if total is None else total + term
            rightward = weight(4) * here
            leftward = weight(3) * here
            from_left = rightward if from_left is None else from_left + rightward
            from_right = leftward if from_right is None else from_right + leftward
        total = total - pltpu.roll(from_left, 1, 1) - pltpu.roll(from_right, cols - 1, 1)
        out_ref[:, r * cols : (r + 1) * cols] = total


def coupled_sums(matrix, state, weights):
    blocks, fields, width, depth = matrix.shape
    _, five, height, cols = weights.shape
    cells = state.shape[1]
    return pl.pallas_call(
        functools.partial(coupled_kernel, height, cols),
        grid=(blocks,),
        in_specs=[
            pl.BlockSpec((1, fields, width, depth), lambda i: (i, 0, 0, 0)),
            pl.BlockSpec((depth, cells), lambda i: (0, 0)),
            pl.BlockSpec((fields * five * height, cols), lambda i: (0, 0)),
        ],
        out_specs=pl.BlockSpec((width, height * cols), lambda i: (i, 0)),
        out_shape=jax.ShapeDtypeStruct((blocks * width, height * cols), jnp.float32),
        scratch_shapes=[pltpu.VMEM((fields * width, cells), jnp.float32)],
        compiler_params=pltpu.CompilerParams(vmem_limit_bytes=40 * MIB),
    )(matrix, state, weights.reshape(fields * five * height, cols))


TOGETHER = 4
GROUP = 16


def solve(resid, right_ref, left_ref, scale_ref):
    nx, ny = resid[0].shape

    def along_cols(fields):
        high, low = split(jnp.concatenate(fields, axis=0))
        both = jnp.dot(
            jnp.concatenate([high, low], axis=1),
            right_ref[...],
            preferred_element_type=jnp.float32,
        )
        both = both[:, :ny] + both[:, ny:]
        return [both[i * nx : (i + 1) * nx] for i in range(len(fields))]

    def along_rows(wide):
        high, low = split(wide)
        both = jnp.dot(
            left_ref[...],
            jnp.concatenate([high, low], axis=0),
            preferred_element_type=jnp.float32,
        )
        return both[:nx] + both[nx:]

    wide = jnp.concatenate(along_cols(resid), axis=1)
    wide = along_rows(wide)
    scale = scale_ref[...]
    wide = wide * jnp.concatenate([scale] * len(resid), axis=1)
    wide = along_rows(wide)
    return along_cols([wide[:, i * ny : (i + 1) * ny] for i in range(len(resid))])


def mean_kernel(current_ref, right_side_ref, weight_ref, out_ref):
    nx, ny = weight_ref.shape[1:]

    def one(mode, carry):
        here = current_ref[:, mode].reshape(nx, ny)
        mean = (
            weight_ref[0] * here
            - weight_ref[1] * pltpu.roll(here, 1, 0)
            - weight_ref[2] * pltpu.roll(here, nx - 1, 0)
            - pltpu.roll(weight_ref[4] * here, 1, 1)
            - pltpu.roll(weight_ref[3] * here, ny - 1, 1)
        )
        value = right_side_ref[:, mode].reshape(nx, ny) - mean
        out_ref[:, mode] = value.reshape(out_ref.shape[0], -1, ny)
        return carry

    lax.fori_loop(0, out_ref.shape[1], one, 0)


def turn_in(turned_ref, coupled_ref, mode_count, slab_count, height, ny):
    group = coupled_ref.shape[1]
    for source in range(mode_count * slab_count):
        first = ((source % slab_count) * mode_count + source // slab_count) * height
        for r in range(height):
            turned_ref[(first + r) * group : (first + r + 1) * group, :] = coupled_ref[
                source, :, r * ny : (r + 1) * ny
            ]


def step_kernel(
    mode_count,
    slab_count,
    current_ref,
    base_ref,
    coupled_ref,
    right_ref,
    left_ref,
    scale_ref,
    solution_ref,
    state_ref,
    turned_ref,
):
    nx, ny = scale_ref.shape
    group = coupled_ref.shape[1]
    height = nx // (mode_count * slab_count)
    turn_in(turned_ref, coupled_ref, mode_count, slab_count, height, ny)

    def several(step, carry):
        first = step * TOGETHER
        resid = []
        for i in range(TOGETHER):
            coupled = turned_ref[pl.ds(first + i, nx, stride=group), :]
            resid.append(base_ref[:, first + i].reshape(nx, ny) - coupled)
        change = solve(resid, right_ref, left_ref, scale_ref)
        for i in range(TOGETHER):
            value = current_ref[:, first + i].reshape(nx, ny) + change[i]
            solution_ref[:, first + i] = value.reshape(slab_count, nx // slab_count, ny)
            turned_ref[pl.ds(first + i, nx, stride=group), :] = value
        return carry

    lax.fori_loop(0, group // TOGETHER, several, 0)

    for target in range(mode_count * slab_count):
        first = ((target % slab_count) * mode_count + target // slab_count) * height
        for r in range(height + 2):
            row = first + r - 1
            if 0 <= row < nx:
                value = turned_ref[row * group : (row + 1) * group, :].astype(jnp.bfloat16)
            else:
                value = jnp.zeros((group, ny), jnp.bfloat16)
            state_ref[target, :, r * ny : (r + 1) * ny] = value


def residual_kernel(mode_count, slab_count, base_ref, coupled_ref, out_ref, turned_ref):
    group = coupled_ref.shape[1]
    ny = base_ref.shape[-1]
    nx = turned_ref.shape[0] // group
    height = nx // (mode_count * slab_count)
    turn_in(turned_ref, coupled_ref, mode_count, slab_count, height, ny)

    def one(mode, carry):
        coupled = turned_ref[pl.ds(mode, nx, stride=group), :]
        out_ref[:, mode] = base_ref[:, mode] - coupled.reshape(slab_count, nx // slab_count, ny)
        return carry

    lax.fori_loop(0, group, one, 0)


def correct_kernel(current_ref, resid_ref, right_ref, left_ref, scale_ref, out_ref):
    nx, ny = scale_ref.shape

    def several(step, carry):
        first = step * TOGETHER
        resid = [resid_ref[:, first + i].reshape(nx, ny) for i in range(TOGETHER)]
        change = solve(resid, right_ref, left_ref, scale_ref)
        for i in range(TOGETHER):
            shape = out_ref.shape[:1] + out_ref.shape[2:]
            out_ref[:, first + i] = current_ref[:, first + i] + change[i].reshape(shape)
        return carry

    lax.fori_loop(0, out_ref.shape[1] // TOGETHER, several, 0)


def whole(array):
    return pl.BlockSpec(array.shape, lambda g: (0,) * array.ndim)


def slabs_of(array):
    slab_count, _, rows, ny = array.shape
    return pl.BlockSpec((slab_count, GROUP, rows, ny), lambda g: (0, g, 0, 0))


def strips_of(shape):
    return pl.BlockSpec((shape[0], GROUP, shape[2]), lambda g: (0, g, 0))


def per_group(kernel, operands, in_specs, out_shape, out_specs, scratch=(), flops=0):
    moved = sum(a.size * a.dtype.itemsize for a in operands)
    return pl.pallas_call(
        kernel,
        grid=(operands[0].shape[1] // GROUP,),
        in_specs=in_specs,
        out_specs=out_specs,
        out_shape=out_shape,
        scratch_shapes=scratch,
        cost_estimate=pl.CostEstimate(flops=flops, bytes_accessed=2 * moved, transcendentals=0),
        compiler_params=pltpu.CompilerParams(vmem_limit_bytes=48 * MIB),
    )(*operands)


def mean_part(current, right_side, weights):
    slabs = slabs_of(current)
    return per_group(
        mean_kernel,
        (current, right_side, weights),
        [slabs, slabs, whole(weights)],
        jax.ShapeDtypeStruct(current.shape, jnp.float32),
        slabs,
    )


def solve_flops(array, tables):
    nx, ny = tables[2].shape
    return array.shape[1] * 8 * 3 * nx * ny * (nx + ny) // 2


def step(current, base, coupled, tables, mode_count, slab_count):
    nx, ny = tables[2].shape
    slabs = slabs_of(current)
    devices, modes, cells = coupled.shape
    halo = (devices, modes, cells + 2 * ny)
    return per_group(
        functools.partial(step_kernel, mode_count, slab_count),
        (current, base, coupled, *tables),
        [slabs, slabs, strips_of(coupled.shape), *map(whole, tables)],
        [
            jax.ShapeDtypeStruct(current.shape, jnp.float32),
            jax.ShapeDtypeStruct(halo, jnp.bfloat16),
        ],
        [slabs, strips_of(halo)],
        [pltpu.VMEM((nx * GROUP, ny), jnp.float32)],
        solve_flops(current, tables),
    )


def last_residual(base, coupled, mode_count, slab_count):
    slab, _, rows, ny = base.shape
    slabs = slabs_of(base)
    return per_group(
        functools.partial(residual_kernel, mode_count, slab_count),
        (base, coupled),
        [slabs, strips_of(coupled.shape)],
        jax.ShapeDtypeStruct(base.shape, jnp.float32),
        slabs,
        [pltpu.VMEM((slab * rows * GROUP, ny), jnp.float32)],
    )


def correct(current, resid, tables):
    slabs = slabs_of(current)
    return per_group(
        correct_kernel,
        (current, resid, *tables),
        [slabs, slabs, *map(whole, tables)],
        jax.ShapeDtypeStruct(current.shape, jnp.float32),
        slabs,
        (),
        solve_flops(current, tables),
    )


def regroup(block, axis):
    count = lax.axis_size(axis)
    here = lax.axis_index(axis)
    own = lax.dynamic_index_in_dim(block, here, 0)
    out = lax.dynamic_update_slice_in_dim(jnp.zeros_like(block), own, here, 0)
    for shift in range(1, count):
        target = lax.rem(here + shift, count)
        source = lax.rem(here + count - shift, count)
        moved = lax.ppermute(
            lax.dynamic_index_in_dim(block, target, 0),
            axis,
            [(i, (i + shift) % count) for i in range(count)],
        )
        out = lax.dynamic_update_slice_in_dim(out, moved, source, 0)
    return out


def local(guess, right_side, mean_coef, field_coef, coupling, coupling_list, pair_count):
    mode_count = lax.axis_size("mode")
    slab_count = lax.axis_size("slab")
    both = ("mode", "slab")
    modes, rows, cols = guess.shape
    fields = field_coef.shape[0]
    nx = rows * slab_count
    devices = mode_count * slab_count
    height = nx // devices
    share = modes // slab_count

    forward = [(i, i + 1) for i in range(slab_count - 1)]
    backward = [(i + 1, i) for i in range(slab_count - 1)]
    low = lax.ppermute(guess[:, -1].astype(jnp.bfloat16), "slab", forward)
    high = lax.ppermute(guess[:, 0].astype(jnp.bfloat16), "slab", backward)
    strips = pack_strips(guess, low, high, mode_count)
    state = lax.all_to_all(strips, "mode", 0, 0, tiled=True)
    state = state.reshape(mode_count * modes, (height + 2) * cols)

    def to_fields(block):
        return regroup(block.reshape(slab_count, share, rows, cols), "slab")

    def to_slabs(block):
        flat = block.reshape(modes, rows, cols)
        return lax.all_to_all(flat, "slab", 0, 0, tiled=True)

    current = to_fields(guess)
    right = to_fields(right_side)

    coefs = jnp.concatenate([mean_coef[None], field_coef], 0)
    coefs = lax.all_gather(coefs, "slab", axis=1, tiled=True)
    weights = stencil_weights(coefs)
    strip = lax.axis_index("slab") * mode_count + lax.axis_index("mode")
    strip_weights = lax.dynamic_slice_in_dim(weights[1:], strip * height, height, axis=2)
    matrix = dense_coupling(coupling, coupling_list, pair_count, fields)

    row_high, row_low = split_table(sine_table(nx))
    col_high, col_low = split_table(sine_table(cols))
    tables = (
        jnp.concatenate(
            [
                jnp.concatenate([col_high, col_low], 1),
                jnp.concatenate([col_high, jnp.zeros_like(col_low)], 1),
            ],
            0,
        ),
        jnp.concatenate(
            [
                jnp.concatenate([row_high, row_high], 1),
                jnp.concatenate([row_low, jnp.zeros_like(row_low)], 1),
            ],
            0,
        ),
        RELAXATION / eigen_table(nx, cols),
    )

    for number in range(ITERS):
        base = mean_part(current, right, weights[0])
        sums = coupled_sums(matrix, state, strip_weights)
        sums = lax.all_to_all(sums, both, 0, 0, tiled=True)
        sums = sums.reshape(devices, share, height * cols)
        if number < ITERS - 1:
            current, state = step(current, base, sums, tables, mode_count, slab_count)
            state = state.reshape(devices * share, (height + 2) * cols)
            state = lax.all_to_all(state, both, 0, 0, tiled=True)
        else:
            resid = last_residual(base, sums, mode_count, slab_count)
            current = correct(current, resid, tables)
    return to_slabs(current), to_slabs(resid)


def solution(mesh):
    placed = (
        P("mode", "slab", None),
        P("mode", "slab", None),
        P("slab", None),
        P(None, "slab", None),
        P(),
        P(),
        P(),
    )
    return jax.shard_map(
        local,
        mesh=mesh,
        in_specs=placed,
        out_specs=(P("mode", "slab", None), P("mode", "slab", None)),
        check_vma=False,
    )
```

```python
import functools
import math

import jax
import jax.numpy as jnp
from jax import lax
from jax.experimental import pallas as pl
from jax.experimental.pallas import tpu as pltpu
from jax.sharding import PartitionSpec as P

ITERS = 2
RELAXATION = 0.6
MIB = 1 << 20


def sine_table(length):
    counter = jnp.arange(length).astype(jnp.float32) + 1.0
    angle = math.pi * counter[:, None] * counter[None, :] / (length + 1)
    return math.sqrt(2.0 / (length + 1)) * jnp.sin(angle)


def eigen_table(first, second):
    along_first = 2.0 * jnp.cos(
        math.pi * (jnp.arange(first).astype(jnp.float32) + 1.0) / (first + 1)
    )
    along_second = 2.0 * jnp.cos(
        math.pi * (jnp.arange(second).astype(jnp.float32) + 1.0) / (second + 1)
    )
    return 4.0 - along_first[:, None] - along_second[None, :]


def stencil_weights(coefs):
    padded = jnp.pad(coefs, [(0, 0), (1, 1), (1, 1)], mode="edge")
    up = 0.5 * (coefs + padded[:, :-2, 1:-1])
    down = 0.5 * (coefs + padded[:, 2:, 1:-1])
    left = 0.5 * (coefs + padded[:, 1:-1, :-2])
    right = 0.5 * (coefs + padded[:, 1:-1, 2:])
    nx, ny = coefs.shape[1:]
    row = lax.broadcasted_iota(jnp.int32, (nx, ny), 0)
    col = lax.broadcasted_iota(jnp.int32, (nx, ny), 1)
    centre = up + down + left + right
    return jnp.stack(
        [
            centre,
            jnp.where(row == 0, 0.0, up),
            jnp.where(row == nx - 1, 0.0, down),
            jnp.where(col == 0, 0.0, left),
            jnp.where(col == ny - 1, 0.0, right),
        ],
        axis=1,
    )


def split(value):
    high = value.astype(jnp.bfloat16)
    low = (value - high.astype(jnp.float32)).astype(jnp.bfloat16)
    return high, low


def split_table(value):
    high = lax.reduce_precision(value, 8, 7)
    return high.astype(jnp.bfloat16), (value - high).astype(jnp.bfloat16)


def pack_kernel(rows, height, x_ref, out_ref):
    strips, modes, cells = out_ref.shape
    cols = cells // height
    for strip in range(strips):
        for r in range(height):
            value = x_ref[pl.ds(strip * height + r, modes, stride=rows), :]
            out_ref[strip, :, r * cols : (r + 1) * cols] = value.astype(jnp.bfloat16)


def pack_strips(block, strips):
    modes, rows, cols = block.shape
    height = rows // strips
    return pl.pallas_call(
        functools.partial(pack_kernel, rows, height),
        out_shape=jax.ShapeDtypeStruct((strips, modes, height * cols), jnp.bfloat16),
        compiler_params=pltpu.CompilerParams(vmem_limit_bytes=32 * MIB),
    )(block.reshape(modes * rows, cols))


def dense_kernel(fields, entry_ref, count_ref, coupling_ref, out_ref):
    block = pl.program_id(0)
    width = coupling_ref.shape[-1]
    out_ref[...] = jnp.zeros_like(out_ref)

    def place(k, carry):
        entry = entry_ref[block, k]
        column = pl.multiple_of((entry // fields) * width, width)
        out_ref[0, entry % fields, :, pl.ds(column, width)] = coupling_ref[0, k]
        return carry

    lax.fori_loop(0, count_ref[block], place, 0)


def dense_coupling(coupling, coupling_list, pair_count, fields):
    blocks, entries, width, _ = coupling.shape
    return pl.pallas_call(
        functools.partial(dense_kernel, fields),
        grid_spec=pltpu.PrefetchScalarGridSpec(
            num_scalar_prefetch=2,
            grid=(blocks,),
            in_specs=[pl.BlockSpec((1, entries, width, width), lambda i, *_: (i, 0, 0, 0))],
            out_specs=pl.BlockSpec(
                (1, fields, width, blocks * width), lambda i, *_: (i, 0, 0, 0)
            ),
        ),
        out_shape=jax.ShapeDtypeStruct((blocks, fields, width, blocks * width), coupling.dtype),
        compiler_params=pltpu.CompilerParams(vmem_limit_bytes=32 * MIB),
    )(coupling_list, pair_count, coupling)


def weight_row(weight_ref, height, field, which, r):
    at = (field * 5 + which) * height + r
    return weight_ref[at : at + 1, :]


def inner_kernel(height, cols, matrix_ref, state_ref, weight_ref, out_ref, sums_ref):
    fields, width, depth = matrix_ref.shape[1:]
    sums_ref[...] = jnp.dot(
        matrix_ref[0].reshape(fields * width, depth),
        state_ref[...],
        preferred_element_type=jnp.float32,
    )
    for r in range(height):
        total = 0.0
        from_left = 0.0
        from_right = 0.0
        for f in range(fields):

            def row(at):
                return sums_ref[f * width : (f + 1) * width, at * cols : (at + 1) * cols]

            weight = functools.partial(weight_row, weight_ref, height, f)
            here = row(r)
            total = total + weight(0, r) * here
            if r > 0:
                total = total - weight(1, r) * row(r - 1)
            if r < height - 1:
                total = total - weight(2, r) * row(r + 1)
            from_left = from_left + weight(4, r) * here
            from_right = from_right + weight(3, r) * here
        total = total - pltpu.roll(from_left, 1, 1) - pltpu.roll(from_right, cols - 1, 1)
        out_ref[:, r * cols : (r + 1) * cols] = total


def border_kernel(height, cols, matrix_ref, above_ref, below_ref, weight_ref, inner_ref, out_ref):
    fields, width, depth = matrix_ref.shape[1:]
    matrix = matrix_ref[0].reshape(fields * width, depth)
    border = jnp.concatenate([above_ref[...], below_ref[...]], axis=1)
    sums = jnp.dot(matrix, border, preferred_element_type=jnp.float32)
    for r in range(height):
        total = inner_ref[:, r * cols : (r + 1) * cols]
        for f in range(fields):
            part = sums[f * width : (f + 1) * width]
            if r == 0:
                total = total - weight_row(weight_ref, height, f, 1, r) * part[:, :cols]
            if r == height - 1:
                total = total - weight_row(weight_ref, height, f, 2, r) * part[:, cols:]
        out_ref[:, r * cols : (r + 1) * cols] = total


def coupled_sums(matrix, state, weights, both):
    blocks, fields, width, depth = matrix.shape
    _, five, height, cols = weights.shape
    cells = state.shape[1]
    weights = weights.reshape(fields * five * height, cols)
    mode_count = lax.axis_size("mode")
    slab_count = lax.axis_size("slab")
    place = [
        (t % mode_count) * slab_count + t // mode_count for t in range(mode_count * slab_count)
    ]
    onward = list(zip(place[:-1], place[1:]))
    above = lax.ppermute(state[:, -cols:], both, onward)
    below = lax.ppermute(state[:, :cols], both, [(b, a) for a, b in onward])
    matrix_spec = pl.BlockSpec((1, fields, width, depth), lambda i: (i, 0, 0, 0))
    weight_spec = pl.BlockSpec(weights.shape, lambda i: (0, 0))
    sums_spec = pl.BlockSpec((width, cells), lambda i: (i, 0))
    sums_shape = jax.ShapeDtypeStruct((blocks * width, cells), jnp.float32)
    params = pltpu.CompilerParams(vmem_limit_bytes=40 * MIB)
    inner = pl.pallas_call(
        functools.partial(inner_kernel, height, cols),
        grid=(blocks,),
        in_specs=[matrix_spec, pl.BlockSpec((depth, cells), lambda i: (0, 0)), weight_spec],
        out_specs=sums_spec,
        out_shape=sums_shape,
        scratch_shapes=[pltpu.VMEM((fields * width, cells), jnp.float32)],
        cost_estimate=pl.CostEstimate(
            flops=2 * matrix.size * cells, bytes_accessed=2 * matrix.size, transcendentals=0
        ),
        compiler_params=params,
    )(matrix, state, weights)
    border_spec = pl.BlockSpec((depth, cols), lambda i: (0, 0))
    return pl.pallas_call(
        functools.partial(border_kernel, height, cols),
        grid=(blocks,),
        in_specs=[matrix_spec, border_spec, border_spec, weight_spec, sums_spec],
        out_specs=sums_spec,
        out_shape=sums_shape,
        compiler_params=params,
    )(matrix, above, below, weights, inner)


TOGETHER = 4
GROUP = 16


def solve(resid, right_ref, left_ref, scale_ref):
    nx, ny = resid[0].shape

    def along_cols(fields):
        high, low = split(jnp.concatenate(fields, axis=0))
        both = jnp.dot(
            jnp.concatenate([high, low], axis=1),
            right_ref[...],
            preferred_element_type=jnp.float32,
        )
        both = both[:, :ny] + both[:, ny:]
        return [both[i * nx : (i + 1) * nx] for i in range(len(fields))]

    def along_rows(wide):
        high, low = split(wide)
        both = jnp.dot(
            left_ref[...],
            jnp.concatenate([high, low], axis=0),
            preferred_element_type=jnp.float32,
        )
        return both[:nx] + both[nx:]

    wide = jnp.concatenate(along_cols(resid), axis=1)
    wide = along_rows(wide)
    scale = scale_ref[...]
    wide = wide * jnp.concatenate([scale] * len(resid), axis=1)
    wide = along_rows(wide)
    return along_cols([wide[:, i * ny : (i + 1) * ny] for i in range(len(resid))])


def mean_kernel(current_ref, right_side_ref, weight_ref, out_ref):
    nx, ny = weight_ref.shape[1:]

    def one(mode, carry):
        here = current_ref[:, mode].reshape(nx, ny)
        mean = (
            weight_ref[0] * here
            - weight_ref[1] * pltpu.roll(here, 1, 0)
            - weight_ref[2] * pltpu.roll(here, nx - 1, 0)
            - pltpu.roll(weight_ref[4] * here, 1, 1)
            - pltpu.roll(weight_ref[3] * here, ny - 1, 1)
        )
        value = right_side_ref[:, mode].reshape(nx, ny) - mean
        out_ref[:, mode] = value.reshape(out_ref.shape[0], -1, ny)
        return carry

    lax.fori_loop(0, out_ref.shape[1], one, 0)


def turn_in(turned_ref, coupled_ref, mode_count, slab_count, height, ny):
    group = coupled_ref.shape[1]
    for source in range(mode_count * slab_count):
        first = ((source % slab_count) * mode_count + source // slab_count) * height
        for r in range(height):
            turned_ref[(first + r) * group : (first + r + 1) * group, :] = coupled_ref[
                source, :, r * ny : (r + 1) * ny
            ]


def step_kernel(
    mode_count,
    slab_count,
    current_ref,
    base_ref,
    coupled_ref,
    right_ref,
    left_ref,
    scale_ref,
    solution_ref,
    state_ref,
    turned_ref,
):
    nx, ny = scale_ref.shape
    group = coupled_ref.shape[1]
    height = nx // (mode_count * slab_count)
    turn_in(turned_ref, coupled_ref, mode_count, slab_count, height, ny)

    def several(step, carry):
        first = step * TOGETHER
        resid = []
        for i in range(TOGETHER):
            coupled = turned_ref[pl.ds(first + i, nx, stride=group), :]
            resid.append(base_ref[:, first + i].reshape(nx, ny) - coupled)
        change = solve(resid, right_ref, left_ref, scale_ref)
        for i in range(TOGETHER):
            value = current_ref[:, first + i].reshape(nx, ny) + change[i]
            solution_ref[:, first + i] = value.reshape(slab_count, nx // slab_count, ny)
            turned_ref[pl.ds(first + i, nx, stride=group), :] = value
        return carry

    lax.fori_loop(0, group // TOGETHER, several, 0)

    for target in range(mode_count * slab_count):
        first = ((target % slab_count) * mode_count + target // slab_count) * height
        for r in range(height):
            row = first + r
            value = turned_ref[row * group : (row + 1) * group, :].astype(jnp.bfloat16)
            state_ref[target, :, r * ny : (r + 1) * ny] = value


def residual_kernel(mode_count, slab_count, base_ref, coupled_ref, out_ref, turned_ref):
    group = coupled_ref.shape[1]
    ny = base_ref.shape[-1]
    nx = turned_ref.shape[0] // group
    height = nx // (mode_count * slab_count)
    turn_in(turned_ref, coupled_ref, mode_count, slab_count, height, ny)

    def one(mode, carry):
        coupled = turned_ref[pl.ds(mode, nx, stride=group), :]
        out_ref[:, mode] = base_ref[:, mode] - coupled.reshape(slab_count, nx // slab_count, ny)
        return carry

    lax.fori_loop(0, group, one, 0)


def correct_kernel(current_ref, resid_ref, right_ref, left_ref, scale_ref, out_ref):
    nx, ny = scale_ref.shape

    def several(step, carry):
        first = step * TOGETHER
        resid = [resid_ref[:, first + i].reshape(nx, ny) for i in range(TOGETHER)]
        change = solve(resid, right_ref, left_ref, scale_ref)
        for i in range(TOGETHER):
            shape = out_ref.shape[:1] + out_ref.shape[2:]
            out_ref[:, first + i] = current_ref[:, first + i] + change[i].reshape(shape)
        return carry

    lax.fori_loop(0, out_ref.shape[1] // TOGETHER, several, 0)


def whole(array):
    return pl.BlockSpec(array.shape, lambda g: (0,) * array.ndim)


def slabs_of(array):
    slab_count, _, rows, ny = array.shape
    return pl.BlockSpec((slab_count, GROUP, rows, ny), lambda g: (0, g, 0, 0))


def strips_of(shape):
    return pl.BlockSpec((shape[0], GROUP, shape[2]), lambda g: (0, g, 0))


def per_group(kernel, operands, in_specs, out_shape, out_specs, scratch=(), flops=0):
    moved = sum(a.size * a.dtype.itemsize for a in operands)
    return pl.pallas_call(
        kernel,
        grid=(operands[0].shape[1] // GROUP,),
        in_specs=in_specs,
        out_specs=out_specs,
        out_shape=out_shape,
        scratch_shapes=scratch,
        cost_estimate=pl.CostEstimate(flops=flops, bytes_accessed=2 * moved, transcendentals=0),
        compiler_params=pltpu.CompilerParams(vmem_limit_bytes=48 * MIB),
    )(*operands)


def mean_part(current, right_side, weights):
    slabs = slabs_of(current)
    return per_group(
        mean_kernel,
        (current, right_side, weights),
        [slabs, slabs, whole(weights)],
        jax.ShapeDtypeStruct(current.shape, jnp.float32),
        slabs,
    )


def solve_flops(array, tables):
    nx, ny = tables[2].shape
    return array.shape[1] * 8 * 3 * nx * ny * (nx + ny) // 2


def step(current, base, coupled, tables, mode_count, slab_count):
    nx, ny = tables[2].shape
    slabs = slabs_of(current)
    return per_group(
        functools.partial(step_kernel, mode_count, slab_count),
        (current, base, coupled, *tables),
        [slabs, slabs, strips_of(coupled.shape), *map(whole, tables)],
        [
            jax.ShapeDtypeStruct(current.shape, jnp.float32),
            jax.ShapeDtypeStruct(coupled.shape, jnp.bfloat16),
        ],
        [slabs, strips_of(coupled.shape)],
        [pltpu.VMEM((nx * GROUP, ny), jnp.float32)],
        solve_flops(current, tables),
    )


def last_residual(base, coupled, mode_count, slab_count):
    slab, _, rows, ny = base.shape
    slabs = slabs_of(base)
    return per_group(
        functools.partial(residual_kernel, mode_count, slab_count),
        (base, coupled),
        [slabs, strips_of(coupled.shape)],
        jax.ShapeDtypeStruct(base.shape, jnp.float32),
        slabs,
        [pltpu.VMEM((slab * rows * GROUP, ny), jnp.float32)],
    )


def correct(current, resid, tables):
    slabs = slabs_of(current)
    return per_group(
        correct_kernel,
        (current, resid, *tables),
        [slabs, slabs, *map(whole, tables)],
        jax.ShapeDtypeStruct(current.shape, jnp.float32),
        slabs,
        (),
        solve_flops(current, tables),
    )


def regroup(block, axis):
    count = lax.axis_size(axis)
    here = lax.axis_index(axis)
    own = lax.dynamic_index_in_dim(block, here, 0)
    out = lax.dynamic_update_slice_in_dim(jnp.zeros_like(block), own, here, 0)
    for shift in range(1, count):
        target = lax.rem(here + shift, count)
        source = lax.rem(here + count - shift, count)
        moved = lax.ppermute(
            lax.dynamic_index_in_dim(block, target, 0),
            axis,
            [(i, (i + shift) % count) for i in range(count)],
        )
        out = lax.dynamic_update_slice_in_dim(out, moved, source, 0)
    return out


def local(guess, right_side, mean_coef, field_coef, coupling, coupling_list, pair_count):
    mode_count = lax.axis_size("mode")
    slab_count = lax.axis_size("slab")
    both = ("mode", "slab")
    modes, rows, cols = guess.shape
    fields = field_coef.shape[0]
    nx = rows * slab_count
    devices = mode_count * slab_count
    height = nx // devices
    share = modes // slab_count

    strips = pack_strips(guess, mode_count)
    state = lax.all_to_all(strips, "mode", 0, 0, tiled=True)
    state = state.reshape(mode_count * modes, height * cols)

    def to_fields(block):
        return regroup(block.reshape(slab_count, share, rows, cols), "slab")

    def to_slabs(block):
        flat = block.reshape(modes, rows, cols)
        return lax.all_to_all(flat, "slab", 0, 0, tiled=True)

    state, current = lax.optimization_barrier((state, to_fields(guess)))
    right = to_fields(right_side)

    coefs = jnp.concatenate([mean_coef[None], field_coef], 0)
    coefs = lax.all_gather(coefs, "slab", axis=1, tiled=True)
    weights = stencil_weights(coefs)
    strip = lax.axis_index("slab") * mode_count + lax.axis_index("mode")
    strip_weights = lax.dynamic_slice_in_dim(weights[1:], strip * height, height, axis=2)
    matrix = dense_coupling(coupling, coupling_list, pair_count, fields)

    row_high, row_low = split_table(sine_table(nx))
    col_high, col_low = split_table(sine_table(cols))
    tables = (
        jnp.concatenate(
            [
                jnp.concatenate([col_high, col_low], 1),
                jnp.concatenate([col_high, jnp.zeros_like(col_low)], 1),
            ],
            0,
        ),
        jnp.concatenate(
            [
                jnp.concatenate([row_high, row_high], 1),
                jnp.concatenate([row_low, jnp.zeros_like(row_low)], 1),
            ],
            0,
        ),
        RELAXATION / eigen_table(nx, cols),
    )

    for number in range(ITERS):
        base = mean_part(current, right, weights[0])
        sums = coupled_sums(matrix, state, strip_weights, both)
        sums = lax.all_to_all(sums, both, 0, 0, tiled=True)
        sums = sums.reshape(devices, share, height * cols)
        if number < ITERS - 1:
            current, state = step(current, base, sums, tables, mode_count, slab_count)
            state = state.reshape(devices * share, height * cols)
            state = lax.all_to_all(state, both, 0, 0, tiled=True)
        else:
            resid = last_residual(base, sums, mode_count, slab_count)
            current = correct(current, resid, tables)
    return to_slabs(current), to_slabs(resid)


def solution(mesh):
    placed = (
        P("mode", "slab", None),
        P("mode", "slab", None),
        P("slab", None),
        P(None, "slab", None),
        P(),
        P(),
        P(),
    )
    return jax.shard_map(
        local,
        mesh=mesh,
        in_specs=placed,
        out_specs=(P("mode", "slab", None), P("mode", "slab", None)),
        check_vma=False,
    )
```

```python
import functools
import math

import jax
import jax.numpy as jnp
from jax import lax
from jax.experimental import pallas as pl
from jax.experimental.pallas import tpu as pltpu
from jax.sharding import PartitionSpec as P

RELAXATION = 0.6
MIB = 1 << 20


def sine_table(length):
    counter = jnp.arange(length).astype(jnp.float32) + 1.0
    angle = math.pi * counter[:, None] * counter[None, :] / (length + 1)
    return math.sqrt(2.0 / (length + 1)) * jnp.sin(angle)


def eigen_table(first, second):
    along_first = 2.0 * jnp.cos(
        math.pi * (jnp.arange(first).astype(jnp.float32) + 1.0) / (first + 1)
    )
    along_second = 2.0 * jnp.cos(
        math.pi * (jnp.arange(second).astype(jnp.float32) + 1.0) / (second + 1)
    )
    return 4.0 - along_first[:, None] - along_second[None, :]


def stencil_weights(coef):
    nx, ny = coef.shape
    row = lax.broadcasted_iota(jnp.int32, (nx, ny), 0)
    col = lax.broadcasted_iota(jnp.int32, (nx, ny), 1)
    sides = (
        (pltpu.roll(coef, 1, 0), row == 0),
        (pltpu.roll(coef, nx - 1, 0), row == nx - 1),
        (pltpu.roll(coef, 1, 1), col == 0),
        (pltpu.roll(coef, ny - 1, 1), col == ny - 1),
    )
    centre = 0.0
    weights = []
    for other, outside in sides:
        weight = 0.5 * (coef + jnp.where(outside, coef, other))
        centre = centre + weight
        weights.append(jnp.where(outside, 0.0, weight))
    return [centre] + weights


def weights_kernel(strip_ref, coef_ref, mean_ref, strip_weight_ref, full_ref):
    _, nx, ny = mean_ref.shape
    fields = coef_ref.shape[1] - 1
    height = strip_weight_ref.shape[0] // (5 * fields)
    for which, weight in enumerate(stencil_weights(coef_ref[:, 0].reshape(nx, ny))):
        mean_ref[which] = weight
    for f in range(fields):
        for which, weight in enumerate(stencil_weights(coef_ref[:, f + 1].reshape(nx, ny))):
            full_ref[...] = weight
            for r in range(height):
                at = (f * 5 + which) * height + r
                strip_weight_ref[at : at + 1, :] = full_ref[
                    pl.ds(strip_ref[0] * height + r, 1), :
                ]


def all_weights(moved, strip, coefs, height):
    slab_count, entries, rows, ny = moved.shape
    nx = slab_count * rows
    last = entries // coefs - 1
    fields = coefs - 1
    return pl.pallas_call(
        weights_kernel,
        grid_spec=pltpu.PrefetchScalarGridSpec(
            num_scalar_prefetch=1,
            grid=(1,),
            in_specs=[pl.BlockSpec((slab_count, coefs, rows, ny), lambda i, *_: (0, last, 0, 0))],
            out_specs=[
                pl.BlockSpec((5, nx, ny), lambda i, *_: (0, 0, 0)),
                pl.BlockSpec((fields * 5 * height, ny), lambda i, *_: (0, 0)),
            ],
            scratch_shapes=[pltpu.VMEM((nx, ny), jnp.float32)],
        ),
        out_shape=[
            jax.ShapeDtypeStruct((5, nx, ny), jnp.float32),
            jax.ShapeDtypeStruct((fields * 5 * height, ny), jnp.float32),
        ],
        compiler_params=pltpu.CompilerParams(vmem_limit_bytes=32 * MIB),
    )(strip.reshape(1), moved)


def split(value):
    high = value.astype(jnp.bfloat16)
    low = (value - high.astype(jnp.float32)).astype(jnp.bfloat16)
    return high, low


def split_table(value):
    high = lax.reduce_precision(value, 8, 7)
    return high.astype(jnp.bfloat16), (value - high).astype(jnp.bfloat16)


LOW = 32
FIRST_POWER = 7
SUM_POWER = 5
SOLUTION_POWER = 4


def encode(value, power):
    square = value * value
    if power == 4:
        result = square * (value * jnp.abs(value))
    elif power == 5:
        result = square * square * value
    else:
        result = (square * square) * (square * value)
    return result.astype(jnp.bfloat16)


def decode(code, power):
    code = code.astype(jnp.float32)
    size = jnp.abs(code)
    value = jnp.exp(jnp.log(size) * (1.0 / power))
    value = jnp.where(size > 0.0, value, 0.0)
    return jnp.where(code < 0.0, -value, value)


def code_scales(nx, ny, entries, width):
    guess_max, mean_max, field_max, coupling_max = 6.0, 2.0, 2.5, 0.0625
    gain = 8.0 * field_max * entries * width * coupling_max * 1.01
    inverse = (min(nx, ny) + 1) ** 2 / 8.0

    def bound(iterate):
        return guess_max + (8.0 * mean_max + gain) * iterate

    change = RELAXATION * inverse * 1.01
    second = guess_max + change * bound(guess_max)
    third = second + change * bound(second)

    def scale(limit, power):
        return 0.8 * 2.0 ** (127.0 / power) / limit

    first = math.sqrt(2.0 * ny) * gain * guess_max
    return (
        min(1.0, scale(first, FIRST_POWER)),
        min(1.0, scale(bound(second), SUM_POWER)),
        min(1.0, scale(third, SOLUTION_POWER)),
    )


def pack_kernel(rows, height, x_ref, out_ref):
    strips, modes, cells = out_ref.shape
    cols = cells // height
    for strip in range(strips):
        for r in range(height):
            value = x_ref[pl.ds(strip * height + r, modes, stride=rows), :]
            out_ref[strip, :, r * cols : (r + 1) * cols] = value.astype(jnp.bfloat16)


def pack_strips(block, strips):
    modes, rows, cols = block.shape
    height = rows // strips
    return pl.pallas_call(
        functools.partial(pack_kernel, rows, height),
        out_shape=jax.ShapeDtypeStruct((strips, modes, height * cols), jnp.bfloat16),
        compiler_params=pltpu.CompilerParams(vmem_limit_bytes=32 * MIB),
    )(block.reshape(modes * rows, cols))


def dense_kernel(fields, entry_ref, count_ref, coupling_ref, out_ref):
    block = pl.program_id(0)
    width = coupling_ref.shape[-1]
    out_ref[...] = jnp.zeros_like(out_ref)

    def place(k, carry):
        entry = entry_ref[block, k]
        column = pl.multiple_of((entry // fields) * width, width)
        out_ref[0, entry % fields, :, pl.ds(column, width)] = coupling_ref[0, k]
        return carry

    lax.fori_loop(0, count_ref[block], place, 0)


def dense_coupling(coupling, coupling_list, pair_count, fields):
    blocks, entries, width, _ = coupling.shape
    return pl.pallas_call(
        functools.partial(dense_kernel, fields),
        grid_spec=pltpu.PrefetchScalarGridSpec(
            num_scalar_prefetch=2,
            grid=(blocks,),
            in_specs=[pl.BlockSpec((1, entries, width, width), lambda i, *_: (i, 0, 0, 0))],
            out_specs=pl.BlockSpec(
                (1, fields, width, blocks * width), lambda i, *_: (i, 0, 0, 0)
            ),
        ),
        out_shape=jax.ShapeDtypeStruct((blocks, fields, width, blocks * width), coupling.dtype),
        compiler_params=pltpu.CompilerParams(vmem_limit_bytes=32 * MIB),
    )(coupling_list, pair_count, coupling)


def low_tiles(height, cols):
    return -(-height * LOW // cols)


def along_cols(fields, right_ref):
    size, ny = fields[0].shape
    high, low = split(jnp.concatenate(fields, axis=0))
    both = jnp.dot(
        jnp.concatenate([high, low], axis=1), right_ref[...], preferred_element_type=jnp.float32
    )
    both = both[:, :ny] + both[:, ny:]
    return [both[i * size : (i + 1) * size] for i in range(len(fields))]


def along_rows(wide, left_ref):
    nx = wide.shape[0]
    high, low = split(wide)
    both = jnp.dot(
        left_ref[...], jnp.concatenate([high, low], axis=0), preferred_element_type=jnp.float32
    )
    return both[:nx] + both[nx:]


def weight_row(weight_ref, height, field, which, r):
    at = (field * 5 + which) * height + r
    return weight_ref[at : at + 1, :]


def inner_kernel(height, cols, matrix_ref, state_ref, weight_ref, out_ref, sums_ref):
    fields, width, depth = matrix_ref.shape[1:]
    sums_ref[...] = jnp.dot(
        matrix_ref[0].reshape(fields * width, depth),
        state_ref[...],
        preferred_element_type=jnp.float32,
    )
    for r in range(height):
        total = 0.0
        from_left = 0.0
        from_right = 0.0
        for f in range(fields):

            def row(at):
                return sums_ref[f * width : (f + 1) * width, at * cols : (at + 1) * cols]

            weight = functools.partial(weight_row, weight_ref, height, f)
            here = row(r)
            total = total + weight(0, r) * here
            if r > 0:
                total = total - weight(1, r) * row(r - 1)
            if r < height - 1:
                total = total - weight(2, r) * row(r + 1)
            from_left = from_left + weight(4, r) * here
            from_right = from_right + weight(3, r) * here
        total = total - pltpu.roll(from_left, 1, 1) - pltpu.roll(from_right, cols - 1, 1)
        out_ref[:, r * cols : (r + 1) * cols] = total


def border_kernel(
    height,
    cols,
    first,
    scale,
    matrix_ref,
    above_ref,
    below_ref,
    weight_ref,
    inner_ref,
    right_ref,
    out_ref,
):
    fields, width, depth = matrix_ref.shape[1:]
    matrix = matrix_ref[0].reshape(fields * width, depth)
    border = jnp.concatenate([above_ref[...], below_ref[...]], axis=1)
    sums = jnp.dot(matrix, border, preferred_element_type=jnp.float32)
    rows = []
    for r in range(height):
        total = inner_ref[:, r * cols : (r + 1) * cols]
        for f in range(fields):
            part = sums[f * width : (f + 1) * width]
            if r == 0:
                total = total - weight_row(weight_ref, height, f, 1, r) * part[:, :cols]
            if r == height - 1:
                total = total - weight_row(weight_ref, height, f, 2, r) * part[:, cols:]
        rows.append(total)
    if not first:
        for r in range(height):
            out_ref[:, r * cols : (r + 1) * cols] = encode(rows[r] * scale, SUM_POWER)
        return
    rows = along_cols(rows, right_ref)
    low_col = lax.broadcasted_iota(jnp.int32, (width, cols), 1) < LOW
    for r in range(height):
        value = rows[r] * scale
        code = encode(value, FIRST_POWER)
        out_ref[:, r * cols : (r + 1) * cols] = code
        rest = jnp.where(low_col, value - decode(code, FIRST_POWER), 0.0)
        place = r % (cols // LOW)
        rest = pltpu.roll(rest, place * LOW, 1) if place else rest
        packed = rest if place == 0 else packed + rest
        if place == cols // LOW - 1 or r == height - 1:
            at = (height + r // (cols // LOW)) * cols
            out_ref[:, at : at + cols] = packed.astype(jnp.bfloat16)


def coupled_sums(matrix, state, weights, right, first, scale, both):
    blocks, fields, width, depth = matrix.shape
    cells = state.shape[1]
    height = weights.shape[0] // (5 * fields)
    cols = cells // height
    mode_count = lax.axis_size("mode")
    slab_count = lax.axis_size("slab")
    place = [
        (t % mode_count) * slab_count + t // mode_count for t in range(mode_count * slab_count)
    ]
    onward = list(zip(place[:-1], place[1:]))
    above = lax.ppermute(state[:, -cols:], both, onward)
    below = lax.ppermute(state[:, :cols], both, [(b, a) for a, b in onward])
    matrix_spec = pl.BlockSpec((1, fields, width, depth), lambda i: (i, 0, 0, 0))
    weight_spec = pl.BlockSpec(weights.shape, lambda i: (0, 0))
    sums_spec = pl.BlockSpec((width, cells), lambda i: (i, 0))
    params = pltpu.CompilerParams(vmem_limit_bytes=40 * MIB)
    inner = pl.pallas_call(
        functools.partial(inner_kernel, height, cols),
        grid=(blocks,),
        in_specs=[matrix_spec, pl.BlockSpec((depth, cells), lambda i: (0, 0)), weight_spec],
        out_specs=sums_spec,
        out_shape=jax.ShapeDtypeStruct((blocks * width, cells), jnp.float32),
        scratch_shapes=[pltpu.VMEM((fields * width, cells), jnp.float32)],
        cost_estimate=pl.CostEstimate(
            flops=2 * matrix.size * cells, bytes_accessed=2 * matrix.size, transcendentals=0
        ),
        compiler_params=params,
    )(matrix, state, weights)
    border_spec = pl.BlockSpec((depth, cols), lambda i: (0, 0))
    sent = cells + (low_tiles(height, cols) * cols if first else 0)
    return pl.pallas_call(
        functools.partial(border_kernel, height, cols, first, scale),
        grid=(blocks,),
        in_specs=[
            matrix_spec,
            border_spec,
            border_spec,
            weight_spec,
            sums_spec,
            pl.BlockSpec(right.shape, lambda i: (0, 0)),
        ],
        out_specs=pl.BlockSpec((width, sent), lambda i: (i, 0)),
        out_shape=jax.ShapeDtypeStruct((blocks * width, sent), jnp.bfloat16),
        compiler_params=params,
    )(matrix, above, below, weights, inner, right)


TOGETHER = 4
GROUP = 16


def solve(spectral, right_ref, left_ref, scale_ref):
    ny = spectral[0].shape[1]
    wide = along_rows(jnp.concatenate(spectral, axis=1), left_ref)
    wide = wide * jnp.concatenate([scale_ref[...]] * len(spectral), axis=1)
    wide = along_rows(wide, left_ref)
    return along_cols([wide[:, i * ny : (i + 1) * ny] for i in range(len(spectral))], right_ref)


def mean_kernel(first, current_ref, right_side_ref, weight_ref, right_ref, out_ref):
    nx, ny = weight_ref.shape[1:]

    def several(number, carry):
        values = []
        for i in range(TOGETHER):
            mode = number * TOGETHER + i
            here = current_ref[:, mode].reshape(nx, ny)
            mean = (
                weight_ref[0] * here
                - weight_ref[1] * pltpu.roll(here, 1, 0)
                - weight_ref[2] * pltpu.roll(here, nx - 1, 0)
                - pltpu.roll(weight_ref[4] * here, 1, 1)
                - pltpu.roll(weight_ref[3] * here, ny - 1, 1)
            )
            values.append(right_side_ref[:, mode].reshape(nx, ny) - mean)
        if first:
            values = along_cols(values, right_ref)
        for i in range(TOGETHER):
            out_ref[:, number * TOGETHER + i] = values[i].reshape(out_ref.shape[0], -1, ny)
        return carry

    lax.fori_loop(0, out_ref.shape[1] // TOGETHER, several, 0)


def turn_in(turned_ref, coupled_ref, mode_count, slab_count, height, first, scale):
    group = coupled_ref.shape[1]
    ny = turned_ref.shape[1]
    low_col = lax.broadcasted_iota(jnp.int32, (group, ny), 1) < LOW
    for source in range(mode_count * slab_count):
        start = ((source % slab_count) * mode_count + source // slab_count) * height
        for r in range(height):
            code = coupled_ref[source, :, r * ny : (r + 1) * ny]
            value = decode(code, FIRST_POWER if first else SUM_POWER)
            if first:
                at = (height + r // (ny // LOW)) * ny
                rest = coupled_ref[source, :, at : at + ny].astype(jnp.float32)
                place = r % (ny // LOW)
                rest = pltpu.roll(rest, ny - place * LOW, 1) if place else rest
                value = value + jnp.where(low_col, rest, 0.0)
            turned_ref[(start + r) * group : (start + r + 1) * group, :] = value * (1.0 / scale)


def step_kernel(
    mode_count,
    slab_count,
    code_scale,
    current_ref,
    base_ref,
    coupled_ref,
    right_ref,
    left_ref,
    scale_ref,
    solution_ref,
    state_ref,
    turned_ref,
):
    nx, ny = scale_ref.shape
    group = coupled_ref.shape[1]
    height = nx // (mode_count * slab_count)
    turn_in(turned_ref, coupled_ref, mode_count, slab_count, height, True, code_scale)

    def several(number, carry):
        start = number * TOGETHER
        resid = []
        for i in range(TOGETHER):
            coupled = turned_ref[pl.ds(start + i, nx, stride=group), :]
            resid.append(base_ref[:, start + i].reshape(nx, ny) - coupled)
        change = solve(resid, right_ref, left_ref, scale_ref)
        for i in range(TOGETHER):
            value = current_ref[:, start + i].reshape(nx, ny) + change[i]
            solution_ref[:, start + i] = value.reshape(slab_count, nx // slab_count, ny)
            turned_ref[pl.ds(start + i, nx, stride=group), :] = value
        return carry

    lax.fori_loop(0, group // TOGETHER, several, 0)

    for target in range(mode_count * slab_count):
        start = ((target % slab_count) * mode_count + target // slab_count) * height
        for r in range(height):
            row = start + r
            value = turned_ref[row * group : (row + 1) * group, :].astype(jnp.bfloat16)
            state_ref[target, :, r * ny : (r + 1) * ny] = value


def residual_kernel(
    mode_count, slab_count, code_scale, base_ref, coupled_ref, out_ref, code_ref, turned_ref
):
    group = coupled_ref.shape[1]
    ny = base_ref.shape[-1]
    nx = turned_ref.shape[0] // group
    height = nx // (mode_count * slab_count)
    turn_in(turned_ref, coupled_ref, mode_count, slab_count, height, False, code_scale)

    def one(mode, carry):
        coupled = turned_ref[pl.ds(mode, nx, stride=group), :]
        value = base_ref[:, mode] - coupled.reshape(slab_count, nx // slab_count, ny)
        out_ref[:, mode] = value
        code_ref[:, mode] = encode(value * code_scale, SUM_POWER)
        return carry

    lax.fori_loop(0, group, one, 0)


def correct_kernel(code_scale, current_ref, resid_ref, right_ref, left_ref, scale_ref, out_ref):
    nx, ny = scale_ref.shape

    def several(number, carry):
        start = number * TOGETHER
        resid = [resid_ref[:, start + i].reshape(nx, ny) for i in range(TOGETHER)]
        change = solve(along_cols(resid, right_ref), right_ref, left_ref, scale_ref)
        for i in range(TOGETHER):
            shape = out_ref.shape[:1] + out_ref.shape[2:]
            value = current_ref[:, start + i] + change[i].reshape(shape)
            out_ref[:, start + i] = encode(value * code_scale, SOLUTION_POWER)
        return carry

    lax.fori_loop(0, out_ref.shape[1] // TOGETHER, several, 0)


def whole(array):
    return pl.BlockSpec(array.shape, lambda g: (0,) * array.ndim)


def slabs_of(array):
    slab_count, _, rows, ny = array.shape
    return pl.BlockSpec((slab_count, GROUP, rows, ny), lambda g: (0, g, 0, 0))


def strips_of(shape):
    return pl.BlockSpec((shape[0], GROUP, shape[2]), lambda g: (0, g, 0))


def per_group(kernel, groups, operands, in_specs, out_shape, out_specs, scratch=(), flops=0):
    moved = sum(a.size * a.dtype.itemsize for a in operands)
    return pl.pallas_call(
        kernel,
        grid=(groups,),
        in_specs=in_specs,
        out_specs=out_specs,
        out_shape=out_shape,
        scratch_shapes=scratch,
        cost_estimate=pl.CostEstimate(flops=flops, bytes_accessed=2 * moved, transcendentals=0),
        compiler_params=pltpu.CompilerParams(vmem_limit_bytes=48 * MIB),
    )(*operands)


def mean_part(current, right_side, weights, right, first):
    slabs = slabs_of(right_side)
    return per_group(
        functools.partial(mean_kernel, first),
        right_side.shape[1] // GROUP,
        (current, right_side, weights, right),
        [slabs, slabs, whole(weights), whole(right)],
        jax.ShapeDtypeStruct(right_side.shape, jnp.float32),
        slabs,
    )


def solve_flops(array, tables):
    nx, ny = tables[2].shape
    return array.shape[1] * 8 * 3 * nx * ny * (nx + ny) // 2


def step(current, base, coupled, tables, mode_count, slab_count, code_scale):
    nx, ny = tables[2].shape
    slabs = slabs_of(base)
    devices, modes, _ = coupled.shape
    state = (devices, modes, nx // devices * ny)
    return per_group(
        functools.partial(step_kernel, mode_count, slab_count, code_scale),
        modes // GROUP,
        (current, base, coupled, *tables),
        [slabs, slabs, strips_of(coupled.shape), *map(whole, tables)],
        [
            jax.ShapeDtypeStruct(base.shape, jnp.float32),
            jax.ShapeDtypeStruct(state, jnp.bfloat16),
        ],
        [slabs, strips_of(state)],
        [pltpu.VMEM((nx * GROUP, ny), jnp.float32)],
        solve_flops(base, tables),
    )


def last_residual(base, coupled, mode_count, slab_count, code_scale):
    slab, modes, rows, ny = base.shape
    slabs = slabs_of(base)
    return per_group(
        functools.partial(residual_kernel, mode_count, slab_count, code_scale),
        modes // GROUP,
        (base, coupled),
        [slabs, strips_of(coupled.shape)],
        [
            jax.ShapeDtypeStruct(base.shape, jnp.float32),
            jax.ShapeDtypeStruct(base.shape, jnp.bfloat16),
        ],
        [slabs, slabs],
        [pltpu.VMEM((slab * rows * GROUP, ny), jnp.float32)],
    )


def correct(current, resid, tables, code_scale):
    slabs = slabs_of(resid)
    return per_group(
        functools.partial(correct_kernel, code_scale),
        resid.shape[1] // GROUP,
        (current, resid, *tables),
        [slabs, slabs, *map(whole, tables)],
        jax.ShapeDtypeStruct(resid.shape, jnp.bfloat16),
        slabs,
        (),
        solve_flops(resid, tables),
    )


def regroup(block, axis, same=None):
    count = lax.axis_size(axis)
    here = lax.axis_index(axis)

    def part(target):
        chosen = lax.dynamic_index_in_dim(block, target, 0)
        return chosen if same is None else jnp.concatenate([chosen, same[None]], axis=1)

    own = part(here)
    out = jnp.zeros((count,) + own.shape[1:], own.dtype)
    out = lax.dynamic_update_slice_in_dim(out, own, here, 0)
    for shift in range(1, count):
        target = lax.rem(here + shift, count)
        source = lax.rem(here + count - shift, count)
        moved = lax.ppermute(part(target), axis, [(i, (i + shift) % count) for i in range(count)])
        out = lax.dynamic_update_slice_in_dim(out, moved, source, 0)
    return out


def local(guess, right_side, mean_coef, field_coef, coupling, coupling_list, pair_count):
    mode_count = lax.axis_size("mode")
    slab_count = lax.axis_size("slab")
    both = ("mode", "slab")
    modes, rows, cols = guess.shape
    fields = field_coef.shape[0]
    nx = rows * slab_count
    devices = mode_count * slab_count
    height = nx // devices
    share = modes // slab_count

    strips = pack_strips(guess, mode_count)
    state = lax.all_to_all(strips, "mode", 0, 0, tiled=True)
    state = state.reshape(mode_count * modes, height * cols)

    def to_slabs(block):
        flat = block.reshape(modes, rows, cols)
        return lax.all_to_all(flat, "slab", 0, 0, tiled=True)

    coefs = jnp.concatenate([mean_coef[None], field_coef], 0)
    current = regroup(guess.reshape(slab_count, share, rows, cols), "slab", coefs)
    state, current = lax.optimization_barrier((state, current))
    right_side = regroup(right_side.reshape(slab_count, share, rows, cols), "slab")

    strip = lax.axis_index("slab") * mode_count + lax.axis_index("mode")
    mean_weights, strip_weights = all_weights(current, strip, fields + 1, height)
    matrix = dense_coupling(coupling, coupling_list, pair_count, fields)

    row_high, row_low = split_table(sine_table(nx))
    col_high, col_low = split_table(sine_table(cols))
    tables = (
        jnp.concatenate(
            [
                jnp.concatenate([col_high, col_low], 1),
                jnp.concatenate([col_high, jnp.zeros_like(col_low)], 1),
            ],
            0,
        ),
        jnp.concatenate(
            [
                jnp.concatenate([row_high, row_high], 1),
                jnp.concatenate([row_low, jnp.zeros_like(row_low)], 1),
            ],
            0,
        ),
        RELAXATION / eigen_table(nx, cols),
    )

    first_scale, sum_scale, solution_scale = code_scales(nx, cols, coupling.shape[1], modes)

    def exchanged_sums(state, first, scale):
        sums = coupled_sums(matrix, state, strip_weights, tables[0], first, scale, both)
        sums = lax.all_to_all(sums, both, 0, 0, tiled=True)
        return sums.reshape(devices, share, -1)

    base = mean_part(current, right_side, mean_weights, tables[0], True)
    sums = exchanged_sums(state, True, first_scale)
    current, state = step(current, base, sums, tables, mode_count, slab_count, first_scale)
    state = state.reshape(devices * share, height * cols)
    state = lax.all_to_all(state, both, 0, 0, tiled=True)

    base = mean_part(current, right_side, mean_weights, tables[0], False)
    sums = exchanged_sums(state, False, sum_scale)
    resid, code = last_residual(base, sums, mode_count, slab_count, sum_scale)
    resid_out = decode(to_slabs(code), SUM_POWER) * (1.0 / sum_scale)
    code = correct(current, resid, tables, solution_scale)
    return decode(to_slabs(code), SOLUTION_POWER) * (1.0 / solution_scale), resid_out


def solution(mesh):
    placed = (
        P("mode", "slab", None),
        P("mode", "slab", None),
        P("slab", None),
        P(None, "slab", None),
        P(),
        P(),
        P(),
    )
    return jax.shard_map(
        local,
        mesh=mesh,
        in_specs=placed,
        out_specs=(P("mode", "slab", None), P("mode", "slab", None)),
        check_vma=False,
    )
```

```python
import functools
import math

import jax
import jax.numpy as jnp
from jax import lax
from jax.experimental import pallas as pl
from jax.experimental.pallas import tpu as pltpu
from jax.sharding import PartitionSpec as P

RELAXATION = 0.6
MIB = 1 << 20


def sine_table(length):
    counter = jnp.arange(length).astype(jnp.float32) + 1.0
    angle = math.pi * counter[:, None] * counter[None, :] / (length + 1)
    return math.sqrt(2.0 / (length + 1)) * jnp.sin(angle)


def eigen_table(first, second):
    along_first = 2.0 * jnp.cos(
        math.pi * (jnp.arange(first).astype(jnp.float32) + 1.0) / (first + 1)
    )
    along_second = 2.0 * jnp.cos(
        math.pi * (jnp.arange(second).astype(jnp.float32) + 1.0) / (second + 1)
    )
    return 4.0 - along_first[:, None] - along_second[None, :]


def stencil_weights(coef):
    nx, ny = coef.shape
    row = lax.broadcasted_iota(jnp.int32, (nx, ny), 0)
    col = lax.broadcasted_iota(jnp.int32, (nx, ny), 1)
    sides = (
        (pltpu.roll(coef, 1, 0), row == 0),
        (pltpu.roll(coef, nx - 1, 0), row == nx - 1),
        (pltpu.roll(coef, 1, 1), col == 0),
        (pltpu.roll(coef, ny - 1, 1), col == ny - 1),
    )
    centre = 0.0
    weights = []
    for other, outside in sides:
        weight = 0.5 * (coef + jnp.where(outside, coef, other))
        centre = centre + weight
        weights.append(jnp.where(outside, 0.0, weight))
    return [centre] + weights


def weights_kernel(strip_ref, coef_ref, mean_ref, strip_weight_ref, full_ref):
    _, nx, ny = mean_ref.shape
    fields = coef_ref.shape[1] - 1
    height = strip_weight_ref.shape[0] // (5 * fields)
    for which, weight in enumerate(stencil_weights(coef_ref[:, 0].reshape(nx, ny))):
        mean_ref[which] = weight
    for f in range(fields):
        for which, weight in enumerate(stencil_weights(coef_ref[:, f + 1].reshape(nx, ny))):
            full_ref[...] = weight
            for r in range(height):
                at = (f * 5 + which) * height + r
                strip_weight_ref[at : at + 1, :] = full_ref[
                    pl.ds(strip_ref[0] * height + r, 1), :
                ]


def all_weights(coefs, strip, height):
    slab_count, entries, rows, ny = coefs.shape
    nx = slab_count * rows
    fields = entries - 1
    return pl.pallas_call(
        weights_kernel,
        grid_spec=pltpu.PrefetchScalarGridSpec(
            num_scalar_prefetch=1,
            grid=(1,),
            in_specs=[pl.BlockSpec(coefs.shape, lambda i, *_: (0, 0, 0, 0))],
            out_specs=[
                pl.BlockSpec((5, nx, ny), lambda i, *_: (0, 0, 0)),
                pl.BlockSpec((fields * 5 * height, ny), lambda i, *_: (0, 0)),
            ],
            scratch_shapes=[pltpu.VMEM((nx, ny), jnp.float32)],
        ),
        out_shape=[
            jax.ShapeDtypeStruct((5, nx, ny), jnp.float32),
            jax.ShapeDtypeStruct((fields * 5 * height, ny), jnp.float32),
        ],
        compiler_params=pltpu.CompilerParams(vmem_limit_bytes=32 * MIB),
    )(strip.reshape(1), coefs)


def split(value):
    high = value.astype(jnp.bfloat16)
    low = (value - high.astype(jnp.float32)).astype(jnp.bfloat16)
    return high, low


def split_table(value):
    high = lax.reduce_precision(value, 8, 7)
    return high.astype(jnp.bfloat16), (value - high).astype(jnp.bfloat16)


LOW = 32
FIRST_POWER = 7
SUM_POWER = 5
SOLUTION_POWER = 4


def encode(value, power):
    square = value * value
    if power == 4:
        result = square * (value * jnp.abs(value))
    elif power == 5:
        result = square * square * value
    else:
        result = (square * square) * (square * value)
    return result.astype(jnp.bfloat16)


def decode(code, power):
    code = code.astype(jnp.float32)
    size = jnp.abs(code)
    value = jnp.exp(jnp.log(size) * (1.0 / power))
    value = jnp.where(size > 0.0, value, 0.0)
    return jnp.where(code < 0.0, -value, value)


def code_scales(nx, ny, entries, width):
    guess_max, mean_max, field_max, coupling_max = 6.0, 2.0, 2.5, 0.0625
    gain = 8.0 * field_max * entries * width * coupling_max * 1.01
    inverse = (min(nx, ny) + 1) ** 2 / 8.0

    def bound(iterate):
        return guess_max + (8.0 * mean_max + gain) * iterate

    change = RELAXATION * inverse * 1.01
    second = guess_max + change * bound(guess_max)
    third = second + change * bound(second)

    def scale(limit, power):
        return 0.8 * 2.0 ** (127.0 / power) / limit

    first = math.sqrt(2.0 * ny) * gain * guess_max
    return (
        min(1.0, scale(first, FIRST_POWER)),
        min(1.0, scale(bound(second), SUM_POWER)),
        min(1.0, scale(third, SOLUTION_POWER)),
    )


def pack_kernel(rows, height, x_ref, out_ref):
    strips, modes, cells = out_ref.shape
    cols = cells // height
    for strip in range(strips):
        for r in range(height):
            value = x_ref[pl.ds(strip * height + r, modes, stride=rows), :]
            out_ref[strip, :, r * cols : (r + 1) * cols] = value.astype(jnp.bfloat16)


def pack_strips(block, strips):
    modes, rows, cols = block.shape
    height = rows // strips
    return pl.pallas_call(
        functools.partial(pack_kernel, rows, height),
        out_shape=jax.ShapeDtypeStruct((strips, modes, height * cols), jnp.bfloat16),
        compiler_params=pltpu.CompilerParams(vmem_limit_bytes=32 * MIB),
    )(block.reshape(modes * rows, cols))


def dense_kernel(fields, entry_ref, count_ref, coupling_ref, out_ref):
    block = pl.program_id(0)
    width = coupling_ref.shape[-1]
    out_ref[...] = jnp.zeros_like(out_ref)

    def place(k, carry):
        entry = entry_ref[block, k]
        column = pl.multiple_of((entry // fields) * width, width)
        out_ref[0, entry % fields, :, pl.ds(column, width)] = coupling_ref[0, k]
        return carry

    lax.fori_loop(0, count_ref[block], place, 0)


def dense_coupling(coupling, coupling_list, pair_count, fields):
    blocks, entries, width, _ = coupling.shape
    return pl.pallas_call(
        functools.partial(dense_kernel, fields),
        grid_spec=pltpu.PrefetchScalarGridSpec(
            num_scalar_prefetch=2,
            grid=(blocks,),
            in_specs=[pl.BlockSpec((1, entries, width, width), lambda i, *_: (i, 0, 0, 0))],
            out_specs=pl.BlockSpec(
                (1, fields, width, blocks * width), lambda i, *_: (i, 0, 0, 0)
            ),
        ),
        out_shape=jax.ShapeDtypeStruct((blocks, fields, width, blocks * width), coupling.dtype),
        compiler_params=pltpu.CompilerParams(vmem_limit_bytes=32 * MIB),
    )(coupling_list, pair_count, coupling)


def low_tiles(height, cols):
    return -(-height * LOW // cols)


def along_cols(fields, right_ref):
    size, ny = fields[0].shape
    high, low = split(jnp.concatenate(fields, axis=0))
    both = jnp.dot(
        jnp.concatenate([high, low], axis=1), right_ref[...], preferred_element_type=jnp.float32
    )
    both = both[:, :ny] + both[:, ny:]
    return [both[i * size : (i + 1) * size] for i in range(len(fields))]


def along_rows(wide, left_ref):
    nx = wide.shape[0]
    high, low = split(wide)
    both = jnp.dot(
        left_ref[...], jnp.concatenate([high, low], axis=0), preferred_element_type=jnp.float32
    )
    return both[:nx] + both[nx:]


def weight_row(weight_ref, height, field, which, r):
    at = (field * 5 + which) * height + r
    return weight_ref[at : at + 1, :]


def inner_kernel(height, cols, matrix_ref, state_ref, weight_ref, out_ref, sums_ref):
    fields, width, depth = matrix_ref.shape[1:]
    sums_ref[...] = jnp.dot(
        matrix_ref[0].reshape(fields * width, depth),
        state_ref[...],
        preferred_element_type=jnp.float32,
    )
    for r in range(height):
        total = 0.0
        from_left = 0.0
        from_right = 0.0
        for f in range(fields):

            def row(at):
                return sums_ref[f * width : (f + 1) * width, at * cols : (at + 1) * cols]

            weight = functools.partial(weight_row, weight_ref, height, f)
            here = row(r)
            total = total + weight(0, r) * here
            if r > 0:
                total = total - weight(1, r) * row(r - 1)
            if r < height - 1:
                total = total - weight(2, r) * row(r + 1)
            from_left = from_left + weight(4, r) * here
            from_right = from_right + weight(3, r) * here
        total = total - pltpu.roll(from_left, 1, 1) - pltpu.roll(from_right, cols - 1, 1)
        out_ref[:, r * cols : (r + 1) * cols] = total


def border_kernel(
    height,
    cols,
    first,
    scale,
    matrix_ref,
    above_ref,
    below_ref,
    weight_ref,
    inner_ref,
    right_ref,
    out_ref,
):
    fields, width, depth = matrix_ref.shape[1:]
    matrix = matrix_ref[0].reshape(fields * width, depth)
    border = jnp.concatenate([above_ref[...], below_ref[...]], axis=1)
    sums = jnp.dot(matrix, border, preferred_element_type=jnp.float32)
    rows = []
    for r in range(height):
        total = inner_ref[:, r * cols : (r + 1) * cols]
        for f in range(fields):
            part = sums[f * width : (f + 1) * width]
            if r == 0:
                total = total - weight_row(weight_ref, height, f, 1, r) * part[:, :cols]
            if r == height - 1:
                total = total - weight_row(weight_ref, height, f, 2, r) * part[:, cols:]
        rows.append(total)
    if not first:
        for r in range(height):
            out_ref[:, r * cols : (r + 1) * cols] = encode(rows[r] * scale, SUM_POWER)
        return
    rows = along_cols(rows, right_ref)
    low_col = lax.broadcasted_iota(jnp.int32, (width, cols), 1) < LOW
    for r in range(height):
        value = rows[r] * scale
        code = encode(value, FIRST_POWER)
        out_ref[:, r * cols : (r + 1) * cols] = code
        rest = jnp.where(low_col, value - decode(code, FIRST_POWER), 0.0)
        place = r % (cols // LOW)
        rest = pltpu.roll(rest, place * LOW, 1) if place else rest
        packed = rest if place == 0 else packed + rest
        if place == cols // LOW - 1 or r == height - 1:
            at = (height + r // (cols // LOW)) * cols
            out_ref[:, at : at + cols] = packed.astype(jnp.bfloat16)


def coupled_sums(matrix, state, weights, right, first, scale, both):
    blocks, fields, width, depth = matrix.shape
    cells = state.shape[1]
    height = weights.shape[0] // (5 * fields)
    cols = cells // height
    mode_count = lax.axis_size("mode")
    slab_count = lax.axis_size("slab")
    place = [
        (t % mode_count) * slab_count + t // mode_count for t in range(mode_count * slab_count)
    ]
    onward = list(zip(place, place[1:] + place[:1]))
    above = lax.ppermute(state[:, -cols:], both, onward)
    below = lax.ppermute(state[:, :cols], both, [(b, a) for a, b in onward])
    matrix_spec = pl.BlockSpec((1, fields, width, depth), lambda i: (i, 0, 0, 0))
    weight_spec = pl.BlockSpec(weights.shape, lambda i: (0, 0))
    sums_spec = pl.BlockSpec((width, cells), lambda i: (i, 0))
    params = pltpu.CompilerParams(vmem_limit_bytes=40 * MIB)
    inner = pl.pallas_call(
        functools.partial(inner_kernel, height, cols),
        grid=(blocks,),
        in_specs=[matrix_spec, pl.BlockSpec((depth, cells), lambda i: (0, 0)), weight_spec],
        out_specs=sums_spec,
        out_shape=jax.ShapeDtypeStruct((blocks * width, cells), jnp.float32),
        scratch_shapes=[pltpu.VMEM((fields * width, cells), jnp.float32)],
        cost_estimate=pl.CostEstimate(
            flops=2 * matrix.size * cells, bytes_accessed=2 * matrix.size, transcendentals=0
        ),
        compiler_params=params,
    )(matrix, state, weights)
    border_spec = pl.BlockSpec((depth, cols), lambda i: (0, 0))
    sent = cells + (low_tiles(height, cols) * cols if first else 0)
    return pl.pallas_call(
        functools.partial(border_kernel, height, cols, first, scale),
        grid=(blocks,),
        in_specs=[
            matrix_spec,
            border_spec,
            border_spec,
            weight_spec,
            sums_spec,
            pl.BlockSpec(right.shape, lambda i: (0, 0)),
        ],
        out_specs=pl.BlockSpec((width, sent), lambda i: (i, 0)),
        out_shape=jax.ShapeDtypeStruct((blocks * width, sent), jnp.bfloat16),
        compiler_params=params,
    )(matrix, above, below, weights, inner, right)


TOGETHER = 8
GROUP = 16


def solve(spectral, right_ref, left_ref, scale_ref):
    ny = spectral[0].shape[1]
    wide = along_rows(jnp.concatenate(spectral, axis=1), left_ref)
    wide = wide * jnp.concatenate([scale_ref[...]] * len(spectral), axis=1)
    wide = along_rows(wide, left_ref)
    return along_cols([wide[:, i * ny : (i + 1) * ny] for i in range(len(spectral))], right_ref)


def mean_kernel(first, current_ref, right_side_ref, weight_ref, right_ref, out_ref):
    nx, ny = weight_ref.shape[1:]

    def several(number, carry):
        values = []
        for i in range(TOGETHER):
            mode = number * TOGETHER + i
            here = current_ref[:, mode].reshape(nx, ny)
            mean = (
                weight_ref[0] * here
                - weight_ref[1] * pltpu.roll(here, 1, 0)
                - weight_ref[2] * pltpu.roll(here, nx - 1, 0)
                - pltpu.roll(weight_ref[4] * here, 1, 1)
                - pltpu.roll(weight_ref[3] * here, ny - 1, 1)
            )
            values.append(right_side_ref[:, mode].reshape(nx, ny) - mean)
        if first:
            values = along_cols(values, right_ref)
        for i in range(TOGETHER):
            out_ref[:, number * TOGETHER + i] = values[i].reshape(out_ref.shape[0], -1, ny)
        return carry

    lax.fori_loop(0, out_ref.shape[1] // TOGETHER, several, 0)


def turn_in(turned_ref, coupled_ref, mode_count, slab_count, height, first, scale):
    group = coupled_ref.shape[1]
    ny = turned_ref.shape[1]
    low_col = lax.broadcasted_iota(jnp.int32, (group, ny), 1) < LOW
    for source in range(mode_count * slab_count):
        start = ((source % slab_count) * mode_count + source // slab_count) * height
        for r in range(height):
            code = coupled_ref[source, :, r * ny : (r + 1) * ny]
            value = decode(code, FIRST_POWER if first else SUM_POWER)
            if first:
                at = (height + r // (ny // LOW)) * ny
                rest = coupled_ref[source, :, at : at + ny].astype(jnp.float32)
                place = r % (ny // LOW)
                rest = pltpu.roll(rest, ny - place * LOW, 1) if place else rest
                value = value + jnp.where(low_col, rest, 0.0)
            turned_ref[(start + r) * group : (start + r + 1) * group, :] = value * (1.0 / scale)


def step_kernel(
    mode_count,
    slab_count,
    code_scale,
    current_ref,
    base_ref,
    coupled_ref,
    right_ref,
    left_ref,
    scale_ref,
    solution_ref,
    state_ref,
    turned_ref,
):
    nx, ny = scale_ref.shape
    group = coupled_ref.shape[1]
    height = nx // (mode_count * slab_count)
    turn_in(turned_ref, coupled_ref, mode_count, slab_count, height, True, code_scale)

    def several(number, carry):
        start = number * TOGETHER
        resid = []
        for i in range(TOGETHER):
            coupled = turned_ref[pl.ds(start + i, nx, stride=group), :]
            resid.append(base_ref[:, start + i].reshape(nx, ny) - coupled)
        change = solve(resid, right_ref, left_ref, scale_ref)
        for i in range(TOGETHER):
            value = current_ref[:, start + i].reshape(nx, ny) + change[i]
            solution_ref[:, start + i] = value.reshape(slab_count, nx // slab_count, ny)
            turned_ref[pl.ds(start + i, nx, stride=group), :] = value
        return carry

    lax.fori_loop(0, group // TOGETHER, several, 0)

    for target in range(mode_count * slab_count):
        start = ((target % slab_count) * mode_count + target // slab_count) * height
        for r in range(height):
            row = start + r
            value = turned_ref[row * group : (row + 1) * group, :].astype(jnp.bfloat16)
            state_ref[target, :, r * ny : (r + 1) * ny] = value


def residual_kernel(
    mode_count, slab_count, code_scale, base_ref, coupled_ref, out_ref, code_ref, turned_ref
):
    group = coupled_ref.shape[1]
    ny = base_ref.shape[-1]
    nx = turned_ref.shape[0] // group
    height = nx // (mode_count * slab_count)
    turn_in(turned_ref, coupled_ref, mode_count, slab_count, height, False, code_scale)

    def one(mode, carry):
        coupled = turned_ref[pl.ds(mode, nx, stride=group), :]
        value = base_ref[:, mode] - coupled.reshape(slab_count, nx // slab_count, ny)
        out_ref[:, mode] = value
        code_ref[:, mode] = encode(value * code_scale, SUM_POWER)
        return carry

    lax.fori_loop(0, group, one, 0)


def correct_kernel(code_scale, current_ref, resid_ref, right_ref, left_ref, scale_ref, out_ref):
    nx, ny = scale_ref.shape

    def several(number, carry):
        start = number * TOGETHER
        resid = [resid_ref[:, start + i].reshape(nx, ny) for i in range(TOGETHER)]
        change = solve(along_cols(resid, right_ref), right_ref, left_ref, scale_ref)
        for i in range(TOGETHER):
            shape = out_ref.shape[:1] + out_ref.shape[2:]
            value = current_ref[:, start + i] + change[i].reshape(shape)
            out_ref[:, start + i] = encode(value * code_scale, SOLUTION_POWER)
        return carry

    lax.fori_loop(0, out_ref.shape[1] // TOGETHER, several, 0)


def whole(array):
    return pl.BlockSpec(array.shape, lambda g: (0,) * array.ndim)


def slabs_of(array):
    slab_count, _, rows, ny = array.shape
    return pl.BlockSpec((slab_count, GROUP, rows, ny), lambda g: (0, g, 0, 0))


def strips_of(shape):
    return pl.BlockSpec((shape[0], GROUP, shape[2]), lambda g: (0, g, 0))


def per_group(kernel, groups, operands, in_specs, out_shape, out_specs, scratch=(), flops=0):
    moved = sum(a.size * a.dtype.itemsize for a in operands)
    return pl.pallas_call(
        kernel,
        grid=(groups,),
        in_specs=in_specs,
        out_specs=out_specs,
        out_shape=out_shape,
        scratch_shapes=scratch,
        cost_estimate=pl.CostEstimate(flops=flops, bytes_accessed=2 * moved, transcendentals=0),
        compiler_params=pltpu.CompilerParams(vmem_limit_bytes=48 * MIB),
    )(*operands)


def mean_part(current, right_side, weights, right, first):
    slabs = slabs_of(right_side)
    return per_group(
        functools.partial(mean_kernel, first),
        right_side.shape[1] // GROUP,
        (current, right_side, weights, right),
        [slabs, slabs, whole(weights), whole(right)],
        jax.ShapeDtypeStruct(right_side.shape, jnp.float32),
        slabs,
    )


def solve_flops(array, tables):
    nx, ny = tables[2].shape
    return array.shape[1] * 8 * 3 * nx * ny * (nx + ny) // 2


def step(current, base, coupled, tables, mode_count, slab_count, code_scale):
    nx, ny = tables[2].shape
    slabs = slabs_of(base)
    devices, modes, _ = coupled.shape
    state = (devices, modes, nx // devices * ny)
    return per_group(
        functools.partial(step_kernel, mode_count, slab_count, code_scale),
        modes // GROUP,
        (current, base, coupled, *tables),
        [slabs, slabs, strips_of(coupled.shape), *map(whole, tables)],
        [
            jax.ShapeDtypeStruct(base.shape, jnp.float32),
            jax.ShapeDtypeStruct(state, jnp.bfloat16),
        ],
        [slabs, strips_of(state)],
        [pltpu.VMEM((nx * GROUP, ny), jnp.float32)],
        solve_flops(base, tables),
    )


def last_residual(base, coupled, mode_count, slab_count, code_scale):
    slab, modes, rows, ny = base.shape
    slabs = slabs_of(base)
    return per_group(
        functools.partial(residual_kernel, mode_count, slab_count, code_scale),
        modes // GROUP,
        (base, coupled),
        [slabs, strips_of(coupled.shape)],
        [
            jax.ShapeDtypeStruct(base.shape, jnp.float32),
            jax.ShapeDtypeStruct(base.shape, jnp.bfloat16),
        ],
        [slabs, slabs],
        [pltpu.VMEM((slab * rows * GROUP, ny), jnp.float32)],
    )


def correct(current, resid, tables, code_scale):
    slabs = slabs_of(resid)
    return per_group(
        functools.partial(correct_kernel, code_scale),
        resid.shape[1] // GROUP,
        (current, resid, *tables),
        [slabs, slabs, *map(whole, tables)],
        jax.ShapeDtypeStruct(resid.shape, jnp.bfloat16),
        slabs,
        (),
        solve_flops(resid, tables),
    )


def collect(parts, axis):
    count = lax.axis_size(axis)
    here = lax.axis_index(axis)
    out = jnp.zeros((count,) + parts[0].shape[1:], parts[0].dtype)
    for shift, part in enumerate(parts):
        source = lax.rem(here + count - shift, count)
        out = lax.dynamic_update_slice_in_dim(out, part, source, 0)
    return out


def onwards(part, axis, shift):
    count = lax.axis_size(axis)
    return lax.ppermute(part, axis, [(i, (i + shift) % count) for i in range(count)])


def regroup(block, axis):
    count = lax.axis_size(axis)
    here = lax.axis_index(axis)
    parts = [lax.dynamic_index_in_dim(block, here, 0)]
    for shift in range(1, count):
        target = lax.rem(here + shift, count)
        parts.append(onwards(lax.dynamic_index_in_dim(block, target, 0), axis, shift))
    return collect(parts, axis)


def spread(block, axis):
    count = lax.axis_size(axis)
    return collect([block[None]] + [onwards(block[None], axis, i) for i in range(1, count)], axis)


def local(guess, right_side, mean_coef, field_coef, coupling, coupling_list, pair_count):
    mode_count = lax.axis_size("mode")
    slab_count = lax.axis_size("slab")
    both = ("mode", "slab")
    modes, rows, cols = guess.shape
    fields = field_coef.shape[0]
    nx = rows * slab_count
    devices = mode_count * slab_count
    height = nx // devices
    share = modes // slab_count

    strips = pack_strips(guess, mode_count)
    state = lax.all_to_all(strips, "mode", 0, 0, tiled=True)
    state = state.reshape(mode_count * modes, height * cols)

    def to_slabs(block):
        flat = block.reshape(modes, rows, cols)
        return lax.all_to_all(flat, "slab", 0, 0, tiled=True)

    coefs = jnp.concatenate([mean_coef[None], field_coef], 0)
    coefs = spread(coefs, "slab")
    current = regroup(guess.reshape(slab_count, share, rows, cols), "slab")
    right_side = regroup(right_side.reshape(slab_count, share, rows, cols), "slab")

    strip = lax.axis_index("slab") * mode_count + lax.axis_index("mode")
    mean_weights, strip_weights = all_weights(coefs, strip, height)
    matrix = dense_coupling(coupling, coupling_list, pair_count, fields)

    row_high, row_low = split_table(sine_table(nx))
    col_high, col_low = split_table(sine_table(cols))
    tables = (
        jnp.concatenate(
            [
                jnp.concatenate([col_high, col_low], 1),
                jnp.concatenate([col_high, jnp.zeros_like(col_low)], 1),
            ],
            0,
        ),
        jnp.concatenate(
            [
                jnp.concatenate([row_high, row_high], 1),
                jnp.concatenate([row_low, jnp.zeros_like(row_low)], 1),
            ],
            0,
        ),
        RELAXATION / eigen_table(nx, cols),
    )

    first_scale, sum_scale, solution_scale = code_scales(nx, cols, coupling.shape[1], modes)

    sums = coupled_sums(matrix, state, strip_weights, tables[0], True, first_scale, both)
    sums, current, right_side = lax.optimization_barrier((sums, current, right_side))
    sums = lax.all_to_all(sums, both, 0, 0, tiled=True).reshape(devices, share, -1)
    base = mean_part(current, right_side, mean_weights, tables[0], True)
    current, state = step(current, base, sums, tables, mode_count, slab_count, first_scale)
    state = state.reshape(devices * share, height * cols)
    state = lax.all_to_all(state, both, 0, 0, tiled=True)

    base = mean_part(current, right_side, mean_weights, tables[0], False)
    sums = coupled_sums(matrix, state, strip_weights, tables[0], False, sum_scale, both)
    sums = lax.all_to_all(sums, both, 0, 0, tiled=True).reshape(devices, share, -1)
    resid, code = last_residual(base, sums, mode_count, slab_count, sum_scale)
    moved = to_slabs(code)
    code = correct(current, resid, tables, solution_scale)
    code, moved = lax.optimization_barrier((code, moved))
    resid_out = decode(moved, SUM_POWER) * (1.0 / sum_scale)
    return decode(to_slabs(code), SOLUTION_POWER) * (1.0 / solution_scale), resid_out


def solution(mesh):
    placed = (
        P("mode", "slab", None),
        P("mode", "slab", None),
        P("slab", None),
        P(None, "slab", None),
        P(),
        P(),
        P(),
    )
    return jax.shard_map(
        local,
        mesh=mesh,
        in_specs=placed,
        out_specs=(P("mode", "slab", None), P("mode", "slab", None)),
        check_vma=False,
    )
```

```python
import functools
import math

import jax
import jax.numpy as jnp
from jax import lax
from jax.experimental import pallas as pl
from jax.experimental.pallas import tpu as pltpu
from jax.sharding import PartitionSpec as P

RELAXATION = 0.6
VMEM_BYTES = 60 << 20
UNROLL = 4


def sine_table(length):
    counter = jnp.arange(length).astype(jnp.float32) + 1.0
    angle = math.pi * counter[:, None] * counter[None, :] / (length + 1)
    return math.sqrt(2.0 / (length + 1)) * jnp.sin(angle)


def eigen_table(first, second):
    along_first = 2.0 * jnp.cos(
        math.pi * (jnp.arange(first).astype(jnp.float32) + 1.0) / (first + 1)
    )
    along_second = 2.0 * jnp.cos(
        math.pi * (jnp.arange(second).astype(jnp.float32) + 1.0) / (second + 1)
    )
    return 4.0 - along_first[:, None] - along_second[None, :]


def stencil_weights(coef):
    nx, ny = coef.shape
    row = lax.broadcasted_iota(jnp.int32, (nx, ny), 0)
    col = lax.broadcasted_iota(jnp.int32, (nx, ny), 1)
    sides = (
        (pltpu.roll(coef, 1, 0), row == 0),
        (pltpu.roll(coef, nx - 1, 0), row == nx - 1),
        (pltpu.roll(coef, 1, 1), col == 0),
        (pltpu.roll(coef, ny - 1, 1), col == ny - 1),
    )
    centre = 0.0
    weights = []
    for other, outside in sides:
        weight = 0.5 * (coef + jnp.where(outside, coef, other))
        centre = centre + weight
        weights.append(jnp.where(outside, 0.0, weight))
    return [centre] + weights


def weights_kernel(strip_ref, coef_ref, mean_ref, strip_weight_ref, full_ref):
    _, nx, ny = mean_ref.shape
    fields = coef_ref.shape[1] - 1
    height = strip_weight_ref.shape[0] // (5 * fields)
    for which, weight in enumerate(stencil_weights(coef_ref[:, 0].reshape(nx, ny))):
        mean_ref[which] = weight
    for f in range(fields):
        for which, weight in enumerate(stencil_weights(coef_ref[:, f + 1].reshape(nx, ny))):
            full_ref[...] = weight
            for r in range(height):
                at = (f * 5 + which) * height + r
                strip_weight_ref[at : at + 1, :] = full_ref[
                    pl.ds(strip_ref[0] * height + r, 1), :
                ]


def all_weights(coefs, strip, height):
    slab_count, entries, rows, ny = coefs.shape
    nx = slab_count * rows
    fields = entries - 1
    return pl.pallas_call(
        weights_kernel,
        grid_spec=pltpu.PrefetchScalarGridSpec(
            num_scalar_prefetch=1,
            grid=(1,),
            in_specs=[pl.BlockSpec(coefs.shape, lambda i, *_: (0, 0, 0, 0))],
            out_specs=[
                pl.BlockSpec((5, nx, ny), lambda i, *_: (0, 0, 0)),
                pl.BlockSpec((fields * 5 * height, ny), lambda i, *_: (0, 0)),
            ],
            scratch_shapes=[pltpu.VMEM((nx, ny), jnp.float32)],
        ),
        out_shape=[
            jax.ShapeDtypeStruct((5, nx, ny), jnp.float32),
            jax.ShapeDtypeStruct((fields * 5 * height, ny), jnp.float32),
        ],
        compiler_params=pltpu.CompilerParams(vmem_limit_bytes=VMEM_BYTES),
    )(strip.reshape(1), coefs)


def split(value):
    high = value.astype(jnp.bfloat16)
    low = (value - high.astype(jnp.float32)).astype(jnp.bfloat16)
    return high, low


def split_table(value):
    high = lax.reduce_precision(value, 8, 7)
    return high.astype(jnp.bfloat16), (value - high).astype(jnp.bfloat16)


LOW = 32
FIRST_POWER = 7
SUM_POWER = 5
SOLUTION_POWER = 4


def encode(value, power):
    square = value * value
    if power == 4:
        result = square * (value * jnp.abs(value))
    elif power == 5:
        result = square * square * value
    else:
        result = (square * square) * (square * value)
    return result.astype(jnp.bfloat16)


def decode(code, power):
    code = code.astype(jnp.float32)
    size = jnp.abs(code)
    value = jnp.exp(jnp.log(size) * (1.0 / power))
    value = jnp.where(size > 0.0, value, 0.0)
    return jnp.where(code < 0.0, -value, value)


def code_scales(nx, ny, entries, width):
    guess_max, mean_max, field_max, coupling_max = 6.0, 2.0, 2.5, 0.0625
    gain = 8.0 * field_max * entries * width * coupling_max * 1.01
    inverse = (min(nx, ny) + 1) ** 2 / 8.0

    def bound(iterate):
        return guess_max + (8.0 * mean_max + gain) * iterate

    change = RELAXATION * inverse * 1.01
    second = guess_max + change * bound(guess_max)
    third = second + change * bound(second)

    def scale(limit, power):
        return 0.8 * 2.0 ** (127.0 / power) / limit

    first = math.sqrt(2.0 * ny) * gain * guess_max
    return (
        min(1.0, scale(first, FIRST_POWER)),
        min(1.0, scale(bound(second), SUM_POWER)),
        min(1.0, scale(third, SOLUTION_POWER)),
    )


def pack_kernel(rows, height, x_ref, out_ref):
    strips, modes, cells = out_ref.shape
    cols = cells // height
    for strip in range(strips):
        for r in range(height):
            value = x_ref[pl.ds(strip * height + r, modes, stride=rows), :]
            out_ref[strip, :, r * cols : (r + 1) * cols] = value.astype(jnp.bfloat16)


def pack_strips(block, strips):
    modes, rows, cols = block.shape
    height = rows // strips
    return pl.pallas_call(
        functools.partial(pack_kernel, rows, height),
        grid=(modes // GROUP,),
        in_specs=[pl.BlockSpec((GROUP * rows, cols), lambda g: (g, 0))],
        out_specs=pl.BlockSpec((strips, GROUP, height * cols), lambda g: (0, g, 0)),
        out_shape=jax.ShapeDtypeStruct((strips, modes, height * cols), jnp.bfloat16),
        compiler_params=pltpu.CompilerParams(vmem_limit_bytes=VMEM_BYTES),
    )(block.reshape(modes * rows, cols))


def dense_kernel(fields, entry_ref, count_ref, coupling_ref, out_ref):
    block = pl.program_id(0)
    width = coupling_ref.shape[-1]
    out_ref[...] = jnp.zeros_like(out_ref)

    def place(k, carry):
        entry = entry_ref[block, k]
        column = pl.multiple_of((entry // fields) * width, width)
        out_ref[0, entry % fields, :, pl.ds(column, width)] = coupling_ref[0, k]
        return carry

    lax.fori_loop(0, count_ref[block], place, 0)


def dense_coupling(coupling, coupling_list, pair_count, fields):
    blocks, entries, width, _ = coupling.shape
    return pl.pallas_call(
        functools.partial(dense_kernel, fields),
        grid_spec=pltpu.PrefetchScalarGridSpec(
            num_scalar_prefetch=2,
            grid=(blocks,),
            in_specs=[pl.BlockSpec((1, entries, width, width), lambda i, *_: (i, 0, 0, 0))],
            out_specs=pl.BlockSpec(
                (1, fields, width, blocks * width), lambda i, *_: (i, 0, 0, 0)
            ),
        ),
        out_shape=jax.ShapeDtypeStruct((blocks, fields, width, blocks * width), coupling.dtype),
        compiler_params=pltpu.CompilerParams(vmem_limit_bytes=VMEM_BYTES),
    )(coupling_list, pair_count, coupling)


def low_tiles(height, cols):
    return -(-height * LOW // cols)


def along_cols(fields, right_ref):
    size, ny = fields[0].shape
    high, low = split(jnp.concatenate(fields, axis=0))
    both = jnp.dot(
        jnp.concatenate([high, low], axis=1), right_ref[...], preferred_element_type=jnp.float32
    )
    both = both[:, :ny] + both[:, ny:]
    return [both[i * size : (i + 1) * size] for i in range(len(fields))]


def along_rows(wide, left_ref):
    nx = wide.shape[0]
    high, low = split(wide)
    both = jnp.dot(
        left_ref[...], jnp.concatenate([high, low], axis=0), preferred_element_type=jnp.float32
    )
    return both[:nx] + both[nx:]


def weight_row(weight_ref, height, field, which, r):
    at = (field * 5 + which) * height + r
    return weight_ref[at : at + 1, :]


def inner_kernel(height, cols, matrix_ref, state_ref, weight_ref, out_ref, *sums_refs):
    blocks, fields, width, depth = matrix_ref.shape
    for block in range(blocks):
        sums_ref = sums_refs[block % len(sums_refs)]
        sums_ref[...] = jnp.dot(
            matrix_ref[block].reshape(fields * width, depth),
            state_ref[...],
            preferred_element_type=jnp.float32,
        )
        for r in range(height):
            total = 0.0
            from_left = 0.0
            from_right = 0.0
            for f in range(fields):

                def row(at):
                    return sums_ref[f * width : (f + 1) * width, at * cols : (at + 1) * cols]

                weight = functools.partial(weight_row, weight_ref, height, f)
                here = row(r)
                total = total + weight(0, r) * here
                if r > 0:
                    total = total - weight(1, r) * row(r - 1)
                if r < height - 1:
                    total = total - weight(2, r) * row(r + 1)
                from_left = from_left + weight(4, r) * here
                from_right = from_right + weight(3, r) * here
            total = total - pltpu.roll(from_left, 1, 1) - pltpu.roll(from_right, cols - 1, 1)
            out_ref[block * width : (block + 1) * width, r * cols : (r + 1) * cols] = total


def border_kernel(
    height,
    cols,
    first,
    scale,
    matrix_ref,
    above_ref,
    below_ref,
    weight_ref,
    inner_ref,
    right_ref,
    out_ref,
):
    blocks, fields, width, depth = matrix_ref.shape
    border = jnp.concatenate([above_ref[...], below_ref[...]], axis=1)
    low_col = lax.broadcasted_iota(jnp.int32, (width, cols), 1) < LOW
    for block in range(blocks):
        matrix = matrix_ref[block].reshape(fields * width, depth)
        sums = jnp.dot(matrix, border, preferred_element_type=jnp.float32)
        modes = slice(block * width, (block + 1) * width)
        rows = []
        for r in range(height):
            total = inner_ref[modes, r * cols : (r + 1) * cols]
            for f in range(fields):
                part = sums[f * width : (f + 1) * width]
                if r == 0:
                    total = total - weight_row(weight_ref, height, f, 1, r) * part[:, :cols]
                if r == height - 1:
                    total = total - weight_row(weight_ref, height, f, 2, r) * part[:, cols:]
            rows.append(total)
        if not first:
            for r in range(height):
                code = encode(rows[r] * scale, SUM_POWER)
                out_ref[modes, r * cols : (r + 1) * cols] = code
            continue
        rows = along_cols(rows, right_ref)
        for r in range(height):
            value = rows[r] * scale
            code = encode(value, FIRST_POWER)
            out_ref[modes, r * cols : (r + 1) * cols] = code
            rest = jnp.where(low_col, value - decode(code, FIRST_POWER), 0.0)
            place = r % (cols // LOW)
            rest = pltpu.roll(rest, place * LOW, 1) if place else rest
            packed = rest if place == 0 else packed + rest
            if place == cols // LOW - 1 or r == height - 1:
                at = (height + r // (cols // LOW)) * cols
                out_ref[modes, at : at + cols] = packed.astype(jnp.bfloat16)


def coupled_sums(matrix, state, weights, right, first, scale, both):
    blocks, fields, width, depth = matrix.shape
    cells = state.shape[1]
    height = weights.shape[0] // (5 * fields)
    cols = cells // height
    mode_count = lax.axis_size("mode")
    slab_count = lax.axis_size("slab")
    place = [
        (t % mode_count) * slab_count + t // mode_count for t in range(mode_count * slab_count)
    ]
    onward = list(zip(place, place[1:] + place[:1]))
    above = lax.ppermute(state[:, -cols:], both, onward)
    below = lax.ppermute(state[:, :cols], both, [(b, a) for a, b in onward])
    unroll = math.gcd(blocks, UNROLL)
    matrix_spec = pl.BlockSpec((unroll, fields, width, depth), lambda i: (i, 0, 0, 0))
    weight_spec = pl.BlockSpec(weights.shape, lambda i: (0, 0))
    sums_spec = pl.BlockSpec((unroll * width, cells), lambda i: (i, 0))
    params = pltpu.CompilerParams(vmem_limit_bytes=VMEM_BYTES)
    inner = pl.pallas_call(
        functools.partial(inner_kernel, height, cols),
        grid=(blocks // unroll,),
        in_specs=[matrix_spec, pl.BlockSpec((depth, cells), lambda i: (0, 0)), weight_spec],
        out_specs=sums_spec,
        out_shape=jax.ShapeDtypeStruct((blocks * width, cells), jnp.float32),
        scratch_shapes=[pltpu.VMEM((fields * width, cells), jnp.float32)] * 2,
        cost_estimate=pl.CostEstimate(
            flops=2 * matrix.size * cells, bytes_accessed=2 * matrix.size, transcendentals=0
        ),
        compiler_params=params,
    )(matrix, state, weights)
    border_spec = pl.BlockSpec((depth, cols), lambda i: (0, 0))
    sent = cells + (low_tiles(height, cols) * cols if first else 0)
    return pl.pallas_call(
        functools.partial(border_kernel, height, cols, first, scale),
        grid=(blocks // unroll,),
        in_specs=[
            matrix_spec,
            border_spec,
            border_spec,
            weight_spec,
            sums_spec,
            pl.BlockSpec(right.shape, lambda i: (0, 0)),
        ],
        out_specs=pl.BlockSpec((unroll * width, sent), lambda i: (i, 0)),
        out_shape=jax.ShapeDtypeStruct((blocks * width, sent), jnp.bfloat16),
        compiler_params=params,
    )(matrix, above, below, weights, inner, right)


TOGETHER = 16
GROUP = 16


def solve(spectral, right_ref, left_ref, scale_ref):
    ny = spectral[0].shape[1]
    wide = along_rows(jnp.concatenate(spectral, axis=1), left_ref)
    wide = wide * jnp.concatenate([scale_ref[...]] * len(spectral), axis=1)
    wide = along_rows(wide, left_ref)
    return along_cols([wide[:, i * ny : (i + 1) * ny] for i in range(len(spectral))], right_ref)


def mean_kernel(first, current_ref, right_side_ref, weight_ref, right_ref, out_ref):
    nx, ny = weight_ref.shape[1:]

    def several(number, carry):
        values = []
        for i in range(TOGETHER):
            mode = number * TOGETHER + i
            here = current_ref[:, mode].reshape(nx, ny)
            mean = (
                weight_ref[0] * here
                - weight_ref[1] * pltpu.roll(here, 1, 0)
                - weight_ref[2] * pltpu.roll(here, nx - 1, 0)
                - pltpu.roll(weight_ref[4] * here, 1, 1)
                - pltpu.roll(weight_ref[3] * here, ny - 1, 1)
            )
            values.append(right_side_ref[:, mode].reshape(nx, ny) - mean)
        if first:
            values = along_cols(values, right_ref)
        for i in range(TOGETHER):
            out_ref[:, number * TOGETHER + i] = values[i].reshape(out_ref.shape[0], -1, ny)
        return carry

    lax.fori_loop(0, out_ref.shape[1] // TOGETHER, several, 0)


def turn_in(turned_ref, coupled_ref, mode_count, slab_count, height, first, scale):
    group = coupled_ref.shape[1]
    ny = turned_ref.shape[1]
    low_col = lax.broadcasted_iota(jnp.int32, (group, ny), 1) < LOW
    for source in range(mode_count * slab_count):
        start = ((source % slab_count) * mode_count + source // slab_count) * height
        for r in range(height):
            code = coupled_ref[source, :, r * ny : (r + 1) * ny]
            value = decode(code, FIRST_POWER if first else SUM_POWER)
            if first:
                at = (height + r // (ny // LOW)) * ny
                rest = coupled_ref[source, :, at : at + ny].astype(jnp.float32)
                place = r % (ny // LOW)
                rest = pltpu.roll(rest, ny - place * LOW, 1) if place else rest
                value = value + jnp.where(low_col, rest, 0.0)
            turned_ref[(start + r) * group : (start + r + 1) * group, :] = value * (1.0 / scale)


def step_kernel(
    mode_count,
    slab_count,
    code_scale,
    current_ref,
    base_ref,
    coupled_ref,
    right_ref,
    left_ref,
    scale_ref,
    solution_ref,
    state_ref,
    turned_ref,
):
    nx, ny = scale_ref.shape
    group = coupled_ref.shape[1]
    height = nx // (mode_count * slab_count)
    turn_in(turned_ref, coupled_ref, mode_count, slab_count, height, True, code_scale)

    def several(number, carry):
        start = number * TOGETHER
        resid = []
        for i in range(TOGETHER):
            coupled = turned_ref[pl.ds(start + i, nx, stride=group), :]
            resid.append(base_ref[:, start + i].reshape(nx, ny) - coupled)
        change = solve(resid, right_ref, left_ref, scale_ref)
        for i in range(TOGETHER):
            value = current_ref[:, start + i].reshape(nx, ny) + change[i]
            solution_ref[:, start + i] = value.reshape(slab_count, nx // slab_count, ny)
            turned_ref[pl.ds(start + i, nx, stride=group), :] = value
        return carry

    lax.fori_loop(0, group // TOGETHER, several, 0)

    for target in range(mode_count * slab_count):
        start = ((target % slab_count) * mode_count + target // slab_count) * height
        for r in range(height):
            row = start + r
            value = turned_ref[row * group : (row + 1) * group, :].astype(jnp.bfloat16)
            state_ref[target, :, r * ny : (r + 1) * ny] = value


def residual_kernel(
    mode_count, slab_count, code_scale, base_ref, coupled_ref, out_ref, code_ref, turned_ref
):
    group = coupled_ref.shape[1]
    ny = base_ref.shape[-1]
    nx = turned_ref.shape[0] // group
    height = nx // (mode_count * slab_count)
    turn_in(turned_ref, coupled_ref, mode_count, slab_count, height, False, code_scale)

    def one(mode, carry):
        coupled = turned_ref[pl.ds(mode, nx, stride=group), :]
        value = base_ref[:, mode] - coupled.reshape(slab_count, nx // slab_count, ny)
        out_ref[:, mode] = value
        code_ref[:, mode] = encode(value * code_scale, SUM_POWER)
        return carry

    lax.fori_loop(0, group, one, 0)


def correct_kernel(code_scale, current_ref, resid_ref, right_ref, left_ref, scale_ref, out_ref):
    nx, ny = scale_ref.shape

    def several(number, carry):
        start = number * TOGETHER
        resid = [resid_ref[:, start + i].reshape(nx, ny) for i in range(TOGETHER)]
        change = solve(along_cols(resid, right_ref), right_ref, left_ref, scale_ref)
        for i in range(TOGETHER):
            shape = out_ref.shape[:1] + out_ref.shape[2:]
            value = current_ref[:, start + i] + change[i].reshape(shape)
            out_ref[:, start + i] = encode(value * code_scale, SOLUTION_POWER)
        return carry

    lax.fori_loop(0, out_ref.shape[1] // TOGETHER, several, 0)


def whole(array):
    return pl.BlockSpec(array.shape, lambda g: (0,) * array.ndim)


def slabs_of(array):
    slab_count, _, rows, ny = array.shape
    return pl.BlockSpec((slab_count, GROUP, rows, ny), lambda g: (0, g, 0, 0))


def strips_of(shape):
    return pl.BlockSpec((shape[0], GROUP, shape[2]), lambda g: (0, g, 0))


def per_group(kernel, groups, operands, in_specs, out_shape, out_specs, scratch=(), flops=0):
    moved = sum(a.size * a.dtype.itemsize for a in operands)
    return pl.pallas_call(
        kernel,
        grid=(groups,),
        in_specs=in_specs,
        out_specs=out_specs,
        out_shape=out_shape,
        scratch_shapes=scratch,
        cost_estimate=pl.CostEstimate(flops=flops, bytes_accessed=2 * moved, transcendentals=0),
        compiler_params=pltpu.CompilerParams(vmem_limit_bytes=VMEM_BYTES),
    )(*operands)


def mean_part(current, right_side, weights, right, first):
    slabs = slabs_of(right_side)
    return per_group(
        functools.partial(mean_kernel, first),
        right_side.shape[1] // GROUP,
        (current, right_side, weights, right),
        [slabs, slabs, whole(weights), whole(right)],
        jax.ShapeDtypeStruct(right_side.shape, jnp.float32),
        slabs,
    )


def solve_flops(array, tables):
    nx, ny = tables[2].shape
    return array.shape[1] * 8 * 3 * nx * ny * (nx + ny) // 2


def step(current, base, coupled, tables, mode_count, slab_count, code_scale):
    nx, ny = tables[2].shape
    slabs = slabs_of(base)
    devices, modes, _ = coupled.shape
    state = (devices, modes, nx // devices * ny)
    return per_group(
        functools.partial(step_kernel, mode_count, slab_count, code_scale),
        modes // GROUP,
        (current, base, coupled, *tables),
        [slabs, slabs, strips_of(coupled.shape), *map(whole, tables)],
        [
            jax.ShapeDtypeStruct(base.shape, jnp.float32),
            jax.ShapeDtypeStruct(state, jnp.bfloat16),
        ],
        [slabs, strips_of(state)],
        [pltpu.VMEM((nx * GROUP, ny), jnp.float32)],
        solve_flops(base, tables),
    )


def last_residual(base, coupled, mode_count, slab_count, code_scale):
    slab, modes, rows, ny = base.shape
    slabs = slabs_of(base)
    return per_group(
        functools.partial(residual_kernel, mode_count, slab_count, code_scale),
        modes // GROUP,
        (base, coupled),
        [slabs, strips_of(coupled.shape)],
        [
            jax.ShapeDtypeStruct(base.shape, jnp.float32),
            jax.ShapeDtypeStruct(base.shape, jnp.bfloat16),
        ],
        [slabs, slabs],
        [pltpu.VMEM((slab * rows * GROUP, ny), jnp.float32)],
    )


def correct(current, resid, tables, code_scale):
    slabs = slabs_of(resid)
    return per_group(
        functools.partial(correct_kernel, code_scale),
        resid.shape[1] // GROUP,
        (current, resid, *tables),
        [slabs, slabs, *map(whole, tables)],
        jax.ShapeDtypeStruct(resid.shape, jnp.bfloat16),
        slabs,
        (),
        solve_flops(resid, tables),
    )


def collect(parts, axis):
    count = lax.axis_size(axis)
    here = lax.axis_index(axis)
    out = jnp.zeros((count,) + parts[0].shape[1:], parts[0].dtype)
    for shift, part in enumerate(parts):
        source = lax.rem(here + count - shift, count)
        out = lax.dynamic_update_slice_in_dim(out, part, source, 0)
    return out


def onwards(part, axis, shift):
    count = lax.axis_size(axis)
    return lax.ppermute(part, axis, [(i, (i + shift) % count) for i in range(count)])


def regroup_parts(block, axis):
    count = lax.axis_size(axis)
    here = lax.axis_index(axis)
    parts = [lax.dynamic_index_in_dim(block, here, 0)]
    for shift in range(1, count):
        target = lax.rem(here + shift, count)
        parts.append(onwards(lax.dynamic_index_in_dim(block, target, 0), axis, shift))
    return parts


def regroup(block, axis):
    return collect(regroup_parts(block, axis), axis)


def spread(block, axis):
    count = lax.axis_size(axis)
    return collect([block[None]] + [onwards(block[None], axis, i) for i in range(1, count)], axis)


def local(guess, right_side, mean_coef, field_coef, coupling, coupling_list, pair_count):
    mode_count = lax.axis_size("mode")
    slab_count = lax.axis_size("slab")
    both = ("mode", "slab")
    modes, rows, cols = guess.shape
    fields = field_coef.shape[0]
    nx = rows * slab_count
    devices = mode_count * slab_count
    height = nx // devices
    share = modes // slab_count

    strips = pack_strips(guess, mode_count)
    coefs = jnp.concatenate([mean_coef[None], field_coef], 0)
    strips, coefs = lax.optimization_barrier((strips, coefs))
    state = lax.all_to_all(strips, "mode", 0, 0, tiled=True)
    state = state.reshape(mode_count * modes, height * cols)

    def to_slabs(block):
        flat = block.reshape(modes, rows, cols)
        return lax.all_to_all(flat, "slab", 0, 0, tiled=True)

    coefs = spread(coefs, "slab")
    current = regroup(guess.reshape(slab_count, share, rows, cols), "slab")
    state, current, right_side = lax.optimization_barrier((state, current, right_side))
    right_parts = regroup_parts(right_side.reshape(slab_count, share, rows, cols), "slab")

    strip = lax.axis_index("slab") * mode_count + lax.axis_index("mode")
    mean_weights, strip_weights = all_weights(coefs, strip, height)
    matrix = dense_coupling(coupling, coupling_list, pair_count, fields)

    row_high, row_low = split_table(sine_table(nx))
    col_high, col_low = split_table(sine_table(cols))
    tables = (
        jnp.concatenate(
            [
                jnp.concatenate([col_high, col_low], 1),
                jnp.concatenate([col_high, jnp.zeros_like(col_low)], 1),
            ],
            0,
        ),
        jnp.concatenate(
            [
                jnp.concatenate([row_high, row_high], 1),
                jnp.concatenate([row_low, jnp.zeros_like(row_low)], 1),
            ],
            0,
        ),
        RELAXATION / eigen_table(nx, cols),
    )

    first_scale, sum_scale, solution_scale = code_scales(nx, cols, coupling.shape[1], modes)

    sums = coupled_sums(matrix, state, strip_weights, tables[0], True, first_scale, both)
    sums, *right_parts[1::2] = lax.optimization_barrier((sums, *right_parts[1::2]))
    sums = lax.all_to_all(sums, both, 0, 0, tiled=True).reshape(devices, share, -1)
    right_side = collect(right_parts, "slab")
    base = mean_part(current, right_side, mean_weights, tables[0], True)
    current, state = step(current, base, sums, tables, mode_count, slab_count, first_scale)
    state = state.reshape(devices * share, height * cols)
    state = lax.all_to_all(state, both, 0, 0, tiled=True)

    base = mean_part(current, right_side, mean_weights, tables[0], False)
    sums = coupled_sums(matrix, state, strip_weights, tables[0], False, sum_scale, both)
    sums = lax.all_to_all(sums, both, 0, 0, tiled=True).reshape(devices, share, -1)
    resid, code = last_residual(base, sums, mode_count, slab_count, sum_scale)
    moved = regroup(code, "slab").reshape(modes, rows, cols)
    resid_out = decode(moved, SUM_POWER) * (1.0 / sum_scale)
    code = correct(current, resid, tables, solution_scale)
    return decode(to_slabs(code), SOLUTION_POWER) * (1.0 / solution_scale), resid_out


def solution(mesh):
    placed = (
        P("mode", "slab", None),
        P("mode", "slab", None),
        P("slab", None),
        P(None, "slab", None),
        P(),
        P(),
        P(),
    )
    return jax.shard_map(
        local,
        mesh=mesh,
        in_specs=placed,
        out_specs=(P("mode", "slab", None), P("mode", "slab", None)),
        check_vma=False,
    )
```

```python
import functools
import math

import jax
import jax.numpy as jnp
from jax import lax
from jax.experimental import pallas as pl
from jax.experimental.pallas import tpu as pltpu
from jax.sharding import PartitionSpec as P

RELAXATION = 0.6
VMEM_BYTES = 60 << 20
SHARED_VMEM_BYTES = 32 << 20
UNROLL = 4


def sine_table(length):
    counter = jnp.arange(length).astype(jnp.float32) + 1.0
    angle = math.pi * counter[:, None] * counter[None, :] / (length + 1)
    return math.sqrt(2.0 / (length + 1)) * jnp.sin(angle)


def eigen_table(first, second):
    along_first = 2.0 * jnp.cos(
        math.pi * (jnp.arange(first).astype(jnp.float32) + 1.0) / (first + 1)
    )
    along_second = 2.0 * jnp.cos(
        math.pi * (jnp.arange(second).astype(jnp.float32) + 1.0) / (second + 1)
    )
    return 4.0 - along_first[:, None] - along_second[None, :]


def stencil_weights(coef):
    nx, ny = coef.shape
    row = lax.broadcasted_iota(jnp.int32, (nx, ny), 0)
    col = lax.broadcasted_iota(jnp.int32, (nx, ny), 1)
    sides = (
        (pltpu.roll(coef, 1, 0), row == 0),
        (pltpu.roll(coef, nx - 1, 0), row == nx - 1),
        (pltpu.roll(coef, 1, 1), col == 0),
        (pltpu.roll(coef, ny - 1, 1), col == ny - 1),
    )
    centre = 0.0
    weights = []
    for other, outside in sides:
        weight = 0.5 * (coef + jnp.where(outside, coef, other))
        centre = centre + weight
        weights.append(jnp.where(outside, 0.0, weight))
    return [centre] + weights


def weights_kernel(strip_ref, coef_ref, mean_ref, strip_weight_ref, full_ref):
    _, nx, ny = mean_ref.shape
    fields = coef_ref.shape[1] - 1
    height = strip_weight_ref.shape[0] // (5 * fields)
    for which, weight in enumerate(stencil_weights(coef_ref[:, 0].reshape(nx, ny))):
        mean_ref[which] = weight
    for f in range(fields):
        for which, weight in enumerate(stencil_weights(coef_ref[:, f + 1].reshape(nx, ny))):
            full_ref[...] = weight
            for r in range(height):
                at = (f * 5 + which) * height + r
                strip_weight_ref[at : at + 1, :] = full_ref[
                    pl.ds(strip_ref[0] * height + r, 1), :
                ]


def all_weights(coefs, strip, height):
    slab_count, entries, rows, ny = coefs.shape
    nx = slab_count * rows
    fields = entries - 1
    return pl.pallas_call(
        weights_kernel,
        grid_spec=pltpu.PrefetchScalarGridSpec(
            num_scalar_prefetch=1,
            grid=(1,),
            in_specs=[pl.BlockSpec(coefs.shape, lambda i, *_: (0, 0, 0, 0))],
            out_specs=[
                pl.BlockSpec((5, nx, ny), lambda i, *_: (0, 0, 0)),
                pl.BlockSpec((fields * 5 * height, ny), lambda i, *_: (0, 0)),
            ],
            scratch_shapes=[pltpu.VMEM((nx, ny), jnp.float32)],
        ),
        out_shape=[
            jax.ShapeDtypeStruct((5, nx, ny), jnp.float32),
            jax.ShapeDtypeStruct((fields * 5 * height, ny), jnp.float32),
        ],
        compiler_params=pltpu.CompilerParams(vmem_limit_bytes=SHARED_VMEM_BYTES),
    )(strip.reshape(1), coefs)


def split(value):
    high = value.astype(jnp.bfloat16)
    low = (value - high.astype(jnp.float32)).astype(jnp.bfloat16)
    return high, low


def split_table(value):
    high = lax.reduce_precision(value, 8, 7)
    return high.astype(jnp.bfloat16), (value - high).astype(jnp.bfloat16)


LOW = 32
FIRST_POWER = 7
SUM_POWER = 5
SOLUTION_POWER = 4


def encode(value, power):
    square = value * value
    if power == 4:
        result = square * (value * jnp.abs(value))
    elif power == 5:
        result = square * square * value
    else:
        result = (square * square) * (square * value)
    return result.astype(jnp.bfloat16)


def decode(code, power):
    code = code.astype(jnp.float32)
    size = jnp.abs(code)
    value = jnp.exp(jnp.log(size) * (1.0 / power))
    value = jnp.where(size > 0.0, value, 0.0)
    return jnp.where(code < 0.0, -value, value)


def code_scales(nx, ny, entries, width):
    guess_max, mean_max, field_max, coupling_max = 6.0, 2.0, 2.5, 0.0625
    gain = 8.0 * field_max * entries * width * coupling_max * 1.01
    inverse = (min(nx, ny) + 1) ** 2 / 8.0

    def bound(iterate):
        return guess_max + (8.0 * mean_max + gain) * iterate

    change = RELAXATION * inverse * 1.01
    second = guess_max + change * bound(guess_max)
    third = second + change * bound(second)

    def scale(limit, power):
        return 0.8 * 2.0 ** (127.0 / power) / limit

    first = math.sqrt(2.0 * ny) * gain * guess_max
    return (
        min(1.0, scale(first, FIRST_POWER)),
        min(1.0, scale(bound(second), SUM_POWER)),
        min(1.0, scale(third, SOLUTION_POWER)),
    )


def pack_kernel(rows, height, x_ref, out_ref):
    strips, modes, cells = out_ref.shape
    cols = cells // height
    for strip in range(strips):
        for r in range(height):
            value = x_ref[pl.ds(strip * height + r, modes, stride=rows), :]
            out_ref[strip, :, r * cols : (r + 1) * cols] = value.astype(jnp.bfloat16)


def pack_strips(block, strips):
    modes, rows, cols = block.shape
    height = rows // strips
    return pl.pallas_call(
        functools.partial(pack_kernel, rows, height),
        grid=(2,),
        in_specs=[pl.BlockSpec((modes // 2 * rows, cols), lambda g: (g, 0))],
        out_specs=pl.BlockSpec((strips, modes // 2, height * cols), lambda g: (0, g, 0)),
        out_shape=jax.ShapeDtypeStruct((strips, modes, height * cols), jnp.bfloat16),
        compiler_params=pltpu.CompilerParams(vmem_limit_bytes=VMEM_BYTES),
    )(block.reshape(modes * rows, cols))


def dense_kernel(fields, entry_ref, count_ref, coupling_ref, out_ref):
    block = pl.program_id(0)
    width = coupling_ref.shape[-1]
    out_ref[...] = jnp.zeros_like(out_ref)

    def place(k, carry):
        entry = entry_ref[block, k]
        column = pl.multiple_of((entry // fields) * width, width)
        out_ref[0, entry % fields, :, pl.ds(column, width)] = coupling_ref[0, k]
        return carry

    lax.fori_loop(0, count_ref[block], place, 0)


def dense_coupling(coupling, coupling_list, pair_count, fields):
    blocks, entries, width, _ = coupling.shape
    return pl.pallas_call(
        functools.partial(dense_kernel, fields),
        grid_spec=pltpu.PrefetchScalarGridSpec(
            num_scalar_prefetch=2,
            grid=(blocks,),
            in_specs=[pl.BlockSpec((1, entries, width, width), lambda i, *_: (i, 0, 0, 0))],
            out_specs=pl.BlockSpec(
                (1, fields, width, blocks * width), lambda i, *_: (i, 0, 0, 0)
            ),
        ),
        out_shape=jax.ShapeDtypeStruct((blocks, fields, width, blocks * width), coupling.dtype),
        compiler_params=pltpu.CompilerParams(vmem_limit_bytes=SHARED_VMEM_BYTES),
    )(coupling_list, pair_count, coupling)


def low_tiles(height, cols):
    return -(-height * LOW // cols)


def along_cols(fields, right_ref):
    size, ny = fields[0].shape
    high, low = split(jnp.concatenate(fields, axis=0))
    both = jnp.dot(
        jnp.concatenate([high, low], axis=1), right_ref[...], preferred_element_type=jnp.float32
    )
    both = both[:, :ny] + both[:, ny:]
    return [both[i * size : (i + 1) * size] for i in range(len(fields))]


def along_rows(wide, left_ref):
    nx = wide.shape[0]
    high, low = split(wide)
    both = jnp.dot(
        left_ref[...], jnp.concatenate([high, low], axis=0), preferred_element_type=jnp.float32
    )
    return both[:nx] + both[nx:]


def weight_row(weight_ref, height, field, which, r):
    at = (field * 5 + which) * height + r
    return weight_ref[at : at + 1, :]


def inner_kernel(height, cols, matrix_ref, state_ref, weight_ref, out_ref, sums_ref):
    blocks, fields, width, depth = matrix_ref.shape
    sums_ref[...] = jnp.dot(
        matrix_ref[...].reshape(blocks * fields * width, depth),
        state_ref[...],
        preferred_element_type=jnp.float32,
    )
    for block in range(blocks):
        for r in range(height):
            total = 0.0
            from_left = 0.0
            from_right = 0.0
            for f in range(fields):

                def row(at):
                    start = (block * fields + f) * width
                    return sums_ref[start : start + width, at * cols : (at + 1) * cols]

                weight = functools.partial(weight_row, weight_ref, height, f)
                here = row(r)
                total = total + weight(0, r) * here
                if r > 0:
                    total = total - weight(1, r) * row(r - 1)
                if r < height - 1:
                    total = total - weight(2, r) * row(r + 1)
                from_left = from_left + weight(4, r) * here
                from_right = from_right + weight(3, r) * here
            total = total - pltpu.roll(from_left, 1, 1) - pltpu.roll(from_right, cols - 1, 1)
            out_ref[block * width : (block + 1) * width, r * cols : (r + 1) * cols] = total


def border_kernel(
    height,
    cols,
    first,
    scale,
    matrix_ref,
    above_ref,
    below_ref,
    weight_ref,
    inner_ref,
    right_ref,
    out_ref,
):
    blocks, fields, width, depth = matrix_ref.shape
    border = jnp.concatenate([above_ref[...], below_ref[...]], axis=1)
    low_col = lax.broadcasted_iota(jnp.int32, (width, cols), 1) < LOW
    matrix = matrix_ref[...].reshape(blocks * fields * width, depth)
    sums = jnp.dot(matrix, border, preferred_element_type=jnp.float32)
    for block in range(blocks):
        modes = slice(block * width, (block + 1) * width)
        rows = []
        for r in range(height):
            total = inner_ref[modes, r * cols : (r + 1) * cols]
            for f in range(fields):
                part = sums[(block * fields + f) * width : (block * fields + f + 1) * width]
                if r == 0:
                    total = total - weight_row(weight_ref, height, f, 1, r) * part[:, :cols]
                if r == height - 1:
                    total = total - weight_row(weight_ref, height, f, 2, r) * part[:, cols:]
            rows.append(total)
        if not first:
            for r in range(height):
                code = encode(rows[r] * scale, SUM_POWER)
                out_ref[modes, r * cols : (r + 1) * cols] = code
            continue
        rows = along_cols(rows, right_ref)
        for r in range(height):
            value = rows[r] * scale
            code = encode(value, FIRST_POWER)
            out_ref[modes, r * cols : (r + 1) * cols] = code
            rest = jnp.where(low_col, value - decode(code, FIRST_POWER), 0.0)
            place = r % (cols // LOW)
            rest = pltpu.roll(rest, place * LOW, 1) if place else rest
            packed = rest if place == 0 else packed + rest
            if place == cols // LOW - 1 or r == height - 1:
                at = (height + r // (cols // LOW)) * cols
                out_ref[modes, at : at + cols] = packed.astype(jnp.bfloat16)


def coupled_sums(matrix, state, weights, right, first, scale, both):
    blocks, fields, width, depth = matrix.shape
    cells = state.shape[1]
    height = weights.shape[0] // (5 * fields)
    cols = cells // height
    mode_count = lax.axis_size("mode")
    slab_count = lax.axis_size("slab")
    place = [
        (t % mode_count) * slab_count + t // mode_count for t in range(mode_count * slab_count)
    ]
    onward = list(zip(place, place[1:] + place[:1]))
    above = lax.ppermute(state[:, -cols:], both, onward)
    below = lax.ppermute(state[:, :cols], both, [(b, a) for a, b in onward])
    unroll = math.gcd(blocks, UNROLL)
    matrix_spec = pl.BlockSpec((unroll, fields, width, depth), lambda i: (i, 0, 0, 0))
    weight_spec = pl.BlockSpec(weights.shape, lambda i: (0, 0))
    sums_spec = pl.BlockSpec((unroll * width, cells), lambda i: (i, 0))
    params = pltpu.CompilerParams(vmem_limit_bytes=SHARED_VMEM_BYTES)
    inner = pl.pallas_call(
        functools.partial(inner_kernel, height, cols),
        grid=(blocks // unroll,),
        in_specs=[matrix_spec, pl.BlockSpec((depth, cells), lambda i: (0, 0)), weight_spec],
        out_specs=sums_spec,
        out_shape=jax.ShapeDtypeStruct((blocks * width, cells), jnp.float32),
        scratch_shapes=[pltpu.VMEM((unroll * fields * width, cells), jnp.float32)],
        cost_estimate=pl.CostEstimate(
            flops=2 * matrix.size * cells, bytes_accessed=2 * matrix.size, transcendentals=0
        ),
        compiler_params=params,
    )(matrix, state, weights)
    border_spec = pl.BlockSpec((depth, cols), lambda i: (0, 0))
    sent = cells + (low_tiles(height, cols) * cols if first else 0)
    return pl.pallas_call(
        functools.partial(border_kernel, height, cols, first, scale),
        grid=(blocks // unroll,),
        in_specs=[
            matrix_spec,
            border_spec,
            border_spec,
            weight_spec,
            sums_spec,
            pl.BlockSpec(right.shape, lambda i: (0, 0)),
        ],
        out_specs=pl.BlockSpec((unroll * width, sent), lambda i: (i, 0)),
        out_shape=jax.ShapeDtypeStruct((blocks * width, sent), jnp.bfloat16),
        compiler_params=params,
    )(matrix, above, below, weights, inner, right)


TOGETHER = 16
GROUP = 16


def solve(spectral, right_ref, left_ref, scale_ref):
    ny = spectral[0].shape[1]
    wide = along_rows(jnp.concatenate(spectral, axis=1), left_ref)
    wide = wide * jnp.concatenate([scale_ref[...]] * len(spectral), axis=1)
    wide = along_rows(wide, left_ref)
    return along_cols([wide[:, i * ny : (i + 1) * ny] for i in range(len(spectral))], right_ref)


def mean_kernel(first, current_ref, right_side_ref, weight_ref, right_ref, out_ref):
    nx, ny = weight_ref.shape[1:]

    def several(number, carry):
        values = []
        for i in range(TOGETHER):
            mode = number * TOGETHER + i
            here = current_ref[:, mode].reshape(nx, ny)
            mean = (
                weight_ref[0] * here
                - weight_ref[1] * pltpu.roll(here, 1, 0)
                - weight_ref[2] * pltpu.roll(here, nx - 1, 0)
                - pltpu.roll(weight_ref[4] * here, 1, 1)
                - pltpu.roll(weight_ref[3] * here, ny - 1, 1)
            )
            values.append(right_side_ref[:, mode].reshape(nx, ny) - mean)
        if first:
            values = along_cols(values, right_ref)
        for i in range(TOGETHER):
            out_ref[:, number * TOGETHER + i] = values[i].reshape(out_ref.shape[0], -1, ny)
        return carry

    lax.fori_loop(0, out_ref.shape[1] // TOGETHER, several, 0)


def turn_in(turned_ref, coupled_ref, mode_count, slab_count, height, first, scale):
    group = coupled_ref.shape[1]
    ny = turned_ref.shape[1]
    low_col = lax.broadcasted_iota(jnp.int32, (group, ny), 1) < LOW
    for source in range(mode_count * slab_count):
        start = ((source % slab_count) * mode_count + source // slab_count) * height
        for r in range(height):
            code = coupled_ref[source, :, r * ny : (r + 1) * ny]
            value = decode(code, FIRST_POWER if first else SUM_POWER)
            if first:
                at = (height + r // (ny // LOW)) * ny
                rest = coupled_ref[source, :, at : at + ny].astype(jnp.float32)
                place = r % (ny // LOW)
                rest = pltpu.roll(rest, ny - place * LOW, 1) if place else rest
                value = value + jnp.where(low_col, rest, 0.0)
            turned_ref[(start + r) * group : (start + r + 1) * group, :] = value * (1.0 / scale)


def step_kernel(
    mode_count,
    slab_count,
    code_scale,
    current_ref,
    base_ref,
    coupled_ref,
    right_ref,
    left_ref,
    scale_ref,
    solution_ref,
    state_ref,
    turned_ref,
):
    nx, ny = scale_ref.shape
    group = coupled_ref.shape[1]
    height = nx // (mode_count * slab_count)
    turn_in(turned_ref, coupled_ref, mode_count, slab_count, height, True, code_scale)

    def several(number, carry):
        start = number * TOGETHER
        resid = []
        for i in range(TOGETHER):
            coupled = turned_ref[pl.ds(start + i, nx, stride=group), :]
            resid.append(base_ref[:, start + i].reshape(nx, ny) - coupled)
        change = solve(resid, right_ref, left_ref, scale_ref)
        for i in range(TOGETHER):
            value = current_ref[:, start + i].reshape(nx, ny) + change[i]
            solution_ref[:, start + i] = value.reshape(slab_count, nx // slab_count, ny)
            turned_ref[pl.ds(start + i, nx, stride=group), :] = value
        return carry

    lax.fori_loop(0, group // TOGETHER, several, 0)

    for target in range(mode_count * slab_count):
        start = ((target % slab_count) * mode_count + target // slab_count) * height
        for r in range(height):
            row = start + r
            value = turned_ref[row * group : (row + 1) * group, :].astype(jnp.bfloat16)
            state_ref[target, :, r * ny : (r + 1) * ny] = value


def residual_kernel(
    mode_count, slab_count, code_scale, here_ref, base_ref, coupled_ref, out_ref, *refs
):
    *code_refs, turned_ref = refs
    group = coupled_ref.shape[1]
    ny = base_ref.shape[-1]
    nx = turned_ref.shape[0] // group
    height = nx // (mode_count * slab_count)
    turn_in(turned_ref, coupled_ref, mode_count, slab_count, height, False, code_scale)

    def one(mode, carry):
        coupled = turned_ref[pl.ds(mode, nx, stride=group), :]
        out_ref[:, mode] = base_ref[:, mode] - coupled.reshape(slab_count, nx // slab_count, ny)
        return carry

    lax.fori_loop(0, group, one, 0)
    for shift, code_ref in enumerate(code_refs):
        slab = lax.rem(here_ref[0] + shift, slab_count)
        code_ref[0] = encode(out_ref[slab] * code_scale, SUM_POWER)


def correct_kernel(code_scale, current_ref, resid_ref, right_ref, left_ref, scale_ref, out_ref):
    nx, ny = scale_ref.shape

    def several(number, carry):
        start = number * TOGETHER
        resid = [resid_ref[:, start + i].reshape(nx, ny) for i in range(TOGETHER)]
        change = solve(along_cols(resid, right_ref), right_ref, left_ref, scale_ref)
        for i in range(TOGETHER):
            shape = out_ref.shape[:1] + out_ref.shape[2:]
            value = current_ref[:, start + i] + change[i].reshape(shape)
            out_ref[:, start + i] = encode(value * code_scale, SOLUTION_POWER)
        return carry

    lax.fori_loop(0, out_ref.shape[1] // TOGETHER, several, 0)


def whole(array):
    return pl.BlockSpec(array.shape, lambda g: (0,) * array.ndim)


def slabs_of(array):
    slab_count, _, rows, ny = array.shape
    return pl.BlockSpec((slab_count, GROUP, rows, ny), lambda g: (0, g, 0, 0))


def strips_of(shape):
    return pl.BlockSpec((shape[0], GROUP, shape[2]), lambda g: (0, g, 0))


def per_group(kernel, groups, operands, in_specs, out_shape, out_specs, scratch=(), flops=0):
    moved = sum(a.size * a.dtype.itemsize for a in operands)
    return pl.pallas_call(
        kernel,
        grid=(groups,),
        in_specs=in_specs,
        out_specs=out_specs,
        out_shape=out_shape,
        scratch_shapes=scratch,
        cost_estimate=pl.CostEstimate(flops=flops, bytes_accessed=2 * moved, transcendentals=0),
        compiler_params=pltpu.CompilerParams(vmem_limit_bytes=VMEM_BYTES),
    )(*operands)


def mean_part(current, right_side, weights, right, first):
    slabs = slabs_of(right_side)
    return per_group(
        functools.partial(mean_kernel, first),
        right_side.shape[1] // GROUP,
        (current, right_side, weights, right),
        [slabs, slabs, whole(weights), whole(right)],
        jax.ShapeDtypeStruct(right_side.shape, jnp.float32),
        slabs,
    )


def solve_flops(array, tables):
    nx, ny = tables[2].shape
    return array.shape[1] * 8 * 3 * nx * ny * (nx + ny) // 2


def step(current, base, coupled, tables, mode_count, slab_count, code_scale):
    nx, ny = tables[2].shape
    slabs = slabs_of(base)
    devices, modes, _ = coupled.shape
    state = (devices, modes, nx // devices * ny)
    return per_group(
        functools.partial(step_kernel, mode_count, slab_count, code_scale),
        modes // GROUP,
        (current, base, coupled, *tables),
        [slabs, slabs, strips_of(coupled.shape), *map(whole, tables)],
        [
            jax.ShapeDtypeStruct(base.shape, jnp.float32),
            jax.ShapeDtypeStruct(state, jnp.bfloat16),
        ],
        [slabs, strips_of(state)],
        [pltpu.VMEM((nx * GROUP, ny), jnp.float32)],
        solve_flops(base, tables),
    )


def last_residual(base, coupled, mode_count, slab_count, code_scale):
    slab, modes, rows, ny = base.shape
    slabs = pl.BlockSpec((slab, GROUP, rows, ny), lambda g, *_: (0, g, 0, 0))
    part = pl.BlockSpec((1, GROUP, rows, ny), lambda g, *_: (0, g, 0, 0))
    devices, _, cells = coupled.shape
    out, *parts = pl.pallas_call(
        functools.partial(residual_kernel, mode_count, slab_count, code_scale),
        grid_spec=pltpu.PrefetchScalarGridSpec(
            num_scalar_prefetch=1,
            grid=(modes // GROUP,),
            in_specs=[slabs, pl.BlockSpec((devices, GROUP, cells), lambda g, *_: (0, g, 0))],
            out_specs=[slabs] + [part] * slab,
            scratch_shapes=[pltpu.VMEM((slab * rows * GROUP, ny), jnp.float32)],
        ),
        out_shape=[jax.ShapeDtypeStruct(base.shape, jnp.float32)]
        + [jax.ShapeDtypeStruct((1, modes, rows, ny), jnp.bfloat16)] * slab,
        cost_estimate=pl.CostEstimate(
            flops=0, bytes_accessed=2 * base.size * 4, transcendentals=0
        ),
        compiler_params=pltpu.CompilerParams(vmem_limit_bytes=VMEM_BYTES),
    )(lax.axis_index("slab").reshape(1), base, coupled)
    return out, parts


def correct(current, resid, tables, code_scale):
    slabs = slabs_of(resid)
    return per_group(
        functools.partial(correct_kernel, code_scale),
        resid.shape[1] // GROUP,
        (current, resid, *tables),
        [slabs, slabs, *map(whole, tables)],
        jax.ShapeDtypeStruct(resid.shape, jnp.bfloat16),
        slabs,
        (),
        solve_flops(resid, tables),
    )


def collect(parts, axis):
    count = lax.axis_size(axis)
    here = lax.axis_index(axis)
    out = jnp.zeros((count,) + parts[0].shape[1:], parts[0].dtype)
    for shift, part in enumerate(parts):
        source = lax.rem(here + count - shift, count)
        out = lax.dynamic_update_slice_in_dim(out, part, source, 0)
    return out


def onwards(part, axis, shift):
    count = lax.axis_size(axis)
    return lax.ppermute(part, axis, [(i, (i + shift) % count) for i in range(count)])


def parts_of(block, axis):
    count = lax.axis_size(axis)
    here = lax.axis_index(axis)
    return [
        lax.dynamic_index_in_dim(block, lax.rem(here + shift, count), 0) for shift in range(count)
    ]


def moved_parts(parts, axis):
    return [parts[0]] + [onwards(parts[i], axis, i) for i in range(1, len(parts))]


def spread(block, axis):
    count = lax.axis_size(axis)
    return collect([block[None]] + [onwards(block[None], axis, i) for i in range(1, count)], axis)


def local(guess, right_side, mean_coef, field_coef, coupling, coupling_list, pair_count):
    mode_count = lax.axis_size("mode")
    slab_count = lax.axis_size("slab")
    both = ("mode", "slab")
    modes, rows, cols = guess.shape
    fields = field_coef.shape[0]
    nx = rows * slab_count
    devices = mode_count * slab_count
    height = nx // devices
    share = modes // slab_count

    strips = pack_strips(guess, mode_count)
    coefs = jnp.concatenate([mean_coef[None], field_coef], 0)
    strips, coefs = lax.optimization_barrier((strips, coefs))
    state = lax.all_to_all(strips, "mode", 0, 0, tiled=True)
    state = state.reshape(mode_count * modes, height * cols)

    def to_slabs(block):
        flat = block.reshape(modes, rows, cols)
        return lax.all_to_all(flat, "slab", 0, 0, tiled=True)

    coefs = spread(coefs, "slab")
    guess_parts = parts_of(guess.reshape(slab_count, share, rows, cols), "slab")
    current = collect(moved_parts(guess_parts, "slab"), "slab")
    right_parts = parts_of(right_side.reshape(slab_count, share, rows, cols), "slab")
    state, current, right_parts = lax.optimization_barrier((state, current, right_parts))
    right_side = collect(moved_parts(right_parts, "slab"), "slab")

    strip = lax.axis_index("slab") * mode_count + lax.axis_index("mode")
    mean_weights, strip_weights = all_weights(coefs, strip, height)
    matrix = dense_coupling(coupling, coupling_list, pair_count, fields)

    row_high, row_low = split_table(sine_table(nx))
    col_high, col_low = split_table(sine_table(cols))
    tables = (
        jnp.concatenate(
            [
                jnp.concatenate([col_high, col_low], 1),
                jnp.concatenate([col_high, jnp.zeros_like(col_low)], 1),
            ],
            0,
        ),
        jnp.concatenate(
            [
                jnp.concatenate([row_high, row_high], 1),
                jnp.concatenate([row_low, jnp.zeros_like(row_low)], 1),
            ],
            0,
        ),
        RELAXATION / eigen_table(nx, cols),
    )

    first_scale, sum_scale, solution_scale = code_scales(nx, cols, coupling.shape[1], modes)

    sums = coupled_sums(matrix, state, strip_weights, tables[0], True, first_scale, both)
    sums, right_side = lax.optimization_barrier((sums, right_side))
    sums = lax.all_to_all(sums, both, 0, 0, tiled=True).reshape(devices, share, -1)
    base = mean_part(current, right_side, mean_weights, tables[0], True)
    current, state = step(current, base, sums, tables, mode_count, slab_count, first_scale)
    state = state.reshape(devices * share, height * cols)
    state = lax.all_to_all(state, both, 0, 0, tiled=True)

    base = mean_part(current, right_side, mean_weights, tables[0], False)
    sums = coupled_sums(matrix, state, strip_weights, tables[0], False, sum_scale, both)
    sums = lax.all_to_all(sums, both, 0, 0, tiled=True).reshape(devices, share, -1)
    resid, parts = last_residual(base, sums, mode_count, slab_count, sum_scale)
    moved = collect(moved_parts(parts, "slab"), "slab").reshape(modes, rows, cols)
    resid_out = decode(moved, SUM_POWER) * (1.0 / sum_scale)
    code = correct(current, resid, tables, solution_scale)
    return decode(to_slabs(code), SOLUTION_POWER) * (1.0 / solution_scale), resid_out


def solution(mesh):
    placed = (
        P("mode", "slab", None),
        P("mode", "slab", None),
        P("slab", None),
        P(None, "slab", None),
        P(),
        P(),
        P(),
    )
    return jax.shard_map(
        local,
        mesh=mesh,
        in_specs=placed,
        out_specs=(P("mode", "slab", None), P("mode", "slab", None)),
        check_vma=False,
    )
```

```python
import functools
import math

import jax
import jax.numpy as jnp
from jax import lax
from jax.experimental import pallas as pl
from jax.experimental.pallas import tpu as pltpu
from jax.sharding import PartitionSpec as P

RELAXATION = 0.6
VMEM_BYTES = 57 << 20
UNROLL = 2


def sine_table(length):
    counter = jnp.arange(length).astype(jnp.float32) + 1.0
    angle = math.pi * counter[:, None] * counter[None, :] / (length + 1)
    return math.sqrt(2.0 / (length + 1)) * jnp.sin(angle)


def eigen_table(first, second):
    along_first = 2.0 * jnp.cos(
        math.pi * (jnp.arange(first).astype(jnp.float32) + 1.0) / (first + 1)
    )
    along_second = 2.0 * jnp.cos(
        math.pi * (jnp.arange(second).astype(jnp.float32) + 1.0) / (second + 1)
    )
    return 4.0 - along_first[:, None] - along_second[None, :]


def stencil_weights(coef):
    nx, ny = coef.shape
    row = lax.broadcasted_iota(jnp.int32, (nx, ny), 0)
    col = lax.broadcasted_iota(jnp.int32, (nx, ny), 1)
    sides = (
        (pltpu.roll(coef, 1, 0), row == 0),
        (pltpu.roll(coef, nx - 1, 0), row == nx - 1),
        (pltpu.roll(coef, 1, 1), col == 0),
        (pltpu.roll(coef, ny - 1, 1), col == ny - 1),
    )
    centre = 0.0
    weights = []
    for other, outside in sides:
        weight = 0.5 * (coef + jnp.where(outside, coef, other))
        centre = centre + weight
        weights.append(jnp.where(outside, 0.0, weight))
    return [centre] + weights


def in_order(here, shift, count):
    return lax.rem(here + count - shift, count)


def weights_kernel(slabs, place_ref, *refs):
    part_refs = refs[:slabs]
    mean_ref, strip_weight_ref, coef_ref, full_ref = refs[slabs:]
    _, nx, ny = mean_ref.shape
    fields = coef_ref.shape[1] - 1
    height = strip_weight_ref.shape[0] // (5 * fields)
    for shift, part_ref in enumerate(part_refs):
        coef_ref[in_order(place_ref[0], shift, slabs)] = part_ref[0]
    for which, weight in enumerate(stencil_weights(coef_ref[:, 0].reshape(nx, ny))):
        mean_ref[which] = weight
    for f in range(fields):
        for which, weight in enumerate(stencil_weights(coef_ref[:, f + 1].reshape(nx, ny))):
            full_ref[...] = weight
            for r in range(height):
                at = (f * 5 + which) * height + r
                strip_weight_ref[at : at + 1, :] = full_ref[
                    pl.ds(place_ref[1] * height + r, 1), :
                ]


def all_weights(parts, place, coefs, height):
    slab_count = len(parts)
    _, entries, rows, ny = parts[0].shape
    nx = slab_count * rows
    last = entries // coefs - 1
    fields = coefs - 1
    return pl.pallas_call(
        functools.partial(weights_kernel, slab_count),
        grid_spec=pltpu.PrefetchScalarGridSpec(
            num_scalar_prefetch=1,
            grid=(1,),
            in_specs=[pl.BlockSpec((1, coefs, rows, ny), lambda i, *_: (0, last, 0, 0))]
            * slab_count,
            out_specs=[
                pl.BlockSpec((5, nx, ny), lambda i, *_: (0, 0, 0)),
                pl.BlockSpec((fields * 5 * height, ny), lambda i, *_: (0, 0)),
            ],
            scratch_shapes=[
                pltpu.VMEM((slab_count, coefs, rows, ny), jnp.float32),
                pltpu.VMEM((nx, ny), jnp.float32),
            ],
        ),
        out_shape=[
            jax.ShapeDtypeStruct((5, nx, ny), jnp.float32),
            jax.ShapeDtypeStruct((fields * 5 * height, ny), jnp.float32),
        ],
        compiler_params=pltpu.CompilerParams(vmem_limit_bytes=VMEM_BYTES),
    )(place, *parts)


def split(value):
    high = value.astype(jnp.bfloat16)
    low = (value - high.astype(jnp.float32)).astype(jnp.bfloat16)
    return high, low


def split_table(value):
    high = lax.reduce_precision(value, 8, 7)
    return high.astype(jnp.bfloat16), (value - high).astype(jnp.bfloat16)


LOW = 32
FIRST_POWER = 7
SUM_POWER = 5
SOLUTION_POWER = 4


def encode(value, power):
    square = value * value
    if power == 4:
        result = square * (value * jnp.abs(value))
    elif power == 5:
        result = square * square * value
    else:
        result = (square * square) * (square * value)
    return result.astype(jnp.bfloat16)


def decode(code, power):
    code = code.astype(jnp.float32)
    size = jnp.abs(code)
    value = jnp.exp(jnp.log(size) * (1.0 / power))
    value = jnp.where(size > 0.0, value, 0.0)
    return jnp.where(code < 0.0, -value, value)


def code_scales(nx, ny, entries, width):
    guess_max, mean_max, field_max, coupling_max = 6.0, 2.0, 2.5, 0.0625
    gain = 8.0 * field_max * entries * width * coupling_max * 1.01
    inverse = (min(nx, ny) + 1) ** 2 / 8.0

    def bound(iterate):
        return guess_max + (8.0 * mean_max + gain) * iterate

    change = RELAXATION * inverse * 1.01
    second = guess_max + change * bound(guess_max)
    third = second + change * bound(second)

    def scale(limit, power):
        return 0.8 * 2.0 ** (127.0 / power) / limit

    first = math.sqrt(2.0 * ny) * gain * guess_max
    return (
        min(1.0, scale(first, FIRST_POWER)),
        min(1.0, scale(bound(second), SUM_POWER)),
        min(1.0, scale(third, SOLUTION_POWER)),
    )


def pack_kernel(rows, height, x_ref, out_ref):
    strips, modes, cells = out_ref.shape
    cols = cells // height
    for strip in range(strips):
        for r in range(height):
            value = x_ref[pl.ds(strip * height + r, modes, stride=rows), :]
            out_ref[strip, :, r * cols : (r + 1) * cols] = value.astype(jnp.bfloat16)


def pack_strips(block, strips):
    modes, rows, cols = block.shape
    height = rows // strips
    return pl.pallas_call(
        functools.partial(pack_kernel, rows, height),
        grid=(2,),
        in_specs=[pl.BlockSpec((modes // 2 * rows, cols), lambda g: (g, 0))],
        out_specs=pl.BlockSpec((strips, modes // 2, height * cols), lambda g: (0, g, 0)),
        out_shape=jax.ShapeDtypeStruct((strips, modes, height * cols), jnp.bfloat16),
        compiler_params=pltpu.CompilerParams(vmem_limit_bytes=VMEM_BYTES),
    )(block.reshape(modes * rows, cols))


def dense_kernel(fields, entry_ref, count_ref, coupling_ref, out_ref):
    block = pl.program_id(0)
    width = coupling_ref.shape[-1]
    out_ref[...] = jnp.zeros_like(out_ref)

    def place(k, carry):
        entry = entry_ref[block, k]
        column = pl.multiple_of((entry // fields) * width, width)
        out_ref[0, entry % fields, :, pl.ds(column, width)] = coupling_ref[0, k]
        return carry

    lax.fori_loop(0, count_ref[block], place, 0)


def dense_coupling(coupling, coupling_list, pair_count, fields):
    blocks, entries, width, _ = coupling.shape
    return pl.pallas_call(
        functools.partial(dense_kernel, fields),
        grid_spec=pltpu.PrefetchScalarGridSpec(
            num_scalar_prefetch=2,
            grid=(blocks,),
            in_specs=[pl.BlockSpec((1, entries, width, width), lambda i, *_: (i, 0, 0, 0))],
            out_specs=pl.BlockSpec(
                (1, fields, width, blocks * width), lambda i, *_: (i, 0, 0, 0)
            ),
        ),
        out_shape=jax.ShapeDtypeStruct((blocks, fields, width, blocks * width), coupling.dtype),
        compiler_params=pltpu.CompilerParams(vmem_limit_bytes=VMEM_BYTES),
    )(coupling_list, pair_count, coupling)


def low_tiles(height, cols):
    return -(-height * LOW // cols)


def along_cols(fields, right_ref):
    size, ny = fields[0].shape
    high, low = split(jnp.concatenate(fields, axis=0))
    both = jnp.dot(
        jnp.concatenate([high, low], axis=1), right_ref[...], preferred_element_type=jnp.float32
    )
    both = both[:, :ny] + both[:, ny:]
    return [both[i * size : (i + 1) * size] for i in range(len(fields))]


def along_rows(wide, left_ref):
    nx = wide.shape[0]
    high, low = split(wide)
    both = jnp.dot(
        left_ref[...], jnp.concatenate([high, low], axis=0), preferred_element_type=jnp.float32
    )
    return both[:nx] + both[nx:]


def weight_row(weight_ref, height, field, which, r):
    at = (field * 5 + which) * height + r
    return weight_ref[at : at + 1, :]


def inner_kernel(height, cols, matrix_ref, state_ref, weight_ref, out_ref, sums_ref):
    blocks, fields, width, depth = matrix_ref.shape
    sums_ref[...] = jnp.dot(
        matrix_ref[...].reshape(blocks * fields * width, depth),
        state_ref[...],
        preferred_element_type=jnp.float32,
    )
    for block in range(blocks):
        for r in range(height):
            total = 0.0
            from_left = 0.0
            from_right = 0.0
            for f in range(fields):

                def row(at):
                    start = (block * fields + f) * width
                    return sums_ref[start : start + width, at * cols : (at + 1) * cols]

                weight = functools.partial(weight_row, weight_ref, height, f)
                here = row(r)
                total = total + weight(0, r) * here
                if r > 0:
                    total = total - weight(1, r) * row(r - 1)
                if r < height - 1:
                    total = total - weight(2, r) * row(r + 1)
                from_left = from_left + weight(4, r) * here
                from_right = from_right + weight(3, r) * here
            total = total - pltpu.roll(from_left, 1, 1) - pltpu.roll(from_right, cols - 1, 1)
            out_ref[block * width : (block + 1) * width, r * cols : (r + 1) * cols] = total


def border_kernel(
    height,
    cols,
    first,
    scale,
    matrix_ref,
    above_ref,
    below_ref,
    weight_ref,
    inner_ref,
    right_ref,
    out_ref,
):
    blocks, fields, width, depth = matrix_ref.shape
    border = jnp.concatenate([above_ref[...], below_ref[...]], axis=1)
    low_col = lax.broadcasted_iota(jnp.int32, (width, cols), 1) < LOW
    matrix = matrix_ref[...].reshape(blocks * fields * width, depth)
    sums = jnp.dot(matrix, border, preferred_element_type=jnp.float32)
    for block in range(blocks):
        modes = slice(block * width, (block + 1) * width)
        rows = []
        for r in range(height):
            total = inner_ref[modes, r * cols : (r + 1) * cols]
            for f in range(fields):
                part = sums[(block * fields + f) * width : (block * fields + f + 1) * width]
                if r == 0:
                    total = total - weight_row(weight_ref, height, f, 1, r) * part[:, :cols]
                if r == height - 1:
                    total = total - weight_row(weight_ref, height, f, 2, r) * part[:, cols:]
            rows.append(total)
        if not first:
            for r in range(height):
                code = encode(rows[r] * scale, SUM_POWER)
                out_ref[modes, r * cols : (r + 1) * cols] = code
            continue
        rows = along_cols(rows, right_ref)
        for r in range(height):
            value = rows[r] * scale
            code = encode(value, FIRST_POWER)
            out_ref[modes, r * cols : (r + 1) * cols] = code
            rest = jnp.where(low_col, value - decode(code, FIRST_POWER), 0.0)
            place = r % (cols // LOW)
            rest = pltpu.roll(rest, place * LOW, 1) if place else rest
            packed = rest if place == 0 else packed + rest
            if place == cols // LOW - 1 or r == height - 1:
                at = (height + r // (cols // LOW)) * cols
                out_ref[modes, at : at + cols] = packed.astype(jnp.bfloat16)


def coupled_sums(matrix, state, weights, right, first, scale, both):
    blocks, fields, width, depth = matrix.shape
    cells = state.shape[1]
    height = weights.shape[0] // (5 * fields)
    cols = cells // height
    mode_count = lax.axis_size("mode")
    slab_count = lax.axis_size("slab")
    place = [
        (t % mode_count) * slab_count + t // mode_count for t in range(mode_count * slab_count)
    ]
    onward = list(zip(place, place[1:] + place[:1]))
    above = lax.ppermute(state[:, -cols:], both, onward)
    below = lax.ppermute(state[:, :cols], both, [(b, a) for a, b in onward])
    unroll = math.gcd(blocks, UNROLL)
    matrix_spec = pl.BlockSpec((unroll, fields, width, depth), lambda i: (i, 0, 0, 0))
    weight_spec = pl.BlockSpec(weights.shape, lambda i: (0, 0))
    sums_spec = pl.BlockSpec((unroll * width, cells), lambda i: (i, 0))
    params = pltpu.CompilerParams(vmem_limit_bytes=VMEM_BYTES)
    inner = pl.pallas_call(
        functools.partial(inner_kernel, height, cols),
        grid=(blocks // unroll,),
        in_specs=[matrix_spec, pl.BlockSpec((depth, cells), lambda i: (0, 0)), weight_spec],
        out_specs=sums_spec,
        out_shape=jax.ShapeDtypeStruct((blocks * width, cells), jnp.float32),
        scratch_shapes=[pltpu.VMEM((unroll * fields * width, cells), jnp.float32)],
        cost_estimate=pl.CostEstimate(
            flops=2 * matrix.size * cells, bytes_accessed=2 * matrix.size, transcendentals=0
        ),
        compiler_params=params,
    )(matrix, state, weights)
    border_spec = pl.BlockSpec((depth, cols), lambda i: (0, 0))
    sent = cells + (low_tiles(height, cols) * cols if first else 0)
    return pl.pallas_call(
        functools.partial(border_kernel, height, cols, first, scale),
        grid=(blocks // unroll,),
        in_specs=[
            matrix_spec,
            border_spec,
            border_spec,
            weight_spec,
            sums_spec,
            pl.BlockSpec(right.shape, lambda i: (0, 0)),
        ],
        out_specs=pl.BlockSpec((unroll * width, sent), lambda i: (i, 0)),
        out_shape=jax.ShapeDtypeStruct((blocks * width, sent), jnp.bfloat16),
        compiler_params=params,
    )(matrix, above, below, weights, inner, right)


TOGETHER = 16
MEAN_TOGETHER = 8
GROUP = 16


def solve(spectral, right_ref, left_ref, scale_ref):
    ny = spectral[0].shape[1]
    wide = along_rows(jnp.concatenate(spectral, axis=1), left_ref)
    wide = wide * jnp.concatenate([scale_ref[...]] * len(spectral), axis=1)
    wide = along_rows(wide, left_ref)
    return along_cols([wide[:, i * ny : (i + 1) * ny] for i in range(len(spectral))], right_ref)


def mean_fields(current_ref, right_side_ref, weight_ref, start):
    nx, ny = weight_ref.shape[1:]
    values = []
    for mode in range(start, start + MEAN_TOGETHER):
        here = current_ref[:, mode].reshape(nx, ny)
        mean = (
            weight_ref[0] * here
            - weight_ref[1] * pltpu.roll(here, 1, 0)
            - weight_ref[2] * pltpu.roll(here, nx - 1, 0)
            - pltpu.roll(weight_ref[4] * here, 1, 1)
            - pltpu.roll(weight_ref[3] * here, ny - 1, 1)
        )
        values.append(right_side_ref[:, mode].reshape(nx, ny) - mean)
    return values


def first_mean_kernel(slabs, place_ref, *refs):
    current_parts = refs[:slabs]
    right_side_parts = refs[slabs : 2 * slabs]
    weight_ref, right_ref, current_ref, right_side_ref, out_ref = refs[2 * slabs :]
    for shift in range(slabs):
        slab = in_order(place_ref[0], shift, slabs)
        current_ref[slab] = current_parts[shift][0]
        right_side_ref[slab] = right_side_parts[shift][0]
    shape = (slabs,) + out_ref.shape[2:]
    for start in range(0, out_ref.shape[1], MEAN_TOGETHER):
        values = mean_fields(current_ref, right_side_ref, weight_ref, start)
        for i, value in enumerate(along_cols(values, right_ref)):
            out_ref[:, start + i] = value.reshape(shape)


def mean_kernel(current_ref, right_side_ref, weight_ref, out_ref):
    shape = out_ref.shape[:1] + out_ref.shape[2:]
    for start in range(0, out_ref.shape[1], MEAN_TOGETHER):
        values = mean_fields(current_ref, right_side_ref, weight_ref, start)
        for i, value in enumerate(values):
            out_ref[:, start + i] = value.reshape(shape)


def turn_in(turned_ref, coupled_ref, mode_count, slab_count, height, first, scale):
    group = coupled_ref.shape[1]
    ny = turned_ref.shape[1]
    low_col = lax.broadcasted_iota(jnp.int32, (group, ny), 1) < LOW
    for source in range(mode_count * slab_count):
        start = ((source % slab_count) * mode_count + source // slab_count) * height
        for r in range(height):
            code = coupled_ref[source, :, r * ny : (r + 1) * ny]
            value = decode(code, FIRST_POWER if first else SUM_POWER)
            if first:
                at = (height + r // (ny // LOW)) * ny
                rest = coupled_ref[source, :, at : at + ny].astype(jnp.float32)
                place = r % (ny // LOW)
                rest = pltpu.roll(rest, ny - place * LOW, 1) if place else rest
                value = value + jnp.where(low_col, rest, 0.0)
            turned_ref[(start + r) * group : (start + r + 1) * group, :] = value * (1.0 / scale)


def step_kernel(
    mode_count,
    slab_count,
    code_scale,
    current_ref,
    base_ref,
    coupled_ref,
    right_ref,
    left_ref,
    scale_ref,
    solution_ref,
    state_ref,
    turned_ref,
):
    nx, ny = scale_ref.shape
    group = coupled_ref.shape[1]
    height = nx // (mode_count * slab_count)
    turn_in(turned_ref, coupled_ref, mode_count, slab_count, height, True, code_scale)

    def several(number, carry):
        start = number * TOGETHER
        resid = []
        for i in range(TOGETHER):
            coupled = turned_ref[pl.ds(start + i, nx, stride=group), :]
            resid.append(base_ref[:, start + i].reshape(nx, ny) - coupled)
        change = solve(resid, right_ref, left_ref, scale_ref)
        for i in range(TOGETHER):
            value = current_ref[:, start + i].reshape(nx, ny) + change[i]
            solution_ref[:, start + i] = value.reshape(slab_count, nx // slab_count, ny)
            turned_ref[pl.ds(start + i, nx, stride=group), :] = value
        return carry

    lax.fori_loop(0, group // TOGETHER, several, 0)

    for target in range(mode_count * slab_count):
        start = ((target % slab_count) * mode_count + target // slab_count) * height
        for r in range(height):
            row = start + r
            value = turned_ref[row * group : (row + 1) * group, :].astype(jnp.bfloat16)
            state_ref[target, :, r * ny : (r + 1) * ny] = value


def residual_kernel(
    mode_count, slab_count, code_scale, here_ref, base_ref, coupled_ref, out_ref, *refs
):
    *code_refs, turned_ref = refs
    group = coupled_ref.shape[1]
    ny = base_ref.shape[-1]
    nx = turned_ref.shape[0] // group
    height = nx // (mode_count * slab_count)
    turn_in(turned_ref, coupled_ref, mode_count, slab_count, height, False, code_scale)

    def one(mode, carry):
        coupled = turned_ref[pl.ds(mode, nx, stride=group), :]
        out_ref[:, mode] = base_ref[:, mode] - coupled.reshape(slab_count, nx // slab_count, ny)
        return carry

    lax.fori_loop(0, group, one, 0)
    for shift, code_ref in enumerate(code_refs):
        slab = lax.rem(here_ref[0] + shift, slab_count)
        code_ref[0] = encode(out_ref[slab] * code_scale, SUM_POWER)


def correct_kernel(code_scale, current_ref, resid_ref, right_ref, left_ref, scale_ref, out_ref):
    nx, ny = scale_ref.shape

    def several(number, carry):
        start = number * TOGETHER
        resid = [resid_ref[:, start + i].reshape(nx, ny) for i in range(TOGETHER)]
        change = solve(along_cols(resid, right_ref), right_ref, left_ref, scale_ref)
        for i in range(TOGETHER):
            shape = out_ref.shape[:1] + out_ref.shape[2:]
            value = current_ref[:, start + i] + change[i].reshape(shape)
            out_ref[:, start + i] = encode(value * code_scale, SOLUTION_POWER)
        return carry

    lax.fori_loop(0, out_ref.shape[1] // TOGETHER, several, 0)


def whole(array):
    return pl.BlockSpec(array.shape, lambda g: (0,) * array.ndim)


def slabs_of(array):
    slab_count, _, rows, ny = array.shape
    return pl.BlockSpec((slab_count, GROUP, rows, ny), lambda g: (0, g, 0, 0))


def strips_of(shape):
    return pl.BlockSpec((shape[0], GROUP, shape[2]), lambda g: (0, g, 0))


def per_group(kernel, groups, operands, in_specs, out_shape, out_specs, scratch=(), flops=0):
    moved = sum(a.size * a.dtype.itemsize for a in operands)
    return pl.pallas_call(
        kernel,
        grid=(groups,),
        in_specs=in_specs,
        out_specs=out_specs,
        out_shape=out_shape,
        scratch_shapes=scratch,
        cost_estimate=pl.CostEstimate(flops=flops, bytes_accessed=2 * moved, transcendentals=0),
        compiler_params=pltpu.CompilerParams(vmem_limit_bytes=VMEM_BYTES),
    )(*operands)


def first_mean_part(place, current_parts, right_side_parts, weights, right):
    slabs = len(right_side_parts)
    _, modes, rows, ny = right_side_parts[0].shape
    part = pl.BlockSpec((1, GROUP, rows, ny), lambda g, *_: (0, g, 0, 0))
    slab = pl.BlockSpec((slabs, GROUP, rows, ny), lambda g, *_: (0, g, 0, 0))
    shape = jax.ShapeDtypeStruct((slabs, modes, rows, ny), jnp.float32)
    return pl.pallas_call(
        functools.partial(first_mean_kernel, slabs),
        grid_spec=pltpu.PrefetchScalarGridSpec(
            num_scalar_prefetch=1,
            grid=(modes // GROUP,),
            in_specs=[part] * (2 * slabs)
            + [
                pl.BlockSpec(weights.shape, lambda g, *_: (0, 0, 0)),
                pl.BlockSpec(right.shape, lambda g, *_: (0, 0)),
            ],
            out_specs=[slab] * 3,
        ),
        out_shape=[shape] * 3,
        compiler_params=pltpu.CompilerParams(vmem_limit_bytes=VMEM_BYTES),
    )(place, *current_parts, *right_side_parts, weights, right)


def mean_part(current, right_side, weights):
    slabs = slabs_of(right_side)
    return per_group(
        mean_kernel,
        right_side.shape[1] // GROUP,
        (current, right_side, weights),
        [slabs, slabs, whole(weights)],
        jax.ShapeDtypeStruct(right_side.shape, jnp.float32),
        slabs,
    )


def solve_flops(array, tables):
    nx, ny = tables[2].shape
    return array.shape[1] * 8 * 3 * nx * ny * (nx + ny) // 2


def step(current, base, coupled, tables, mode_count, slab_count, code_scale):
    nx, ny = tables[2].shape
    slabs = slabs_of(base)
    devices, modes, _ = coupled.shape
    state = (devices, modes, nx // devices * ny)
    return per_group(
        functools.partial(step_kernel, mode_count, slab_count, code_scale),
        modes // GROUP,
        (current, base, coupled, *tables),
        [slabs, slabs, strips_of(coupled.shape), *map(whole, tables)],
        [
            jax.ShapeDtypeStruct(base.shape, jnp.float32),
            jax.ShapeDtypeStruct(state, jnp.bfloat16),
        ],
        [slabs, strips_of(state)],
        [pltpu.VMEM((nx * GROUP, ny), jnp.float32)],
        solve_flops(base, tables),
    )


def last_residual(base, coupled, mode_count, slab_count, code_scale):
    slab, modes, rows, ny = base.shape
    slabs = pl.BlockSpec((slab, GROUP, rows, ny), lambda g, *_: (0, g, 0, 0))
    part = pl.BlockSpec((1, GROUP, rows, ny), lambda g, *_: (0, g, 0, 0))
    devices, _, cells = coupled.shape
    out, *parts = pl.pallas_call(
        functools.partial(residual_kernel, mode_count, slab_count, code_scale),
        grid_spec=pltpu.PrefetchScalarGridSpec(
            num_scalar_prefetch=1,
            grid=(modes // GROUP,),
            in_specs=[slabs, pl.BlockSpec((devices, GROUP, cells), lambda g, *_: (0, g, 0))],
            out_specs=[slabs] + [part] * slab,
            scratch_shapes=[pltpu.VMEM((slab * rows * GROUP, ny), jnp.float32)],
        ),
        out_shape=[jax.ShapeDtypeStruct(base.shape, jnp.float32)]
        + [jax.ShapeDtypeStruct((1, modes, rows, ny), jnp.bfloat16)] * slab,
        cost_estimate=pl.CostEstimate(
            flops=0, bytes_accessed=2 * base.size * 4, transcendentals=0
        ),
        compiler_params=pltpu.CompilerParams(vmem_limit_bytes=VMEM_BYTES),
    )(lax.axis_index("slab").reshape(1), base, coupled)
    return out, parts


def correct(current, resid, tables, code_scale):
    slabs = slabs_of(resid)
    return per_group(
        functools.partial(correct_kernel, code_scale),
        resid.shape[1] // GROUP,
        (current, resid, *tables),
        [slabs, slabs, *map(whole, tables)],
        jax.ShapeDtypeStruct(resid.shape, jnp.bfloat16),
        slabs,
        (),
        solve_flops(resid, tables),
    )


def collect(parts, axis):
    count = lax.axis_size(axis)
    here = lax.axis_index(axis)
    out = jnp.zeros((count,) + parts[0].shape[1:], parts[0].dtype)
    for shift, part in enumerate(parts):
        source = lax.rem(here + count - shift, count)
        out = lax.dynamic_update_slice_in_dim(out, part, source, 0)
    return out


def onwards(part, axis, shift):
    count = lax.axis_size(axis)
    return lax.ppermute(part, axis, [(i, (i + shift) % count) for i in range(count)])


def parts_of(block, axis):
    count = lax.axis_size(axis)
    here = lax.axis_index(axis)
    return [
        lax.dynamic_index_in_dim(block, lax.rem(here + shift, count), 0) for shift in range(count)
    ]


def moved_parts(parts, axis):
    return [parts[0]] + [onwards(parts[i], axis, i) for i in range(1, len(parts))]


def local(guess, right_side, mean_coef, field_coef, coupling, coupling_list, pair_count):
    mode_count = lax.axis_size("mode")
    slab_count = lax.axis_size("slab")
    both = ("mode", "slab")
    modes, rows, cols = guess.shape
    fields = field_coef.shape[0]
    nx = rows * slab_count
    devices = mode_count * slab_count
    height = nx // devices
    share = modes // slab_count

    strips = pack_strips(guess, mode_count)
    coefs = jnp.concatenate([mean_coef[None], field_coef], 0)[None]
    state = lax.all_to_all(strips, "mode", 0, 0, tiled=True)
    state = state.reshape(mode_count * modes, height * cols)

    def to_slabs(block):
        flat = block.reshape(modes, rows, cols)
        return lax.all_to_all(flat, "slab", 0, 0, tiled=True)

    guess_parts = parts_of(guess.reshape(slab_count, share, rows, cols), "slab")
    guess_parts = [jnp.concatenate([part, coefs], axis=1) for part in guess_parts]
    guess_parts = moved_parts(guess_parts, "slab")
    right_parts = parts_of(right_side.reshape(slab_count, share, rows, cols), "slab")
    state, guess_parts, right_parts = lax.optimization_barrier((state, guess_parts, right_parts))
    right_parts = moved_parts(right_parts, "slab")

    slab = lax.axis_index("slab")
    place = jnp.stack([slab, slab * mode_count + lax.axis_index("mode")])
    mean_weights, strip_weights = all_weights(guess_parts, place, fields + 1, height)
    matrix = dense_coupling(coupling, coupling_list, pair_count, fields)

    row_high, row_low = split_table(sine_table(nx))
    col_high, col_low = split_table(sine_table(cols))
    tables = (
        jnp.concatenate(
            [
                jnp.concatenate([col_high, col_low], 1),
                jnp.concatenate([col_high, jnp.zeros_like(col_low)], 1),
            ],
            0,
        ),
        jnp.concatenate(
            [
                jnp.concatenate([row_high, row_high], 1),
                jnp.concatenate([row_low, jnp.zeros_like(row_low)], 1),
            ],
            0,
        ),
        RELAXATION / eigen_table(nx, cols),
    )

    first_scale, sum_scale, solution_scale = code_scales(nx, cols, coupling.shape[1], modes)

    sums = coupled_sums(matrix, state, strip_weights, tables[0], True, first_scale, both)
    sums, right_parts = lax.optimization_barrier((sums, right_parts))
    sums = lax.all_to_all(sums, both, 0, 0, tiled=True).reshape(devices, share, -1)
    current, right_side, base = first_mean_part(
        place, guess_parts, right_parts, mean_weights, tables[0]
    )
    current, state = step(current, base, sums, tables, mode_count, slab_count, first_scale)
    state = state.reshape(devices * share, height * cols)
    state = lax.all_to_all(state, both, 0, 0, tiled=True)

    base = mean_part(current, right_side, mean_weights)
    sums = coupled_sums(matrix, state, strip_weights, tables[0], False, sum_scale, both)
    sums = lax.all_to_all(sums, both, 0, 0, tiled=True).reshape(devices, share, -1)
    resid, parts = last_residual(base, sums, mode_count, slab_count, sum_scale)
    moved = collect(moved_parts(parts, "slab"), "slab").reshape(modes, rows, cols)
    resid_out = decode(moved, SUM_POWER) * (1.0 / sum_scale)
    code = correct(current, resid, tables, solution_scale)
    return decode(to_slabs(code), SOLUTION_POWER) * (1.0 / solution_scale), resid_out


def solution(mesh):
    placed = (
        P("mode", "slab", None),
        P("mode", "slab", None),
        P("slab", None),
        P(None, "slab", None),
        P(),
        P(),
        P(),
    )
    return jax.shard_map(
        local,
        mesh=mesh,
        in_specs=placed,
        out_specs=(P("mode", "slab", None), P("mode", "slab", None)),
        check_vma=False,
    )
```

```python
import functools
import math

import jax
import jax.numpy as jnp
from jax import lax
from jax.experimental import pallas as pl
from jax.experimental.pallas import tpu as pltpu
from jax.sharding import PartitionSpec as P

RELAXATION = 0.6
VMEM_BYTES = 60 << 20
SHARED_VMEM_BYTES = 48 << 20
COUPLING_VMEM_BYTES = 32 << 20
UNROLL = 4


def sine_table(length):
    counter = jnp.arange(length).astype(jnp.float32) + 1.0
    angle = math.pi * counter[:, None] * counter[None, :] / (length + 1)
    return math.sqrt(2.0 / (length + 1)) * jnp.sin(angle)


def eigen_table(first, second):
    along_first = 2.0 * jnp.cos(
        math.pi * (jnp.arange(first).astype(jnp.float32) + 1.0) / (first + 1)
    )
    along_second = 2.0 * jnp.cos(
        math.pi * (jnp.arange(second).astype(jnp.float32) + 1.0) / (second + 1)
    )
    return 4.0 - along_first[:, None] - along_second[None, :]


def stencil_weights(coef):
    nx, ny = coef.shape
    row = lax.broadcasted_iota(jnp.int32, (nx, ny), 0)
    col = lax.broadcasted_iota(jnp.int32, (nx, ny), 1)
    sides = (
        (pltpu.roll(coef, 1, 0), row == 0),
        (pltpu.roll(coef, nx - 1, 0), row == nx - 1),
        (pltpu.roll(coef, 1, 1), col == 0),
        (pltpu.roll(coef, ny - 1, 1), col == ny - 1),
    )
    centre = 0.0
    weights = []
    for other, outside in sides:
        weight = 0.5 * (coef + jnp.where(outside, coef, other))
        centre = centre + weight
        weights.append(jnp.where(outside, 0.0, weight))
    return [centre] + weights


def in_order(here, shift, count):
    return lax.rem(here + count - shift, count)


def weights_kernel(slabs, place_ref, *refs):
    part_refs = refs[:slabs]
    mean_ref, strip_weight_ref, coef_ref, full_ref = refs[slabs:]
    _, nx, ny = mean_ref.shape
    fields = coef_ref.shape[1] - 1
    height = strip_weight_ref.shape[0] // (5 * fields)
    for shift, part_ref in enumerate(part_refs):
        coef_ref[in_order(place_ref[0], shift, slabs)] = part_ref[0]
    for which, weight in enumerate(stencil_weights(coef_ref[:, 0].reshape(nx, ny))):
        mean_ref[which] = weight
    for f in range(fields):
        for which, weight in enumerate(stencil_weights(coef_ref[:, f + 1].reshape(nx, ny))):
            full_ref[...] = weight
            for r in range(height):
                at = (f * 5 + which) * height + r
                strip_weight_ref[at : at + 1, :] = full_ref[
                    pl.ds(place_ref[1] * height + r, 1), :
                ]


def all_weights(parts, place, height):
    slab_count = len(parts)
    _, coefs, rows, ny = parts[0].shape
    nx = slab_count * rows
    fields = coefs - 1
    return pl.pallas_call(
        functools.partial(weights_kernel, slab_count),
        grid_spec=pltpu.PrefetchScalarGridSpec(
            num_scalar_prefetch=1,
            grid=(1,),
            in_specs=[pl.BlockSpec((1, coefs, rows, ny), lambda i, *_: (0, 0, 0, 0))]
            * slab_count,
            out_specs=[
                pl.BlockSpec((5, nx, ny), lambda i, *_: (0, 0, 0)),
                pl.BlockSpec((fields * 5 * height, ny), lambda i, *_: (0, 0)),
            ],
            scratch_shapes=[
                pltpu.VMEM((slab_count, coefs, rows, ny), jnp.float32),
                pltpu.VMEM((nx, ny), jnp.float32),
            ],
        ),
        out_shape=[
            jax.ShapeDtypeStruct((5, nx, ny), jnp.float32),
            jax.ShapeDtypeStruct((fields * 5 * height, ny), jnp.float32),
        ],
        compiler_params=pltpu.CompilerParams(vmem_limit_bytes=COUPLING_VMEM_BYTES),
    )(place, *parts)


def split(value):
    high = value.astype(jnp.bfloat16)
    low = (value - high.astype(jnp.float32)).astype(jnp.bfloat16)
    return high, low


def split_table(value):
    high = lax.reduce_precision(value, 8, 7)
    return high.astype(jnp.bfloat16), (value - high).astype(jnp.bfloat16)


LOW = 32
FIRST_POWER = 7
SUM_POWER = 5
SOLUTION_POWER = 4


def encode(value, power):
    square = value * value
    if power == 4:
        result = square * (value * jnp.abs(value))
    elif power == 5:
        result = square * square * value
    else:
        result = (square * square) * (square * value)
    return result.astype(jnp.bfloat16)


def decode(code, power):
    code = code.astype(jnp.float32)
    size = jnp.abs(code)
    value = jnp.exp(jnp.log(size) * (1.0 / power))
    value = jnp.where(size > 0.0, value, 0.0)
    return jnp.where(code < 0.0, -value, value)


def code_scales(nx, ny, entries, width):
    guess_max, mean_max, field_max, coupling_max = 6.0, 2.0, 2.5, 0.0625
    gain = 8.0 * field_max * entries * width * coupling_max * 1.01
    inverse = (min(nx, ny) + 1) ** 2 / 8.0

    def bound(iterate):
        return guess_max + (8.0 * mean_max + gain) * iterate

    change = RELAXATION * inverse * 1.01
    second = guess_max + change * bound(guess_max)
    third = second + change * bound(second)

    def scale(limit, power):
        return 0.8 * 2.0 ** (127.0 / power) / limit

    first = math.sqrt(2.0 * ny) * gain * guess_max
    return (
        min(1.0, scale(first, FIRST_POWER)),
        min(1.0, scale(bound(second), SUM_POWER)),
        min(1.0, scale(third, SOLUTION_POWER)),
    )


def pack_kernel(rows, height, x_ref, out_ref):
    strips, modes, cells = out_ref.shape
    cols = cells // height
    for strip in range(strips):
        for r in range(height):
            value = x_ref[pl.ds(strip * height + r, modes, stride=rows), :]
            out_ref[strip, :, r * cols : (r + 1) * cols] = value.astype(jnp.bfloat16)


def pack_strips(block, strips):
    modes, rows, cols = block.shape
    height = rows // strips
    return pl.pallas_call(
        functools.partial(pack_kernel, rows, height),
        grid=(2,),
        in_specs=[pl.BlockSpec((modes // 2 * rows, cols), lambda g: (g, 0))],
        out_specs=pl.BlockSpec((strips, modes // 2, height * cols), lambda g: (0, g, 0)),
        out_shape=jax.ShapeDtypeStruct((strips, modes, height * cols), jnp.bfloat16),
        compiler_params=pltpu.CompilerParams(vmem_limit_bytes=VMEM_BYTES),
    )(block.reshape(modes * rows, cols))


def dense_kernel(fields, entry_ref, count_ref, coupling_ref, out_ref):
    block = pl.program_id(0)
    width = coupling_ref.shape[-1]
    out_ref[...] = jnp.zeros_like(out_ref)

    def place(k, carry):
        entry = entry_ref[block, k]
        column = pl.multiple_of((entry // fields) * width, width)
        out_ref[0, entry % fields, :, pl.ds(column, width)] = coupling_ref[0, k]
        return carry

    lax.fori_loop(0, count_ref[block], place, 0)


def dense_coupling(coupling, coupling_list, pair_count, fields):
    blocks, entries, width, _ = coupling.shape
    return pl.pallas_call(
        functools.partial(dense_kernel, fields),
        grid_spec=pltpu.PrefetchScalarGridSpec(
            num_scalar_prefetch=2,
            grid=(blocks,),
            in_specs=[pl.BlockSpec((1, entries, width, width), lambda i, *_: (i, 0, 0, 0))],
            out_specs=pl.BlockSpec(
                (1, fields, width, blocks * width), lambda i, *_: (i, 0, 0, 0)
            ),
        ),
        out_shape=jax.ShapeDtypeStruct((blocks, fields, width, blocks * width), coupling.dtype),
        compiler_params=pltpu.CompilerParams(vmem_limit_bytes=COUPLING_VMEM_BYTES),
    )(coupling_list, pair_count, coupling)


def low_tiles(height, cols):
    return -(-height * LOW // cols)


def along_cols(fields, right_ref):
    size, ny = fields[0].shape
    high, low = split(jnp.concatenate(fields, axis=0))
    both = jnp.dot(
        jnp.concatenate([high, low], axis=1), right_ref[...], preferred_element_type=jnp.float32
    )
    both = both[:, :ny] + both[:, ny:]
    return [both[i * size : (i + 1) * size] for i in range(len(fields))]


def along_rows(wide, left_ref):
    nx = wide.shape[0]
    high, low = split(wide)
    both = jnp.dot(
        left_ref[...], jnp.concatenate([high, low], axis=0), preferred_element_type=jnp.float32
    )
    return both[:nx] + both[nx:]


def weight_row(weight_ref, height, field, which, r):
    at = (field * 5 + which) * height + r
    return weight_ref[at : at + 1, :]


def inner_kernel(height, cols, matrix_ref, state_ref, weight_ref, out_ref, sums_ref):
    blocks, fields, width, depth = matrix_ref.shape
    sums_ref[...] = jnp.dot(
        matrix_ref[...].reshape(blocks * fields * width, depth),
        state_ref[...],
        preferred_element_type=jnp.float32,
    )
    for block in range(blocks):
        for r in range(height):
            total = 0.0
            from_left = 0.0
            from_right = 0.0
            for f in range(fields):

                def row(at):
                    start = (block * fields + f) * width
                    return sums_ref[start : start + width, at * cols : (at + 1) * cols]

                weight = functools.partial(weight_row, weight_ref, height, f)
                here = row(r)
                total = total + weight(0, r) * here
                if r > 0:
                    total = total - weight(1, r) * row(r - 1)
                if r < height - 1:
                    total = total - weight(2, r) * row(r + 1)
                from_left = from_left + weight(4, r) * here
                from_right = from_right + weight(3, r) * here
            total = total - pltpu.roll(from_left, 1, 1) - pltpu.roll(from_right, cols - 1, 1)
            out_ref[block * width : (block + 1) * width, r * cols : (r + 1) * cols] = total


def border_kernel(
    height,
    cols,
    first,
    scale,
    matrix_ref,
    above_ref,
    below_ref,
    weight_ref,
    inner_ref,
    right_ref,
    out_ref,
):
    blocks, fields, width, depth = matrix_ref.shape
    border = jnp.concatenate([above_ref[...], below_ref[...]], axis=1)
    low_col = lax.broadcasted_iota(jnp.int32, (width, cols), 1) < LOW
    matrix = matrix_ref[...].reshape(blocks * fields * width, depth)
    sums = jnp.dot(matrix, border, preferred_element_type=jnp.float32)
    for block in range(blocks):
        modes = slice(block * width, (block + 1) * width)
        rows = []
        for r in range(height):
            total = inner_ref[modes, r * cols : (r + 1) * cols]
            for f in range(fields):
                part = sums[(block * fields + f) * width : (block * fields + f + 1) * width]
                if r == 0:
                    total = total - weight_row(weight_ref, height, f, 1, r) * part[:, :cols]
                if r == height - 1:
                    total = total - weight_row(weight_ref, height, f, 2, r) * part[:, cols:]
            rows.append(total)
        if not first:
            for r in range(height):
                code = encode(rows[r] * scale, SUM_POWER)
                out_ref[modes, r * cols : (r + 1) * cols] = code
            continue
        rows = along_cols(rows, right_ref)
        for r in range(height):
            value = rows[r] * scale
            code = encode(value, FIRST_POWER)
            out_ref[modes, r * cols : (r + 1) * cols] = code
            rest = jnp.where(low_col, value - decode(code, FIRST_POWER), 0.0)
            place = r % (cols // LOW)
            rest = pltpu.roll(rest, place * LOW, 1) if place else rest
            packed = rest if place == 0 else packed + rest
            if place == cols // LOW - 1 or r == height - 1:
                at = (height + r // (cols // LOW)) * cols
                out_ref[modes, at : at + cols] = packed.astype(jnp.bfloat16)


def coupled_sums(matrix, state, weights, right, first, scale, both):
    blocks, fields, width, depth = matrix.shape
    cells = state.shape[1]
    height = weights.shape[0] // (5 * fields)
    cols = cells // height
    mode_count = lax.axis_size("mode")
    slab_count = lax.axis_size("slab")
    place = [
        (t % mode_count) * slab_count + t // mode_count for t in range(mode_count * slab_count)
    ]
    onward = list(zip(place, place[1:] + place[:1]))
    above = lax.ppermute(state[:, -cols:], both, onward)
    below = lax.ppermute(state[:, :cols], both, [(b, a) for a, b in onward])
    unroll = math.gcd(blocks, UNROLL)
    matrix_spec = pl.BlockSpec((unroll, fields, width, depth), lambda i: (i, 0, 0, 0))
    weight_spec = pl.BlockSpec(weights.shape, lambda i: (0, 0))
    sums_spec = pl.BlockSpec((unroll * width, cells), lambda i: (i, 0))
    params = pltpu.CompilerParams(vmem_limit_bytes=COUPLING_VMEM_BYTES)
    inner = pl.pallas_call(
        functools.partial(inner_kernel, height, cols),
        grid=(blocks // unroll,),
        in_specs=[matrix_spec, pl.BlockSpec((depth, cells), lambda i: (0, 0)), weight_spec],
        out_specs=sums_spec,
        out_shape=jax.ShapeDtypeStruct((blocks * width, cells), jnp.float32),
        scratch_shapes=[pltpu.VMEM((unroll * fields * width, cells), jnp.float32)],
        cost_estimate=pl.CostEstimate(
            flops=2 * matrix.size * cells, bytes_accessed=2 * matrix.size, transcendentals=0
        ),
        compiler_params=params,
    )(matrix, state, weights)
    border_spec = pl.BlockSpec((depth, cols), lambda i: (0, 0))
    sent = cells + (low_tiles(height, cols) * cols if first else 0)
    return pl.pallas_call(
        functools.partial(border_kernel, height, cols, first, scale),
        grid=(blocks // unroll,),
        in_specs=[
            matrix_spec,
            border_spec,
            border_spec,
            weight_spec,
            sums_spec,
            pl.BlockSpec(right.shape, lambda i: (0, 0)),
        ],
        out_specs=pl.BlockSpec((unroll * width, sent), lambda i: (i, 0)),
        out_shape=jax.ShapeDtypeStruct((blocks * width, sent), jnp.bfloat16),
        compiler_params=params,
    )(matrix, above, below, weights, inner, right)


TOGETHER = 16
MEAN_TOGETHER = 8
GROUP = 16


def solve(spectral, right_ref, left_ref, scale_ref):
    ny = spectral[0].shape[1]
    wide = along_rows(jnp.concatenate(spectral, axis=1), left_ref)
    wide = wide * jnp.concatenate([scale_ref[...]] * len(spectral), axis=1)
    wide = along_rows(wide, left_ref)
    return along_cols([wide[:, i * ny : (i + 1) * ny] for i in range(len(spectral))], right_ref)


def mean_fields(current_ref, right_side_ref, weight_ref, start):
    nx, ny = weight_ref.shape[1:]
    values = []
    for mode in range(start, start + MEAN_TOGETHER):
        here = current_ref[:, mode].reshape(nx, ny)
        mean = (
            weight_ref[0] * here
            - weight_ref[1] * pltpu.roll(here, 1, 0)
            - weight_ref[2] * pltpu.roll(here, nx - 1, 0)
            - pltpu.roll(weight_ref[4] * here, 1, 1)
            - pltpu.roll(weight_ref[3] * here, ny - 1, 1)
        )
        values.append(right_side_ref[:, mode].reshape(nx, ny) - mean)
    return values


def first_mean_kernel(slabs, place_ref, *refs):
    current_parts = refs[:slabs]
    right_side_parts = refs[slabs : 2 * slabs]
    weight_ref, right_ref, current_ref, right_side_ref, out_ref = refs[2 * slabs :]
    for shift in range(slabs):
        slab = in_order(place_ref[0], shift, slabs)
        current_ref[slab] = current_parts[shift][0]
        right_side_ref[slab] = right_side_parts[shift][0]
    shape = (slabs,) + out_ref.shape[2:]
    for start in range(0, out_ref.shape[1], MEAN_TOGETHER):
        values = mean_fields(current_ref, right_side_ref, weight_ref, start)
        for i, value in enumerate(along_cols(values, right_ref)):
            out_ref[:, start + i] = value.reshape(shape)


def mean_kernel(current_ref, right_side_ref, weight_ref, out_ref):
    shape = out_ref.shape[:1] + out_ref.shape[2:]
    for start in range(0, out_ref.shape[1], MEAN_TOGETHER):
        values = mean_fields(current_ref, right_side_ref, weight_ref, start)
        for i, value in enumerate(values):
            out_ref[:, start + i] = value.reshape(shape)


def turn_in(turned_ref, coupled_ref, mode_count, slab_count, height, first, scale):
    group = coupled_ref.shape[1]
    ny = turned_ref.shape[1]
    low_col = lax.broadcasted_iota(jnp.int32, (group, ny), 1) < LOW
    for source in range(mode_count * slab_count):
        start = ((source % slab_count) * mode_count + source // slab_count) * height
        for r in range(height):
            code = coupled_ref[source, :, r * ny : (r + 1) * ny]
            value = decode(code, FIRST_POWER if first else SUM_POWER)
            if first:
                at = (height + r // (ny // LOW)) * ny
                rest = coupled_ref[source, :, at : at + ny].astype(jnp.float32)
                place = r % (ny // LOW)
                rest = pltpu.roll(rest, ny - place * LOW, 1) if place else rest
                value = value + jnp.where(low_col, rest, 0.0)
            turned_ref[(start + r) * group : (start + r + 1) * group, :] = value * (1.0 / scale)


def step_kernel(
    mode_count,
    slab_count,
    code_scale,
    current_ref,
    base_ref,
    coupled_ref,
    right_ref,
    left_ref,
    scale_ref,
    solution_ref,
    state_ref,
    turned_ref,
):
    nx, ny = scale_ref.shape
    group = coupled_ref.shape[1]
    height = nx // (mode_count * slab_count)
    turn_in(turned_ref, coupled_ref, mode_count, slab_count, height, True, code_scale)

    def several(number, carry):
        start = number * TOGETHER
        resid = []
        for i in range(TOGETHER):
            coupled = turned_ref[pl.ds(start + i, nx, stride=group), :]
            resid.append(base_ref[:, start + i].reshape(nx, ny) - coupled)
        change = solve(resid, right_ref, left_ref, scale_ref)
        for i in range(TOGETHER):
            value = current_ref[:, start + i].reshape(nx, ny) + change[i]
            solution_ref[:, start + i] = value.reshape(slab_count, nx // slab_count, ny)
            turned_ref[pl.ds(start + i, nx, stride=group), :] = value
        return carry

    lax.fori_loop(0, group // TOGETHER, several, 0)

    for target in range(mode_count * slab_count):
        start = ((target % slab_count) * mode_count + target // slab_count) * height
        for r in range(height):
            row = start + r
            value = turned_ref[row * group : (row + 1) * group, :].astype(jnp.bfloat16)
            state_ref[target, :, r * ny : (r + 1) * ny] = value


def residual_kernel(
    mode_count, slab_count, code_scale, here_ref, base_ref, coupled_ref, out_ref, *refs
):
    *code_refs, turned_ref = refs
    group = coupled_ref.shape[1]
    ny = base_ref.shape[-1]
    nx = turned_ref.shape[0] // group
    height = nx // (mode_count * slab_count)
    turn_in(turned_ref, coupled_ref, mode_count, slab_count, height, False, code_scale)

    def one(mode, carry):
        coupled = turned_ref[pl.ds(mode, nx, stride=group), :]
        out_ref[:, mode] = base_ref[:, mode] - coupled.reshape(slab_count, nx // slab_count, ny)
        return carry

    lax.fori_loop(0, group, one, 0)
    for shift, code_ref in enumerate(code_refs):
        slab = lax.rem(here_ref[0] + shift, slab_count)
        code_ref[0] = encode(out_ref[slab] * code_scale, SUM_POWER)


def correct_kernel(code_scale, current_ref, resid_ref, right_ref, left_ref, scale_ref, out_ref):
    nx, ny = scale_ref.shape

    def several(number, carry):
        start = number * TOGETHER
        resid = [resid_ref[:, start + i].reshape(nx, ny) for i in range(TOGETHER)]
        change = solve(along_cols(resid, right_ref), right_ref, left_ref, scale_ref)
        for i in range(TOGETHER):
            shape = out_ref.shape[:1] + out_ref.shape[2:]
            value = current_ref[:, start + i] + change[i].reshape(shape)
            out_ref[:, start + i] = encode(value * code_scale, SOLUTION_POWER)
        return carry

    lax.fori_loop(0, out_ref.shape[1] // TOGETHER, several, 0)


def whole(array):
    return pl.BlockSpec(array.shape, lambda g: (0,) * array.ndim)


def slabs_of(array):
    slab_count, _, rows, ny = array.shape
    return pl.BlockSpec((slab_count, GROUP, rows, ny), lambda g: (0, g, 0, 0))


def strips_of(shape):
    return pl.BlockSpec((shape[0], GROUP, shape[2]), lambda g: (0, g, 0))


def per_group(
    kernel, groups, operands, in_specs, out_shape, out_specs, scratch=(), flops=0, vmem=SHARED_VMEM_BYTES
):
    moved = sum(a.size * a.dtype.itemsize for a in operands)
    return pl.pallas_call(
        kernel,
        grid=(groups,),
        in_specs=in_specs,
        out_specs=out_specs,
        out_shape=out_shape,
        scratch_shapes=scratch,
        cost_estimate=pl.CostEstimate(flops=flops, bytes_accessed=2 * moved, transcendentals=0),
        compiler_params=pltpu.CompilerParams(vmem_limit_bytes=vmem),
    )(*operands)


def first_mean_part(place, current_parts, right_side_parts, weights, right):
    slabs = len(right_side_parts)
    _, modes, rows, ny = right_side_parts[0].shape
    part = pl.BlockSpec((1, GROUP, rows, ny), lambda g, *_: (0, g, 0, 0))
    slab = pl.BlockSpec((slabs, GROUP, rows, ny), lambda g, *_: (0, g, 0, 0))
    shape = jax.ShapeDtypeStruct((slabs, modes, rows, ny), jnp.float32)
    return pl.pallas_call(
        functools.partial(first_mean_kernel, slabs),
        grid_spec=pltpu.PrefetchScalarGridSpec(
            num_scalar_prefetch=1,
            grid=(modes // GROUP,),
            in_specs=[part] * (2 * slabs)
            + [
                pl.BlockSpec(weights.shape, lambda g, *_: (0, 0, 0)),
                pl.BlockSpec(right.shape, lambda g, *_: (0, 0)),
            ],
            out_specs=[slab] * 3,
        ),
        out_shape=[shape] * 3,
        compiler_params=pltpu.CompilerParams(vmem_limit_bytes=SHARED_VMEM_BYTES),
    )(place, *current_parts, *right_side_parts, weights, right)


def mean_part(current, right_side, weights):
    slabs = slabs_of(right_side)
    return per_group(
        mean_kernel,
        right_side.shape[1] // GROUP,
        (current, right_side, weights),
        [slabs, slabs, whole(weights)],
        jax.ShapeDtypeStruct(right_side.shape, jnp.float32),
        slabs,
    )


def solve_flops(array, tables):
    nx, ny = tables[2].shape
    return array.shape[1] * 8 * 3 * nx * ny * (nx + ny) // 2


def step(current, base, coupled, tables, mode_count, slab_count, code_scale):
    nx, ny = tables[2].shape
    slabs = slabs_of(base)
    devices, modes, _ = coupled.shape
    state = (devices, modes, nx // devices * ny)
    return per_group(
        functools.partial(step_kernel, mode_count, slab_count, code_scale),
        modes // GROUP,
        (current, base, coupled, *tables),
        [slabs, slabs, strips_of(coupled.shape), *map(whole, tables)],
        [
            jax.ShapeDtypeStruct(base.shape, jnp.float32),
            jax.ShapeDtypeStruct(state, jnp.bfloat16),
        ],
        [slabs, strips_of(state)],
        [pltpu.VMEM((nx * GROUP, ny), jnp.float32)],
        solve_flops(base, tables),
    )


def last_residual(base, coupled, mode_count, slab_count, code_scale):
    slab, modes, rows, ny = base.shape
    slabs = pl.BlockSpec((slab, GROUP, rows, ny), lambda g, *_: (0, g, 0, 0))
    part = pl.BlockSpec((1, GROUP, rows, ny), lambda g, *_: (0, g, 0, 0))
    devices, _, cells = coupled.shape
    out, *parts = pl.pallas_call(
        functools.partial(residual_kernel, mode_count, slab_count, code_scale),
        grid_spec=pltpu.PrefetchScalarGridSpec(
            num_scalar_prefetch=1,
            grid=(modes // GROUP,),
            in_specs=[slabs, pl.BlockSpec((devices, GROUP, cells), lambda g, *_: (0, g, 0))],
            out_specs=[slabs] + [part] * slab,
            scratch_shapes=[pltpu.VMEM((slab * rows * GROUP, ny), jnp.float32)],
        ),
        out_shape=[jax.ShapeDtypeStruct(base.shape, jnp.float32)]
        + [jax.ShapeDtypeStruct((1, modes, rows, ny), jnp.bfloat16)] * slab,
        cost_estimate=pl.CostEstimate(
            flops=0, bytes_accessed=2 * base.size * 4, transcendentals=0
        ),
        compiler_params=pltpu.CompilerParams(vmem_limit_bytes=SHARED_VMEM_BYTES),
    )(lax.axis_index("slab").reshape(1), base, coupled)
    return out, parts


def correct(current, resid, tables, code_scale):
    slabs = slabs_of(resid)
    return per_group(
        functools.partial(correct_kernel, code_scale),
        resid.shape[1] // GROUP,
        (current, resid, *tables),
        [slabs, slabs, *map(whole, tables)],
        jax.ShapeDtypeStruct(resid.shape, jnp.bfloat16),
        slabs,
        (),
        solve_flops(resid, tables),
        VMEM_BYTES,
    )


def collect(parts, axis):
    count = lax.axis_size(axis)
    here = lax.axis_index(axis)
    out = jnp.zeros((count,) + parts[0].shape[1:], parts[0].dtype)
    for shift, part in enumerate(parts):
        source = lax.rem(here + count - shift, count)
        out = lax.dynamic_update_slice_in_dim(out, part, source, 0)
    return out


def onwards(part, axis, shift):
    count = lax.axis_size(axis)
    return lax.ppermute(part, axis, [(i, (i + shift) % count) for i in range(count)])


def parts_of(block, axis):
    count = lax.axis_size(axis)
    here = lax.axis_index(axis)
    return [
        lax.dynamic_index_in_dim(block, lax.rem(here + shift, count), 0) for shift in range(count)
    ]


def moved_parts(parts, axis):
    return [parts[0]] + [onwards(parts[i], axis, i) for i in range(1, len(parts))]


def local(guess, right_side, mean_coef, field_coef, coupling, coupling_list, pair_count):
    mode_count = lax.axis_size("mode")
    slab_count = lax.axis_size("slab")
    both = ("mode", "slab")
    modes, rows, cols = guess.shape
    fields = field_coef.shape[0]
    nx = rows * slab_count
    devices = mode_count * slab_count
    height = nx // devices
    share = modes // slab_count

    strips = pack_strips(guess, mode_count)
    coefs = jnp.concatenate([mean_coef[None], field_coef], 0)[None]
    strips, coefs = lax.optimization_barrier((strips, coefs))
    state = lax.all_to_all(strips, "mode", 0, 0, tiled=True)
    state = state.reshape(mode_count * modes, height * cols)

    def to_slabs(block):
        flat = block.reshape(modes, rows, cols)
        return lax.all_to_all(flat, "slab", 0, 0, tiled=True)

    coef_parts = moved_parts([coefs] * slab_count, "slab")
    guess_parts = parts_of(guess.reshape(slab_count, share, rows, cols), "slab")
    guess_parts = moved_parts(guess_parts, "slab")
    right_parts = parts_of(right_side.reshape(slab_count, share, rows, cols), "slab")
    guess_parts, right_parts = lax.optimization_barrier((guess_parts, right_parts))
    right_parts = moved_parts(right_parts, "slab")

    slab = lax.axis_index("slab")
    place = jnp.stack([slab, slab * mode_count + lax.axis_index("mode")])
    coef_parts, coupling = lax.optimization_barrier((coef_parts, coupling))
    mean_weights, strip_weights = all_weights(coef_parts, place, height)
    matrix = dense_coupling(coupling, coupling_list, pair_count, fields)

    row_high, row_low = split_table(sine_table(nx))
    col_high, col_low = split_table(sine_table(cols))
    tables = (
        jnp.concatenate(
            [
                jnp.concatenate([col_high, col_low], 1),
                jnp.concatenate([col_high, jnp.zeros_like(col_low)], 1),
            ],
            0,
        ),
        jnp.concatenate(
            [
                jnp.concatenate([row_high, row_high], 1),
                jnp.concatenate([row_low, jnp.zeros_like(row_low)], 1),
            ],
            0,
        ),
        RELAXATION / eigen_table(nx, cols),
    )

    first_scale, sum_scale, solution_scale = code_scales(nx, cols, coupling.shape[1], modes)

    sums = coupled_sums(matrix, state, strip_weights, tables[0], True, first_scale, both)
    sums, right_parts = lax.optimization_barrier((sums, right_parts))
    sums = lax.all_to_all(sums, both, 0, 0, tiled=True).reshape(devices, share, -1)
    current, right_side, base = first_mean_part(
        place, guess_parts, right_parts, mean_weights, tables[0]
    )
    current, state = step(current, base, sums, tables, mode_count, slab_count, first_scale)
    state = state.reshape(devices * share, height * cols)
    state = lax.all_to_all(state, both, 0, 0, tiled=True)

    base = mean_part(current, right_side, mean_weights)
    sums = coupled_sums(matrix, state, strip_weights, tables[0], False, sum_scale, both)
    sums = lax.all_to_all(sums, both, 0, 0, tiled=True).reshape(devices, share, -1)
    resid, parts = last_residual(base, sums, mode_count, slab_count, sum_scale)
    moved = collect(moved_parts(parts, "slab"), "slab").reshape(modes, rows, cols)
    resid_out = decode(moved, SUM_POWER) * (1.0 / sum_scale)
    code = correct(current, resid, tables, solution_scale)
    return decode(to_slabs(code), SOLUTION_POWER) * (1.0 / solution_scale), resid_out


def solution(mesh):
    placed = (
        P("mode", "slab", None),
        P("mode", "slab", None),
        P("slab", None),
        P(None, "slab", None),
        P(),
        P(),
        P(),
    )
    return jax.shard_map(
        local,
        mesh=mesh,
        in_specs=placed,
        out_specs=(P("mode", "slab", None), P("mode", "slab", None)),
        check_vma=False,
    )
```

```python
import functools
import math

import jax
import jax.numpy as jnp
from jax import lax
from jax.experimental import pallas as pl
from jax.experimental.pallas import tpu as pltpu
from jax.sharding import PartitionSpec as P

RELAXATION = 0.6
VMEM_BYTES = 60 << 20
SHARED_VMEM_BYTES = 48 << 20
SMALL_VMEM_BYTES = 9 << 20
UNROLL = 4


def sine_table(length):
    counter = jnp.arange(length).astype(jnp.float32) + 1.0
    angle = math.pi * counter[:, None] * counter[None, :] / (length + 1)
    return math.sqrt(2.0 / (length + 1)) * jnp.sin(angle)


def eigen_table(first, second):
    along_first = 2.0 * jnp.cos(
        math.pi * (jnp.arange(first).astype(jnp.float32) + 1.0) / (first + 1)
    )
    along_second = 2.0 * jnp.cos(
        math.pi * (jnp.arange(second).astype(jnp.float32) + 1.0) / (second + 1)
    )
    return 4.0 - along_first[:, None] - along_second[None, :]


def stencil_weights(coef):
    nx, ny = coef.shape
    row = lax.broadcasted_iota(jnp.int32, (nx, ny), 0)
    col = lax.broadcasted_iota(jnp.int32, (nx, ny), 1)
    sides = (
        (pltpu.roll(coef, 1, 0), row == 0),
        (pltpu.roll(coef, nx - 1, 0), row == nx - 1),
        (pltpu.roll(coef, 1, 1), col == 0),
        (pltpu.roll(coef, ny - 1, 1), col == ny - 1),
    )
    centre = 0.0
    weights = []
    for other, outside in sides:
        weight = 0.5 * (coef + jnp.where(outside, coef, other))
        centre = centre + weight
        weights.append(jnp.where(outside, 0.0, weight))
    return [centre] + weights


def in_order(here, shift, count):
    return lax.rem(here + count - shift, count)


def in_order(here, shift, count):
    return lax.rem(here + count - shift, count)


def strip_weights_kernel(slabs, height, place_ref, *refs):
    part_refs = refs[:slabs]
    out_ref, coef_ref = refs[slabs:]
    _, nx, ny = coef_ref.shape
    rows = nx // slabs
    fields = out_ref.shape[0] // (5 * height)
    for shift, part_ref in enumerate(part_refs):
        start = in_order(place_ref[0], shift, slabs) * rows
        coef_ref[:, pl.ds(pl.multiple_of(start, rows), rows), :] = part_ref[0]
    col = lax.broadcasted_iota(jnp.int32, (1, ny), 1)
    first = place_ref[1] * height
    for f in range(fields):
        lines = []
        for r in range(-1, height + 1):
            at = jnp.clip(first + r, 0, nx - 1)
            lines.append(coef_ref[f + 1, pl.ds(at, 1), :])
        for r in range(height):
            here = lines[r + 1]
            up = 0.5 * (here + lines[r])
            down = 0.5 * (here + lines[r + 2])
            left = 0.5 * (here + jnp.where(col == 0, here, pltpu.roll(here, 1, 1)))
            right = 0.5 * (here + jnp.where(col == ny - 1, here, pltpu.roll(here, ny - 1, 1)))
            weights = (
                up + down + left + right,
                jnp.where(first + r == 0, 0.0, up),
                jnp.where(first + r == nx - 1, 0.0, down),
                jnp.where(col == 0, 0.0, left),
                jnp.where(col == ny - 1, 0.0, right),
            )
            for which, weight in enumerate(weights):
                at = (f * 5 + which) * height + r
                out_ref[at : at + 1, :] = weight


def mean_weights_kernel(slabs, place_ref, *refs):
    part_refs = refs[:slabs]
    out_ref, coef_ref = refs[slabs:]
    _, nx, ny = out_ref.shape
    for shift, part_ref in enumerate(part_refs):
        coef_ref[in_order(place_ref[0], shift, slabs)] = part_ref[0, 0]
    for which, weight in enumerate(stencil_weights(coef_ref[...].reshape(nx, ny))):
        out_ref[which] = weight


def weights_of(kernel, parts, place, coefs, out, scratch):
    _, entries, rows, ny = parts[0].shape
    last = entries // coefs - 1
    return pl.pallas_call(
        kernel,
        grid_spec=pltpu.PrefetchScalarGridSpec(
            num_scalar_prefetch=1,
            grid=(1,),
            in_specs=[pl.BlockSpec((1, coefs, rows, ny), lambda i, *_: (0, last, 0, 0))]
            * len(parts),
            out_specs=pl.BlockSpec(out, lambda i, *_: (0,) * len(out)),
            scratch_shapes=[pltpu.VMEM(scratch, jnp.float32)],
        ),
        out_shape=jax.ShapeDtypeStruct(out, jnp.float32),
        compiler_params=pltpu.CompilerParams(vmem_limit_bytes=SMALL_VMEM_BYTES),
    )(place, *parts)


def strip_weights_of(parts, place, coefs, height):
    slabs = len(parts)
    _, _, rows, ny = parts[0].shape
    kernel = functools.partial(strip_weights_kernel, slabs, height)
    out = ((coefs - 1) * 5 * height, ny)
    return weights_of(kernel, parts, place, coefs, out, (coefs, slabs * rows, ny))


def mean_weights_of(parts, place, coefs):
    slabs = len(parts)
    _, _, rows, ny = parts[0].shape
    kernel = functools.partial(mean_weights_kernel, slabs)
    return weights_of(kernel, parts, place, coefs, (5, slabs * rows, ny), (slabs, rows, ny))


def split(value):
    high = value.astype(jnp.bfloat16)
    low = (value - high.astype(jnp.float32)).astype(jnp.bfloat16)
    return high, low


def split_table(value):
    high = lax.reduce_precision(value, 8, 7)
    return high.astype(jnp.bfloat16), (value - high).astype(jnp.bfloat16)


LOW = 32
FIRST_POWER = 7
SUM_POWER = 5
SOLUTION_POWER = 4


def encode(value, power):
    square = value * value
    if power == 4:
        result = square * (value * jnp.abs(value))
    elif power == 5:
        result = square * square * value
    else:
        result = (square * square) * (square * value)
    return result.astype(jnp.bfloat16)


def decode(code, power):
    code = code.astype(jnp.float32)
    size = jnp.abs(code)
    value = jnp.exp(jnp.log(size) * (1.0 / power))
    value = jnp.where(size > 0.0, value, 0.0)
    return jnp.where(code < 0.0, -value, value)


def code_scales(nx, ny, entries, width):
    guess_max, mean_max, field_max, coupling_max = 6.0, 2.0, 2.5, 0.0625
    gain = 8.0 * field_max * entries * width * coupling_max * 1.01
    inverse = (min(nx, ny) + 1) ** 2 / 8.0

    def bound(iterate):
        return guess_max + (8.0 * mean_max + gain) * iterate

    change = RELAXATION * inverse * 1.01
    second = guess_max + change * bound(guess_max)
    third = second + change * bound(second)

    def scale(limit, power):
        return 0.8 * 2.0 ** (127.0 / power) / limit

    first = math.sqrt(2.0 * ny) * gain * guess_max
    return (
        min(1.0, scale(first, FIRST_POWER)),
        min(1.0, scale(bound(second), SUM_POWER)),
        min(1.0, scale(third, SOLUTION_POWER)),
    )


def pack_kernel(rows, height, x_ref, out_ref):
    strips, modes, cells = out_ref.shape
    cols = cells // height
    for strip in range(strips):
        for r in range(height):
            value = x_ref[pl.ds(strip * height + r, modes, stride=rows), :]
            out_ref[strip, :, r * cols : (r + 1) * cols] = value.astype(jnp.bfloat16)


def pack_strips(block, strips):
    modes, rows, cols = block.shape
    height = rows // strips
    return pl.pallas_call(
        functools.partial(pack_kernel, rows, height),
        grid=(2,),
        in_specs=[pl.BlockSpec((modes // 2 * rows, cols), lambda g: (g, 0))],
        out_specs=pl.BlockSpec((strips, modes // 2, height * cols), lambda g: (0, g, 0)),
        out_shape=jax.ShapeDtypeStruct((strips, modes, height * cols), jnp.bfloat16),
        compiler_params=pltpu.CompilerParams(vmem_limit_bytes=VMEM_BYTES),
    )(block.reshape(modes * rows, cols))


def dense_kernel(fields, entry_ref, count_ref, coupling_ref, out_ref):
    block = pl.program_id(0)
    width = coupling_ref.shape[-1]
    out_ref[...] = jnp.zeros_like(out_ref)

    def place(k, carry):
        entry = entry_ref[block, k]
        column = pl.multiple_of((entry // fields) * width, width)
        out_ref[0, entry % fields, :, pl.ds(column, width)] = coupling_ref[0, k]
        return carry

    lax.fori_loop(0, count_ref[block], place, 0)


def dense_coupling(coupling, coupling_list, pair_count, fields):
    blocks, entries, width, _ = coupling.shape
    moved = 2 * width * width * (entries + fields * blocks) * coupling.dtype.itemsize
    return pl.pallas_call(
        functools.partial(dense_kernel, fields),
        grid_spec=pltpu.PrefetchScalarGridSpec(
            num_scalar_prefetch=2,
            grid=(blocks,),
            in_specs=[pl.BlockSpec((1, entries, width, width), lambda i, *_: (i, 0, 0, 0))],
            out_specs=pl.BlockSpec(
                (1, fields, width, blocks * width), lambda i, *_: (i, 0, 0, 0)
            ),
        ),
        out_shape=jax.ShapeDtypeStruct((blocks, fields, width, blocks * width), coupling.dtype),
        compiler_params=pltpu.CompilerParams(vmem_limit_bytes=SMALL_VMEM_BYTES + moved),
    )(coupling_list, pair_count, coupling)


def low_tiles(height, cols):
    return -(-height * LOW // cols)


def along_cols(fields, right_ref):
    size, ny = fields[0].shape
    high, low = split(jnp.concatenate(fields, axis=0))
    both = jnp.dot(
        jnp.concatenate([high, low], axis=1), right_ref[...], preferred_element_type=jnp.float32
    )
    both = both[:, :ny] + both[:, ny:]
    return [both[i * size : (i + 1) * size] for i in range(len(fields))]


def along_rows(wide, left_ref):
    nx = wide.shape[0]
    high, low = split(wide)
    both = jnp.dot(
        left_ref[...], jnp.concatenate([high, low], axis=0), preferred_element_type=jnp.float32
    )
    return both[:nx] + both[nx:]


def weight_row(weight_ref, height, field, which, r):
    at = (field * 5 + which) * height + r
    return weight_ref[at : at + 1, :]


def inner_kernel(height, cols, matrix_ref, state_ref, weight_ref, out_ref, sums_ref):
    blocks, fields, width, depth = matrix_ref.shape
    sums_ref[...] = jnp.dot(
        matrix_ref[...].reshape(blocks * fields * width, depth),
        state_ref[...],
        preferred_element_type=jnp.float32,
    )
    for block in range(blocks):
        for r in range(height):
            total = 0.0
            from_left = 0.0
            from_right = 0.0
            for f in range(fields):

                def row(at):
                    start = (block * fields + f) * width
                    return sums_ref[start : start + width, at * cols : (at + 1) * cols]

                weight = functools.partial(weight_row, weight_ref, height, f)
                here = row(r)
                total = total + weight(0, r) * here
                if r > 0:
                    total = total - weight(1, r) * row(r - 1)
                if r < height - 1:
                    total = total - weight(2, r) * row(r + 1)
                from_left = from_left + weight(4, r) * here
                from_right = from_right + weight(3, r) * here
            total = total - pltpu.roll(from_left, 1, 1) - pltpu.roll(from_right, cols - 1, 1)
            out_ref[block * width : (block + 1) * width, r * cols : (r + 1) * cols] = total


def border_kernel(
    height,
    cols,
    first,
    scale,
    matrix_ref,
    above_ref,
    below_ref,
    weight_ref,
    inner_ref,
    right_ref,
    out_ref,
):
    blocks, fields, width, depth = matrix_ref.shape
    border = jnp.concatenate([above_ref[...], below_ref[...]], axis=1)
    low_col = lax.broadcasted_iota(jnp.int32, (width, cols), 1) < LOW
    matrix = matrix_ref[...].reshape(blocks * fields * width, depth)
    sums = jnp.dot(matrix, border, preferred_element_type=jnp.float32)
    for block in range(blocks):
        modes = slice(block * width, (block + 1) * width)
        rows = []
        for r in range(height):
            total = inner_ref[modes, r * cols : (r + 1) * cols]
            for f in range(fields):
                part = sums[(block * fields + f) * width : (block * fields + f + 1) * width]
                if r == 0:
                    total = total - weight_row(weight_ref, height, f, 1, r) * part[:, :cols]
                if r == height - 1:
                    total = total - weight_row(weight_ref, height, f, 2, r) * part[:, cols:]
            rows.append(total)
        if not first:
            for r in range(height):
                code = encode(rows[r] * scale, SUM_POWER)
                out_ref[modes, r * cols : (r + 1) * cols] = code
            continue
        rows = along_cols(rows, right_ref)
        for r in range(height):
            value = rows[r] * scale
            code = encode(value, FIRST_POWER)
            out_ref[modes, r * cols : (r + 1) * cols] = code
            rest = jnp.where(low_col, value - decode(code, FIRST_POWER), 0.0)
            place = r % (cols // LOW)
            rest = pltpu.roll(rest, place * LOW, 1) if place else rest
            packed = rest if place == 0 else packed + rest
            if place == cols // LOW - 1 or r == height - 1:
                at = (height + r // (cols // LOW)) * cols
                out_ref[modes, at : at + cols] = packed.astype(jnp.bfloat16)


def coupled_sums(matrix, state, weights, right, first, scale, both):
    blocks, fields, width, depth = matrix.shape
    cells = state.shape[1]
    height = weights.shape[0] // (5 * fields)
    cols = cells // height
    mode_count = lax.axis_size("mode")
    slab_count = lax.axis_size("slab")
    place = [
        (t % mode_count) * slab_count + t // mode_count for t in range(mode_count * slab_count)
    ]
    onward = list(zip(place, place[1:] + place[:1]))
    above = lax.ppermute(state[:, -cols:], both, onward)
    below = lax.ppermute(state[:, :cols], both, [(b, a) for a, b in onward])
    unroll = math.gcd(blocks, UNROLL)
    matrix_spec = pl.BlockSpec((unroll, fields, width, depth), lambda i: (i, 0, 0, 0))
    weight_spec = pl.BlockSpec(weights.shape, lambda i: (0, 0))
    sums_spec = pl.BlockSpec((unroll * width, cells), lambda i: (i, 0))
    moved = 2 * unroll * fields * width * depth * matrix.dtype.itemsize
    params = pltpu.CompilerParams(vmem_limit_bytes=2 * SMALL_VMEM_BYTES + moved)
    inner = pl.pallas_call(
        functools.partial(inner_kernel, height, cols),
        grid=(blocks // unroll,),
        in_specs=[matrix_spec, pl.BlockSpec((depth, cells), lambda i: (0, 0)), weight_spec],
        out_specs=sums_spec,
        out_shape=jax.ShapeDtypeStruct((blocks * width, cells), jnp.float32),
        scratch_shapes=[pltpu.VMEM((unroll * fields * width, cells), jnp.float32)],
        cost_estimate=pl.CostEstimate(
            flops=2 * matrix.size * cells, bytes_accessed=2 * matrix.size, transcendentals=0
        ),
        compiler_params=params,
    )(matrix, state, weights)
    border_spec = pl.BlockSpec((depth, cols), lambda i: (0, 0))
    sent = cells + (low_tiles(height, cols) * cols if first else 0)
    return pl.pallas_call(
        functools.partial(border_kernel, height, cols, first, scale),
        grid=(blocks // unroll,),
        in_specs=[
            matrix_spec,
            border_spec,
            border_spec,
            weight_spec,
            sums_spec,
            pl.BlockSpec(right.shape, lambda i: (0, 0)),
        ],
        out_specs=pl.BlockSpec((unroll * width, sent), lambda i: (i, 0)),
        out_shape=jax.ShapeDtypeStruct((blocks * width, sent), jnp.bfloat16),
        compiler_params=params,
    )(matrix, above, below, weights, inner, right)


TOGETHER = 16
MEAN_TOGETHER = 8
GROUP = 16


def solve(spectral, right_ref, left_ref, scale_ref):
    ny = spectral[0].shape[1]
    wide = along_rows(jnp.concatenate(spectral, axis=1), left_ref)
    wide = wide * jnp.concatenate([scale_ref[...]] * len(spectral), axis=1)
    wide = along_rows(wide, left_ref)
    return along_cols([wide[:, i * ny : (i + 1) * ny] for i in range(len(spectral))], right_ref)


def mean_fields(current_ref, right_side_ref, weight_ref, start):
    nx, ny = weight_ref.shape[1:]
    values = []
    for mode in range(start, start + MEAN_TOGETHER):
        here = current_ref[:, mode].reshape(nx, ny)
        mean = (
            weight_ref[0] * here
            - weight_ref[1] * pltpu.roll(here, 1, 0)
            - weight_ref[2] * pltpu.roll(here, nx - 1, 0)
            - pltpu.roll(weight_ref[4] * here, 1, 1)
            - pltpu.roll(weight_ref[3] * here, ny - 1, 1)
        )
        values.append(right_side_ref[:, mode].reshape(nx, ny) - mean)
    return values


def first_mean_kernel(slabs, place_ref, *refs):
    current_parts = refs[:slabs]
    right_side_parts = refs[slabs : 2 * slabs]
    weight_ref, right_ref, current_ref, right_side_ref, out_ref = refs[2 * slabs :]
    for shift in range(slabs):
        slab = in_order(place_ref[0], shift, slabs)
        current_ref[slab] = current_parts[shift][0]
        right_side_ref[slab] = right_side_parts[shift][0]
    shape = (slabs,) + out_ref.shape[2:]
    for start in range(0, out_ref.shape[1], MEAN_TOGETHER):
        values = mean_fields(current_ref, right_side_ref, weight_ref, start)
        for i, value in enumerate(along_cols(values, right_ref)):
            out_ref[:, start + i] = value.reshape(shape)


def mean_kernel(current_ref, right_side_ref, weight_ref, out_ref):
    shape = out_ref.shape[:1] + out_ref.shape[2:]
    for start in range(0, out_ref.shape[1], MEAN_TOGETHER):
        values = mean_fields(current_ref, right_side_ref, weight_ref, start)
        for i, value in enumerate(values):
            out_ref[:, start + i] = value.reshape(shape)


def turn_in(turned_ref, coupled_ref, mode_count, slab_count, height, first, scale):
    group = coupled_ref.shape[1]
    ny = turned_ref.shape[1]
    low_col = lax.broadcasted_iota(jnp.int32, (group, ny), 1) < LOW
    for source in range(mode_count * slab_count):
        start = ((source % slab_count) * mode_count + source // slab_count) * height
        for r in range(height):
            code = coupled_ref[source, :, r * ny : (r + 1) * ny]
            value = decode(code, FIRST_POWER if first else SUM_POWER)
            if first:
                at = (height + r // (ny // LOW)) * ny
                rest = coupled_ref[source, :, at : at + ny].astype(jnp.float32)
                place = r % (ny // LOW)
                rest = pltpu.roll(rest, ny - place * LOW, 1) if place else rest
                value = value + jnp.where(low_col, rest, 0.0)
            turned_ref[(start + r) * group : (start + r + 1) * group, :] = value * (1.0 / scale)


def step_kernel(
    mode_count,
    slab_count,
    code_scale,
    current_ref,
    base_ref,
    coupled_ref,
    right_ref,
    left_ref,
    scale_ref,
    solution_ref,
    state_ref,
    turned_ref,
):
    nx, ny = scale_ref.shape
    group = coupled_ref.shape[1]
    height = nx // (mode_count * slab_count)
    turn_in(turned_ref, coupled_ref, mode_count, slab_count, height, True, code_scale)

    def several(number, carry):
        start = number * TOGETHER
        resid = []
        for i in range(TOGETHER):
            coupled = turned_ref[pl.ds(start + i, nx, stride=group), :]
            resid.append(base_ref[:, start + i].reshape(nx, ny) - coupled)
        change = solve(resid, right_ref, left_ref, scale_ref)
        for i in range(TOGETHER):
            value = current_ref[:, start + i].reshape(nx, ny) + change[i]
            solution_ref[:, start + i] = value.reshape(slab_count, nx // slab_count, ny)
            turned_ref[pl.ds(start + i, nx, stride=group), :] = value
        return carry

    lax.fori_loop(0, group // TOGETHER, several, 0)

    for target in range(mode_count * slab_count):
        start = ((target % slab_count) * mode_count + target // slab_count) * height
        for r in range(height):
            row = start + r
            value = turned_ref[row * group : (row + 1) * group, :].astype(jnp.bfloat16)
            state_ref[target, :, r * ny : (r + 1) * ny] = value


def residual_kernel(
    mode_count, slab_count, code_scale, here_ref, base_ref, coupled_ref, out_ref, *refs
):
    *code_refs, turned_ref = refs
    group = coupled_ref.shape[1]
    ny = base_ref.shape[-1]
    nx = turned_ref.shape[0] // group
    height = nx // (mode_count * slab_count)
    turn_in(turned_ref, coupled_ref, mode_count, slab_count, height, False, code_scale)

    def one(mode, carry):
        coupled = turned_ref[pl.ds(mode, nx, stride=group), :]
        out_ref[:, mode] = base_ref[:, mode] - coupled.reshape(slab_count, nx // slab_count, ny)
        return carry

    lax.fori_loop(0, group, one, 0)
    for shift, code_ref in enumerate(code_refs):
        slab = lax.rem(here_ref[0] + shift, slab_count)
        code_ref[0] = encode(out_ref[slab] * code_scale, SUM_POWER)


def correct_kernel(code_scale, current_ref, resid_ref, right_ref, left_ref, scale_ref, out_ref):
    nx, ny = scale_ref.shape

    def several(number, carry):
        start = number * TOGETHER
        resid = [resid_ref[:, start + i].reshape(nx, ny) for i in range(TOGETHER)]
        change = solve(along_cols(resid, right_ref), right_ref, left_ref, scale_ref)
        for i in range(TOGETHER):
            shape = out_ref.shape[:1] + out_ref.shape[2:]
            value = current_ref[:, start + i] + change[i].reshape(shape)
            out_ref[:, start + i] = encode(value * code_scale, SOLUTION_POWER)
        return carry

    lax.fori_loop(0, out_ref.shape[1] // TOGETHER, several, 0)


def whole(array):
    return pl.BlockSpec(array.shape, lambda g: (0,) * array.ndim)


def slabs_of(array):
    slab_count, _, rows, ny = array.shape
    return pl.BlockSpec((slab_count, GROUP, rows, ny), lambda g: (0, g, 0, 0))


def strips_of(shape):
    return pl.BlockSpec((shape[0], GROUP, shape[2]), lambda g: (0, g, 0))


def per_group(
    kernel, groups, operands, in_specs, out_shape, out_specs, scratch=(), flops=0, vmem=SHARED_VMEM_BYTES
):
    moved = sum(a.size * a.dtype.itemsize for a in operands)
    return pl.pallas_call(
        kernel,
        grid=(groups,),
        in_specs=in_specs,
        out_specs=out_specs,
        out_shape=out_shape,
        scratch_shapes=scratch,
        cost_estimate=pl.CostEstimate(flops=flops, bytes_accessed=2 * moved, transcendentals=0),
        compiler_params=pltpu.CompilerParams(vmem_limit_bytes=vmem),
    )(*operands)


def first_mean_part(place, current_parts, right_side_parts, weights, right):
    slabs = len(right_side_parts)
    _, modes, rows, ny = right_side_parts[0].shape
    part = pl.BlockSpec((1, GROUP, rows, ny), lambda g, *_: (0, g, 0, 0))
    slab = pl.BlockSpec((slabs, GROUP, rows, ny), lambda g, *_: (0, g, 0, 0))
    shape = jax.ShapeDtypeStruct((slabs, modes, rows, ny), jnp.float32)
    return pl.pallas_call(
        functools.partial(first_mean_kernel, slabs),
        grid_spec=pltpu.PrefetchScalarGridSpec(
            num_scalar_prefetch=1,
            grid=(modes // GROUP,),
            in_specs=[part] * (2 * slabs)
            + [
                pl.BlockSpec(weights.shape, lambda g, *_: (0, 0, 0)),
                pl.BlockSpec(right.shape, lambda g, *_: (0, 0)),
            ],
            out_specs=[slab] * 3,
        ),
        out_shape=[shape] * 3,
        compiler_params=pltpu.CompilerParams(vmem_limit_bytes=SHARED_VMEM_BYTES),
    )(place, *current_parts, *right_side_parts, weights, right)


def mean_part(current, right_side, weights):
    slabs = slabs_of(right_side)
    return per_group(
        mean_kernel,
        right_side.shape[1] // GROUP,
        (current, right_side, weights),
        [slabs, slabs, whole(weights)],
        jax.ShapeDtypeStruct(right_side.shape, jnp.float32),
        slabs,
    )


def solve_flops(array, tables):
    nx, ny = tables[2].shape
    return array.shape[1] * 8 * 3 * nx * ny * (nx + ny) // 2


def step(current, base, coupled, tables, mode_count, slab_count, code_scale):
    nx, ny = tables[2].shape
    slabs = slabs_of(base)
    devices, modes, _ = coupled.shape
    state = (devices, modes, nx // devices * ny)
    return per_group(
        functools.partial(step_kernel, mode_count, slab_count, code_scale),
        modes // GROUP,
        (current, base, coupled, *tables),
        [slabs, slabs, strips_of(coupled.shape), *map(whole, tables)],
        [
            jax.ShapeDtypeStruct(base.shape, jnp.float32),
            jax.ShapeDtypeStruct(state, jnp.bfloat16),
        ],
        [slabs, strips_of(state)],
        [pltpu.VMEM((nx * GROUP, ny), jnp.float32)],
        solve_flops(base, tables),
    )


def last_residual(base, coupled, mode_count, slab_count, code_scale):
    slab, modes, rows, ny = base.shape
    slabs = pl.BlockSpec((slab, GROUP, rows, ny), lambda g, *_: (0, g, 0, 0))
    part = pl.BlockSpec((1, GROUP, rows, ny), lambda g, *_: (0, g, 0, 0))
    devices, _, cells = coupled.shape
    out, *parts = pl.pallas_call(
        functools.partial(residual_kernel, mode_count, slab_count, code_scale),
        grid_spec=pltpu.PrefetchScalarGridSpec(
            num_scalar_prefetch=1,
            grid=(modes // GROUP,),
            in_specs=[slabs, pl.BlockSpec((devices, GROUP, cells), lambda g, *_: (0, g, 0))],
            out_specs=[slabs] + [part] * slab,
            scratch_shapes=[pltpu.VMEM((slab * rows * GROUP, ny), jnp.float32)],
        ),
        out_shape=[jax.ShapeDtypeStruct(base.shape, jnp.float32)]
        + [jax.ShapeDtypeStruct((1, modes, rows, ny), jnp.bfloat16)] * slab,
        cost_estimate=pl.CostEstimate(
            flops=0, bytes_accessed=2 * base.size * 4, transcendentals=0
        ),
        compiler_params=pltpu.CompilerParams(vmem_limit_bytes=SHARED_VMEM_BYTES),
    )(lax.axis_index("slab").reshape(1), base, coupled)
    return out, parts


def correct(current, resid, tables, code_scale):
    slabs = slabs_of(resid)
    return per_group(
        functools.partial(correct_kernel, code_scale),
        resid.shape[1] // GROUP,
        (current, resid, *tables),
        [slabs, slabs, *map(whole, tables)],
        jax.ShapeDtypeStruct(resid.shape, jnp.bfloat16),
        slabs,
        (),
        solve_flops(resid, tables),
        VMEM_BYTES,
    )


def collect(parts, axis):
    count = lax.axis_size(axis)
    here = lax.axis_index(axis)
    out = jnp.zeros((count,) + parts[0].shape[1:], parts[0].dtype)
    for shift, part in enumerate(parts):
        source = lax.rem(here + count - shift, count)
        out = lax.dynamic_update_slice_in_dim(out, part, source, 0)
    return out


def onwards(part, axis, shift):
    count = lax.axis_size(axis)
    return lax.ppermute(part, axis, [(i, (i + shift) % count) for i in range(count)])


def parts_of(block, axis):
    count = lax.axis_size(axis)
    here = lax.axis_index(axis)
    return [
        lax.dynamic_index_in_dim(block, lax.rem(here + shift, count), 0) for shift in range(count)
    ]


def moved_parts(parts, axis):
    return [parts[0]] + [onwards(parts[i], axis, i) for i in range(1, len(parts))]


def local(guess, right_side, mean_coef, field_coef, coupling, coupling_list, pair_count):
    mode_count = lax.axis_size("mode")
    slab_count = lax.axis_size("slab")
    both = ("mode", "slab")
    modes, rows, cols = guess.shape
    fields = field_coef.shape[0]
    nx = rows * slab_count
    devices = mode_count * slab_count
    height = nx // devices
    share = modes // slab_count

    strips = pack_strips(guess, mode_count)
    coefs = jnp.concatenate([mean_coef[None], field_coef], 0)[None]
    state = lax.all_to_all(strips, "mode", 0, 0, tiled=True)
    state = state.reshape(mode_count * modes, height * cols)

    def to_slabs(block):
        flat = block.reshape(modes, rows, cols)
        return lax.all_to_all(flat, "slab", 0, 0, tiled=True)

    guess_parts = parts_of(guess.reshape(slab_count, share, rows, cols), "slab")
    guess_parts = [jnp.concatenate([part, coefs], axis=1) for part in guess_parts]
    guess_parts = moved_parts(guess_parts, "slab")
    right_parts = parts_of(right_side.reshape(slab_count, share, rows, cols), "slab")
    state, guess_parts, right_parts = lax.optimization_barrier((state, guess_parts, right_parts))
    right_parts = moved_parts(right_parts, "slab")

    slab = lax.axis_index("slab")
    place = jnp.stack([slab, slab * mode_count + lax.axis_index("mode")])
    strip_weights = strip_weights_of(guess_parts, place, fields + 1, height)
    mean_weights = mean_weights_of(guess_parts, place, fields + 1)
    matrix = dense_coupling(coupling, coupling_list, pair_count, fields)

    row_high, row_low = split_table(sine_table(nx))
    col_high, col_low = split_table(sine_table(cols))
    tables = (
        jnp.concatenate(
            [
                jnp.concatenate([col_high, col_low], 1),
                jnp.concatenate([col_high, jnp.zeros_like(col_low)], 1),
            ],
            0,
        ),
        jnp.concatenate(
            [
                jnp.concatenate([row_high, row_high], 1),
                jnp.concatenate([row_low, jnp.zeros_like(row_low)], 1),
            ],
            0,
        ),
        RELAXATION / eigen_table(nx, cols),
    )

    first_scale, sum_scale, solution_scale = code_scales(nx, cols, coupling.shape[1], modes)

    sums = coupled_sums(matrix, state, strip_weights, tables[0], True, first_scale, both)
    sums, right_parts = lax.optimization_barrier((sums, right_parts))
    sums = lax.all_to_all(sums, both, 0, 0, tiled=True).reshape(devices, share, -1)
    current, right_side, base = first_mean_part(
        place, guess_parts, right_parts, mean_weights, tables[0]
    )
    current, state = step(current, base, sums, tables, mode_count, slab_count, first_scale)
    state = state.reshape(devices * share, height * cols)
    state = lax.all_to_all(state, both, 0, 0, tiled=True)

    base = mean_part(current, right_side, mean_weights)
    sums = coupled_sums(matrix, state, strip_weights, tables[0], False, sum_scale, both)
    sums = lax.all_to_all(sums, both, 0, 0, tiled=True).reshape(devices, share, -1)
    resid, parts = last_residual(base, sums, mode_count, slab_count, sum_scale)
    moved = collect(moved_parts(parts, "slab"), "slab").reshape(modes, rows, cols)
    resid_out = decode(moved, SUM_POWER) * (1.0 / sum_scale)
    code = correct(current, resid, tables, solution_scale)
    return decode(to_slabs(code), SOLUTION_POWER) * (1.0 / solution_scale), resid_out


def solution(mesh):
    placed = (
        P("mode", "slab", None),
        P("mode", "slab", None),
        P("slab", None),
        P(None, "slab", None),
        P(),
        P(),
        P(),
    )
    return jax.shard_map(
        local,
        mesh=mesh,
        in_specs=placed,
        out_specs=(P("mode", "slab", None), P("mode", "slab", None)),
        check_vma=False,
    )
```

```python
import functools
import math

import jax
import jax.numpy as jnp
from jax import lax
from jax.experimental import pallas as pl
from jax.experimental.pallas import tpu as pltpu
from jax.sharding import PartitionSpec as P

RELAXATION = 0.6
VMEM_BYTES = 60 << 20
SHARED_VMEM_BYTES = 48 << 20
SMALL_VMEM_BYTES = 9 << 20
UNROLL = 4


def sine_table(length):
    counter = jnp.arange(length).astype(jnp.float32) + 1.0
    angle = math.pi * counter[:, None] * counter[None, :] / (length + 1)
    return math.sqrt(2.0 / (length + 1)) * jnp.sin(angle)


def eigen_table(first, second):
    along_first = 2.0 * jnp.cos(
        math.pi * (jnp.arange(first).astype(jnp.float32) + 1.0) / (first + 1)
    )
    along_second = 2.0 * jnp.cos(
        math.pi * (jnp.arange(second).astype(jnp.float32) + 1.0) / (second + 1)
    )
    return 4.0 - along_first[:, None] - along_second[None, :]


def stencil_weights(coef):
    nx, ny = coef.shape
    row = lax.broadcasted_iota(jnp.int32, (nx, ny), 0)
    col = lax.broadcasted_iota(jnp.int32, (nx, ny), 1)
    sides = (
        (pltpu.roll(coef, 1, 0), row == 0),
        (pltpu.roll(coef, nx - 1, 0), row == nx - 1),
        (pltpu.roll(coef, 1, 1), col == 0),
        (pltpu.roll(coef, ny - 1, 1), col == ny - 1),
    )
    centre = 0.0
    weights = []
    for other, outside in sides:
        weight = 0.5 * (coef + jnp.where(outside, coef, other))
        centre = centre + weight
        weights.append(jnp.where(outside, 0.0, weight))
    return [centre] + weights


def in_order(here, shift, count):
    return lax.rem(here + count - shift, count)


def in_order(here, shift, count):
    return lax.rem(here + count - shift, count)


MARGIN = 8


def strip_weights_kernel(slabs, height, place_ref, own_ref, low_ref, high_ref, out_ref, coef_ref):
    _, rows, ny = own_ref.shape
    nx = slabs * rows
    fields = out_ref.shape[0] // (5 * height)
    for f in range(1, fields + 1):
        coef_ref[f, MARGIN - 1 : MARGIN, :] = low_ref[f : f + 1, :]
        coef_ref[f, MARGIN : MARGIN + rows, :] = own_ref[f]
        coef_ref[f, MARGIN + rows : MARGIN + rows + 1, :] = high_ref[f : f + 1, :]
    offset = MARGIN - place_ref[0] * rows
    col = lax.broadcasted_iota(jnp.int32, (1, ny), 1)
    first = place_ref[1] * height
    for f in range(fields):
        lines = []
        for r in range(-1, height + 1):
            at = jnp.clip(first + r, 0, nx - 1)
            lines.append(coef_ref[f + 1, pl.ds(at + offset, 1), :])
        for r in range(height):
            here = lines[r + 1]
            up = 0.5 * (here + lines[r])
            down = 0.5 * (here + lines[r + 2])
            left = 0.5 * (here + jnp.where(col == 0, here, pltpu.roll(here, 1, 1)))
            right = 0.5 * (here + jnp.where(col == ny - 1, here, pltpu.roll(here, ny - 1, 1)))
            weights = (
                up + down + left + right,
                jnp.where(first + r == 0, 0.0, up),
                jnp.where(first + r == nx - 1, 0.0, down),
                jnp.where(col == 0, 0.0, left),
                jnp.where(col == ny - 1, 0.0, right),
            )
            for which, weight in enumerate(weights):
                at = (f * 5 + which) * height + r
                out_ref[at : at + 1, :] = weight


def mean_weights_kernel(slabs, place_ref, *refs):
    part_refs = refs[:slabs]
    out_ref, coef_ref = refs[slabs:]
    _, nx, ny = out_ref.shape
    for shift, part_ref in enumerate(part_refs):
        coef_ref[in_order(place_ref[0], shift, slabs)] = part_ref[0, 0]
    for which, weight in enumerate(stencil_weights(coef_ref[...].reshape(nx, ny))):
        out_ref[which] = weight


def strip_weights_of(own, low, high, place, slabs, height):
    coefs, rows, ny = own.shape
    out = ((coefs - 1) * 5 * height, ny)
    edge = pl.BlockSpec((coefs, ny), lambda i, *_: (0, 0))
    return pl.pallas_call(
        functools.partial(strip_weights_kernel, slabs, height),
        grid_spec=pltpu.PrefetchScalarGridSpec(
            num_scalar_prefetch=1,
            grid=(1,),
            in_specs=[pl.BlockSpec((coefs, rows, ny), lambda i, *_: (0, 0, 0)), edge, edge],
            out_specs=pl.BlockSpec(out, lambda i, *_: (0, 0)),
            scratch_shapes=[pltpu.VMEM((coefs, rows + 2 * MARGIN, ny), jnp.float32)],
        ),
        out_shape=jax.ShapeDtypeStruct(out, jnp.float32),
        compiler_params=pltpu.CompilerParams(vmem_limit_bytes=SMALL_VMEM_BYTES),
    )(place, own, low, high)


def mean_weights_of(parts, place, coefs):
    slabs = len(parts)
    _, entries, rows, ny = parts[0].shape
    last = entries // coefs - 1
    out = (5, slabs * rows, ny)
    return pl.pallas_call(
        functools.partial(mean_weights_kernel, slabs),
        grid_spec=pltpu.PrefetchScalarGridSpec(
            num_scalar_prefetch=1,
            grid=(1,),
            in_specs=[pl.BlockSpec((1, coefs, rows, ny), lambda i, *_: (0, last, 0, 0))] * slabs,
            out_specs=pl.BlockSpec(out, lambda i, *_: (0, 0, 0)),
            scratch_shapes=[pltpu.VMEM((slabs, rows, ny), jnp.float32)],
        ),
        out_shape=jax.ShapeDtypeStruct(out, jnp.float32),
        compiler_params=pltpu.CompilerParams(vmem_limit_bytes=SMALL_VMEM_BYTES),
    )(place, *parts)


def split(value):
    high = value.astype(jnp.bfloat16)
    low = (value - high.astype(jnp.float32)).astype(jnp.bfloat16)
    return high, low


def split_table(value):
    high = lax.reduce_precision(value, 8, 7)
    return high.astype(jnp.bfloat16), (value - high).astype(jnp.bfloat16)


LOW = 32
FIRST_POWER = 7
SUM_POWER = 5
SOLUTION_POWER = 4


def encode(value, power):
    square = value * value
    if power == 4:
        result = square * (value * jnp.abs(value))
    elif power == 5:
        result = square * square * value
    else:
        result = (square * square) * (square * value)
    return result.astype(jnp.bfloat16)


def decode(code, power):
    code = code.astype(jnp.float32)
    size = jnp.abs(code)
    value = jnp.exp(jnp.log(size) * (1.0 / power))
    value = jnp.where(size > 0.0, value, 0.0)
    return jnp.where(code < 0.0, -value, value)


def code_scales(nx, ny, entries, width):
    guess_max, mean_max, field_max, coupling_max = 6.0, 2.0, 2.5, 0.0625
    gain = 8.0 * field_max * entries * width * coupling_max * 1.01
    inverse = (min(nx, ny) + 1) ** 2 / 8.0

    def bound(iterate):
        return guess_max + (8.0 * mean_max + gain) * iterate

    change = RELAXATION * inverse * 1.01
    second = guess_max + change * bound(guess_max)
    third = second + change * bound(second)

    def scale(limit, power):
        return 0.8 * 2.0 ** (127.0 / power) / limit

    first = math.sqrt(2.0 * ny) * gain * guess_max
    return (
        min(1.0, scale(first, FIRST_POWER)),
        min(1.0, scale(bound(second), SUM_POWER)),
        min(1.0, scale(third, SOLUTION_POWER)),
    )


def pack_kernel(rows, height, x_ref, out_ref):
    strips, modes, cells = out_ref.shape
    cols = cells // height
    for strip in range(strips):
        for r in range(height):
            value = x_ref[pl.ds(strip * height + r, modes, stride=rows), :]
            out_ref[strip, :, r * cols : (r + 1) * cols] = value.astype(jnp.bfloat16)


def pack_strips(block, strips):
    modes, rows, cols = block.shape
    height = rows // strips
    return pl.pallas_call(
        functools.partial(pack_kernel, rows, height),
        grid=(2,),
        in_specs=[pl.BlockSpec((modes // 2 * rows, cols), lambda g: (g, 0))],
        out_specs=pl.BlockSpec((strips, modes // 2, height * cols), lambda g: (0, g, 0)),
        out_shape=jax.ShapeDtypeStruct((strips, modes, height * cols), jnp.bfloat16),
        compiler_params=pltpu.CompilerParams(vmem_limit_bytes=VMEM_BYTES),
    )(block.reshape(modes * rows, cols))


def dense_kernel(fields, entry_ref, count_ref, coupling_ref, out_ref):
    block = pl.program_id(0)
    width = coupling_ref.shape[-1]
    out_ref[...] = jnp.zeros_like(out_ref)

    def place(k, carry):
        entry = entry_ref[block, k]
        column = pl.multiple_of((entry // fields) * width, width)
        out_ref[0, entry % fields, :, pl.ds(column, width)] = coupling_ref[0, k]
        return carry

    lax.fori_loop(0, count_ref[block], place, 0)


def dense_coupling(coupling, coupling_list, pair_count, fields):
    blocks, entries, width, _ = coupling.shape
    return pl.pallas_call(
        functools.partial(dense_kernel, fields),
        grid_spec=pltpu.PrefetchScalarGridSpec(
            num_scalar_prefetch=2,
            grid=(blocks,),
            in_specs=[pl.BlockSpec((1, entries, width, width), lambda i, *_: (i, 0, 0, 0))],
            out_specs=pl.BlockSpec(
                (1, fields, width, blocks * width), lambda i, *_: (i, 0, 0, 0)
            ),
        ),
        out_shape=jax.ShapeDtypeStruct((blocks, fields, width, blocks * width), coupling.dtype),
        compiler_params=pltpu.CompilerParams(vmem_limit_bytes=VMEM_BYTES),
    )(coupling_list, pair_count, coupling)


def low_tiles(height, cols):
    return -(-height * LOW // cols)


def along_cols(fields, right_ref):
    size, ny = fields[0].shape
    high, low = split(jnp.concatenate(fields, axis=0))
    both = jnp.dot(
        jnp.concatenate([high, low], axis=1), right_ref[...], preferred_element_type=jnp.float32
    )
    both = both[:, :ny] + both[:, ny:]
    return [both[i * size : (i + 1) * size] for i in range(len(fields))]


def along_rows(wide, left_ref):
    nx = wide.shape[0]
    high, low = split(wide)
    both = jnp.dot(
        left_ref[...], jnp.concatenate([high, low], axis=0), preferred_element_type=jnp.float32
    )
    return both[:nx] + both[nx:]


def weight_row(weight_ref, height, field, which, r):
    at = (field * 5 + which) * height + r
    return weight_ref[at : at + 1, :]


def inner_kernel(height, cols, matrix_ref, state_ref, weight_ref, out_ref, sums_ref):
    blocks, fields, width, depth = matrix_ref.shape
    sums_ref[...] = jnp.dot(
        matrix_ref[...].reshape(blocks * fields * width, depth),
        state_ref[...],
        preferred_element_type=jnp.float32,
    )
    for block in range(blocks):
        for r in range(height):
            total = 0.0
            from_left = 0.0
            from_right = 0.0
            for f in range(fields):

                def row(at):
                    start = (block * fields + f) * width
                    return sums_ref[start : start + width, at * cols : (at + 1) * cols]

                weight = functools.partial(weight_row, weight_ref, height, f)
                here = row(r)
                total = total + weight(0, r) * here
                if r > 0:
                    total = total - weight(1, r) * row(r - 1)
                if r < height - 1:
                    total = total - weight(2, r) * row(r + 1)
                from_left = from_left + weight(4, r) * here
                from_right = from_right + weight(3, r) * here
            total = total - pltpu.roll(from_left, 1, 1) - pltpu.roll(from_right, cols - 1, 1)
            out_ref[block * width : (block + 1) * width, r * cols : (r + 1) * cols] = total


def border_kernel(
    height,
    cols,
    first,
    scale,
    matrix_ref,
    above_ref,
    below_ref,
    weight_ref,
    inner_ref,
    right_ref,
    out_ref,
):
    blocks, fields, width, depth = matrix_ref.shape
    border = jnp.concatenate([above_ref[...], below_ref[...]], axis=1)
    low_col = lax.broadcasted_iota(jnp.int32, (width, cols), 1) < LOW
    matrix = matrix_ref[...].reshape(blocks * fields * width, depth)
    sums = jnp.dot(matrix, border, preferred_element_type=jnp.float32)
    for block in range(blocks):
        modes = slice(block * width, (block + 1) * width)
        rows = []
        for r in range(height):
            total = inner_ref[modes, r * cols : (r + 1) * cols]
            for f in range(fields):
                part = sums[(block * fields + f) * width : (block * fields + f + 1) * width]
                if r == 0:
                    total = total - weight_row(weight_ref, height, f, 1, r) * part[:, :cols]
                if r == height - 1:
                    total = total - weight_row(weight_ref, height, f, 2, r) * part[:, cols:]
            rows.append(total)
        if not first:
            for r in range(height):
                code = encode(rows[r] * scale, SUM_POWER)
                out_ref[modes, r * cols : (r + 1) * cols] = code
            continue
        rows = along_cols(rows, right_ref)
        for r in range(height):
            value = rows[r] * scale
            code = encode(value, FIRST_POWER)
            out_ref[modes, r * cols : (r + 1) * cols] = code
            rest = jnp.where(low_col, value - decode(code, FIRST_POWER), 0.0)
            place = r % (cols // LOW)
            rest = pltpu.roll(rest, place * LOW, 1) if place else rest
            packed = rest if place == 0 else packed + rest
            if place == cols // LOW - 1 or r == height - 1:
                at = (height + r // (cols // LOW)) * cols
                out_ref[modes, at : at + cols] = packed.astype(jnp.bfloat16)


def coupled_sums(matrix, state, borders, weights, right, first, scale, both):
    blocks, fields, width, depth = matrix.shape
    cells = state.shape[1]
    height = weights.shape[0] // (5 * fields)
    cols = cells // height
    mode_count = lax.axis_size("mode")
    slab_count = lax.axis_size("slab")
    place = [
        (t % mode_count) * slab_count + t // mode_count for t in range(mode_count * slab_count)
    ]
    onward = list(zip(place, place[1:] + place[:1]))
    above = lax.ppermute(borders[1], both, onward)
    below = lax.ppermute(borders[0], both, [(b, a) for a, b in onward])
    unroll = math.gcd(blocks, UNROLL)
    matrix_spec = pl.BlockSpec((unroll, fields, width, depth), lambda i: (i, 0, 0, 0))
    weight_spec = pl.BlockSpec(weights.shape, lambda i: (0, 0))
    sums_spec = pl.BlockSpec((unroll * width, cells), lambda i: (i, 0))
    moved = 2 * unroll * fields * width * depth * matrix.dtype.itemsize
    params = pltpu.CompilerParams(vmem_limit_bytes=2 * SMALL_VMEM_BYTES + moved)
    inner = pl.pallas_call(
        functools.partial(inner_kernel, height, cols),
        grid=(blocks // unroll,),
        in_specs=[matrix_spec, pl.BlockSpec((depth, cells), lambda i: (0, 0)), weight_spec],
        out_specs=sums_spec,
        out_shape=jax.ShapeDtypeStruct((blocks * width, cells), jnp.float32),
        scratch_shapes=[pltpu.VMEM((unroll * fields * width, cells), jnp.float32)],
        cost_estimate=pl.CostEstimate(
            flops=2 * matrix.size * cells, bytes_accessed=2 * matrix.size, transcendentals=0
        ),
        compiler_params=params,
    )(matrix, state, weights)
    border_spec = pl.BlockSpec((depth, cols), lambda i: (0, 0))
    sent = cells + (low_tiles(height, cols) * cols if first else 0)
    return pl.pallas_call(
        functools.partial(border_kernel, height, cols, first, scale),
        grid=(blocks // unroll,),
        in_specs=[
            matrix_spec,
            border_spec,
            border_spec,
            weight_spec,
            sums_spec,
            pl.BlockSpec(right.shape, lambda i: (0, 0)),
        ],
        out_specs=pl.BlockSpec((unroll * width, sent), lambda i: (i, 0)),
        out_shape=jax.ShapeDtypeStruct((blocks * width, sent), jnp.bfloat16),
        compiler_params=params,
    )(matrix, above, below, weights, inner, right)


TOGETHER = 16
MEAN_TOGETHER = 8
GROUP = 16


def solve(spectral, right_ref, left_ref, scale_ref):
    ny = spectral[0].shape[1]
    wide = along_rows(jnp.concatenate(spectral, axis=1), left_ref)
    wide = wide * jnp.concatenate([scale_ref[...]] * len(spectral), axis=1)
    wide = along_rows(wide, left_ref)
    return along_cols([wide[:, i * ny : (i + 1) * ny] for i in range(len(spectral))], right_ref)


def mean_fields(current_ref, right_side_ref, weight_ref, start):
    nx, ny = weight_ref.shape[1:]
    values = []
    for mode in range(start, start + MEAN_TOGETHER):
        here = current_ref[:, mode].reshape(nx, ny)
        mean = (
            weight_ref[0] * here
            - weight_ref[1] * pltpu.roll(here, 1, 0)
            - weight_ref[2] * pltpu.roll(here, nx - 1, 0)
            - pltpu.roll(weight_ref[4] * here, 1, 1)
            - pltpu.roll(weight_ref[3] * here, ny - 1, 1)
        )
        values.append(right_side_ref[:, mode].reshape(nx, ny) - mean)
    return values


def first_mean_kernel(slabs, place_ref, *refs):
    current_parts = refs[:slabs]
    right_side_parts = refs[slabs : 2 * slabs]
    weight_ref, right_ref, current_ref, right_side_ref, out_ref = refs[2 * slabs :]
    for shift in range(slabs):
        slab = in_order(place_ref[0], shift, slabs)
        current_ref[slab] = current_parts[shift][0]
        right_side_ref[slab] = right_side_parts[shift][0]
    shape = (slabs,) + out_ref.shape[2:]
    for start in range(0, out_ref.shape[1], MEAN_TOGETHER):
        values = mean_fields(current_ref, right_side_ref, weight_ref, start)
        for i, value in enumerate(along_cols(values, right_ref)):
            out_ref[:, start + i] = value.reshape(shape)


def mean_kernel(current_ref, right_side_ref, weight_ref, out_ref):
    shape = out_ref.shape[:1] + out_ref.shape[2:]
    for start in range(0, out_ref.shape[1], MEAN_TOGETHER):
        values = mean_fields(current_ref, right_side_ref, weight_ref, start)
        for i, value in enumerate(values):
            out_ref[:, start + i] = value.reshape(shape)


def turn_in(turned_ref, coupled_ref, mode_count, slab_count, height, first, scale):
    group = coupled_ref.shape[1]
    ny = turned_ref.shape[1]
    low_col = lax.broadcasted_iota(jnp.int32, (group, ny), 1) < LOW
    for source in range(mode_count * slab_count):
        start = ((source % slab_count) * mode_count + source // slab_count) * height
        for r in range(height):
            code = coupled_ref[source, :, r * ny : (r + 1) * ny]
            value = decode(code, FIRST_POWER if first else SUM_POWER)
            if first:
                at = (height + r // (ny // LOW)) * ny
                rest = coupled_ref[source, :, at : at + ny].astype(jnp.float32)
                place = r % (ny // LOW)
                rest = pltpu.roll(rest, ny - place * LOW, 1) if place else rest
                value = value + jnp.where(low_col, rest, 0.0)
            turned_ref[(start + r) * group : (start + r + 1) * group, :] = value * (1.0 / scale)


def step_kernel(
    mode_count,
    slab_count,
    code_scale,
    current_ref,
    base_ref,
    coupled_ref,
    right_ref,
    left_ref,
    scale_ref,
    solution_ref,
    state_ref,
    turned_ref,
):
    nx, ny = scale_ref.shape
    group = coupled_ref.shape[1]
    height = nx // (mode_count * slab_count)
    turn_in(turned_ref, coupled_ref, mode_count, slab_count, height, True, code_scale)

    def several(number, carry):
        start = number * TOGETHER
        resid = []
        for i in range(TOGETHER):
            coupled = turned_ref[pl.ds(start + i, nx, stride=group), :]
            resid.append(base_ref[:, start + i].reshape(nx, ny) - coupled)
        change = solve(resid, right_ref, left_ref, scale_ref)
        for i in range(TOGETHER):
            value = current_ref[:, start + i].reshape(nx, ny) + change[i]
            solution_ref[:, start + i] = value.reshape(slab_count, nx // slab_count, ny)
            turned_ref[pl.ds(start + i, nx, stride=group), :] = value
        return carry

    lax.fori_loop(0, group // TOGETHER, several, 0)

    for target in range(mode_count * slab_count):
        start = ((target % slab_count) * mode_count + target // slab_count) * height
        for r in range(height):
            row = start + r
            value = turned_ref[row * group : (row + 1) * group, :].astype(jnp.bfloat16)
            state_ref[target, :, r * ny : (r + 1) * ny] = value


def residual_kernel(
    mode_count, slab_count, code_scale, here_ref, base_ref, coupled_ref, out_ref, *refs
):
    *code_refs, turned_ref = refs
    group = coupled_ref.shape[1]
    ny = base_ref.shape[-1]
    nx = turned_ref.shape[0] // group
    height = nx // (mode_count * slab_count)
    turn_in(turned_ref, coupled_ref, mode_count, slab_count, height, False, code_scale)

    def one(mode, carry):
        coupled = turned_ref[pl.ds(mode, nx, stride=group), :]
        out_ref[:, mode] = base_ref[:, mode] - coupled.reshape(slab_count, nx // slab_count, ny)
        return carry

    lax.fori_loop(0, group, one, 0)
    for shift, code_ref in enumerate(code_refs):
        slab = lax.rem(here_ref[0] + shift, slab_count)
        code_ref[0] = encode(out_ref[slab] * code_scale, SUM_POWER)


def correct_kernel(code_scale, current_ref, resid_ref, right_ref, left_ref, scale_ref, out_ref):
    nx, ny = scale_ref.shape

    def several(number, carry):
        start = number * TOGETHER
        resid = [resid_ref[:, start + i].reshape(nx, ny) for i in range(TOGETHER)]
        change = solve(along_cols(resid, right_ref), right_ref, left_ref, scale_ref)
        for i in range(TOGETHER):
            shape = out_ref.shape[:1] + out_ref.shape[2:]
            value = current_ref[:, start + i] + change[i].reshape(shape)
            out_ref[:, start + i] = encode(value * code_scale, SOLUTION_POWER)
        return carry

    lax.fori_loop(0, out_ref.shape[1] // TOGETHER, several, 0)


def whole(array):
    return pl.BlockSpec(array.shape, lambda g: (0,) * array.ndim)


def slabs_of(array):
    slab_count, _, rows, ny = array.shape
    return pl.BlockSpec((slab_count, GROUP, rows, ny), lambda g: (0, g, 0, 0))


def strips_of(shape):
    return pl.BlockSpec((shape[0], GROUP, shape[2]), lambda g: (0, g, 0))


def per_group(
    kernel, groups, operands, in_specs, out_shape, out_specs, scratch=(), flops=0, vmem=SHARED_VMEM_BYTES
):
    moved = sum(a.size * a.dtype.itemsize for a in operands)
    return pl.pallas_call(
        kernel,
        grid=(groups,),
        in_specs=in_specs,
        out_specs=out_specs,
        out_shape=out_shape,
        scratch_shapes=scratch,
        cost_estimate=pl.CostEstimate(flops=flops, bytes_accessed=2 * moved, transcendentals=0),
        compiler_params=pltpu.CompilerParams(vmem_limit_bytes=vmem),
    )(*operands)


def first_mean_part(place, current_parts, right_side_parts, weights, right):
    slabs = len(right_side_parts)
    _, modes, rows, ny = right_side_parts[0].shape
    part = pl.BlockSpec((1, GROUP, rows, ny), lambda g, *_: (0, g, 0, 0))
    slab = pl.BlockSpec((slabs, GROUP, rows, ny), lambda g, *_: (0, g, 0, 0))
    shape = jax.ShapeDtypeStruct((slabs, modes, rows, ny), jnp.float32)
    return pl.pallas_call(
        functools.partial(first_mean_kernel, slabs),
        grid_spec=pltpu.PrefetchScalarGridSpec(
            num_scalar_prefetch=1,
            grid=(modes // GROUP,),
            in_specs=[part] * (2 * slabs)
            + [
                pl.BlockSpec(weights.shape, lambda g, *_: (0, 0, 0)),
                pl.BlockSpec(right.shape, lambda g, *_: (0, 0)),
            ],
            out_specs=[slab] * 3,
        ),
        out_shape=[shape] * 3,
        compiler_params=pltpu.CompilerParams(vmem_limit_bytes=SHARED_VMEM_BYTES),
    )(place, *current_parts, *right_side_parts, weights, right)


def mean_part(current, right_side, weights):
    slabs = slabs_of(right_side)
    return per_group(
        mean_kernel,
        right_side.shape[1] // GROUP,
        (current, right_side, weights),
        [slabs, slabs, whole(weights)],
        jax.ShapeDtypeStruct(right_side.shape, jnp.float32),
        slabs,
    )


def solve_flops(array, tables):
    nx, ny = tables[2].shape
    return array.shape[1] * 8 * 3 * nx * ny * (nx + ny) // 2


def step(current, base, coupled, tables, mode_count, slab_count, code_scale):
    nx, ny = tables[2].shape
    slabs = slabs_of(base)
    devices, modes, _ = coupled.shape
    state = (devices, modes, nx // devices * ny)
    return per_group(
        functools.partial(step_kernel, mode_count, slab_count, code_scale),
        modes // GROUP,
        (current, base, coupled, *tables),
        [slabs, slabs, strips_of(coupled.shape), *map(whole, tables)],
        [
            jax.ShapeDtypeStruct(base.shape, jnp.float32),
            jax.ShapeDtypeStruct(state, jnp.bfloat16),
        ],
        [slabs, strips_of(state)],
        [pltpu.VMEM((nx * GROUP, ny), jnp.float32)],
        solve_flops(base, tables),
    )


def last_residual(base, coupled, mode_count, slab_count, code_scale):
    slab, modes, rows, ny = base.shape
    slabs = pl.BlockSpec((slab, GROUP, rows, ny), lambda g, *_: (0, g, 0, 0))
    part = pl.BlockSpec((1, GROUP, rows, ny), lambda g, *_: (0, g, 0, 0))
    devices, _, cells = coupled.shape
    out, *parts = pl.pallas_call(
        functools.partial(residual_kernel, mode_count, slab_count, code_scale),
        grid_spec=pltpu.PrefetchScalarGridSpec(
            num_scalar_prefetch=1,
            grid=(modes // GROUP,),
            in_specs=[slabs, pl.BlockSpec((devices, GROUP, cells), lambda g, *_: (0, g, 0))],
            out_specs=[slabs] + [part] * slab,
            scratch_shapes=[pltpu.VMEM((slab * rows * GROUP, ny), jnp.float32)],
        ),
        out_shape=[jax.ShapeDtypeStruct(base.shape, jnp.float32)]
        + [jax.ShapeDtypeStruct((1, modes, rows, ny), jnp.bfloat16)] * slab,
        cost_estimate=pl.CostEstimate(
            flops=0, bytes_accessed=2 * base.size * 4, transcendentals=0
        ),
        compiler_params=pltpu.CompilerParams(vmem_limit_bytes=SHARED_VMEM_BYTES),
    )(lax.axis_index("slab").reshape(1), base, coupled)
    return out, parts


def correct(current, resid, tables, code_scale):
    slabs = slabs_of(resid)
    return per_group(
        functools.partial(correct_kernel, code_scale),
        resid.shape[1] // GROUP,
        (current, resid, *tables),
        [slabs, slabs, *map(whole, tables)],
        jax.ShapeDtypeStruct(resid.shape, jnp.bfloat16),
        slabs,
        (),
        solve_flops(resid, tables),
    )


def collect(parts, axis):
    count = lax.axis_size(axis)
    here = lax.axis_index(axis)
    out = jnp.zeros((count,) + parts[0].shape[1:], parts[0].dtype)
    for shift, part in enumerate(parts):
        source = lax.rem(here + count - shift, count)
        out = lax.dynamic_update_slice_in_dim(out, part, source, 0)
    return out


def onwards(part, axis, shift):
    count = lax.axis_size(axis)
    return lax.ppermute(part, axis, [(i, (i + shift) % count) for i in range(count)])


def parts_of(block, axis):
    count = lax.axis_size(axis)
    here = lax.axis_index(axis)
    return [
        lax.dynamic_index_in_dim(block, lax.rem(here + shift, count), 0) for shift in range(count)
    ]


def moved_parts(parts, axis):
    return [parts[0]] + [onwards(parts[i], axis, i) for i in range(1, len(parts))]


def local(guess, right_side, mean_coef, field_coef, coupling, coupling_list, pair_count):
    mode_count = lax.axis_size("mode")
    slab_count = lax.axis_size("slab")
    both = ("mode", "slab")
    modes, rows, cols = guess.shape
    fields = field_coef.shape[0]
    nx = rows * slab_count
    devices = mode_count * slab_count
    height = nx // devices
    share = modes // slab_count

    strips = pack_strips(guess, mode_count)
    coefs = jnp.concatenate([mean_coef[None], field_coef], 0)[None]
    strips, coefs = lax.optimization_barrier((strips, coefs))
    state = lax.all_to_all(strips, "mode", 0, 0, tiled=True)
    state = state.reshape(mode_count * modes, height * cols)

    def to_slabs(block):
        flat = block.reshape(modes, rows, cols)
        return lax.all_to_all(flat, "slab", 0, 0, tiled=True)

    borders = (state[:, :cols], state[:, -cols:])

    slab = lax.axis_index("slab")
    place = jnp.stack([slab, slab * mode_count + lax.axis_index("mode")])
    forward = [(i, i + 1) for i in range(slab_count - 1)]
    low = lax.ppermute(coefs[0, :, -1], "slab", forward)
    high = lax.ppermute(coefs[0, :, 0], "slab", [(b, a) for a, b in forward])
    strip_weights = strip_weights_of(coefs[0], low, high, place, slab_count, height)

    guess_parts = parts_of(guess.reshape(slab_count, share, rows, cols), "slab")
    guess_parts = [jnp.concatenate([part, coefs], axis=1) for part in guess_parts]
    guess_parts = moved_parts(guess_parts, "slab")
    right_parts = parts_of(right_side.reshape(slab_count, share, rows, cols), "slab")
    guess_parts, right_parts, _ = lax.optimization_barrier((guess_parts, right_parts, borders))
    right_parts = moved_parts(right_parts, "slab")
    mean_weights = mean_weights_of(guess_parts, place, fields + 1)
    matrix = dense_coupling(coupling, coupling_list, pair_count, fields)

    row_high, row_low = split_table(sine_table(nx))
    col_high, col_low = split_table(sine_table(cols))
    tables = (
        jnp.concatenate(
            [
                jnp.concatenate([col_high, col_low], 1),
                jnp.concatenate([col_high, jnp.zeros_like(col_low)], 1),
            ],
            0,
        ),
        jnp.concatenate(
            [
                jnp.concatenate([row_high, row_high], 1),
                jnp.concatenate([row_low, jnp.zeros_like(row_low)], 1),
            ],
            0,
        ),
        RELAXATION / eigen_table(nx, cols),
    )

    first_scale, sum_scale, solution_scale = code_scales(nx, cols, coupling.shape[1], modes)

    sums = coupled_sums(
        matrix, state, borders, strip_weights, tables[0], True, first_scale, both
    )
    sums, *right_parts[1::2] = lax.optimization_barrier((sums, *right_parts[1::2]))
    sums = lax.all_to_all(sums, both, 0, 0, tiled=True).reshape(devices, share, -1)
    current, right_side, base = first_mean_part(
        place, guess_parts, right_parts, mean_weights, tables[0]
    )
    current, state = step(current, base, sums, tables, mode_count, slab_count, first_scale)
    state = state.reshape(devices * share, height * cols)
    state = lax.all_to_all(state, both, 0, 0, tiled=True)

    base = mean_part(current, right_side, mean_weights)
    borders = (state[:, :cols], state[:, -cols:])
    sums = coupled_sums(
        matrix, state, borders, strip_weights, tables[0], False, sum_scale, both
    )
    sums = lax.all_to_all(sums, both, 0, 0, tiled=True).reshape(devices, share, -1)
    resid, parts = last_residual(base, sums, mode_count, slab_count, sum_scale)
    moved = collect(moved_parts(parts, "slab"), "slab").reshape(modes, rows, cols)
    resid_out = decode(moved, SUM_POWER) * (1.0 / sum_scale)
    code = correct(current, resid, tables, solution_scale)
    return decode(to_slabs(code), SOLUTION_POWER) * (1.0 / solution_scale), resid_out


def solution(mesh):
    placed = (
        P("mode", "slab", None),
        P("mode", "slab", None),
        P("slab", None),
        P(None, "slab", None),
        P(),
        P(),
        P(),
    )
    return jax.shard_map(
        local,
        mesh=mesh,
        in_specs=placed,
        out_specs=(P("mode", "slab", None), P("mode", "slab", None)),
        check_vma=False,
    )
```

```python
import functools
import math

import jax
import jax.numpy as jnp
from jax import lax
from jax.experimental import pallas as pl
from jax.experimental.pallas import tpu as pltpu
from jax.sharding import PartitionSpec as P

RELAXATION = 0.6
VMEM_BYTES = 60 << 20
SHARED_VMEM_BYTES = 48 << 20
SMALL_VMEM_BYTES = 9 << 20
UNROLL = 4


def sine_table(length):
    counter = jnp.arange(length).astype(jnp.float32) + 1.0
    angle = math.pi * counter[:, None] * counter[None, :] / (length + 1)
    return math.sqrt(2.0 / (length + 1)) * jnp.sin(angle)


def eigen_table(first, second):
    along_first = 2.0 * jnp.cos(
        math.pi * (jnp.arange(first).astype(jnp.float32) + 1.0) / (first + 1)
    )
    along_second = 2.0 * jnp.cos(
        math.pi * (jnp.arange(second).astype(jnp.float32) + 1.0) / (second + 1)
    )
    return 4.0 - along_first[:, None] - along_second[None, :]


def stencil_weights(coef):
    nx, ny = coef.shape
    row = lax.broadcasted_iota(jnp.int32, (nx, ny), 0)
    col = lax.broadcasted_iota(jnp.int32, (nx, ny), 1)
    sides = (
        (pltpu.roll(coef, 1, 0), row == 0),
        (pltpu.roll(coef, nx - 1, 0), row == nx - 1),
        (pltpu.roll(coef, 1, 1), col == 0),
        (pltpu.roll(coef, ny - 1, 1), col == ny - 1),
    )
    centre = 0.0
    weights = []
    for other, outside in sides:
        weight = 0.5 * (coef + jnp.where(outside, coef, other))
        centre = centre + weight
        weights.append(jnp.where(outside, 0.0, weight))
    return [centre] + weights


def in_order(here, shift, count):
    return lax.rem(here + count - shift, count)


def in_order(here, shift, count):
    return lax.rem(here + count - shift, count)


MARGIN = 8


def strip_weights_kernel(slabs, height, place_ref, own_ref, low_ref, high_ref, out_ref, coef_ref):
    _, rows, ny = own_ref.shape
    nx = slabs * rows
    fields = out_ref.shape[0] // (5 * height)
    for f in range(1, fields + 1):
        coef_ref[f, MARGIN - 1 : MARGIN, :] = low_ref[f : f + 1, :]
        coef_ref[f, MARGIN : MARGIN + rows, :] = own_ref[f]
        coef_ref[f, MARGIN + rows : MARGIN + rows + 1, :] = high_ref[f : f + 1, :]
    offset = MARGIN - place_ref[0] * rows
    col = lax.broadcasted_iota(jnp.int32, (1, ny), 1)
    first = place_ref[1] * height
    for f in range(fields):
        lines = []
        for r in range(-1, height + 1):
            at = jnp.clip(first + r, 0, nx - 1)
            lines.append(coef_ref[f + 1, pl.ds(at + offset, 1), :])
        for r in range(height):
            here = lines[r + 1]
            up = 0.5 * (here + lines[r])
            down = 0.5 * (here + lines[r + 2])
            left = 0.5 * (here + jnp.where(col == 0, here, pltpu.roll(here, 1, 1)))
            right = 0.5 * (here + jnp.where(col == ny - 1, here, pltpu.roll(here, ny - 1, 1)))
            weights = (
                up + down + left + right,
                jnp.where(first + r == 0, 0.0, up),
                jnp.where(first + r == nx - 1, 0.0, down),
                jnp.where(col == 0, 0.0, left),
                jnp.where(col == ny - 1, 0.0, right),
            )
            for which, weight in enumerate(weights):
                at = (f * 5 + which) * height + r
                out_ref[at : at + 1, :] = weight


def mean_weights_kernel(slabs, place_ref, *refs):
    part_refs = refs[:slabs]
    out_ref, coef_ref = refs[slabs:]
    _, nx, ny = out_ref.shape
    for shift, part_ref in enumerate(part_refs):
        coef_ref[in_order(place_ref[0], shift, slabs)] = part_ref[0, 0]
    for which, weight in enumerate(stencil_weights(coef_ref[...].reshape(nx, ny))):
        out_ref[which] = weight


def strip_weights_of(own, low, high, place, slabs, height):
    coefs, rows, ny = own.shape
    out = ((coefs - 1) * 5 * height, ny)
    edge = pl.BlockSpec((coefs, ny), lambda i, *_: (0, 0))
    return pl.pallas_call(
        functools.partial(strip_weights_kernel, slabs, height),
        grid_spec=pltpu.PrefetchScalarGridSpec(
            num_scalar_prefetch=1,
            grid=(1,),
            in_specs=[pl.BlockSpec((coefs, rows, ny), lambda i, *_: (0, 0, 0)), edge, edge],
            out_specs=pl.BlockSpec(out, lambda i, *_: (0, 0)),
            scratch_shapes=[pltpu.VMEM((coefs, rows + 2 * MARGIN, ny), jnp.float32)],
        ),
        out_shape=jax.ShapeDtypeStruct(out, jnp.float32),
        compiler_params=pltpu.CompilerParams(vmem_limit_bytes=SMALL_VMEM_BYTES),
    )(place, own, low, high)


def mean_weights_of(parts, place, coefs):
    slabs = len(parts)
    _, entries, rows, ny = parts[0].shape
    last = entries // coefs - 1
    out = (5, slabs * rows, ny)
    return pl.pallas_call(
        functools.partial(mean_weights_kernel, slabs),
        grid_spec=pltpu.PrefetchScalarGridSpec(
            num_scalar_prefetch=1,
            grid=(1,),
            in_specs=[pl.BlockSpec((1, coefs, rows, ny), lambda i, *_: (0, last, 0, 0))] * slabs,
            out_specs=pl.BlockSpec(out, lambda i, *_: (0, 0, 0)),
            scratch_shapes=[pltpu.VMEM((slabs, rows, ny), jnp.float32)],
        ),
        out_shape=jax.ShapeDtypeStruct(out, jnp.float32),
        compiler_params=pltpu.CompilerParams(vmem_limit_bytes=SMALL_VMEM_BYTES),
    )(place, *parts)


def split(value):
    high = value.astype(jnp.bfloat16)
    low = (value - high.astype(jnp.float32)).astype(jnp.bfloat16)
    return high, low


def split_table(value):
    high = lax.reduce_precision(value, 8, 7)
    return high.astype(jnp.bfloat16), (value - high).astype(jnp.bfloat16)


LOW = 32
FIRST_POWER = 7
SUM_POWER = 5
SOLUTION_POWER = 4


def encode(value, power):
    square = value * value
    if power == 4:
        result = square * (value * jnp.abs(value))
    elif power == 5:
        result = square * square * value
    else:
        result = (square * square) * (square * value)
    return result.astype(jnp.bfloat16)


def decode(code, power):
    code = code.astype(jnp.float32)
    size = jnp.abs(code)
    value = jnp.exp(jnp.log(size) * (1.0 / power))
    value = jnp.where(size > 0.0, value, 0.0)
    return jnp.where(code < 0.0, -value, value)


def code_scales(nx, ny, entries, width):
    guess_max, mean_max, field_max, coupling_max = 6.0, 2.0, 2.5, 0.0625
    gain = 8.0 * field_max * entries * width * coupling_max * 1.01
    inverse = (min(nx, ny) + 1) ** 2 / 8.0

    def bound(iterate):
        return guess_max + (8.0 * mean_max + gain) * iterate

    change = RELAXATION * inverse * 1.01
    second = guess_max + change * bound(guess_max)
    third = second + change * bound(second)

    def scale(limit, power):
        return 0.8 * 2.0 ** (127.0 / power) / limit

    first = math.sqrt(2.0 * ny) * gain * guess_max
    return (
        min(1.0, scale(first, FIRST_POWER)),
        min(1.0, scale(bound(second), SUM_POWER)),
        min(1.0, scale(third, SOLUTION_POWER)),
    )


def pack_kernel(rows, height, x_ref, out_ref):
    strips, modes, cells = out_ref.shape
    cols = cells // height
    for strip in range(strips):
        for r in range(height):
            value = x_ref[pl.ds(strip * height + r, modes, stride=rows), :]
            out_ref[strip, :, r * cols : (r + 1) * cols] = value.astype(jnp.bfloat16)


def pack_strips(block, strips):
    modes, rows, cols = block.shape
    height = rows // strips
    return pl.pallas_call(
        functools.partial(pack_kernel, rows, height),
        grid=(2,),
        in_specs=[pl.BlockSpec((modes // 2 * rows, cols), lambda g: (g, 0))],
        out_specs=pl.BlockSpec((strips, modes // 2, height * cols), lambda g: (0, g, 0)),
        out_shape=jax.ShapeDtypeStruct((strips, modes, height * cols), jnp.bfloat16),
        compiler_params=pltpu.CompilerParams(vmem_limit_bytes=VMEM_BYTES),
    )(block.reshape(modes * rows, cols))


def dense_kernel(fields, entry_ref, count_ref, coupling_ref, out_ref):
    block = pl.program_id(0)
    width = coupling_ref.shape[-1]
    out_ref[...] = jnp.zeros_like(out_ref)

    def place(k, carry):
        entry = entry_ref[block, k]
        column = pl.multiple_of((entry // fields) * width, width)
        out_ref[0, entry % fields, :, pl.ds(column, width)] = coupling_ref[0, k]
        return carry

    lax.fori_loop(0, count_ref[block], place, 0)


def dense_coupling(coupling, coupling_list, pair_count, fields):
    blocks, entries, width, _ = coupling.shape
    return pl.pallas_call(
        functools.partial(dense_kernel, fields),
        grid_spec=pltpu.PrefetchScalarGridSpec(
            num_scalar_prefetch=2,
            grid=(blocks,),
            in_specs=[pl.BlockSpec((1, entries, width, width), lambda i, *_: (i, 0, 0, 0))],
            out_specs=pl.BlockSpec(
                (1, fields, width, blocks * width), lambda i, *_: (i, 0, 0, 0)
            ),
        ),
        out_shape=jax.ShapeDtypeStruct((blocks, fields, width, blocks * width), coupling.dtype),
        compiler_params=pltpu.CompilerParams(vmem_limit_bytes=VMEM_BYTES),
    )(coupling_list, pair_count, coupling)


def low_tiles(height, cols):
    return -(-height * LOW // cols)


def along_cols(fields, right_ref):
    size, ny = fields[0].shape
    high, low = split(jnp.concatenate(fields, axis=0))
    both = jnp.dot(
        jnp.concatenate([high, low], axis=1), right_ref[...], preferred_element_type=jnp.float32
    )
    both = both[:, :ny] + both[:, ny:]
    return [both[i * size : (i + 1) * size] for i in range(len(fields))]


def along_rows(wide, left_ref):
    nx = wide.shape[0]
    high, low = split(wide)
    both = jnp.dot(
        left_ref[...], jnp.concatenate([high, low], axis=0), preferred_element_type=jnp.float32
    )
    return both[:nx] + both[nx:]


def weight_row(weight_ref, height, field, which, r):
    at = (field * 5 + which) * height + r
    return weight_ref[at : at + 1, :]


def inner_kernel(height, cols, matrix_ref, state_ref, weight_ref, out_ref, sums_ref):
    blocks, fields, width, depth = matrix_ref.shape
    sums_ref[...] = jnp.dot(
        matrix_ref[...].reshape(blocks * fields * width, depth),
        state_ref[...],
        preferred_element_type=jnp.float32,
    )
    for block in range(blocks):
        for r in range(height):
            total = 0.0
            from_left = 0.0
            from_right = 0.0
            for f in range(fields):

                def row(at):
                    start = (block * fields + f) * width
                    return sums_ref[start : start + width, at * cols : (at + 1) * cols]

                weight = functools.partial(weight_row, weight_ref, height, f)
                here = row(r)
                total = total + weight(0, r) * here
                if r > 0:
                    total = total - weight(1, r) * row(r - 1)
                if r < height - 1:
                    total = total - weight(2, r) * row(r + 1)
                from_left = from_left + weight(4, r) * here
                from_right = from_right + weight(3, r) * here
            total = total - pltpu.roll(from_left, 1, 1) - pltpu.roll(from_right, cols - 1, 1)
            out_ref[block * width : (block + 1) * width, r * cols : (r + 1) * cols] = total


def border_kernel(
    height,
    cols,
    first,
    scale,
    matrix_ref,
    above_ref,
    below_ref,
    weight_ref,
    inner_ref,
    right_ref,
    out_ref,
):
    blocks, fields, width, depth = matrix_ref.shape
    border = jnp.concatenate([above_ref[...], below_ref[...]], axis=1)
    low_col = lax.broadcasted_iota(jnp.int32, (width, cols), 1) < LOW
    matrix = matrix_ref[...].reshape(blocks * fields * width, depth)
    sums = jnp.dot(matrix, border, preferred_element_type=jnp.float32)
    for block in range(blocks):
        modes = slice(block * width, (block + 1) * width)
        rows = []
        for r in range(height):
            total = inner_ref[modes, r * cols : (r + 1) * cols]
            for f in range(fields):
                part = sums[(block * fields + f) * width : (block * fields + f + 1) * width]
                if r == 0:
                    total = total - weight_row(weight_ref, height, f, 1, r) * part[:, :cols]
                if r == height - 1:
                    total = total - weight_row(weight_ref, height, f, 2, r) * part[:, cols:]
            rows.append(total)
        if not first:
            for r in range(height):
                code = encode(rows[r] * scale, SUM_POWER)
                out_ref[modes, r * cols : (r + 1) * cols] = code
            continue
        rows = along_cols(rows, right_ref)
        for r in range(height):
            value = rows[r] * scale
            code = encode(value, FIRST_POWER)
            out_ref[modes, r * cols : (r + 1) * cols] = code
            rest = jnp.where(low_col, value - decode(code, FIRST_POWER), 0.0)
            place = r % (cols // LOW)
            rest = pltpu.roll(rest, place * LOW, 1) if place else rest
            packed = rest if place == 0 else packed + rest
            if place == cols // LOW - 1 or r == height - 1:
                at = (height + r // (cols // LOW)) * cols
                out_ref[modes, at : at + cols] = packed.astype(jnp.bfloat16)


def coupled_sums(matrix, state, borders, weights, right, first, scale, both):
    blocks, fields, width, depth = matrix.shape
    cells = state.shape[1]
    height = weights.shape[0] // (5 * fields)
    cols = cells // height
    mode_count = lax.axis_size("mode")
    slab_count = lax.axis_size("slab")
    place = [
        (t % mode_count) * slab_count + t // mode_count for t in range(mode_count * slab_count)
    ]
    onward = list(zip(place, place[1:] + place[:1]))
    above = lax.ppermute(borders[1], both, onward)
    below = lax.ppermute(borders[0], both, [(b, a) for a, b in onward])
    unroll = math.gcd(blocks, UNROLL)
    matrix_spec = pl.BlockSpec((unroll, fields, width, depth), lambda i: (i, 0, 0, 0))
    weight_spec = pl.BlockSpec(weights.shape, lambda i: (0, 0))
    sums_spec = pl.BlockSpec((unroll * width, cells), lambda i: (i, 0))
    moved = 2 * unroll * fields * width * depth * matrix.dtype.itemsize
    params = pltpu.CompilerParams(vmem_limit_bytes=2 * SMALL_VMEM_BYTES + moved)
    inner = pl.pallas_call(
        functools.partial(inner_kernel, height, cols),
        grid=(blocks // unroll,),
        in_specs=[matrix_spec, pl.BlockSpec((depth, cells), lambda i: (0, 0)), weight_spec],
        out_specs=sums_spec,
        out_shape=jax.ShapeDtypeStruct((blocks * width, cells), jnp.float32),
        scratch_shapes=[pltpu.VMEM((unroll * fields * width, cells), jnp.float32)],
        cost_estimate=pl.CostEstimate(
            flops=2 * matrix.size * cells, bytes_accessed=2 * matrix.size, transcendentals=0
        ),
        compiler_params=params,
    )(matrix, state, weights)
    border_spec = pl.BlockSpec((depth, cols), lambda i: (0, 0))
    sent = cells + (low_tiles(height, cols) * cols if first else 0)
    return pl.pallas_call(
        functools.partial(border_kernel, height, cols, first, scale),
        grid=(blocks // unroll,),
        in_specs=[
            matrix_spec,
            border_spec,
            border_spec,
            weight_spec,
            sums_spec,
            pl.BlockSpec(right.shape, lambda i: (0, 0)),
        ],
        out_specs=pl.BlockSpec((unroll * width, sent), lambda i: (i, 0)),
        out_shape=jax.ShapeDtypeStruct((blocks * width, sent), jnp.bfloat16),
        compiler_params=params,
    )(matrix, above, below, weights, inner, right)


TOGETHER = 16
MEAN_TOGETHER = 8
GROUP = 16


def solve(spectral, right_ref, left_ref, scale_ref):
    ny = spectral[0].shape[1]
    wide = along_rows(jnp.concatenate(spectral, axis=1), left_ref)
    wide = wide * jnp.concatenate([scale_ref[...]] * len(spectral), axis=1)
    wide = along_rows(wide, left_ref)
    return along_cols([wide[:, i * ny : (i + 1) * ny] for i in range(len(spectral))], right_ref)


def mean_fields(current_ref, right_side_ref, weight_ref, start):
    nx, ny = weight_ref.shape[1:]
    values = []
    for mode in range(start, start + MEAN_TOGETHER):
        here = current_ref[:, mode].reshape(nx, ny)
        mean = (
            weight_ref[0] * here
            - weight_ref[1] * pltpu.roll(here, 1, 0)
            - weight_ref[2] * pltpu.roll(here, nx - 1, 0)
            - pltpu.roll(weight_ref[4] * here, 1, 1)
            - pltpu.roll(weight_ref[3] * here, ny - 1, 1)
        )
        values.append(right_side_ref[:, mode].reshape(nx, ny) - mean)
    return values


def first_mean_kernel(slabs, place_ref, *refs):
    current_parts = refs[:slabs]
    right_side_parts = refs[slabs : 2 * slabs]
    weight_ref, right_ref, current_ref, right_side_ref, out_ref = refs[2 * slabs :]
    for shift in range(slabs):
        slab = in_order(place_ref[0], shift, slabs)
        current_ref[slab] = current_parts[shift][0]
        right_side_ref[slab] = right_side_parts[shift][0]
    shape = (slabs,) + out_ref.shape[2:]
    for start in range(0, out_ref.shape[1], MEAN_TOGETHER):
        values = mean_fields(current_ref, right_side_ref, weight_ref, start)
        for i, value in enumerate(along_cols(values, right_ref)):
            out_ref[:, start + i] = value.reshape(shape)


def mean_kernel(current_ref, right_side_ref, weight_ref, out_ref):
    shape = out_ref.shape[:1] + out_ref.shape[2:]
    for start in range(0, out_ref.shape[1], MEAN_TOGETHER):
        values = mean_fields(current_ref, right_side_ref, weight_ref, start)
        for i, value in enumerate(values):
            out_ref[:, start + i] = value.reshape(shape)


def turn_in(turned_ref, coupled_ref, mode_count, slab_count, height, first, scale):
    group = coupled_ref.shape[1]
    ny = turned_ref.shape[1]
    low_col = lax.broadcasted_iota(jnp.int32, (group, ny), 1) < LOW
    for source in range(mode_count * slab_count):
        start = ((source % slab_count) * mode_count + source // slab_count) * height
        for r in range(height):
            code = coupled_ref[source, :, r * ny : (r + 1) * ny]
            value = decode(code, FIRST_POWER if first else SUM_POWER)
            if first:
                at = (height + r // (ny // LOW)) * ny
                rest = coupled_ref[source, :, at : at + ny].astype(jnp.float32)
                place = r % (ny // LOW)
                rest = pltpu.roll(rest, ny - place * LOW, 1) if place else rest
                value = value + jnp.where(low_col, rest, 0.0)
            turned_ref[(start + r) * group : (start + r + 1) * group, :] = value * (1.0 / scale)


def step_kernel(
    mode_count,
    slab_count,
    code_scale,
    current_ref,
    base_ref,
    coupled_ref,
    right_ref,
    left_ref,
    scale_ref,
    solution_ref,
    state_ref,
    turned_ref,
):
    nx, ny = scale_ref.shape
    group = coupled_ref.shape[1]
    height = nx // (mode_count * slab_count)
    turn_in(turned_ref, coupled_ref, mode_count, slab_count, height, True, code_scale)

    def several(number, carry):
        start = number * TOGETHER
        resid = []
        for i in range(TOGETHER):
            coupled = turned_ref[pl.ds(start + i, nx, stride=group), :]
            resid.append(base_ref[:, start + i].reshape(nx, ny) - coupled)
        change = solve(resid, right_ref, left_ref, scale_ref)
        for i in range(TOGETHER):
            value = current_ref[:, start + i].reshape(nx, ny) + change[i]
            solution_ref[:, start + i] = value.reshape(slab_count, nx // slab_count, ny)
            turned_ref[pl.ds(start + i, nx, stride=group), :] = value
        return carry

    lax.fori_loop(0, group // TOGETHER, several, 0)

    for target in range(mode_count * slab_count):
        start = ((target % slab_count) * mode_count + target // slab_count) * height
        for r in range(height):
            row = start + r
            value = turned_ref[row * group : (row + 1) * group, :].astype(jnp.bfloat16)
            state_ref[target, :, r * ny : (r + 1) * ny] = value


def residual_kernel(
    mode_count, slab_count, code_scale, here_ref, base_ref, coupled_ref, out_ref, *refs
):
    *code_refs, turned_ref = refs
    group = coupled_ref.shape[1]
    ny = base_ref.shape[-1]
    nx = turned_ref.shape[0] // group
    height = nx // (mode_count * slab_count)
    turn_in(turned_ref, coupled_ref, mode_count, slab_count, height, False, code_scale)

    def one(mode, carry):
        coupled = turned_ref[pl.ds(mode, nx, stride=group), :]
        out_ref[:, mode] = base_ref[:, mode] - coupled.reshape(slab_count, nx // slab_count, ny)
        return carry

    lax.fori_loop(0, group, one, 0)
    for shift, code_ref in enumerate(code_refs):
        slab = lax.rem(here_ref[0] + shift, slab_count)
        code_ref[0] = encode(out_ref[slab] * code_scale, SUM_POWER)


def correct_kernel(code_scale, current_ref, resid_ref, right_ref, left_ref, scale_ref, out_ref):
    nx, ny = scale_ref.shape

    def several(number, carry):
        start = number * TOGETHER
        resid = [resid_ref[:, start + i].reshape(nx, ny) for i in range(TOGETHER)]
        change = solve(along_cols(resid, right_ref), right_ref, left_ref, scale_ref)
        for i in range(TOGETHER):
            shape = out_ref.shape[:1] + out_ref.shape[2:]
            value = current_ref[:, start + i] + change[i].reshape(shape)
            out_ref[:, start + i] = encode(value * code_scale, SOLUTION_POWER)
        return carry

    lax.fori_loop(0, out_ref.shape[1] // TOGETHER, several, 0)


def whole(array):
    return pl.BlockSpec(array.shape, lambda g: (0,) * array.ndim)


def slabs_of(array):
    slab_count, _, rows, ny = array.shape
    return pl.BlockSpec((slab_count, GROUP, rows, ny), lambda g: (0, g, 0, 0))


def strips_of(shape):
    return pl.BlockSpec((shape[0], GROUP, shape[2]), lambda g: (0, g, 0))


def per_group(
    kernel, groups, operands, in_specs, out_shape, out_specs, scratch=(), flops=0, vmem=SHARED_VMEM_BYTES
):
    moved = sum(a.size * a.dtype.itemsize for a in operands)
    return pl.pallas_call(
        kernel,
        grid=(groups,),
        in_specs=in_specs,
        out_specs=out_specs,
        out_shape=out_shape,
        scratch_shapes=scratch,
        cost_estimate=pl.CostEstimate(flops=flops, bytes_accessed=2 * moved, transcendentals=0),
        compiler_params=pltpu.CompilerParams(vmem_limit_bytes=vmem),
    )(*operands)


def first_mean_part(place, current_parts, right_side_parts, weights, right):
    slabs = len(right_side_parts)
    _, modes, rows, ny = right_side_parts[0].shape
    part = pl.BlockSpec((1, GROUP, rows, ny), lambda g, *_: (0, g, 0, 0))
    slab = pl.BlockSpec((slabs, GROUP, rows, ny), lambda g, *_: (0, g, 0, 0))
    shape = jax.ShapeDtypeStruct((slabs, modes, rows, ny), jnp.float32)
    return pl.pallas_call(
        functools.partial(first_mean_kernel, slabs),
        grid_spec=pltpu.PrefetchScalarGridSpec(
            num_scalar_prefetch=1,
            grid=(modes // GROUP,),
            in_specs=[part] * (2 * slabs)
            + [
                pl.BlockSpec(weights.shape, lambda g, *_: (0, 0, 0)),
                pl.BlockSpec(right.shape, lambda g, *_: (0, 0)),
            ],
            out_specs=[slab] * 3,
        ),
        out_shape=[shape] * 3,
        compiler_params=pltpu.CompilerParams(vmem_limit_bytes=3 * SMALL_VMEM_BYTES),
    )(place, *current_parts, *right_side_parts, weights, right)


def mean_part(current, right_side, weights):
    slabs = slabs_of(right_side)
    return per_group(
        mean_kernel,
        right_side.shape[1] // GROUP,
        (current, right_side, weights),
        [slabs, slabs, whole(weights)],
        jax.ShapeDtypeStruct(right_side.shape, jnp.float32),
        slabs,
    )


def solve_flops(array, tables):
    nx, ny = tables[2].shape
    return array.shape[1] * 8 * 3 * nx * ny * (nx + ny) // 2


def step(current, base, coupled, tables, mode_count, slab_count, code_scale):
    nx, ny = tables[2].shape
    slabs = slabs_of(base)
    devices, modes, _ = coupled.shape
    state = (devices, modes, nx // devices * ny)
    return per_group(
        functools.partial(step_kernel, mode_count, slab_count, code_scale),
        modes // GROUP,
        (current, base, coupled, *tables),
        [slabs, slabs, strips_of(coupled.shape), *map(whole, tables)],
        [
            jax.ShapeDtypeStruct(base.shape, jnp.float32),
            jax.ShapeDtypeStruct(state, jnp.bfloat16),
        ],
        [slabs, strips_of(state)],
        [pltpu.VMEM((nx * GROUP, ny), jnp.float32)],
        solve_flops(base, tables),
    )


def last_residual(base, coupled, mode_count, slab_count, code_scale):
    slab, modes, rows, ny = base.shape
    slabs = pl.BlockSpec((slab, GROUP, rows, ny), lambda g, *_: (0, g, 0, 0))
    part = pl.BlockSpec((1, GROUP, rows, ny), lambda g, *_: (0, g, 0, 0))
    devices, _, cells = coupled.shape
    out, *parts = pl.pallas_call(
        functools.partial(residual_kernel, mode_count, slab_count, code_scale),
        grid_spec=pltpu.PrefetchScalarGridSpec(
            num_scalar_prefetch=1,
            grid=(modes // GROUP,),
            in_specs=[slabs, pl.BlockSpec((devices, GROUP, cells), lambda g, *_: (0, g, 0))],
            out_specs=[slabs] + [part] * slab,
            scratch_shapes=[pltpu.VMEM((slab * rows * GROUP, ny), jnp.float32)],
        ),
        out_shape=[jax.ShapeDtypeStruct(base.shape, jnp.float32)]
        + [jax.ShapeDtypeStruct((1, modes, rows, ny), jnp.bfloat16)] * slab,
        cost_estimate=pl.CostEstimate(
            flops=0, bytes_accessed=2 * base.size * 4, transcendentals=0
        ),
        compiler_params=pltpu.CompilerParams(vmem_limit_bytes=SHARED_VMEM_BYTES),
    )(lax.axis_index("slab").reshape(1), base, coupled)
    return out, parts


def correct(current, resid, tables, code_scale):
    slabs = slabs_of(resid)
    return per_group(
        functools.partial(correct_kernel, code_scale),
        resid.shape[1] // GROUP,
        (current, resid, *tables),
        [slabs, slabs, *map(whole, tables)],
        jax.ShapeDtypeStruct(resid.shape, jnp.bfloat16),
        slabs,
        (),
        solve_flops(resid, tables),
    )


def collect(parts, axis):
    count = lax.axis_size(axis)
    here = lax.axis_index(axis)
    out = jnp.zeros((count,) + parts[0].shape[1:], parts[0].dtype)
    for shift, part in enumerate(parts):
        source = lax.rem(here + count - shift, count)
        out = lax.dynamic_update_slice_in_dim(out, part, source, 0)
    return out


def onwards(part, axis, shift):
    count = lax.axis_size(axis)
    return lax.ppermute(part, axis, [(i, (i + shift) % count) for i in range(count)])


def parts_of(block, axis):
    count = lax.axis_size(axis)
    here = lax.axis_index(axis)
    return [
        lax.dynamic_index_in_dim(block, lax.rem(here + shift, count), 0) for shift in range(count)
    ]


def moved_parts(parts, axis):
    return [parts[0]] + [onwards(parts[i], axis, i) for i in range(1, len(parts))]


def local(guess, right_side, mean_coef, field_coef, coupling, coupling_list, pair_count):
    mode_count = lax.axis_size("mode")
    slab_count = lax.axis_size("slab")
    both = ("mode", "slab")
    modes, rows, cols = guess.shape
    fields = field_coef.shape[0]
    nx = rows * slab_count
    devices = mode_count * slab_count
    height = nx // devices
    share = modes // slab_count

    strips = pack_strips(guess, mode_count)
    coefs = jnp.concatenate([mean_coef[None], field_coef], 0)[None]
    strips, coefs = lax.optimization_barrier((strips, coefs))
    state = lax.all_to_all(strips, "mode", 0, 0, tiled=True)
    state = state.reshape(mode_count * modes, height * cols)

    def to_slabs(block):
        flat = block.reshape(modes, rows, cols)
        return lax.all_to_all(flat, "slab", 0, 0, tiled=True)

    matrix = dense_coupling(coupling, coupling_list, pair_count, fields)

    slab = lax.axis_index("slab")
    place = jnp.stack([slab, slab * mode_count + lax.axis_index("mode")])
    forward = [(i, i + 1) for i in range(slab_count - 1)]
    low = lax.ppermute(coefs[0, :, -1], "slab", forward)
    high = lax.ppermute(coefs[0, :, 0], "slab", [(b, a) for a, b in forward])
    strip_weights = strip_weights_of(coefs[0], low, high, place, slab_count, height)

    state, matrix, strip_weights = lax.optimization_barrier((state, matrix, strip_weights))
    borders = (state[:, :cols], state[:, -cols:])

    guess_parts = parts_of(guess.reshape(slab_count, share, rows, cols), "slab")
    guess_parts = [jnp.concatenate([part, coefs], axis=1) for part in guess_parts]
    guess_parts = moved_parts(guess_parts, "slab")
    right_parts = parts_of(right_side.reshape(slab_count, share, rows, cols), "slab")
    guess_parts, right_parts, _ = lax.optimization_barrier((guess_parts, right_parts, borders))
    right_parts = moved_parts(right_parts, "slab")
    mean_weights = mean_weights_of(guess_parts, place, fields + 1)

    row_high, row_low = split_table(sine_table(nx))
    col_high, col_low = split_table(sine_table(cols))
    tables = (
        jnp.concatenate(
            [
                jnp.concatenate([col_high, col_low], 1),
                jnp.concatenate([col_high, jnp.zeros_like(col_low)], 1),
            ],
            0,
        ),
        jnp.concatenate(
            [
                jnp.concatenate([row_high, row_high], 1),
                jnp.concatenate([row_low, jnp.zeros_like(row_low)], 1),
            ],
            0,
        ),
        RELAXATION / eigen_table(nx, cols),
    )

    first_scale, sum_scale, solution_scale = code_scales(nx, cols, coupling.shape[1], modes)

    sums = coupled_sums(
        matrix, state, borders, strip_weights, tables[0], True, first_scale, both
    )
    sums, right_parts = lax.optimization_barrier((sums, right_parts))
    sums = lax.all_to_all(sums, both, 0, 0, tiled=True).reshape(devices, share, -1)
    current, right_side, base = first_mean_part(
        place, guess_parts, right_parts, mean_weights, tables[0]
    )
    current, state = step(current, base, sums, tables, mode_count, slab_count, first_scale)
    state = state.reshape(devices * share, height * cols)
    state = lax.all_to_all(state, both, 0, 0, tiled=True)

    base = mean_part(current, right_side, mean_weights)
    borders = (state[:, :cols], state[:, -cols:])
    sums = coupled_sums(
        matrix, state, borders, strip_weights, tables[0], False, sum_scale, both
    )
    sums = lax.all_to_all(sums, both, 0, 0, tiled=True).reshape(devices, share, -1)
    resid, parts = last_residual(base, sums, mode_count, slab_count, sum_scale)
    moved = collect(moved_parts(parts, "slab"), "slab").reshape(modes, rows, cols)
    resid_out = decode(moved, SUM_POWER) * (1.0 / sum_scale)
    code = correct(current, resid, tables, solution_scale)
    return decode(to_slabs(code), SOLUTION_POWER) * (1.0 / solution_scale), resid_out


def solution(mesh):
    placed = (
        P("mode", "slab", None),
        P("mode", "slab", None),
        P("slab", None),
        P(None, "slab", None),
        P(),
        P(),
        P(),
    )
    return jax.shard_map(
        local,
        mesh=mesh,
        in_specs=placed,
        out_specs=(P("mode", "slab", None), P("mode", "slab", None)),
        check_vma=False,
    )
```

```python
import functools
import math

import jax
import jax.numpy as jnp
from jax import lax
from jax.experimental import pallas as pl
from jax.experimental.pallas import tpu as pltpu
from jax.sharding import PartitionSpec as P

RELAXATION = 0.6
VMEM_BYTES = 60 << 20
SHARED_VMEM_BYTES = 48 << 20
SMALL_VMEM_BYTES = 9 << 20
UNROLL = 4


def sine_table(length):
    counter = jnp.arange(length).astype(jnp.float32) + 1.0
    angle = math.pi * counter[:, None] * counter[None, :] / (length + 1)
    return math.sqrt(2.0 / (length + 1)) * jnp.sin(angle)


def eigen_table(first, second):
    along_first = 2.0 * jnp.cos(
        math.pi * (jnp.arange(first).astype(jnp.float32) + 1.0) / (first + 1)
    )
    along_second = 2.0 * jnp.cos(
        math.pi * (jnp.arange(second).astype(jnp.float32) + 1.0) / (second + 1)
    )
    return 4.0 - along_first[:, None] - along_second[None, :]


def stencil_weights(coef):
    nx, ny = coef.shape
    row = lax.broadcasted_iota(jnp.int32, (nx, ny), 0)
    col = lax.broadcasted_iota(jnp.int32, (nx, ny), 1)
    sides = (
        (pltpu.roll(coef, 1, 0), row == 0),
        (pltpu.roll(coef, nx - 1, 0), row == nx - 1),
        (pltpu.roll(coef, 1, 1), col == 0),
        (pltpu.roll(coef, ny - 1, 1), col == ny - 1),
    )
    centre = 0.0
    weights = []
    for other, outside in sides:
        weight = 0.5 * (coef + jnp.where(outside, coef, other))
        centre = centre + weight
        weights.append(jnp.where(outside, 0.0, weight))
    return [centre] + weights


def in_order(here, shift, count):
    return lax.rem(here + count - shift, count)


def in_order(here, shift, count):
    return lax.rem(here + count - shift, count)


MARGIN = 8


def strip_weights_kernel(slabs, height, place_ref, own_ref, low_ref, high_ref, out_ref, coef_ref):
    _, rows, ny = own_ref.shape
    nx = slabs * rows
    fields = out_ref.shape[0] // (5 * height)
    for f in range(1, fields + 1):
        coef_ref[f, MARGIN - 1 : MARGIN, :] = low_ref[f : f + 1, :]
        coef_ref[f, MARGIN : MARGIN + rows, :] = own_ref[f]
        coef_ref[f, MARGIN + rows : MARGIN + rows + 1, :] = high_ref[f : f + 1, :]
    offset = MARGIN - place_ref[0] * rows
    col = lax.broadcasted_iota(jnp.int32, (1, ny), 1)
    first = place_ref[1] * height
    for f in range(fields):
        lines = []
        for r in range(-1, height + 1):
            at = jnp.clip(first + r, 0, nx - 1)
            lines.append(coef_ref[f + 1, pl.ds(at + offset, 1), :])
        for r in range(height):
            here = lines[r + 1]
            up = 0.5 * (here + lines[r])
            down = 0.5 * (here + lines[r + 2])
            left = 0.5 * (here + jnp.where(col == 0, here, pltpu.roll(here, 1, 1)))
            right = 0.5 * (here + jnp.where(col == ny - 1, here, pltpu.roll(here, ny - 1, 1)))
            weights = (
                up + down + left + right,
                jnp.where(first + r == 0, 0.0, up),
                jnp.where(first + r == nx - 1, 0.0, down),
                jnp.where(col == 0, 0.0, left),
                jnp.where(col == ny - 1, 0.0, right),
            )
            for which, weight in enumerate(weights):
                at = (f * 5 + which) * height + r
                out_ref[at : at + 1, :] = weight


def mean_weights_kernel(slabs, place_ref, *refs):
    part_refs = refs[:slabs]
    out_ref, coef_ref = refs[slabs:]
    _, nx, ny = out_ref.shape
    for shift, part_ref in enumerate(part_refs):
        coef_ref[in_order(place_ref[0], shift, slabs)] = part_ref[0, 0]
    for which, weight in enumerate(stencil_weights(coef_ref[...].reshape(nx, ny))):
        out_ref[which] = weight


def strip_weights_of(own, low, high, place, slabs, height):
    coefs, rows, ny = own.shape
    out = ((coefs - 1) * 5 * height, ny)
    edge = pl.BlockSpec((coefs, ny), lambda i, *_: (0, 0))
    return pl.pallas_call(
        functools.partial(strip_weights_kernel, slabs, height),
        grid_spec=pltpu.PrefetchScalarGridSpec(
            num_scalar_prefetch=1,
            grid=(1,),
            in_specs=[pl.BlockSpec((coefs, rows, ny), lambda i, *_: (0, 0, 0)), edge, edge],
            out_specs=pl.BlockSpec(out, lambda i, *_: (0, 0)),
            scratch_shapes=[pltpu.VMEM((coefs, rows + 2 * MARGIN, ny), jnp.float32)],
        ),
        out_shape=jax.ShapeDtypeStruct(out, jnp.float32),
        compiler_params=pltpu.CompilerParams(vmem_limit_bytes=SMALL_VMEM_BYTES),
    )(place, own, low, high)


def mean_weights_of(parts, place, coefs):
    slabs = len(parts)
    _, entries, rows, ny = parts[0].shape
    last = entries // coefs - 1
    out = (5, slabs * rows, ny)
    return pl.pallas_call(
        functools.partial(mean_weights_kernel, slabs),
        grid_spec=pltpu.PrefetchScalarGridSpec(
            num_scalar_prefetch=1,
            grid=(1,),
            in_specs=[pl.BlockSpec((1, coefs, rows, ny), lambda i, *_: (0, last, 0, 0))] * slabs,
            out_specs=pl.BlockSpec(out, lambda i, *_: (0, 0, 0)),
            scratch_shapes=[pltpu.VMEM((slabs, rows, ny), jnp.float32)],
        ),
        out_shape=jax.ShapeDtypeStruct(out, jnp.float32),
        compiler_params=pltpu.CompilerParams(vmem_limit_bytes=SMALL_VMEM_BYTES),
    )(place, *parts)


def split(value):
    high = value.astype(jnp.bfloat16)
    low = (value - high.astype(jnp.float32)).astype(jnp.bfloat16)
    return high, low


def split_table(value):
    high = lax.reduce_precision(value, 8, 7)
    return high.astype(jnp.bfloat16), (value - high).astype(jnp.bfloat16)


LOW = 32
FIRST_POWER = 7
SUM_POWER = 5
SOLUTION_POWER = 4


def encode(value, power):
    square = value * value
    if power == 4:
        result = square * (value * jnp.abs(value))
    elif power == 5:
        result = square * square * value
    else:
        result = (square * square) * (square * value)
    return result.astype(jnp.bfloat16)


def decode(code, power):
    code = code.astype(jnp.float32)
    size = jnp.abs(code)
    value = jnp.exp(jnp.log(size) * (1.0 / power))
    value = jnp.where(size > 0.0, value, 0.0)
    return jnp.where(code < 0.0, -value, value)


def code_scales(nx, ny, entries, width):
    guess_max, mean_max, field_max, coupling_max = 6.0, 2.0, 2.5, 0.0625
    gain = 8.0 * field_max * entries * width * coupling_max * 1.01
    inverse = (min(nx, ny) + 1) ** 2 / 8.0

    def bound(iterate):
        return guess_max + (8.0 * mean_max + gain) * iterate

    change = RELAXATION * inverse * 1.01
    second = guess_max + change * bound(guess_max)
    third = second + change * bound(second)

    def scale(limit, power):
        return 0.8 * 2.0 ** (127.0 / power) / limit

    first = math.sqrt(2.0 * ny) * gain * guess_max
    return (
        min(1.0, scale(first, FIRST_POWER)),
        min(1.0, scale(bound(second), SUM_POWER)),
        min(1.0, scale(third, SOLUTION_POWER)),
    )


def pack_kernel(rows, height, x_ref, out_ref):
    strips, modes, cells = out_ref.shape
    cols = cells // height
    for strip in range(strips):
        for r in range(height):
            value = x_ref[pl.ds(strip * height + r, modes, stride=rows), :]
            out_ref[strip, :, r * cols : (r + 1) * cols] = value.astype(jnp.bfloat16)


def pack_strips(block, strips):
    modes, rows, cols = block.shape
    height = rows // strips
    return pl.pallas_call(
        functools.partial(pack_kernel, rows, height),
        grid=(2,),
        in_specs=[pl.BlockSpec((modes // 2 * rows, cols), lambda g: (g, 0))],
        out_specs=pl.BlockSpec((strips, modes // 2, height * cols), lambda g: (0, g, 0)),
        out_shape=jax.ShapeDtypeStruct((strips, modes, height * cols), jnp.bfloat16),
        compiler_params=pltpu.CompilerParams(vmem_limit_bytes=VMEM_BYTES),
    )(block.reshape(modes * rows, cols))


def dense_kernel(fields, entry_ref, count_ref, coupling_ref, out_ref):
    block = pl.program_id(0)
    width = coupling_ref.shape[-1]
    out_ref[...] = jnp.zeros_like(out_ref)

    def place(k, carry):
        entry = entry_ref[block, k]
        column = pl.multiple_of((entry // fields) * width, width)
        out_ref[0, entry % fields, :, pl.ds(column, width)] = coupling_ref[0, k]
        return carry

    lax.fori_loop(0, count_ref[block], place, 0)


def dense_coupling(coupling, coupling_list, pair_count, fields):
    blocks, entries, width, _ = coupling.shape
    moved = 2 * width * width * (entries + fields * blocks) * coupling.dtype.itemsize
    return pl.pallas_call(
        functools.partial(dense_kernel, fields),
        grid_spec=pltpu.PrefetchScalarGridSpec(
            num_scalar_prefetch=2,
            grid=(blocks,),
            in_specs=[pl.BlockSpec((1, entries, width, width), lambda i, *_: (i, 0, 0, 0))],
            out_specs=pl.BlockSpec(
                (1, fields, width, blocks * width), lambda i, *_: (i, 0, 0, 0)
            ),
        ),
        out_shape=jax.ShapeDtypeStruct((blocks, fields, width, blocks * width), coupling.dtype),
        compiler_params=pltpu.CompilerParams(vmem_limit_bytes=SMALL_VMEM_BYTES + moved),
    )(coupling_list, pair_count, coupling)


def low_tiles(height, cols):
    return -(-height * LOW // cols)


def along_cols(fields, right_ref):
    size, ny = fields[0].shape
    high, low = split(jnp.concatenate(fields, axis=0))
    both = jnp.dot(
        jnp.concatenate([high, low], axis=1), right_ref[...], preferred_element_type=jnp.float32
    )
    both = both[:, :ny] + both[:, ny:]
    return [both[i * size : (i + 1) * size] for i in range(len(fields))]


def along_rows(wide, left_ref):
    nx = wide.shape[0]
    high, low = split(wide)
    both = jnp.dot(
        left_ref[...], jnp.concatenate([high, low], axis=0), preferred_element_type=jnp.float32
    )
    return both[:nx] + both[nx:]


def weight_row(weight_ref, height, field, which, r):
    at = (field * 5 + which) * height + r
    return weight_ref[at : at + 1, :]


def inner_kernel(height, cols, matrix_ref, state_ref, weight_ref, out_ref, sums_ref):
    blocks, fields, width, depth = matrix_ref.shape
    sums_ref[...] = jnp.dot(
        matrix_ref[...].reshape(blocks * fields * width, depth),
        state_ref[...],
        preferred_element_type=jnp.float32,
    )
    for block in range(blocks):
        for r in range(height):
            total = 0.0
            from_left = 0.0
            from_right = 0.0
            for f in range(fields):

                def row(at):
                    start = (block * fields + f) * width
                    return sums_ref[start : start + width, at * cols : (at + 1) * cols]

                weight = functools.partial(weight_row, weight_ref, height, f)
                here = row(r)
                total = total + weight(0, r) * here
                if r > 0:
                    total = total - weight(1, r) * row(r - 1)
                if r < height - 1:
                    total = total - weight(2, r) * row(r + 1)
                from_left = from_left + weight(4, r) * here
                from_right = from_right + weight(3, r) * here
            total = total - pltpu.roll(from_left, 1, 1) - pltpu.roll(from_right, cols - 1, 1)
            out_ref[block * width : (block + 1) * width, r * cols : (r + 1) * cols] = total


def border_kernel(
    height,
    cols,
    first,
    scale,
    matrix_ref,
    above_ref,
    below_ref,
    weight_ref,
    inner_ref,
    right_ref,
    out_ref,
):
    blocks, fields, width, depth = matrix_ref.shape
    border = jnp.concatenate([above_ref[...], below_ref[...]], axis=1)
    low_col = lax.broadcasted_iota(jnp.int32, (width, cols), 1) < LOW
    matrix = matrix_ref[...].reshape(blocks * fields * width, depth)
    sums = jnp.dot(matrix, border, preferred_element_type=jnp.float32)
    for block in range(blocks):
        modes = slice(block * width, (block + 1) * width)
        rows = []
        for r in range(height):
            total = inner_ref[modes, r * cols : (r + 1) * cols]
            for f in range(fields):
                part = sums[(block * fields + f) * width : (block * fields + f + 1) * width]
                if r == 0:
                    total = total - weight_row(weight_ref, height, f, 1, r) * part[:, :cols]
                if r == height - 1:
                    total = total - weight_row(weight_ref, height, f, 2, r) * part[:, cols:]
            rows.append(total)
        if not first:
            for r in range(height):
                code = encode(rows[r] * scale, SUM_POWER)
                out_ref[modes, r * cols : (r + 1) * cols] = code
            continue
        rows = along_cols(rows, right_ref)
        for r in range(height):
            value = rows[r] * scale
            code = encode(value, FIRST_POWER)
            out_ref[modes, r * cols : (r + 1) * cols] = code
            rest = jnp.where(low_col, value - decode(code, FIRST_POWER), 0.0)
            place = r % (cols // LOW)
            rest = pltpu.roll(rest, place * LOW, 1) if place else rest
            packed = rest if place == 0 else packed + rest
            if place == cols // LOW - 1 or r == height - 1:
                at = (height + r // (cols // LOW)) * cols
                out_ref[modes, at : at + cols] = packed.astype(jnp.bfloat16)


def coupled_sums(matrix, state, borders, weights, right, first, scale, both):
    blocks, fields, width, depth = matrix.shape
    cells = state.shape[1]
    height = weights.shape[0] // (5 * fields)
    cols = cells // height
    mode_count = lax.axis_size("mode")
    slab_count = lax.axis_size("slab")
    place = [
        (t % mode_count) * slab_count + t // mode_count for t in range(mode_count * slab_count)
    ]
    onward = list(zip(place, place[1:] + place[:1]))
    above = lax.ppermute(borders[1], both, onward)
    below = lax.ppermute(borders[0], both, [(b, a) for a, b in onward])
    unroll = math.gcd(blocks, UNROLL)
    matrix_spec = pl.BlockSpec((unroll, fields, width, depth), lambda i: (i, 0, 0, 0))
    weight_spec = pl.BlockSpec(weights.shape, lambda i: (0, 0))
    sums_spec = pl.BlockSpec((unroll * width, cells), lambda i: (i, 0))
    moved = 2 * unroll * fields * width * depth * matrix.dtype.itemsize
    params = pltpu.CompilerParams(vmem_limit_bytes=2 * SMALL_VMEM_BYTES + moved)
    inner = pl.pallas_call(
        functools.partial(inner_kernel, height, cols),
        grid=(blocks // unroll,),
        in_specs=[matrix_spec, pl.BlockSpec((depth, cells), lambda i: (0, 0)), weight_spec],
        out_specs=sums_spec,
        out_shape=jax.ShapeDtypeStruct((blocks * width, cells), jnp.float32),
        scratch_shapes=[pltpu.VMEM((unroll * fields * width, cells), jnp.float32)],
        cost_estimate=pl.CostEstimate(
            flops=2 * matrix.size * cells, bytes_accessed=2 * matrix.size, transcendentals=0
        ),
        compiler_params=params,
    )(matrix, state, weights)
    border_spec = pl.BlockSpec((depth, cols), lambda i: (0, 0))
    sent = cells + (low_tiles(height, cols) * cols if first else 0)
    return pl.pallas_call(
        functools.partial(border_kernel, height, cols, first, scale),
        grid=(blocks // unroll,),
        in_specs=[
            matrix_spec,
            border_spec,
            border_spec,
            weight_spec,
            sums_spec,
            pl.BlockSpec(right.shape, lambda i: (0, 0)),
        ],
        out_specs=pl.BlockSpec((unroll * width, sent), lambda i: (i, 0)),
        out_shape=jax.ShapeDtypeStruct((blocks * width, sent), jnp.bfloat16),
        compiler_params=params,
    )(matrix, above, below, weights, inner, right)


TOGETHER = 16
MEAN_TOGETHER = 8
GROUP = 16


def solve(spectral, right_ref, left_ref, scale_ref):
    ny = spectral[0].shape[1]
    wide = along_rows(jnp.concatenate(spectral, axis=1), left_ref)
    wide = wide * jnp.concatenate([scale_ref[...]] * len(spectral), axis=1)
    wide = along_rows(wide, left_ref)
    return along_cols([wide[:, i * ny : (i + 1) * ny] for i in range(len(spectral))], right_ref)


def mean_fields(current_ref, right_side_ref, weight_ref, start):
    nx, ny = weight_ref.shape[1:]
    values = []
    for mode in range(start, start + MEAN_TOGETHER):
        here = current_ref[:, mode].reshape(nx, ny)
        mean = (
            weight_ref[0] * here
            - weight_ref[1] * pltpu.roll(here, 1, 0)
            - weight_ref[2] * pltpu.roll(here, nx - 1, 0)
            - pltpu.roll(weight_ref[4] * here, 1, 1)
            - pltpu.roll(weight_ref[3] * here, ny - 1, 1)
        )
        values.append(right_side_ref[:, mode].reshape(nx, ny) - mean)
    return values


def first_mean_kernel(slabs, place_ref, *refs):
    current_parts = refs[:slabs]
    right_side_parts = refs[slabs : 2 * slabs]
    weight_ref, right_ref, current_ref, right_side_ref, out_ref = refs[2 * slabs :]
    for shift in range(slabs):
        slab = in_order(place_ref[0], shift, slabs)
        current_ref[slab] = current_parts[shift][0]
        right_side_ref[slab] = right_side_parts[shift][0]
    shape = (slabs,) + out_ref.shape[2:]
    for start in range(0, out_ref.shape[1], MEAN_TOGETHER):
        values = mean_fields(current_ref, right_side_ref, weight_ref, start)
        for i, value in enumerate(along_cols(values, right_ref)):
            out_ref[:, start + i] = value.reshape(shape)


def mean_kernel(current_ref, right_side_ref, weight_ref, out_ref):
    shape = out_ref.shape[:1] + out_ref.shape[2:]
    for start in range(0, out_ref.shape[1], MEAN_TOGETHER):
        values = mean_fields(current_ref, right_side_ref, weight_ref, start)
        for i, value in enumerate(values):
            out_ref[:, start + i] = value.reshape(shape)


def turn_in(turned_ref, coupled_ref, mode_count, slab_count, height, first, scale):
    group = coupled_ref.shape[1]
    ny = turned_ref.shape[1]
    low_col = lax.broadcasted_iota(jnp.int32, (group, ny), 1) < LOW
    for source in range(mode_count * slab_count):
        start = ((source % slab_count) * mode_count + source // slab_count) * height
        for r in range(height):
            code = coupled_ref[source, :, r * ny : (r + 1) * ny]
            value = decode(code, FIRST_POWER if first else SUM_POWER)
            if first:
                at = (height + r // (ny // LOW)) * ny
                rest = coupled_ref[source, :, at : at + ny].astype(jnp.float32)
                place = r % (ny // LOW)
                rest = pltpu.roll(rest, ny - place * LOW, 1) if place else rest
                value = value + jnp.where(low_col, rest, 0.0)
            turned_ref[(start + r) * group : (start + r + 1) * group, :] = value * (1.0 / scale)


def step_kernel(
    mode_count,
    slab_count,
    code_scale,
    current_ref,
    base_ref,
    coupled_ref,
    right_ref,
    left_ref,
    scale_ref,
    solution_ref,
    state_ref,
    turned_ref,
):
    nx, ny = scale_ref.shape
    group = coupled_ref.shape[1]
    height = nx // (mode_count * slab_count)
    turn_in(turned_ref, coupled_ref, mode_count, slab_count, height, True, code_scale)

    def several(number, carry):
        start = number * TOGETHER
        resid = []
        for i in range(TOGETHER):
            coupled = turned_ref[pl.ds(start + i, nx, stride=group), :]
            resid.append(base_ref[:, start + i].reshape(nx, ny) - coupled)
        change = solve(resid, right_ref, left_ref, scale_ref)
        for i in range(TOGETHER):
            value = current_ref[:, start + i].reshape(nx, ny) + change[i]
            solution_ref[:, start + i] = value.reshape(slab_count, nx // slab_count, ny)
            turned_ref[pl.ds(start + i, nx, stride=group), :] = value
        return carry

    lax.fori_loop(0, group // TOGETHER, several, 0)

    for target in range(mode_count * slab_count):
        start = ((target % slab_count) * mode_count + target // slab_count) * height
        for r in range(height):
            row = start + r
            value = turned_ref[row * group : (row + 1) * group, :].astype(jnp.bfloat16)
            state_ref[target, :, r * ny : (r + 1) * ny] = value


def residual_kernel(
    mode_count, slab_count, code_scale, here_ref, base_ref, coupled_ref, out_ref, *refs
):
    *code_refs, turned_ref = refs
    group = coupled_ref.shape[1]
    ny = base_ref.shape[-1]
    nx = turned_ref.shape[0] // group
    height = nx // (mode_count * slab_count)
    turn_in(turned_ref, coupled_ref, mode_count, slab_count, height, False, code_scale)

    def one(mode, carry):
        coupled = turned_ref[pl.ds(mode, nx, stride=group), :]
        out_ref[:, mode] = base_ref[:, mode] - coupled.reshape(slab_count, nx // slab_count, ny)
        return carry

    lax.fori_loop(0, group, one, 0)
    for shift, code_ref in enumerate(code_refs):
        slab = lax.rem(here_ref[0] + shift, slab_count)
        code_ref[0] = encode(out_ref[slab] * code_scale, SUM_POWER)


def correct_kernel(code_scale, current_ref, resid_ref, right_ref, left_ref, scale_ref, out_ref):
    nx, ny = scale_ref.shape

    def several(number, carry):
        start = number * TOGETHER
        resid = [resid_ref[:, start + i].reshape(nx, ny) for i in range(TOGETHER)]
        change = solve(along_cols(resid, right_ref), right_ref, left_ref, scale_ref)
        for i in range(TOGETHER):
            shape = out_ref.shape[:1] + out_ref.shape[2:]
            value = current_ref[:, start + i] + change[i].reshape(shape)
            out_ref[:, start + i] = encode(value * code_scale, SOLUTION_POWER)
        return carry

    lax.fori_loop(0, out_ref.shape[1] // TOGETHER, several, 0)


def whole(array):
    return pl.BlockSpec(array.shape, lambda g: (0,) * array.ndim)


def slabs_of(array):
    slab_count, _, rows, ny = array.shape
    return pl.BlockSpec((slab_count, GROUP, rows, ny), lambda g: (0, g, 0, 0))


def strips_of(shape):
    return pl.BlockSpec((shape[0], GROUP, shape[2]), lambda g: (0, g, 0))


def per_group(
    kernel, groups, operands, in_specs, out_shape, out_specs, scratch=(), flops=0, vmem=SHARED_VMEM_BYTES
):
    moved = sum(a.size * a.dtype.itemsize for a in operands)
    return pl.pallas_call(
        kernel,
        grid=(groups,),
        in_specs=in_specs,
        out_specs=out_specs,
        out_shape=out_shape,
        scratch_shapes=scratch,
        cost_estimate=pl.CostEstimate(flops=flops, bytes_accessed=2 * moved, transcendentals=0),
        compiler_params=pltpu.CompilerParams(vmem_limit_bytes=vmem),
    )(*operands)


def first_mean_part(place, current_parts, right_side_parts, weights, right):
    slabs = len(right_side_parts)
    _, modes, rows, ny = right_side_parts[0].shape
    part = pl.BlockSpec((1, GROUP, rows, ny), lambda g, *_: (0, g, 0, 0))
    slab = pl.BlockSpec((slabs, GROUP, rows, ny), lambda g, *_: (0, g, 0, 0))
    shape = jax.ShapeDtypeStruct((slabs, modes, rows, ny), jnp.float32)
    return pl.pallas_call(
        functools.partial(first_mean_kernel, slabs),
        grid_spec=pltpu.PrefetchScalarGridSpec(
            num_scalar_prefetch=1,
            grid=(modes // GROUP,),
            in_specs=[part] * (2 * slabs)
            + [
                pl.BlockSpec(weights.shape, lambda g, *_: (0, 0, 0)),
                pl.BlockSpec(right.shape, lambda g, *_: (0, 0)),
            ],
            out_specs=[slab] * 3,
        ),
        out_shape=[shape] * 3,
        compiler_params=pltpu.CompilerParams(vmem_limit_bytes=SHARED_VMEM_BYTES),
    )(place, *current_parts, *right_side_parts, weights, right)


def mean_part(current, right_side, weights):
    slabs = slabs_of(right_side)
    return per_group(
        mean_kernel,
        right_side.shape[1] // GROUP,
        (current, right_side, weights),
        [slabs, slabs, whole(weights)],
        jax.ShapeDtypeStruct(right_side.shape, jnp.float32),
        slabs,
    )


def solve_flops(array, tables):
    nx, ny = tables[2].shape
    return array.shape[1] * 8 * 3 * nx * ny * (nx + ny) // 2


def step(current, base, coupled, tables, mode_count, slab_count, code_scale):
    nx, ny = tables[2].shape
    slabs = slabs_of(base)
    devices, modes, _ = coupled.shape
    state = (devices, modes, nx // devices * ny)
    return per_group(
        functools.partial(step_kernel, mode_count, slab_count, code_scale),
        modes // GROUP,
        (current, base, coupled, *tables),
        [slabs, slabs, strips_of(coupled.shape), *map(whole, tables)],
        [
            jax.ShapeDtypeStruct(base.shape, jnp.float32),
            jax.ShapeDtypeStruct(state, jnp.bfloat16),
        ],
        [slabs, strips_of(state)],
        [pltpu.VMEM((nx * GROUP, ny), jnp.float32)],
        solve_flops(base, tables),
    )


def last_residual(base, coupled, mode_count, slab_count, code_scale):
    slab, modes, rows, ny = base.shape
    slabs = pl.BlockSpec((slab, GROUP, rows, ny), lambda g, *_: (0, g, 0, 0))
    part = pl.BlockSpec((1, GROUP, rows, ny), lambda g, *_: (0, g, 0, 0))
    devices, _, cells = coupled.shape
    out, *parts = pl.pallas_call(
        functools.partial(residual_kernel, mode_count, slab_count, code_scale),
        grid_spec=pltpu.PrefetchScalarGridSpec(
            num_scalar_prefetch=1,
            grid=(modes // GROUP,),
            in_specs=[slabs, pl.BlockSpec((devices, GROUP, cells), lambda g, *_: (0, g, 0))],
            out_specs=[slabs] + [part] * slab,
            scratch_shapes=[pltpu.VMEM((slab * rows * GROUP, ny), jnp.float32)],
        ),
        out_shape=[jax.ShapeDtypeStruct(base.shape, jnp.float32)]
        + [jax.ShapeDtypeStruct((1, modes, rows, ny), jnp.bfloat16)] * slab,
        cost_estimate=pl.CostEstimate(
            flops=0, bytes_accessed=2 * base.size * 4, transcendentals=0
        ),
        compiler_params=pltpu.CompilerParams(vmem_limit_bytes=SHARED_VMEM_BYTES),
    )(lax.axis_index("slab").reshape(1), base, coupled)
    return out, parts


def correct(current, resid, tables, code_scale):
    slabs = slabs_of(resid)
    return per_group(
        functools.partial(correct_kernel, code_scale),
        resid.shape[1] // GROUP,
        (current, resid, *tables),
        [slabs, slabs, *map(whole, tables)],
        jax.ShapeDtypeStruct(resid.shape, jnp.bfloat16),
        slabs,
        (),
        solve_flops(resid, tables),
    )


def collect(parts, axis):
    count = lax.axis_size(axis)
    here = lax.axis_index(axis)
    out = jnp.zeros((count,) + parts[0].shape[1:], parts[0].dtype)
    for shift, part in enumerate(parts):
        source = lax.rem(here + count - shift, count)
        out = lax.dynamic_update_slice_in_dim(out, part, source, 0)
    return out


def onwards(part, axis, shift):
    count = lax.axis_size(axis)
    return lax.ppermute(part, axis, [(i, (i + shift) % count) for i in range(count)])


def parts_of(block, axis):
    count = lax.axis_size(axis)
    here = lax.axis_index(axis)
    return [
        lax.dynamic_index_in_dim(block, lax.rem(here + shift, count), 0) for shift in range(count)
    ]


def moved_parts(parts, axis):
    return [parts[0]] + [onwards(parts[i], axis, i) for i in range(1, len(parts))]


def local(guess, right_side, mean_coef, field_coef, coupling, coupling_list, pair_count):
    mode_count = lax.axis_size("mode")
    slab_count = lax.axis_size("slab")
    both = ("mode", "slab")
    modes, rows, cols = guess.shape
    fields = field_coef.shape[0]
    nx = rows * slab_count
    devices = mode_count * slab_count
    height = nx // devices
    share = modes // slab_count

    strips = pack_strips(guess, mode_count)
    coefs = jnp.concatenate([mean_coef[None], field_coef], 0)[None]
    strips, coefs = lax.optimization_barrier((strips, coefs))
    state = lax.all_to_all(strips, "mode", 0, 0, tiled=True)
    state = state.reshape(mode_count * modes, height * cols)

    def to_slabs(block):
        flat = block.reshape(modes, rows, cols)
        return lax.all_to_all(flat, "slab", 0, 0, tiled=True)

    matrix = dense_coupling(coupling, coupling_list, pair_count, fields)

    slab = lax.axis_index("slab")
    place = jnp.stack([slab, slab * mode_count + lax.axis_index("mode")])
    forward = [(i, i + 1) for i in range(slab_count - 1)]
    low = lax.ppermute(coefs[0, :, -1], "slab", forward)
    high = lax.ppermute(coefs[0, :, 0], "slab", [(b, a) for a, b in forward])
    strip_weights = strip_weights_of(coefs[0], low, high, place, slab_count, height)

    state, matrix, strip_weights = lax.optimization_barrier((state, matrix, strip_weights))
    borders = (state[:, :cols], state[:, -cols:])

    guess_parts = parts_of(guess.reshape(slab_count, share, rows, cols), "slab")
    guess_parts = [jnp.concatenate([part, coefs], axis=1) for part in guess_parts]
    guess_parts = moved_parts(guess_parts, "slab")
    right_parts = parts_of(right_side.reshape(slab_count, share, rows, cols), "slab")
    guess_parts, right_parts, _ = lax.optimization_barrier((guess_parts, right_parts, borders))
    right_parts = moved_parts(right_parts, "slab")
    mean_weights = mean_weights_of(guess_parts, place, fields + 1)

    row_high, row_low = split_table(sine_table(nx))
    col_high, col_low = split_table(sine_table(cols))
    tables = (
        jnp.concatenate(
            [
                jnp.concatenate([col_high, col_low], 1),
                jnp.concatenate([col_high, jnp.zeros_like(col_low)], 1),
            ],
            0,
        ),
        jnp.concatenate(
            [
                jnp.concatenate([row_high, row_high], 1),
                jnp.concatenate([row_low, jnp.zeros_like(row_low)], 1),
            ],
            0,
        ),
        RELAXATION / eigen_table(nx, cols),
    )

    first_scale, sum_scale, solution_scale = code_scales(nx, cols, coupling.shape[1], modes)

    sums = coupled_sums(
        matrix, state, borders, strip_weights, tables[0], True, first_scale, both
    )
    sums, right_parts = lax.optimization_barrier((sums, right_parts))
    sums = lax.all_to_all(sums, both, 0, 0, tiled=True).reshape(devices, share, -1)
    current, right_side, base = first_mean_part(
        place, guess_parts, right_parts, mean_weights, tables[0]
    )
    current, state = step(current, base, sums, tables, mode_count, slab_count, first_scale)
    state = state.reshape(devices * share, height * cols)
    state = lax.all_to_all(state, both, 0, 0, tiled=True)

    base = mean_part(current, right_side, mean_weights)
    borders = (state[:, :cols], state[:, -cols:])
    sums = coupled_sums(
        matrix, state, borders, strip_weights, tables[0], False, sum_scale, both
    )
    sums = lax.all_to_all(sums, both, 0, 0, tiled=True).reshape(devices, share, -1)
    resid, parts = last_residual(base, sums, mode_count, slab_count, sum_scale)
    moved = collect(moved_parts(parts, "slab"), "slab").reshape(modes, rows, cols)
    resid_out = decode(moved, SUM_POWER) * (1.0 / sum_scale)
    code = correct(current, resid, tables, solution_scale)
    return decode(to_slabs(code), SOLUTION_POWER) * (1.0 / solution_scale), resid_out


def solution(mesh):
    placed = (
        P("mode", "slab", None),
        P("mode", "slab", None),
        P("slab", None),
        P(None, "slab", None),
        P(),
        P(),
        P(),
    )
    return jax.shard_map(
        local,
        mesh=mesh,
        in_specs=placed,
        out_specs=(P("mode", "slab", None), P("mode", "slab", None)),
        check_vma=False,
    )
```

```python
import functools
import math

import jax
import jax.numpy as jnp
from jax import lax
from jax.experimental import pallas as pl
from jax.experimental.pallas import tpu as pltpu
from jax.sharding import PartitionSpec as P

RELAXATION = 0.6
VMEM_BYTES = 60 << 20
SHARED_VMEM_BYTES = 48 << 20
SMALL_VMEM_BYTES = 9 << 20
UNROLL = 4


def sine_table(length):
    counter = jnp.arange(length).astype(jnp.float32) + 1.0
    angle = math.pi * counter[:, None] * counter[None, :] / (length + 1)
    return math.sqrt(2.0 / (length + 1)) * jnp.sin(angle)


def eigen_table(first, second):
    along_first = 2.0 * jnp.cos(
        math.pi * (jnp.arange(first).astype(jnp.float32) + 1.0) / (first + 1)
    )
    along_second = 2.0 * jnp.cos(
        math.pi * (jnp.arange(second).astype(jnp.float32) + 1.0) / (second + 1)
    )
    return 4.0 - along_first[:, None] - along_second[None, :]


def stencil_weights(coef):
    nx, ny = coef.shape
    row = lax.broadcasted_iota(jnp.int32, (nx, ny), 0)
    col = lax.broadcasted_iota(jnp.int32, (nx, ny), 1)
    sides = (
        (pltpu.roll(coef, 1, 0), row == 0),
        (pltpu.roll(coef, nx - 1, 0), row == nx - 1),
        (pltpu.roll(coef, 1, 1), col == 0),
        (pltpu.roll(coef, ny - 1, 1), col == ny - 1),
    )
    centre = 0.0
    weights = []
    for other, outside in sides:
        weight = 0.5 * (coef + jnp.where(outside, coef, other))
        centre = centre + weight
        weights.append(jnp.where(outside, 0.0, weight))
    return [centre] + weights


def in_order(here, shift, count):
    return lax.rem(here + count - shift, count)


def in_order(here, shift, count):
    return lax.rem(here + count - shift, count)


def strip_weights_kernel(slabs, height, place_ref, *refs):
    part_refs = refs[:slabs]
    out_ref, coef_ref = refs[slabs:]
    _, nx, ny = coef_ref.shape
    rows = nx // slabs
    fields = out_ref.shape[0] // (5 * height)
    for shift, part_ref in enumerate(part_refs):
        start = in_order(place_ref[0], shift, slabs) * rows
        coef_ref[:, pl.ds(pl.multiple_of(start, rows), rows), :] = part_ref[0]
    col = lax.broadcasted_iota(jnp.int32, (1, ny), 1)
    first = place_ref[1] * height
    for f in range(fields):
        lines = []
        for r in range(-1, height + 1):
            at = jnp.clip(first + r, 0, nx - 1)
            lines.append(coef_ref[f + 1, pl.ds(at, 1), :])
        for r in range(height):
            here = lines[r + 1]
            up = 0.5 * (here + lines[r])
            down = 0.5 * (here + lines[r + 2])
            left = 0.5 * (here + jnp.where(col == 0, here, pltpu.roll(here, 1, 1)))
            right = 0.5 * (here + jnp.where(col == ny - 1, here, pltpu.roll(here, ny - 1, 1)))
            weights = (
                up + down + left + right,
                jnp.where(first + r == 0, 0.0, up),
                jnp.where(first + r == nx - 1, 0.0, down),
                jnp.where(col == 0, 0.0, left),
                jnp.where(col == ny - 1, 0.0, right),
            )
            for which, weight in enumerate(weights):
                at = (f * 5 + which) * height + r
                out_ref[at : at + 1, :] = weight


def mean_weights_kernel(slabs, place_ref, *refs):
    part_refs = refs[:slabs]
    out_ref, coef_ref = refs[slabs:]
    _, nx, ny = out_ref.shape
    for shift, part_ref in enumerate(part_refs):
        coef_ref[in_order(place_ref[0], shift, slabs)] = part_ref[0, 0]
    for which, weight in enumerate(stencil_weights(coef_ref[...].reshape(nx, ny))):
        out_ref[which] = weight


def weights_of(kernel, parts, place, coefs, out, scratch):
    _, entries, rows, ny = parts[0].shape
    last = entries // coefs - 1
    return pl.pallas_call(
        kernel,
        grid_spec=pltpu.PrefetchScalarGridSpec(
            num_scalar_prefetch=1,
            grid=(1,),
            in_specs=[pl.BlockSpec((1, coefs, rows, ny), lambda i, *_: (0, last, 0, 0))]
            * len(parts),
            out_specs=pl.BlockSpec(out, lambda i, *_: (0,) * len(out)),
            scratch_shapes=[pltpu.VMEM(scratch, jnp.float32)],
        ),
        out_shape=jax.ShapeDtypeStruct(out, jnp.float32),
        compiler_params=pltpu.CompilerParams(vmem_limit_bytes=SMALL_VMEM_BYTES),
    )(place, *parts)


def strip_weights_of(parts, place, coefs, height):
    slabs = len(parts)
    _, _, rows, ny = parts[0].shape
    kernel = functools.partial(strip_weights_kernel, slabs, height)
    out = ((coefs - 1) * 5 * height, ny)
    return weights_of(kernel, parts, place, coefs, out, (coefs, slabs * rows, ny))


def mean_weights_of(parts, place, coefs):
    slabs = len(parts)
    _, _, rows, ny = parts[0].shape
    kernel = functools.partial(mean_weights_kernel, slabs)
    return weights_of(kernel, parts, place, coefs, (5, slabs * rows, ny), (slabs, rows, ny))


def split(value):
    high = value.astype(jnp.bfloat16)
    low = (value - high.astype(jnp.float32)).astype(jnp.bfloat16)
    return high, low


def split_table(value):
    high = lax.reduce_precision(value, 8, 7)
    return high.astype(jnp.bfloat16), (value - high).astype(jnp.bfloat16)


LOW = 32
FIRST_POWER = 7
SUM_POWER = 5
SOLUTION_POWER = 4


def encode(value, power):
    square = value * value
    if power == 4:
        result = square * (value * jnp.abs(value))
    elif power == 5:
        result = square * square * value
    else:
        result = (square * square) * (square * value)
    return result.astype(jnp.bfloat16)


def decode(code, power):
    code = code.astype(jnp.float32)
    size = jnp.abs(code)
    value = jnp.exp(jnp.log(size) * (1.0 / power))
    value = jnp.where(size > 0.0, value, 0.0)
    return jnp.where(code < 0.0, -value, value)


def code_scales(nx, ny, entries, width):
    guess_max, mean_max, field_max, coupling_max = 6.0, 2.0, 2.5, 0.0625
    gain = 8.0 * field_max * entries * width * coupling_max * 1.01
    inverse = (min(nx, ny) + 1) ** 2 / 8.0

    def bound(iterate):
        return guess_max + (8.0 * mean_max + gain) * iterate

    change = RELAXATION * inverse * 1.01
    second = guess_max + change * bound(guess_max)
    third = second + change * bound(second)

    def scale(limit, power):
        return 0.8 * 2.0 ** (127.0 / power) / limit

    first = math.sqrt(2.0 * ny) * gain * guess_max
    return (
        min(1.0, scale(first, FIRST_POWER)),
        min(1.0, scale(bound(second), SUM_POWER)),
        min(1.0, scale(third, SOLUTION_POWER)),
    )


def pack_kernel(rows, height, x_ref, out_ref):
    strips, modes, cells = out_ref.shape
    cols = cells // height
    for strip in range(strips):
        for r in range(height):
            value = x_ref[pl.ds(strip * height + r, modes, stride=rows), :]
            out_ref[strip, :, r * cols : (r + 1) * cols] = value.astype(jnp.bfloat16)


def pack_strips(block, strips):
    modes, rows, cols = block.shape
    height = rows // strips
    return pl.pallas_call(
        functools.partial(pack_kernel, rows, height),
        grid=(2,),
        in_specs=[pl.BlockSpec((modes // 2 * rows, cols), lambda g: (g, 0))],
        out_specs=pl.BlockSpec((strips, modes // 2, height * cols), lambda g: (0, g, 0)),
        out_shape=jax.ShapeDtypeStruct((strips, modes, height * cols), jnp.bfloat16),
        compiler_params=pltpu.CompilerParams(vmem_limit_bytes=VMEM_BYTES),
    )(block.reshape(modes * rows, cols))


def dense_kernel(fields, entry_ref, count_ref, coupling_ref, out_ref):
    block = pl.program_id(0)
    width = coupling_ref.shape[-1]
    out_ref[...] = jnp.zeros_like(out_ref)

    def place(k, carry):
        entry = entry_ref[block, k]
        column = pl.multiple_of((entry // fields) * width, width)
        out_ref[0, entry % fields, :, pl.ds(column, width)] = coupling_ref[0, k]
        return carry

    lax.fori_loop(0, count_ref[block], place, 0)


def dense_coupling(coupling, coupling_list, pair_count, fields):
    blocks, entries, width, _ = coupling.shape
    moved = 2 * width * width * (entries + fields * blocks) * coupling.dtype.itemsize
    return pl.pallas_call(
        functools.partial(dense_kernel, fields),
        grid_spec=pltpu.PrefetchScalarGridSpec(
            num_scalar_prefetch=2,
            grid=(blocks,),
            in_specs=[pl.BlockSpec((1, entries, width, width), lambda i, *_: (i, 0, 0, 0))],
            out_specs=pl.BlockSpec(
                (1, fields, width, blocks * width), lambda i, *_: (i, 0, 0, 0)
            ),
        ),
        out_shape=jax.ShapeDtypeStruct((blocks, fields, width, blocks * width), coupling.dtype),
        compiler_params=pltpu.CompilerParams(vmem_limit_bytes=SMALL_VMEM_BYTES + moved),
    )(coupling_list, pair_count, coupling)


def low_tiles(height, cols):
    return -(-height * LOW // cols)


def along_cols(fields, right_ref):
    size, ny = fields[0].shape
    high, low = split(jnp.concatenate(fields, axis=0))
    both = jnp.dot(
        jnp.concatenate([high, low], axis=1), right_ref[...], preferred_element_type=jnp.float32
    )
    both = both[:, :ny] + both[:, ny:]
    return [both[i * size : (i + 1) * size] for i in range(len(fields))]


def along_rows(wide, left_ref):
    nx = wide.shape[0]
    high, low = split(wide)
    both = jnp.dot(
        left_ref[...], jnp.concatenate([high, low], axis=0), preferred_element_type=jnp.float32
    )
    return both[:nx] + both[nx:]


def weight_row(weight_ref, height, field, which, r):
    at = (field * 5 + which) * height + r
    return weight_ref[at : at + 1, :]


def inner_kernel(height, cols, matrix_ref, state_ref, weight_ref, out_ref, sums_ref):
    blocks, fields, width, depth = matrix_ref.shape
    sums_ref[...] = jnp.dot(
        matrix_ref[...].reshape(blocks * fields * width, depth),
        state_ref[...],
        preferred_element_type=jnp.float32,
    )
    for block in range(blocks):
        for r in range(height):
            total = 0.0
            from_left = 0.0
            from_right = 0.0
            for f in range(fields):

                def row(at):
                    start = (block * fields + f) * width
                    return sums_ref[start : start + width, at * cols : (at + 1) * cols]

                weight = functools.partial(weight_row, weight_ref, height, f)
                here = row(r)
                total = total + weight(0, r) * here
                if r > 0:
                    total = total - weight(1, r) * row(r - 1)
                if r < height - 1:
                    total = total - weight(2, r) * row(r + 1)
                from_left = from_left + weight(4, r) * here
                from_right = from_right + weight(3, r) * here
            total = total - pltpu.roll(from_left, 1, 1) - pltpu.roll(from_right, cols - 1, 1)
            out_ref[block * width : (block + 1) * width, r * cols : (r + 1) * cols] = total


def border_kernel(
    height,
    cols,
    first,
    scale,
    matrix_ref,
    above_ref,
    below_ref,
    weight_ref,
    inner_ref,
    right_ref,
    out_ref,
):
    blocks, fields, width, depth = matrix_ref.shape
    border = jnp.concatenate([above_ref[...], below_ref[...]], axis=1)
    low_col = lax.broadcasted_iota(jnp.int32, (width, cols), 1) < LOW
    matrix = matrix_ref[...].reshape(blocks * fields * width, depth)
    sums = jnp.dot(matrix, border, preferred_element_type=jnp.float32)
    for block in range(blocks):
        modes = slice(block * width, (block + 1) * width)
        rows = []
        for r in range(height):
            total = inner_ref[modes, r * cols : (r + 1) * cols]
            for f in range(fields):
                part = sums[(block * fields + f) * width : (block * fields + f + 1) * width]
                if r == 0:
                    total = total - weight_row(weight_ref, height, f, 1, r) * part[:, :cols]
                if r == height - 1:
                    total = total - weight_row(weight_ref, height, f, 2, r) * part[:, cols:]
            rows.append(total)
        if not first:
            for r in range(height):
                code = encode(rows[r] * scale, SUM_POWER)
                out_ref[modes, r * cols : (r + 1) * cols] = code
            continue
        rows = along_cols(rows, right_ref)
        for r in range(height):
            value = rows[r] * scale
            code = encode(value, FIRST_POWER)
            out_ref[modes, r * cols : (r + 1) * cols] = code
            rest = jnp.where(low_col, value - decode(code, FIRST_POWER), 0.0)
            place = r % (cols // LOW)
            rest = pltpu.roll(rest, place * LOW, 1) if place else rest
            packed = rest if place == 0 else packed + rest
            if place == cols // LOW - 1 or r == height - 1:
                at = (height + r // (cols // LOW)) * cols
                out_ref[modes, at : at + cols] = packed.astype(jnp.bfloat16)


def coupled_sums(matrix, state, weights, right, first, scale, both):
    blocks, fields, width, depth = matrix.shape
    cells = state.shape[1]
    height = weights.shape[0] // (5 * fields)
    cols = cells // height
    mode_count = lax.axis_size("mode")
    slab_count = lax.axis_size("slab")
    place = [
        (t % mode_count) * slab_count + t // mode_count for t in range(mode_count * slab_count)
    ]
    onward = list(zip(place, place[1:] + place[:1]))
    above = lax.ppermute(state[:, -cols:], both, onward)
    below = lax.ppermute(state[:, :cols], both, [(b, a) for a, b in onward])
    unroll = math.gcd(blocks, UNROLL)
    matrix_spec = pl.BlockSpec((unroll, fields, width, depth), lambda i: (i, 0, 0, 0))
    weight_spec = pl.BlockSpec(weights.shape, lambda i: (0, 0))
    sums_spec = pl.BlockSpec((unroll * width, cells), lambda i: (i, 0))
    moved = 2 * unroll * fields * width * depth * matrix.dtype.itemsize
    params = pltpu.CompilerParams(vmem_limit_bytes=2 * SMALL_VMEM_BYTES + moved)
    inner = pl.pallas_call(
        functools.partial(inner_kernel, height, cols),
        grid=(blocks // unroll,),
        in_specs=[matrix_spec, pl.BlockSpec((depth, cells), lambda i: (0, 0)), weight_spec],
        out_specs=sums_spec,
        out_shape=jax.ShapeDtypeStruct((blocks * width, cells), jnp.float32),
        scratch_shapes=[pltpu.VMEM((unroll * fields * width, cells), jnp.float32)],
        cost_estimate=pl.CostEstimate(
            flops=2 * matrix.size * cells, bytes_accessed=2 * matrix.size, transcendentals=0
        ),
        compiler_params=params,
    )(matrix, state, weights)
    border_spec = pl.BlockSpec((depth, cols), lambda i: (0, 0))
    sent = cells + (low_tiles(height, cols) * cols if first else 0)
    return pl.pallas_call(
        functools.partial(border_kernel, height, cols, first, scale),
        grid=(blocks // unroll,),
        in_specs=[
            matrix_spec,
            border_spec,
            border_spec,
            weight_spec,
            sums_spec,
            pl.BlockSpec(right.shape, lambda i: (0, 0)),
        ],
        out_specs=pl.BlockSpec((unroll * width, sent), lambda i: (i, 0)),
        out_shape=jax.ShapeDtypeStruct((blocks * width, sent), jnp.bfloat16),
        compiler_params=params,
    )(matrix, above, below, weights, inner, right)


TOGETHER = 16
MEAN_TOGETHER = 8
GROUP = 16


def solve(spectral, right_ref, left_ref, scale_ref):
    ny = spectral[0].shape[1]
    wide = along_rows(jnp.concatenate(spectral, axis=1), left_ref)
    wide = wide * jnp.concatenate([scale_ref[...]] * len(spectral), axis=1)
    wide = along_rows(wide, left_ref)
    return along_cols([wide[:, i * ny : (i + 1) * ny] for i in range(len(spectral))], right_ref)


def mean_fields(current_ref, right_side_ref, weight_ref, start):
    nx, ny = weight_ref.shape[1:]
    values = []
    for mode in range(start, start + MEAN_TOGETHER):
        here = current_ref[:, mode].reshape(nx, ny)
        mean = (
            weight_ref[0] * here
            - weight_ref[1] * pltpu.roll(here, 1, 0)
            - weight_ref[2] * pltpu.roll(here, nx - 1, 0)
            - pltpu.roll(weight_ref[4] * here, 1, 1)
            - pltpu.roll(weight_ref[3] * here, ny - 1, 1)
        )
        values.append(right_side_ref[:, mode].reshape(nx, ny) - mean)
    return values


def first_mean_kernel(slabs, place_ref, *refs):
    current_parts = refs[:slabs]
    right_side_parts = refs[slabs : 2 * slabs]
    weight_ref, right_ref, current_ref, right_side_ref, out_ref = refs[2 * slabs :]
    for shift in range(slabs):
        slab = in_order(place_ref[0], shift, slabs)
        current_ref[slab] = current_parts[shift][0]
        right_side_ref[slab] = right_side_parts[shift][0]
    shape = (slabs,) + out_ref.shape[2:]
    for start in range(0, out_ref.shape[1], MEAN_TOGETHER):
        values = mean_fields(current_ref, right_side_ref, weight_ref, start)
        for i, value in enumerate(along_cols(values, right_ref)):
            out_ref[:, start + i] = value.reshape(shape)


def mean_kernel(current_ref, right_side_ref, weight_ref, out_ref):
    shape = out_ref.shape[:1] + out_ref.shape[2:]
    for start in range(0, out_ref.shape[1], MEAN_TOGETHER):
        values = mean_fields(current_ref, right_side_ref, weight_ref, start)
        for i, value in enumerate(values):
            out_ref[:, start + i] = value.reshape(shape)


def turn_in(turned_ref, coupled_ref, mode_count, slab_count, height, first, scale):
    group = coupled_ref.shape[1]
    ny = turned_ref.shape[1]
    low_col = lax.broadcasted_iota(jnp.int32, (group, ny), 1) < LOW
    for source in range(mode_count * slab_count):
        start = ((source % slab_count) * mode_count + source // slab_count) * height
        for r in range(height):
            code = coupled_ref[source, :, r * ny : (r + 1) * ny]
            value = decode(code, FIRST_POWER if first else SUM_POWER)
            if first:
                at = (height + r // (ny // LOW)) * ny
                rest = coupled_ref[source, :, at : at + ny].astype(jnp.float32)
                place = r % (ny // LOW)
                rest = pltpu.roll(rest, ny - place * LOW, 1) if place else rest
                value = value + jnp.where(low_col, rest, 0.0)
            turned_ref[(start + r) * group : (start + r + 1) * group, :] = value * (1.0 / scale)


def step_kernel(
    mode_count,
    slab_count,
    code_scale,
    current_ref,
    base_ref,
    coupled_ref,
    right_ref,
    left_ref,
    scale_ref,
    solution_ref,
    state_ref,
    turned_ref,
):
    nx, ny = scale_ref.shape
    group = coupled_ref.shape[1]
    height = nx // (mode_count * slab_count)
    turn_in(turned_ref, coupled_ref, mode_count, slab_count, height, True, code_scale)

    def several(number, carry):
        start = number * TOGETHER
        resid = []
        for i in range(TOGETHER):
            coupled = turned_ref[pl.ds(start + i, nx, stride=group), :]
            resid.append(base_ref[:, start + i].reshape(nx, ny) - coupled)
        change = solve(resid, right_ref, left_ref, scale_ref)
        for i in range(TOGETHER):
            value = current_ref[:, start + i].reshape(nx, ny) + change[i]
            solution_ref[:, start + i] = value.reshape(slab_count, nx // slab_count, ny)
            turned_ref[pl.ds(start + i, nx, stride=group), :] = value
        return carry

    lax.fori_loop(0, group // TOGETHER, several, 0)

    for target in range(mode_count * slab_count):
        start = ((target % slab_count) * mode_count + target // slab_count) * height
        for r in range(height):
            row = start + r
            value = turned_ref[row * group : (row + 1) * group, :].astype(jnp.bfloat16)
            state_ref[target, :, r * ny : (r + 1) * ny] = value


def residual_kernel(
    mode_count, slab_count, code_scale, here_ref, base_ref, coupled_ref, out_ref, *refs
):
    *code_refs, turned_ref = refs
    group = coupled_ref.shape[1]
    ny = base_ref.shape[-1]
    nx = turned_ref.shape[0] // group
    height = nx // (mode_count * slab_count)
    turn_in(turned_ref, coupled_ref, mode_count, slab_count, height, False, code_scale)

    def one(mode, carry):
        coupled = turned_ref[pl.ds(mode, nx, stride=group), :]
        out_ref[:, mode] = base_ref[:, mode] - coupled.reshape(slab_count, nx // slab_count, ny)
        return carry

    lax.fori_loop(0, group, one, 0)
    for shift, code_ref in enumerate(code_refs):
        slab = lax.rem(here_ref[0] + shift, slab_count)
        code_ref[0] = encode(out_ref[slab] * code_scale, SUM_POWER)


def correct_kernel(code_scale, current_ref, resid_ref, right_ref, left_ref, scale_ref, out_ref):
    nx, ny = scale_ref.shape

    def several(number, carry):
        start = number * TOGETHER
        resid = [resid_ref[:, start + i].reshape(nx, ny) for i in range(TOGETHER)]
        change = solve(along_cols(resid, right_ref), right_ref, left_ref, scale_ref)
        for i in range(TOGETHER):
            shape = out_ref.shape[:1] + out_ref.shape[2:]
            value = current_ref[:, start + i] + change[i].reshape(shape)
            out_ref[:, start + i] = encode(value * code_scale, SOLUTION_POWER)
        return carry

    lax.fori_loop(0, out_ref.shape[1] // TOGETHER, several, 0)


def whole(array):
    return pl.BlockSpec(array.shape, lambda g: (0,) * array.ndim)


def slabs_of(array):
    slab_count, _, rows, ny = array.shape
    return pl.BlockSpec((slab_count, GROUP, rows, ny), lambda g: (0, g, 0, 0))


def strips_of(shape):
    return pl.BlockSpec((shape[0], GROUP, shape[2]), lambda g: (0, g, 0))


def per_group(
    kernel, groups, operands, in_specs, out_shape, out_specs, scratch=(), flops=0, vmem=SHARED_VMEM_BYTES
):
    moved = sum(a.size * a.dtype.itemsize for a in operands)
    return pl.pallas_call(
        kernel,
        grid=(groups,),
        in_specs=in_specs,
        out_specs=out_specs,
        out_shape=out_shape,
        scratch_shapes=scratch,
        cost_estimate=pl.CostEstimate(flops=flops, bytes_accessed=2 * moved, transcendentals=0),
        compiler_params=pltpu.CompilerParams(vmem_limit_bytes=vmem),
    )(*operands)


def first_mean_part(place, current_parts, right_side_parts, weights, right):
    slabs = len(right_side_parts)
    _, modes, rows, ny = right_side_parts[0].shape
    part = pl.BlockSpec((1, GROUP, rows, ny), lambda g, *_: (0, g, 0, 0))
    slab = pl.BlockSpec((slabs, GROUP, rows, ny), lambda g, *_: (0, g, 0, 0))
    shape = jax.ShapeDtypeStruct((slabs, modes, rows, ny), jnp.float32)
    return pl.pallas_call(
        functools.partial(first_mean_kernel, slabs),
        grid_spec=pltpu.PrefetchScalarGridSpec(
            num_scalar_prefetch=1,
            grid=(modes // GROUP,),
            in_specs=[part] * (2 * slabs)
            + [
                pl.BlockSpec(weights.shape, lambda g, *_: (0, 0, 0)),
                pl.BlockSpec(right.shape, lambda g, *_: (0, 0)),
            ],
            out_specs=[slab] * 3,
        ),
        out_shape=[shape] * 3,
        compiler_params=pltpu.CompilerParams(vmem_limit_bytes=SHARED_VMEM_BYTES),
    )(place, *current_parts, *right_side_parts, weights, right)


def mean_part(current, right_side, weights):
    slabs = slabs_of(right_side)
    return per_group(
        mean_kernel,
        right_side.shape[1] // GROUP,
        (current, right_side, weights),
        [slabs, slabs, whole(weights)],
        jax.ShapeDtypeStruct(right_side.shape, jnp.float32),
        slabs,
    )


def solve_flops(array, tables):
    nx, ny = tables[2].shape
    return array.shape[1] * 8 * 3 * nx * ny * (nx + ny) // 2


def step(current, base, coupled, tables, mode_count, slab_count, code_scale):
    nx, ny = tables[2].shape
    slabs = slabs_of(base)
    devices, modes, _ = coupled.shape
    state = (devices, modes, nx // devices * ny)
    return per_group(
        functools.partial(step_kernel, mode_count, slab_count, code_scale),
        modes // GROUP,
        (current, base, coupled, *tables),
        [slabs, slabs, strips_of(coupled.shape), *map(whole, tables)],
        [
            jax.ShapeDtypeStruct(base.shape, jnp.float32),
            jax.ShapeDtypeStruct(state, jnp.bfloat16),
        ],
        [slabs, strips_of(state)],
        [pltpu.VMEM((nx * GROUP, ny), jnp.float32)],
        solve_flops(base, tables),
    )


def last_residual(base, coupled, mode_count, slab_count, code_scale):
    slab, modes, rows, ny = base.shape
    slabs = pl.BlockSpec((slab, GROUP, rows, ny), lambda g, *_: (0, g, 0, 0))
    part = pl.BlockSpec((1, GROUP, rows, ny), lambda g, *_: (0, g, 0, 0))
    devices, _, cells = coupled.shape
    out, *parts = pl.pallas_call(
        functools.partial(residual_kernel, mode_count, slab_count, code_scale),
        grid_spec=pltpu.PrefetchScalarGridSpec(
            num_scalar_prefetch=1,
            grid=(modes // GROUP,),
            in_specs=[slabs, pl.BlockSpec((devices, GROUP, cells), lambda g, *_: (0, g, 0))],
            out_specs=[slabs] + [part] * slab,
            scratch_shapes=[pltpu.VMEM((slab * rows * GROUP, ny), jnp.float32)],
        ),
        out_shape=[jax.ShapeDtypeStruct(base.shape, jnp.float32)]
        + [jax.ShapeDtypeStruct((1, modes, rows, ny), jnp.bfloat16)] * slab,
        cost_estimate=pl.CostEstimate(
            flops=0, bytes_accessed=2 * base.size * 4, transcendentals=0
        ),
        compiler_params=pltpu.CompilerParams(vmem_limit_bytes=SHARED_VMEM_BYTES),
    )(lax.axis_index("slab").reshape(1), base, coupled)
    return out, parts


def correct(current, resid, tables, code_scale):
    slabs = slabs_of(resid)
    return per_group(
        functools.partial(correct_kernel, code_scale),
        resid.shape[1] // GROUP,
        (current, resid, *tables),
        [slabs, slabs, *map(whole, tables)],
        jax.ShapeDtypeStruct(resid.shape, jnp.bfloat16),
        slabs,
        (),
        solve_flops(resid, tables),
    )


def collect(parts, axis):
    count = lax.axis_size(axis)
    here = lax.axis_index(axis)
    out = jnp.zeros((count,) + parts[0].shape[1:], parts[0].dtype)
    for shift, part in enumerate(parts):
        source = lax.rem(here + count - shift, count)
        out = lax.dynamic_update_slice_in_dim(out, part, source, 0)
    return out


def onwards(part, axis, shift):
    count = lax.axis_size(axis)
    return lax.ppermute(part, axis, [(i, (i + shift) % count) for i in range(count)])


def parts_of(block, axis):
    count = lax.axis_size(axis)
    here = lax.axis_index(axis)
    return [
        lax.dynamic_index_in_dim(block, lax.rem(here + shift, count), 0) for shift in range(count)
    ]


def moved_parts(parts, axis):
    return [parts[0]] + [onwards(parts[i], axis, i) for i in range(1, len(parts))]


def local(guess, right_side, mean_coef, field_coef, coupling, coupling_list, pair_count):
    mode_count = lax.axis_size("mode")
    slab_count = lax.axis_size("slab")
    both = ("mode", "slab")
    modes, rows, cols = guess.shape
    fields = field_coef.shape[0]
    nx = rows * slab_count
    devices = mode_count * slab_count
    height = nx // devices
    share = modes // slab_count

    strips = pack_strips(guess, mode_count)
    coefs = jnp.concatenate([mean_coef[None], field_coef], 0)[None]
    state = lax.all_to_all(strips, "mode", 0, 0, tiled=True)
    state = state.reshape(mode_count * modes, height * cols)

    def to_slabs(block):
        flat = block.reshape(modes, rows, cols)
        return lax.all_to_all(flat, "slab", 0, 0, tiled=True)

    guess_parts = parts_of(guess.reshape(slab_count, share, rows, cols), "slab")
    guess_parts = [jnp.concatenate([part, coefs], axis=1) for part in guess_parts]
    guess_parts = moved_parts(guess_parts, "slab")
    right_parts = parts_of(right_side.reshape(slab_count, share, rows, cols), "slab")
    state, guess_parts, right_parts = lax.optimization_barrier((state, guess_parts, right_parts))
    right_parts = moved_parts(right_parts, "slab")

    slab = lax.axis_index("slab")
    place = jnp.stack([slab, slab * mode_count + lax.axis_index("mode")])
    strip_weights = strip_weights_of(guess_parts, place, fields + 1, height)
    mean_weights = mean_weights_of(guess_parts, place, fields + 1)
    matrix = dense_coupling(coupling, coupling_list, pair_count, fields)

    row_high, row_low = split_table(sine_table(nx))
    col_high, col_low = split_table(sine_table(cols))
    tables = (
        jnp.concatenate(
            [
                jnp.concatenate([col_high, col_low], 1),
                jnp.concatenate([col_high, jnp.zeros_like(col_low)], 1),
            ],
            0,
        ),
        jnp.concatenate(
            [
                jnp.concatenate([row_high, row_high], 1),
                jnp.concatenate([row_low, jnp.zeros_like(row_low)], 1),
            ],
            0,
        ),
        RELAXATION / eigen_table(nx, cols),
    )

    first_scale, sum_scale, solution_scale = code_scales(nx, cols, coupling.shape[1], modes)

    sums = coupled_sums(matrix, state, strip_weights, tables[0], True, first_scale, both)
    sums, right_parts = lax.optimization_barrier((sums, right_parts))
    sums = lax.all_to_all(sums, both, 0, 0, tiled=True).reshape(devices, share, -1)
    current, right_side, base = first_mean_part(
        place, guess_parts, right_parts, mean_weights, tables[0]
    )
    current, state = step(current, base, sums, tables, mode_count, slab_count, first_scale)
    state = state.reshape(devices * share, height * cols)
    state = lax.all_to_all(state, both, 0, 0, tiled=True)

    base = mean_part(current, right_side, mean_weights)
    sums = coupled_sums(matrix, state, strip_weights, tables[0], False, sum_scale, both)
    sums = lax.all_to_all(sums, both, 0, 0, tiled=True).reshape(devices, share, -1)
    resid, parts = last_residual(base, sums, mode_count, slab_count, sum_scale)
    moved = collect(moved_parts(parts, "slab"), "slab").reshape(modes, rows, cols)
    resid_out = decode(moved, SUM_POWER) * (1.0 / sum_scale)
    code = correct(current, resid, tables, solution_scale)
    return decode(to_slabs(code), SOLUTION_POWER) * (1.0 / solution_scale), resid_out


def solution(mesh):
    placed = (
        P("mode", "slab", None),
        P("mode", "slab", None),
        P("slab", None),
        P(None, "slab", None),
        P(),
        P(),
        P(),
    )
    return jax.shard_map(
        local,
        mesh=mesh,
        in_specs=placed,
        out_specs=(P("mode", "slab", None), P("mode", "slab", None)),
        check_vma=False,
    )
```

```python
import functools
import math

import jax
import jax.numpy as jnp
from jax import lax
from jax.experimental import pallas as pl
from jax.experimental.pallas import tpu as pltpu
from jax.sharding import PartitionSpec as P

RELAXATION = 0.6
VMEM_BYTES = 60 << 20
SHARED_VMEM_BYTES = 48 << 20
STEP_VMEM_BYTES = 40 << 20
SMALL_VMEM_BYTES = 9 << 20
UNROLL = 4


def sine_table(length):
    counter = jnp.arange(length).astype(jnp.float32) + 1.0
    angle = math.pi * counter[:, None] * counter[None, :] / (length + 1)
    return math.sqrt(2.0 / (length + 1)) * jnp.sin(angle)


def eigen_table(first, second):
    along_first = 2.0 * jnp.cos(
        math.pi * (jnp.arange(first).astype(jnp.float32) + 1.0) / (first + 1)
    )
    along_second = 2.0 * jnp.cos(
        math.pi * (jnp.arange(second).astype(jnp.float32) + 1.0) / (second + 1)
    )
    return 4.0 - along_first[:, None] - along_second[None, :]


def stencil_weights(coef):
    nx, ny = coef.shape
    row = lax.broadcasted_iota(jnp.int32, (nx, ny), 0)
    col = lax.broadcasted_iota(jnp.int32, (nx, ny), 1)
    sides = (
        (pltpu.roll(coef, 1, 0), row == 0),
        (pltpu.roll(coef, nx - 1, 0), row == nx - 1),
        (pltpu.roll(coef, 1, 1), col == 0),
        (pltpu.roll(coef, ny - 1, 1), col == ny - 1),
    )
    centre = 0.0
    weights = []
    for other, outside in sides:
        weight = 0.5 * (coef + jnp.where(outside, coef, other))
        centre = centre + weight
        weights.append(jnp.where(outside, 0.0, weight))
    return [centre] + weights


def in_order(here, shift, count):
    return lax.rem(here + count - shift, count)


def in_order(here, shift, count):
    return lax.rem(here + count - shift, count)


def strip_weights_kernel(slabs, height, place_ref, *refs):
    part_refs = refs[:slabs]
    out_ref, coef_ref = refs[slabs:]
    _, nx, ny = coef_ref.shape
    rows = nx // slabs
    fields = out_ref.shape[0] // (5 * height)
    for shift, part_ref in enumerate(part_refs):
        start = in_order(place_ref[0], shift, slabs) * rows
        coef_ref[:, pl.ds(pl.multiple_of(start, rows), rows), :] = part_ref[0]
    col = lax.broadcasted_iota(jnp.int32, (1, ny), 1)
    first = place_ref[1] * height
    for f in range(fields):
        lines = []
        for r in range(-1, height + 1):
            at = jnp.clip(first + r, 0, nx - 1)
            lines.append(coef_ref[f + 1, pl.ds(at, 1), :])
        for r in range(height):
            here = lines[r + 1]
            up = 0.5 * (here + lines[r])
            down = 0.5 * (here + lines[r + 2])
            left = 0.5 * (here + jnp.where(col == 0, here, pltpu.roll(here, 1, 1)))
            right = 0.5 * (here + jnp.where(col == ny - 1, here, pltpu.roll(here, ny - 1, 1)))
            weights = (
                up + down + left + right,
                jnp.where(first + r == 0, 0.0, up),
                jnp.where(first + r == nx - 1, 0.0, down),
                jnp.where(col == 0, 0.0, left),
                jnp.where(col == ny - 1, 0.0, right),
            )
            for which, weight in enumerate(weights):
                at = (f * 5 + which) * height + r
                out_ref[at : at + 1, :] = weight


def mean_weights_kernel(slabs, place_ref, *refs):
    part_refs = refs[:slabs]
    out_ref, coef_ref = refs[slabs:]
    _, nx, ny = out_ref.shape
    for shift, part_ref in enumerate(part_refs):
        coef_ref[in_order(place_ref[0], shift, slabs)] = part_ref[0, 0]
    for which, weight in enumerate(stencil_weights(coef_ref[...].reshape(nx, ny))):
        out_ref[which] = weight


def weights_of(kernel, parts, place, coefs, out, scratch):
    _, entries, rows, ny = parts[0].shape
    last = entries // coefs - 1
    return pl.pallas_call(
        kernel,
        grid_spec=pltpu.PrefetchScalarGridSpec(
            num_scalar_prefetch=1,
            grid=(1,),
            in_specs=[pl.BlockSpec((1, coefs, rows, ny), lambda i, *_: (0, last, 0, 0))]
            * len(parts),
            out_specs=pl.BlockSpec(out, lambda i, *_: (0,) * len(out)),
            scratch_shapes=[pltpu.VMEM(scratch, jnp.float32)],
        ),
        out_shape=jax.ShapeDtypeStruct(out, jnp.float32),
        compiler_params=pltpu.CompilerParams(vmem_limit_bytes=SMALL_VMEM_BYTES),
    )(place, *parts)


def strip_weights_of(parts, place, coefs, height):
    slabs = len(parts)
    _, _, rows, ny = parts[0].shape
    kernel = functools.partial(strip_weights_kernel, slabs, height)
    out = ((coefs - 1) * 5 * height, ny)
    return weights_of(kernel, parts, place, coefs, out, (coefs, slabs * rows, ny))


def mean_weights_of(parts, place, coefs):
    slabs = len(parts)
    _, _, rows, ny = parts[0].shape
    kernel = functools.partial(mean_weights_kernel, slabs)
    return weights_of(kernel, parts, place, coefs, (5, slabs * rows, ny), (slabs, rows, ny))


def split(value):
    high = value.astype(jnp.bfloat16)
    low = (value - high.astype(jnp.float32)).astype(jnp.bfloat16)
    return high, low


def split_table(value):
    high = lax.reduce_precision(value, 8, 7)
    return high.astype(jnp.bfloat16), (value - high).astype(jnp.bfloat16)


LOW = 32
FIRST_POWER = 7
SUM_POWER = 5
SOLUTION_POWER = 4


def encode(value, power):
    square = value * value
    if power == 4:
        result = square * (value * jnp.abs(value))
    elif power == 5:
        result = square * square * value
    else:
        result = (square * square) * (square * value)
    return result.astype(jnp.bfloat16)


def decode(code, power):
    code = code.astype(jnp.float32)
    size = jnp.abs(code)
    if power == 4:
        value = jnp.sqrt(jnp.sqrt(size))
    else:
        value = jnp.exp(jnp.log(size) * (1.0 / power))
        value = jnp.where(size > 0.0, value, 0.0)
    return jnp.where(code < 0.0, -value, value)


def code_scales(nx, ny, entries, width):
    guess_max, mean_max, field_max, coupling_max = 6.0, 2.0, 2.5, 0.0625
    gain = 8.0 * field_max * entries * width * coupling_max * 1.01
    inverse = (min(nx, ny) + 1) ** 2 / 8.0

    def bound(iterate):
        return guess_max + (8.0 * mean_max + gain) * iterate

    change = RELAXATION * inverse * 1.01
    second = guess_max + change * bound(guess_max)
    third = second + change * bound(second)

    def scale(limit, power):
        return 0.8 * 2.0 ** (127.0 / power) / limit

    first = math.sqrt(2.0 * ny) * gain * guess_max
    return (
        min(1.0, scale(first, FIRST_POWER)),
        min(1.0, scale(bound(second), SUM_POWER)),
        min(1.0, scale(third, SOLUTION_POWER)),
    )


def pack_kernel(rows, height, x_ref, out_ref):
    strips, modes, cells = out_ref.shape
    cols = cells // height
    for strip in range(strips):
        for r in range(height):
            value = x_ref[pl.ds(strip * height + r, modes, stride=rows), :]
            out_ref[strip, :, r * cols : (r + 1) * cols] = value.astype(jnp.bfloat16)


def pack_strips(block, strips):
    modes, rows, cols = block.shape
    height = rows // strips
    return pl.pallas_call(
        functools.partial(pack_kernel, rows, height),
        grid=(2,),
        in_specs=[pl.BlockSpec((modes // 2 * rows, cols), lambda g: (g, 0))],
        out_specs=pl.BlockSpec((strips, modes // 2, height * cols), lambda g: (0, g, 0)),
        out_shape=jax.ShapeDtypeStruct((strips, modes, height * cols), jnp.bfloat16),
        compiler_params=pltpu.CompilerParams(vmem_limit_bytes=VMEM_BYTES),
    )(block.reshape(modes * rows, cols))


def dense_kernel(fields, entry_ref, count_ref, coupling_ref, out_ref):
    block = pl.program_id(0)
    width = coupling_ref.shape[-1]
    out_ref[...] = jnp.zeros_like(out_ref)

    def place(k, carry):
        entry = entry_ref[block, k]
        column = pl.multiple_of((entry // fields) * width, width)
        out_ref[0, entry % fields, :, pl.ds(column, width)] = coupling_ref[0, k]
        return carry

    lax.fori_loop(0, count_ref[block], place, 0)


def dense_coupling(coupling, coupling_list, pair_count, fields):
    blocks, entries, width, _ = coupling.shape
    moved = 2 * width * width * (entries + fields * blocks) * coupling.dtype.itemsize
    return pl.pallas_call(
        functools.partial(dense_kernel, fields),
        grid_spec=pltpu.PrefetchScalarGridSpec(
            num_scalar_prefetch=2,
            grid=(blocks,),
            in_specs=[pl.BlockSpec((1, entries, width, width), lambda i, *_: (i, 0, 0, 0))],
            out_specs=pl.BlockSpec(
                (1, fields, width, blocks * width), lambda i, *_: (i, 0, 0, 0)
            ),
        ),
        out_shape=jax.ShapeDtypeStruct((blocks, fields, width, blocks * width), coupling.dtype),
        compiler_params=pltpu.CompilerParams(vmem_limit_bytes=SMALL_VMEM_BYTES + moved),
    )(coupling_list, pair_count, coupling)


def low_tiles(height, cols):
    return -(-height * LOW // cols)


def along_cols(fields, right_ref):
    size, ny = fields[0].shape
    high, low = split(jnp.concatenate(fields, axis=0))
    both = jnp.dot(
        jnp.concatenate([high, low], axis=1), right_ref[...], preferred_element_type=jnp.float32
    )
    both = both[:, :ny] + both[:, ny:]
    return [both[i * size : (i + 1) * size] for i in range(len(fields))]


def along_rows(wide, left_ref):
    nx = wide.shape[0]
    high, low = split(wide)
    both = jnp.dot(
        left_ref[...], jnp.concatenate([high, low], axis=0), preferred_element_type=jnp.float32
    )
    return both[:nx] + both[nx:]


def weight_row(weight_ref, height, field, which, r):
    at = (field * 5 + which) * height + r
    return weight_ref[at : at + 1, :]


def inner_kernel(height, cols, matrix_ref, state_ref, weight_ref, out_ref, sums_ref):
    blocks, fields, width, depth = matrix_ref.shape
    sums_ref[...] = jnp.dot(
        matrix_ref[...].reshape(blocks * fields * width, depth),
        state_ref[...],
        preferred_element_type=jnp.float32,
    )
    for block in range(blocks):
        for r in range(height):
            total = 0.0
            from_left = 0.0
            from_right = 0.0
            for f in range(fields):

                def row(at):
                    start = (block * fields + f) * width
                    return sums_ref[start : start + width, at * cols : (at + 1) * cols]

                weight = functools.partial(weight_row, weight_ref, height, f)
                here = row(r)
                total = total + weight(0, r) * here
                if r > 0:
                    total = total - weight(1, r) * row(r - 1)
                if r < height - 1:
                    total = total - weight(2, r) * row(r + 1)
                from_left = from_left + weight(4, r) * here
                from_right = from_right + weight(3, r) * here
            total = total - pltpu.roll(from_left, 1, 1) - pltpu.roll(from_right, cols - 1, 1)
            out_ref[block * width : (block + 1) * width, r * cols : (r + 1) * cols] = total


def border_kernel(
    height,
    cols,
    first,
    scale,
    matrix_ref,
    above_ref,
    below_ref,
    weight_ref,
    inner_ref,
    right_ref,
    out_ref,
):
    blocks, fields, width, depth = matrix_ref.shape
    border = jnp.concatenate([above_ref[...], below_ref[...]], axis=1)
    low_col = lax.broadcasted_iota(jnp.int32, (width, cols), 1) < LOW
    matrix = matrix_ref[...].reshape(blocks * fields * width, depth)
    sums = jnp.dot(matrix, border, preferred_element_type=jnp.float32)
    for block in range(blocks):
        modes = slice(block * width, (block + 1) * width)
        rows = []
        for r in range(height):
            total = inner_ref[modes, r * cols : (r + 1) * cols]
            for f in range(fields):
                part = sums[(block * fields + f) * width : (block * fields + f + 1) * width]
                if r == 0:
                    total = total - weight_row(weight_ref, height, f, 1, r) * part[:, :cols]
                if r == height - 1:
                    total = total - weight_row(weight_ref, height, f, 2, r) * part[:, cols:]
            rows.append(total)
        if not first:
            for r in range(height):
                code = encode(rows[r] * scale, SUM_POWER)
                out_ref[modes, r * cols : (r + 1) * cols] = code
            continue
        rows = along_cols(rows, right_ref)
        for r in range(height):
            value = rows[r] * scale
            code = encode(value, FIRST_POWER)
            out_ref[modes, r * cols : (r + 1) * cols] = code
            rest = jnp.where(low_col, value - decode(code, FIRST_POWER), 0.0)
            place = r % (cols // LOW)
            rest = pltpu.roll(rest, place * LOW, 1) if place else rest
            packed = rest if place == 0 else packed + rest
            if place == cols // LOW - 1 or r == height - 1:
                at = (height + r // (cols // LOW)) * cols
                out_ref[modes, at : at + cols] = packed.astype(jnp.bfloat16)


def coupled_sums(matrix, state, weights, right, first, scale, both):
    blocks, fields, width, depth = matrix.shape
    cells = state.shape[1]
    height = weights.shape[0] // (5 * fields)
    cols = cells // height
    mode_count = lax.axis_size("mode")
    slab_count = lax.axis_size("slab")
    place = [
        (t % mode_count) * slab_count + t // mode_count for t in range(mode_count * slab_count)
    ]
    onward = list(zip(place, place[1:] + place[:1]))
    above = lax.ppermute(state[:, -cols:], both, onward)
    below = lax.ppermute(state[:, :cols], both, [(b, a) for a, b in onward])
    unroll = math.gcd(blocks, UNROLL)
    matrix_spec = pl.BlockSpec((unroll, fields, width, depth), lambda i: (i, 0, 0, 0))
    weight_spec = pl.BlockSpec(weights.shape, lambda i: (0, 0))
    sums_spec = pl.BlockSpec((unroll * width, cells), lambda i: (i, 0))
    moved = 2 * unroll * fields * width * depth * matrix.dtype.itemsize
    params = pltpu.CompilerParams(vmem_limit_bytes=2 * SMALL_VMEM_BYTES + moved)
    inner = pl.pallas_call(
        functools.partial(inner_kernel, height, cols),
        grid=(blocks // unroll,),
        in_specs=[matrix_spec, pl.BlockSpec((depth, cells), lambda i: (0, 0)), weight_spec],
        out_specs=sums_spec,
        out_shape=jax.ShapeDtypeStruct((blocks * width, cells), jnp.float32),
        scratch_shapes=[pltpu.VMEM((unroll * fields * width, cells), jnp.float32)],
        cost_estimate=pl.CostEstimate(
            flops=2 * matrix.size * cells, bytes_accessed=2 * matrix.size, transcendentals=0
        ),
        compiler_params=params,
    )(matrix, state, weights)
    border_spec = pl.BlockSpec((depth, cols), lambda i: (0, 0))
    sent = cells + (low_tiles(height, cols) * cols if first else 0)
    return pl.pallas_call(
        functools.partial(border_kernel, height, cols, first, scale),
        grid=(blocks // unroll,),
        in_specs=[
            matrix_spec,
            border_spec,
            border_spec,
            weight_spec,
            sums_spec,
            pl.BlockSpec(right.shape, lambda i: (0, 0)),
        ],
        out_specs=pl.BlockSpec((unroll * width, sent), lambda i: (i, 0)),
        out_shape=jax.ShapeDtypeStruct((blocks * width, sent), jnp.bfloat16),
        compiler_params=params,
    )(matrix, above, below, weights, inner, right)


TOGETHER = 16
MEAN_TOGETHER = 8
GROUP = 16


def solve(spectral, right_ref, left_ref, scale_ref):
    ny = spectral[0].shape[1]
    wide = along_rows(jnp.concatenate(spectral, axis=1), left_ref)
    wide = wide * jnp.concatenate([scale_ref[...]] * len(spectral), axis=1)
    wide = along_rows(wide, left_ref)
    return along_cols([wide[:, i * ny : (i + 1) * ny] for i in range(len(spectral))], right_ref)


def mean_fields(current_ref, right_side_ref, weight_ref, start):
    nx, ny = weight_ref.shape[1:]
    values = []
    for mode in range(start, start + MEAN_TOGETHER):
        here = current_ref[:, mode].reshape(nx, ny)
        mean = (
            weight_ref[0] * here
            - weight_ref[1] * pltpu.roll(here, 1, 0)
            - weight_ref[2] * pltpu.roll(here, nx - 1, 0)
            - pltpu.roll(weight_ref[4] * here, 1, 1)
            - pltpu.roll(weight_ref[3] * here, ny - 1, 1)
        )
        values.append(right_side_ref[:, mode].reshape(nx, ny) - mean)
    return values


def first_mean_kernel(slabs, place_ref, *refs):
    current_parts = refs[:slabs]
    right_side_parts = refs[slabs : 2 * slabs]
    weight_ref, right_ref, current_ref, right_side_ref, out_ref = refs[2 * slabs :]
    for shift in range(slabs):
        slab = in_order(place_ref[0], shift, slabs)
        current_ref[slab] = current_parts[shift][0]
        right_side_ref[slab] = right_side_parts[shift][0]
    shape = (slabs,) + out_ref.shape[2:]
    for start in range(0, out_ref.shape[1], MEAN_TOGETHER):
        values = mean_fields(current_ref, right_side_ref, weight_ref, start)
        for i, value in enumerate(along_cols(values, right_ref)):
            out_ref[:, start + i] = value.reshape(shape)


def mean_kernel(current_ref, right_side_ref, weight_ref, out_ref):
    shape = out_ref.shape[:1] + out_ref.shape[2:]
    for start in range(0, out_ref.shape[1], MEAN_TOGETHER):
        values = mean_fields(current_ref, right_side_ref, weight_ref, start)
        for i, value in enumerate(values):
            out_ref[:, start + i] = value.reshape(shape)


def turn_in(turned_ref, coupled_ref, mode_count, slab_count, height, first, scale):
    group = coupled_ref.shape[1]
    ny = turned_ref.shape[1]
    low_col = lax.broadcasted_iota(jnp.int32, (group, ny), 1) < LOW
    for source in range(mode_count * slab_count):
        start = ((source % slab_count) * mode_count + source // slab_count) * height
        for r in range(height):
            code = coupled_ref[source, :, r * ny : (r + 1) * ny]
            value = decode(code, FIRST_POWER if first else SUM_POWER)
            if first:
                at = (height + r // (ny // LOW)) * ny
                rest = coupled_ref[source, :, at : at + ny].astype(jnp.float32)
                place = r % (ny // LOW)
                rest = pltpu.roll(rest, ny - place * LOW, 1) if place else rest
                value = value + jnp.where(low_col, rest, 0.0)
            turned_ref[(start + r) * group : (start + r + 1) * group, :] = value * (1.0 / scale)


def step_kernel(
    mode_count,
    slab_count,
    code_scale,
    current_ref,
    base_ref,
    coupled_ref,
    right_ref,
    left_ref,
    scale_ref,
    solution_ref,
    state_ref,
    turned_ref,
):
    nx, ny = scale_ref.shape
    group = coupled_ref.shape[1]
    height = nx // (mode_count * slab_count)
    turn_in(turned_ref, coupled_ref, mode_count, slab_count, height, True, code_scale)

    def several(number, carry):
        start = number * TOGETHER
        resid = []
        for i in range(TOGETHER):
            coupled = turned_ref[pl.ds(start + i, nx, stride=group), :]
            resid.append(base_ref[:, start + i].reshape(nx, ny) - coupled)
        change = solve(resid, right_ref, left_ref, scale_ref)
        for i in range(TOGETHER):
            value = current_ref[:, start + i].reshape(nx, ny) + change[i]
            solution_ref[:, start + i] = value.reshape(slab_count, nx // slab_count, ny)
            turned_ref[pl.ds(start + i, nx, stride=group), :] = value
        return carry

    lax.fori_loop(0, group // TOGETHER, several, 0)

    for target in range(mode_count * slab_count):
        start = ((target % slab_count) * mode_count + target // slab_count) * height
        for r in range(height):
            row = start + r
            value = turned_ref[row * group : (row + 1) * group, :].astype(jnp.bfloat16)
            state_ref[target, :, r * ny : (r + 1) * ny] = value


def residual_kernel(
    mode_count, slab_count, code_scale, here_ref, base_ref, coupled_ref, out_ref, *refs
):
    *code_refs, turned_ref = refs
    group = coupled_ref.shape[1]
    ny = base_ref.shape[-1]
    nx = turned_ref.shape[0] // group
    height = nx // (mode_count * slab_count)
    turn_in(turned_ref, coupled_ref, mode_count, slab_count, height, False, code_scale)

    def one(mode, carry):
        coupled = turned_ref[pl.ds(mode, nx, stride=group), :]
        out_ref[:, mode] = base_ref[:, mode] - coupled.reshape(slab_count, nx // slab_count, ny)
        return carry

    lax.fori_loop(0, group, one, 0)
    for shift, code_ref in enumerate(code_refs):
        slab = lax.rem(here_ref[0] + shift, slab_count)
        code_ref[0] = encode(out_ref[slab] * code_scale, SUM_POWER)


def correct_kernel(code_scale, current_ref, resid_ref, right_ref, left_ref, scale_ref, out_ref):
    nx, ny = scale_ref.shape

    def several(number, carry):
        start = number * TOGETHER
        resid = [resid_ref[:, start + i].reshape(nx, ny) for i in range(TOGETHER)]
        change = solve(along_cols(resid, right_ref), right_ref, left_ref, scale_ref)
        for i in range(TOGETHER):
            shape = out_ref.shape[:1] + out_ref.shape[2:]
            value = current_ref[:, start + i] + change[i].reshape(shape)
            out_ref[:, start + i] = encode(value * code_scale, SOLUTION_POWER)
        return carry

    lax.fori_loop(0, out_ref.shape[1] // TOGETHER, several, 0)


def whole(array):
    return pl.BlockSpec(array.shape, lambda g: (0,) * array.ndim)


def slabs_of(array):
    slab_count, _, rows, ny = array.shape
    return pl.BlockSpec((slab_count, GROUP, rows, ny), lambda g: (0, g, 0, 0))


def strips_of(shape):
    return pl.BlockSpec((shape[0], GROUP, shape[2]), lambda g: (0, g, 0))


def per_group(
    kernel, groups, operands, in_specs, out_shape, out_specs, scratch=(), flops=0, vmem=SHARED_VMEM_BYTES
):
    moved = sum(a.size * a.dtype.itemsize for a in operands)
    return pl.pallas_call(
        kernel,
        grid=(groups,),
        in_specs=in_specs,
        out_specs=out_specs,
        out_shape=out_shape,
        scratch_shapes=scratch,
        cost_estimate=pl.CostEstimate(flops=flops, bytes_accessed=2 * moved, transcendentals=0),
        compiler_params=pltpu.CompilerParams(vmem_limit_bytes=vmem),
    )(*operands)


def first_mean_part(place, current_parts, right_side_parts, weights, right):
    slabs = len(right_side_parts)
    _, modes, rows, ny = right_side_parts[0].shape
    part = pl.BlockSpec((1, GROUP, rows, ny), lambda g, *_: (0, g, 0, 0))
    slab = pl.BlockSpec((slabs, GROUP, rows, ny), lambda g, *_: (0, g, 0, 0))
    shape = jax.ShapeDtypeStruct((slabs, modes, rows, ny), jnp.float32)
    return pl.pallas_call(
        functools.partial(first_mean_kernel, slabs),
        grid_spec=pltpu.PrefetchScalarGridSpec(
            num_scalar_prefetch=1,
            grid=(modes // GROUP,),
            in_specs=[part] * (2 * slabs)
            + [
                pl.BlockSpec(weights.shape, lambda g, *_: (0, 0, 0)),
                pl.BlockSpec(right.shape, lambda g, *_: (0, 0)),
            ],
            out_specs=[slab] * 3,
        ),
        out_shape=[shape] * 3,
        compiler_params=pltpu.CompilerParams(vmem_limit_bytes=VMEM_BYTES),
    )(place, *current_parts, *right_side_parts, weights, right)


def mean_part(current, right_side, weights):
    slabs = slabs_of(right_side)
    return per_group(
        mean_kernel,
        right_side.shape[1] // GROUP,
        (current, right_side, weights),
        [slabs, slabs, whole(weights)],
        jax.ShapeDtypeStruct(right_side.shape, jnp.float32),
        slabs,
    )


def solve_flops(array, tables):
    nx, ny = tables[2].shape
    return array.shape[1] * 8 * 3 * nx * ny * (nx + ny) // 2


def step(current, base, coupled, tables, mode_count, slab_count, code_scale):
    nx, ny = tables[2].shape
    slabs = slabs_of(base)
    devices, modes, _ = coupled.shape
    state = (devices, modes, nx // devices * ny)
    return per_group(
        functools.partial(step_kernel, mode_count, slab_count, code_scale),
        modes // GROUP,
        (current, base, coupled, *tables),
        [slabs, slabs, strips_of(coupled.shape), *map(whole, tables)],
        [
            jax.ShapeDtypeStruct(base.shape, jnp.float32),
            jax.ShapeDtypeStruct(state, jnp.bfloat16),
        ],
        [slabs, strips_of(state)],
        [pltpu.VMEM((nx * GROUP, ny), jnp.float32)],
        solve_flops(base, tables),
        STEP_VMEM_BYTES,
    )


def last_residual(base, coupled, mode_count, slab_count, code_scale):
    slab, modes, rows, ny = base.shape
    slabs = pl.BlockSpec((slab, GROUP, rows, ny), lambda g, *_: (0, g, 0, 0))
    part = pl.BlockSpec((1, GROUP, rows, ny), lambda g, *_: (0, g, 0, 0))
    devices, _, cells = coupled.shape
    out, *parts = pl.pallas_call(
        functools.partial(residual_kernel, mode_count, slab_count, code_scale),
        grid_spec=pltpu.PrefetchScalarGridSpec(
            num_scalar_prefetch=1,
            grid=(modes // GROUP,),
            in_specs=[slabs, pl.BlockSpec((devices, GROUP, cells), lambda g, *_: (0, g, 0))],
            out_specs=[slabs] + [part] * slab,
            scratch_shapes=[pltpu.VMEM((slab * rows * GROUP, ny), jnp.float32)],
        ),
        out_shape=[jax.ShapeDtypeStruct(base.shape, jnp.float32)]
        + [jax.ShapeDtypeStruct((1, modes, rows, ny), jnp.bfloat16)] * slab,
        cost_estimate=pl.CostEstimate(
            flops=0, bytes_accessed=2 * base.size * 4, transcendentals=0
        ),
        compiler_params=pltpu.CompilerParams(vmem_limit_bytes=SHARED_VMEM_BYTES),
    )(lax.axis_index("slab").reshape(1), base, coupled)
    return out, parts


def correct(current, resid, tables, code_scale):
    slabs = slabs_of(resid)
    return per_group(
        functools.partial(correct_kernel, code_scale),
        resid.shape[1] // GROUP,
        (current, resid, *tables),
        [slabs, slabs, *map(whole, tables)],
        jax.ShapeDtypeStruct(resid.shape, jnp.bfloat16),
        slabs,
        (),
        solve_flops(resid, tables),
    )


def collect(parts, axis):
    count = lax.axis_size(axis)
    here = lax.axis_index(axis)
    out = jnp.zeros((count,) + parts[0].shape[1:], parts[0].dtype)
    for shift, part in enumerate(parts):
        source = lax.rem(here + count - shift, count)
        out = lax.dynamic_update_slice_in_dim(out, part, source, 0)
    return out


def onwards(part, axis, shift):
    count = lax.axis_size(axis)
    return lax.ppermute(part, axis, [(i, (i + shift) % count) for i in range(count)])


def parts_of(block, axis):
    count = lax.axis_size(axis)
    here = lax.axis_index(axis)
    return [
        lax.dynamic_index_in_dim(block, lax.rem(here + shift, count), 0) for shift in range(count)
    ]


def moved_parts(parts, axis):
    return [parts[0]] + [onwards(parts[i], axis, i) for i in range(1, len(parts))]


def local(guess, right_side, mean_coef, field_coef, coupling, coupling_list, pair_count):
    mode_count = lax.axis_size("mode")
    slab_count = lax.axis_size("slab")
    both = ("mode", "slab")
    modes, rows, cols = guess.shape
    fields = field_coef.shape[0]
    nx = rows * slab_count
    devices = mode_count * slab_count
    height = nx // devices
    share = modes // slab_count

    strips = pack_strips(guess, mode_count)
    coefs = jnp.concatenate([mean_coef[None], field_coef], 0)[None]
    state = lax.all_to_all(strips, "mode", 0, 0, tiled=True)
    state = state.reshape(mode_count * modes, height * cols)

    def to_slabs(block):
        flat = block.reshape(modes, rows, cols)
        return lax.all_to_all(flat, "slab", 0, 0, tiled=True)

    guess_parts = parts_of(guess.reshape(slab_count, share, rows, cols), "slab")
    guess_parts = [jnp.concatenate([part, coefs], axis=1) for part in guess_parts]
    guess_parts = moved_parts(guess_parts, "slab")
    right_parts = parts_of(right_side.reshape(slab_count, share, rows, cols), "slab")
    state, guess_parts, right_parts = lax.optimization_barrier((state, guess_parts, right_parts))
    right_parts = moved_parts(right_parts, "slab")

    slab = lax.axis_index("slab")
    place = jnp.stack([slab, slab * mode_count + lax.axis_index("mode")])
    strip_weights = strip_weights_of(guess_parts, place, fields + 1, height)
    mean_weights = mean_weights_of(guess_parts, place, fields + 1)
    matrix = dense_coupling(coupling, coupling_list, pair_count, fields)

    row_high, row_low = split_table(sine_table(nx))
    col_high, col_low = split_table(sine_table(cols))
    tables = (
        jnp.concatenate(
            [
                jnp.concatenate([col_high, col_low], 1),
                jnp.concatenate([col_high, jnp.zeros_like(col_low)], 1),
            ],
            0,
        ),
        jnp.concatenate(
            [
                jnp.concatenate([row_high, row_high], 1),
                jnp.concatenate([row_low, jnp.zeros_like(row_low)], 1),
            ],
            0,
        ),
        RELAXATION / eigen_table(nx, cols),
    )

    first_scale, sum_scale, solution_scale = code_scales(nx, cols, coupling.shape[1], modes)

    sums = coupled_sums(matrix, state, strip_weights, tables[0], True, first_scale, both)
    sums, right_parts = lax.optimization_barrier((sums, right_parts))
    sums = lax.all_to_all(sums, both, 0, 0, tiled=True).reshape(devices, share, -1)
    current, right_side, base = first_mean_part(
        place, guess_parts, right_parts, mean_weights, tables[0]
    )
    current, state = step(current, base, sums, tables, mode_count, slab_count, first_scale)
    state = state.reshape(devices * share, height * cols)
    state = lax.all_to_all(state, both, 0, 0, tiled=True)

    base = mean_part(current, right_side, mean_weights)
    sums = coupled_sums(matrix, state, strip_weights, tables[0], False, sum_scale, both)
    sums = lax.all_to_all(sums, both, 0, 0, tiled=True).reshape(devices, share, -1)
    resid, parts = last_residual(base, sums, mode_count, slab_count, sum_scale)
    moved = collect(moved_parts(parts, "slab"), "slab").reshape(modes, rows, cols)
    resid_out = decode(moved, SUM_POWER) * (1.0 / sum_scale)
    code = correct(current, resid, tables, solution_scale)
    return decode(to_slabs(code), SOLUTION_POWER) * (1.0 / solution_scale), resid_out


def solution(mesh):
    placed = (
        P("mode", "slab", None),
        P("mode", "slab", None),
        P("slab", None),
        P(None, "slab", None),
        P(),
        P(),
        P(),
    )
    return jax.shard_map(
        local,
        mesh=mesh,
        in_specs=placed,
        out_specs=(P("mode", "slab", None), P("mode", "slab", None)),
        check_vma=False,
    )
```

```python
import functools
import math

import jax
import jax.numpy as jnp
from jax import lax
from jax.experimental import pallas as pl
from jax.experimental.pallas import tpu as pltpu
from jax.sharding import PartitionSpec as P

RELAXATION = 0.6
VMEM_BYTES = 60 << 20
SHARED_VMEM_BYTES = 48 << 20
SMALL_VMEM_BYTES = 9 << 20
UNROLL = 4


def sine_table(length):
    counter = jnp.arange(length).astype(jnp.float32) + 1.0
    angle = math.pi * counter[:, None] * counter[None, :] / (length + 1)
    return math.sqrt(2.0 / (length + 1)) * jnp.sin(angle)


def eigen_table(first, second):
    along_first = 2.0 * jnp.cos(
        math.pi * (jnp.arange(first).astype(jnp.float32) + 1.0) / (first + 1)
    )
    along_second = 2.0 * jnp.cos(
        math.pi * (jnp.arange(second).astype(jnp.float32) + 1.0) / (second + 1)
    )
    return 4.0 - along_first[:, None] - along_second[None, :]


def stencil_weights(coef):
    nx, ny = coef.shape
    row = lax.broadcasted_iota(jnp.int32, (nx, ny), 0)
    col = lax.broadcasted_iota(jnp.int32, (nx, ny), 1)
    sides = (
        (pltpu.roll(coef, 1, 0), row == 0),
        (pltpu.roll(coef, nx - 1, 0), row == nx - 1),
        (pltpu.roll(coef, 1, 1), col == 0),
        (pltpu.roll(coef, ny - 1, 1), col == ny - 1),
    )
    centre = 0.0
    weights = []
    for other, outside in sides:
        weight = 0.5 * (coef + jnp.where(outside, coef, other))
        centre = centre + weight
        weights.append(jnp.where(outside, 0.0, weight))
    return [centre] + weights


def in_order(here, shift, count):
    return lax.rem(here + count - shift, count)


def in_order(here, shift, count):
    return lax.rem(here + count - shift, count)


def strip_weights_kernel(slabs, height, place_ref, *refs):
    part_refs = refs[:slabs]
    out_ref, coef_ref = refs[slabs:]
    _, nx, ny = coef_ref.shape
    rows = nx // slabs
    fields = out_ref.shape[0] // (5 * height)
    for shift, part_ref in enumerate(part_refs):
        start = in_order(place_ref[0], shift, slabs) * rows
        coef_ref[:, pl.ds(pl.multiple_of(start, rows), rows), :] = part_ref[0]
    col = lax.broadcasted_iota(jnp.int32, (1, ny), 1)
    first = place_ref[1] * height
    for f in range(fields):
        lines = []
        for r in range(-1, height + 1):
            at = jnp.clip(first + r, 0, nx - 1)
            lines.append(coef_ref[f + 1, pl.ds(at, 1), :])
        for r in range(height):
            here = lines[r + 1]
            up = 0.5 * (here + lines[r])
            down = 0.5 * (here + lines[r + 2])
            left = 0.5 * (here + jnp.where(col == 0, here, pltpu.roll(here, 1, 1)))
            right = 0.5 * (here + jnp.where(col == ny - 1, here, pltpu.roll(here, ny - 1, 1)))
            weights = (
                up + down + left + right,
                jnp.where(first + r == 0, 0.0, up),
                jnp.where(first + r == nx - 1, 0.0, down),
                jnp.where(col == 0, 0.0, left),
                jnp.where(col == ny - 1, 0.0, right),
            )
            for which, weight in enumerate(weights):
                at = (f * 5 + which) * height + r
                out_ref[at : at + 1, :] = weight


def mean_weights_kernel(slabs, place_ref, *refs):
    part_refs = refs[:slabs]
    out_ref, coef_ref = refs[slabs:]
    _, nx, ny = out_ref.shape
    for shift, part_ref in enumerate(part_refs):
        coef_ref[in_order(place_ref[0], shift, slabs)] = part_ref[0, 0]
    for which, weight in enumerate(stencil_weights(coef_ref[...].reshape(nx, ny))):
        out_ref[which] = weight


def weights_of(kernel, parts, place, coefs, out, scratch):
    _, entries, rows, ny = parts[0].shape
    last = entries // coefs - 1
    return pl.pallas_call(
        kernel,
        grid_spec=pltpu.PrefetchScalarGridSpec(
            num_scalar_prefetch=1,
            grid=(1,),
            in_specs=[pl.BlockSpec((1, coefs, rows, ny), lambda i, *_: (0, last, 0, 0))]
            * len(parts),
            out_specs=pl.BlockSpec(out, lambda i, *_: (0,) * len(out)),
            scratch_shapes=[pltpu.VMEM(scratch, jnp.float32)],
        ),
        out_shape=jax.ShapeDtypeStruct(out, jnp.float32),
        compiler_params=pltpu.CompilerParams(vmem_limit_bytes=SMALL_VMEM_BYTES),
    )(place, *parts)


def strip_weights_of(parts, place, coefs, height):
    slabs = len(parts)
    _, _, rows, ny = parts[0].shape
    kernel = functools.partial(strip_weights_kernel, slabs, height)
    out = ((coefs - 1) * 5 * height, ny)
    return weights_of(kernel, parts, place, coefs, out, (coefs, slabs * rows, ny))


def mean_weights_of(parts, place, coefs):
    slabs = len(parts)
    _, _, rows, ny = parts[0].shape
    kernel = functools.partial(mean_weights_kernel, slabs)
    return weights_of(kernel, parts, place, coefs, (5, slabs * rows, ny), (slabs, rows, ny))


def split(value):
    high = value.astype(jnp.bfloat16)
    low = (value - high.astype(jnp.float32)).astype(jnp.bfloat16)
    return high, low


def split_table(value):
    high = lax.reduce_precision(value, 8, 7)
    return high.astype(jnp.bfloat16), (value - high).astype(jnp.bfloat16)


LOW = 32
FIRST_POWER = 7
SUM_POWER = 5
SOLUTION_POWER = 4


def encode(value, power):
    square = value * value
    if power == 4:
        result = square * (value * jnp.abs(value))
    elif power == 5:
        result = square * square * value
    else:
        result = (square * square) * (square * value)
    return result.astype(jnp.bfloat16)


def decode(code, power):
    code = code.astype(jnp.float32)
    size = jnp.abs(code)
    value = jnp.exp(jnp.log(size) * (1.0 / power))
    value = jnp.where(size > 0.0, value, 0.0)
    return jnp.where(code < 0.0, -value, value)


def code_scales(nx, ny, entries, width):
    guess_max, mean_max, field_max, coupling_max = 6.0, 2.0, 2.5, 0.0625
    gain = 8.0 * field_max * entries * width * coupling_max * 1.01
    inverse = (min(nx, ny) + 1) ** 2 / 8.0

    def bound(iterate):
        return guess_max + (8.0 * mean_max + gain) * iterate

    change = RELAXATION * inverse * 1.01
    second = guess_max + change * bound(guess_max)
    third = second + change * bound(second)

    def scale(limit, power):
        return 0.8 * 2.0 ** (127.0 / power) / limit

    first = math.sqrt(2.0 * ny) * gain * guess_max
    return (
        min(1.0, scale(first, FIRST_POWER)),
        min(1.0, scale(bound(second), SUM_POWER)),
        min(1.0, scale(third, SOLUTION_POWER)),
    )


def pack_kernel(rows, height, x_ref, out_ref):
    strips, modes, cells = out_ref.shape
    cols = cells // height
    for strip in range(strips):
        for r in range(height):
            value = x_ref[pl.ds(strip * height + r, modes, stride=rows), :]
            out_ref[strip, :, r * cols : (r + 1) * cols] = value.astype(jnp.bfloat16)


def pack_strips(block, strips):
    modes, rows, cols = block.shape
    height = rows // strips
    return pl.pallas_call(
        functools.partial(pack_kernel, rows, height),
        grid=(2,),
        in_specs=[pl.BlockSpec((modes // 2 * rows, cols), lambda g: (g, 0))],
        out_specs=pl.BlockSpec((strips, modes // 2, height * cols), lambda g: (0, g, 0)),
        out_shape=jax.ShapeDtypeStruct((strips, modes, height * cols), jnp.bfloat16),
        compiler_params=pltpu.CompilerParams(vmem_limit_bytes=VMEM_BYTES),
    )(block.reshape(modes * rows, cols))


def dense_kernel(fields, entry_ref, count_ref, coupling_ref, out_ref):
    block = pl.program_id(0)
    width = coupling_ref.shape[-1]
    out_ref[...] = jnp.zeros_like(out_ref)

    def place(k, carry):
        entry = entry_ref[block, k]
        column = pl.multiple_of((entry // fields) * width, width)
        out_ref[0, entry % fields, :, pl.ds(column, width)] = coupling_ref[0, k]
        return carry

    lax.fori_loop(0, count_ref[block], place, 0)


def dense_coupling(coupling, coupling_list, pair_count, fields):
    blocks, entries, width, _ = coupling.shape
    moved = 2 * width * width * (entries + fields * blocks) * coupling.dtype.itemsize
    return pl.pallas_call(
        functools.partial(dense_kernel, fields),
        grid_spec=pltpu.PrefetchScalarGridSpec(
            num_scalar_prefetch=2,
            grid=(blocks,),
            in_specs=[pl.BlockSpec((1, entries, width, width), lambda i, *_: (i, 0, 0, 0))],
            out_specs=pl.BlockSpec(
                (1, fields, width, blocks * width), lambda i, *_: (i, 0, 0, 0)
            ),
        ),
        out_shape=jax.ShapeDtypeStruct((blocks, fields, width, blocks * width), coupling.dtype),
        compiler_params=pltpu.CompilerParams(vmem_limit_bytes=SMALL_VMEM_BYTES + moved),
    )(coupling_list, pair_count, coupling)


def low_tiles(height, cols):
    return -(-height * LOW // cols)


def along_cols(fields, right_ref):
    size, ny = fields[0].shape
    high, low = split(jnp.concatenate(fields, axis=0))
    both = jnp.dot(
        jnp.concatenate([high, low], axis=1), right_ref[...], preferred_element_type=jnp.float32
    )
    both = both[:, :ny] + both[:, ny:]
    return [both[i * size : (i + 1) * size] for i in range(len(fields))]


def along_rows(wide, left_ref):
    nx = wide.shape[0]
    high, low = split(wide)
    both = jnp.dot(
        left_ref[...], jnp.concatenate([high, low], axis=0), preferred_element_type=jnp.float32
    )
    return both[:nx] + both[nx:]


def weight_row(weight_ref, height, field, which, r):
    at = (field * 5 + which) * height + r
    return weight_ref[at : at + 1, :]


def inner_kernel(height, cols, matrix_ref, state_ref, weight_ref, out_ref, sums_ref):
    blocks, fields, width, depth = matrix_ref.shape
    sums_ref[...] = jnp.dot(
        matrix_ref[...].reshape(blocks * fields * width, depth),
        state_ref[...],
        preferred_element_type=jnp.float32,
    )
    for block in range(blocks):
        for r in range(height):
            total = 0.0
            from_left = 0.0
            from_right = 0.0
            for f in range(fields):

                def row(at):
                    start = (block * fields + f) * width
                    return sums_ref[start : start + width, at * cols : (at + 1) * cols]

                weight = functools.partial(weight_row, weight_ref, height, f)
                here = row(r)
                total = total + weight(0, r) * here
                if r > 0:
                    total = total - weight(1, r) * row(r - 1)
                if r < height - 1:
                    total = total - weight(2, r) * row(r + 1)
                from_left = from_left + weight(4, r) * here
                from_right = from_right + weight(3, r) * here
            total = total - pltpu.roll(from_left, 1, 1) - pltpu.roll(from_right, cols - 1, 1)
            out_ref[block * width : (block + 1) * width, r * cols : (r + 1) * cols] = total


def border_kernel(
    height,
    cols,
    first,
    scale,
    matrix_ref,
    above_ref,
    below_ref,
    weight_ref,
    inner_ref,
    right_ref,
    out_ref,
):
    blocks, fields, width, depth = matrix_ref.shape
    border = jnp.concatenate([above_ref[...], below_ref[...]], axis=1)
    low_col = lax.broadcasted_iota(jnp.int32, (width, cols), 1) < LOW
    matrix = matrix_ref[...].reshape(blocks * fields * width, depth)
    sums = jnp.dot(matrix, border, preferred_element_type=jnp.float32)
    for block in range(blocks):
        modes = slice(block * width, (block + 1) * width)
        rows = []
        for r in range(height):
            total = inner_ref[modes, r * cols : (r + 1) * cols]
            for f in range(fields):
                part = sums[(block * fields + f) * width : (block * fields + f + 1) * width]
                if r == 0:
                    total = total - weight_row(weight_ref, height, f, 1, r) * part[:, :cols]
                if r == height - 1:
                    total = total - weight_row(weight_ref, height, f, 2, r) * part[:, cols:]
            rows.append(total)
        if not first:
            for r in range(height):
                code = encode(rows[r] * scale, SUM_POWER)
                out_ref[modes, r * cols : (r + 1) * cols] = code
            continue
        rows = along_cols(rows, right_ref)
        for r in range(height):
            value = rows[r] * scale
            code = encode(value, FIRST_POWER)
            out_ref[modes, r * cols : (r + 1) * cols] = code
            rest = jnp.where(low_col, value - decode(code, FIRST_POWER), 0.0)
            place = r % (cols // LOW)
            rest = pltpu.roll(rest, place * LOW, 1) if place else rest
            packed = rest if place == 0 else packed + rest
            if place == cols // LOW - 1 or r == height - 1:
                at = (height + r // (cols // LOW)) * cols
                out_ref[modes, at : at + cols] = packed.astype(jnp.bfloat16)


def coupled_sums(matrix, state, weights, right, first, scale, both):
    blocks, fields, width, depth = matrix.shape
    cells = state.shape[1]
    height = weights.shape[0] // (5 * fields)
    cols = cells // height
    mode_count = lax.axis_size("mode")
    slab_count = lax.axis_size("slab")
    place = [
        (t % mode_count) * slab_count + t // mode_count for t in range(mode_count * slab_count)
    ]
    onward = list(zip(place, place[1:] + place[:1]))
    above = lax.ppermute(state[:, -cols:], both, onward)
    below = lax.ppermute(state[:, :cols], both, [(b, a) for a, b in onward])
    unroll = math.gcd(blocks, UNROLL)
    matrix_spec = pl.BlockSpec((unroll, fields, width, depth), lambda i: (i, 0, 0, 0))
    weight_spec = pl.BlockSpec(weights.shape, lambda i: (0, 0))
    sums_spec = pl.BlockSpec((unroll * width, cells), lambda i: (i, 0))
    moved = 2 * unroll * fields * width * depth * matrix.dtype.itemsize
    params = pltpu.CompilerParams(vmem_limit_bytes=2 * SMALL_VMEM_BYTES + moved)
    inner = pl.pallas_call(
        functools.partial(inner_kernel, height, cols),
        grid=(blocks // unroll,),
        in_specs=[matrix_spec, pl.BlockSpec((depth, cells), lambda i: (0, 0)), weight_spec],
        out_specs=sums_spec,
        out_shape=jax.ShapeDtypeStruct((blocks * width, cells), jnp.float32),
        scratch_shapes=[pltpu.VMEM((unroll * fields * width, cells), jnp.float32)],
        cost_estimate=pl.CostEstimate(
            flops=2 * matrix.size * cells, bytes_accessed=2 * matrix.size, transcendentals=0
        ),
        compiler_params=params,
    )(matrix, state, weights)
    border_spec = pl.BlockSpec((depth, cols), lambda i: (0, 0))
    sent = cells + (low_tiles(height, cols) * cols if first else 0)
    return pl.pallas_call(
        functools.partial(border_kernel, height, cols, first, scale),
        grid=(blocks // unroll,),
        in_specs=[
            matrix_spec,
            border_spec,
            border_spec,
            weight_spec,
            sums_spec,
            pl.BlockSpec(right.shape, lambda i: (0, 0)),
        ],
        out_specs=pl.BlockSpec((unroll * width, sent), lambda i: (i, 0)),
        out_shape=jax.ShapeDtypeStruct((blocks * width, sent), jnp.bfloat16),
        compiler_params=params,
    )(matrix, above, below, weights, inner, right)


TOGETHER = 16
MEAN_TOGETHER = 8
GROUP = 16


def solve(spectral, right_ref, left_ref, scale_ref):
    ny = spectral[0].shape[1]
    wide = along_rows(jnp.concatenate(spectral, axis=1), left_ref)
    wide = wide * jnp.concatenate([scale_ref[...]] * len(spectral), axis=1)
    wide = along_rows(wide, left_ref)
    return along_cols([wide[:, i * ny : (i + 1) * ny] for i in range(len(spectral))], right_ref)


def mean_fields(current_ref, right_side_ref, weight_ref, start):
    nx, ny = weight_ref.shape[1:]
    values = []
    for mode in range(start, start + MEAN_TOGETHER):
        here = current_ref[:, mode].reshape(nx, ny)
        mean = (
            weight_ref[0] * here
            - weight_ref[1] * pltpu.roll(here, 1, 0)
            - weight_ref[2] * pltpu.roll(here, nx - 1, 0)
            - pltpu.roll(weight_ref[4] * here, 1, 1)
            - pltpu.roll(weight_ref[3] * here, ny - 1, 1)
        )
        values.append(right_side_ref[:, mode].reshape(nx, ny) - mean)
    return values


def first_mean_kernel(slabs, place_ref, *refs):
    current_parts = refs[:slabs]
    right_side_parts = refs[slabs : 2 * slabs]
    weight_ref, right_ref, current_ref, right_side_ref, out_ref = refs[2 * slabs :]
    for shift in range(slabs):
        slab = in_order(place_ref[0], shift, slabs)
        current_ref[slab] = current_parts[shift][0]
        right_side_ref[slab] = right_side_parts[shift][0]
    shape = (slabs,) + out_ref.shape[2:]
    for start in range(0, out_ref.shape[1], MEAN_TOGETHER):
        values = mean_fields(current_ref, right_side_ref, weight_ref, start)
        for i, value in enumerate(along_cols(values, right_ref)):
            out_ref[:, start + i] = value.reshape(shape)


def mean_kernel(current_ref, right_side_ref, weight_ref, out_ref):
    shape = out_ref.shape[:1] + out_ref.shape[2:]
    for start in range(0, out_ref.shape[1], MEAN_TOGETHER):
        values = mean_fields(current_ref, right_side_ref, weight_ref, start)
        for i, value in enumerate(values):
            out_ref[:, start + i] = value.reshape(shape)


def turn_in(turned_ref, coupled_ref, mode_count, slab_count, height, first, scale):
    group = coupled_ref.shape[1]
    ny = turned_ref.shape[1]
    low_col = lax.broadcasted_iota(jnp.int32, (group, ny), 1) < LOW
    for source in range(mode_count * slab_count):
        start = ((source % slab_count) * mode_count + source // slab_count) * height
        for r in range(height):
            code = coupled_ref[source, :, r * ny : (r + 1) * ny]
            value = decode(code, FIRST_POWER if first else SUM_POWER)
            if first:
                at = (height + r // (ny // LOW)) * ny
                rest = coupled_ref[source, :, at : at + ny].astype(jnp.float32)
                place = r % (ny // LOW)
                rest = pltpu.roll(rest, ny - place * LOW, 1) if place else rest
                value = value + jnp.where(low_col, rest, 0.0)
            turned_ref[(start + r) * group : (start + r + 1) * group, :] = value * (1.0 / scale)


def step_kernel(
    mode_count,
    slab_count,
    code_scale,
    current_ref,
    base_ref,
    coupled_ref,
    right_ref,
    left_ref,
    scale_ref,
    solution_ref,
    state_ref,
    turned_ref,
):
    nx, ny = scale_ref.shape
    group = coupled_ref.shape[1]
    height = nx // (mode_count * slab_count)
    turn_in(turned_ref, coupled_ref, mode_count, slab_count, height, True, code_scale)

    def several(number, carry):
        start = number * TOGETHER
        resid = []
        for i in range(TOGETHER):
            coupled = turned_ref[pl.ds(start + i, nx, stride=group), :]
            resid.append(base_ref[:, start + i].reshape(nx, ny) - coupled)
        change = solve(resid, right_ref, left_ref, scale_ref)
        for i in range(TOGETHER):
            value = current_ref[:, start + i].reshape(nx, ny) + change[i]
            solution_ref[:, start + i] = value.reshape(slab_count, nx // slab_count, ny)
            turned_ref[pl.ds(start + i, nx, stride=group), :] = value
        return carry

    lax.fori_loop(0, group // TOGETHER, several, 0)

    for target in range(mode_count * slab_count):
        start = ((target % slab_count) * mode_count + target // slab_count) * height
        for r in range(height):
            row = start + r
            value = turned_ref[row * group : (row + 1) * group, :].astype(jnp.bfloat16)
            state_ref[target, :, r * ny : (r + 1) * ny] = value


def residual_kernel(
    mode_count, slab_count, code_scale, here_ref, base_ref, coupled_ref, out_ref, *refs
):
    *code_refs, turned_ref = refs
    group = coupled_ref.shape[1]
    ny = base_ref.shape[-1]
    nx = turned_ref.shape[0] // group
    height = nx // (mode_count * slab_count)
    turn_in(turned_ref, coupled_ref, mode_count, slab_count, height, False, code_scale)

    def one(mode, carry):
        coupled = turned_ref[pl.ds(mode, nx, stride=group), :]
        out_ref[:, mode] = base_ref[:, mode] - coupled.reshape(slab_count, nx // slab_count, ny)
        return carry

    lax.fori_loop(0, group, one, 0)
    for shift, code_ref in enumerate(code_refs):
        slab = lax.rem(here_ref[0] + shift, slab_count)
        code_ref[0] = encode(out_ref[slab] * code_scale, SUM_POWER)


def correct_kernel(code_scale, current_ref, resid_ref, right_ref, left_ref, scale_ref, out_ref):
    nx, ny = scale_ref.shape

    def several(number, carry):
        start = number * TOGETHER
        resid = [resid_ref[:, start + i].reshape(nx, ny) for i in range(TOGETHER)]
        change = solve(along_cols(resid, right_ref), right_ref, left_ref, scale_ref)
        for i in range(TOGETHER):
            shape = out_ref.shape[:1] + out_ref.shape[2:]
            value = current_ref[:, start + i] + change[i].reshape(shape)
            out_ref[:, start + i] = encode(value * code_scale, SOLUTION_POWER)
        return carry

    lax.fori_loop(0, out_ref.shape[1] // TOGETHER, several, 0)


def whole(array):
    return pl.BlockSpec(array.shape, lambda g: (0,) * array.ndim)


def slabs_of(array):
    slab_count, _, rows, ny = array.shape
    return pl.BlockSpec((slab_count, GROUP, rows, ny), lambda g: (0, g, 0, 0))


def strips_of(shape):
    return pl.BlockSpec((shape[0], GROUP, shape[2]), lambda g: (0, g, 0))


def per_group(
    kernel, groups, operands, in_specs, out_shape, out_specs, scratch=(), flops=0, vmem=SHARED_VMEM_BYTES
):
    moved = sum(a.size * a.dtype.itemsize for a in operands)
    return pl.pallas_call(
        kernel,
        grid=(groups,),
        in_specs=in_specs,
        out_specs=out_specs,
        out_shape=out_shape,
        scratch_shapes=scratch,
        cost_estimate=pl.CostEstimate(flops=flops, bytes_accessed=2 * moved, transcendentals=0),
        compiler_params=pltpu.CompilerParams(vmem_limit_bytes=vmem),
    )(*operands)


def first_mean_part(place, current_parts, right_side_parts, weights, right):
    slabs = len(right_side_parts)
    _, modes, rows, ny = right_side_parts[0].shape
    part = pl.BlockSpec((1, GROUP, rows, ny), lambda g, *_: (0, g, 0, 0))
    slab = pl.BlockSpec((slabs, GROUP, rows, ny), lambda g, *_: (0, g, 0, 0))
    shape = jax.ShapeDtypeStruct((slabs, modes, rows, ny), jnp.float32)
    return pl.pallas_call(
        functools.partial(first_mean_kernel, slabs),
        grid_spec=pltpu.PrefetchScalarGridSpec(
            num_scalar_prefetch=1,
            grid=(modes // GROUP,),
            in_specs=[part] * (2 * slabs)
            + [
                pl.BlockSpec(weights.shape, lambda g, *_: (0, 0, 0)),
                pl.BlockSpec(right.shape, lambda g, *_: (0, 0)),
            ],
            out_specs=[slab] * 3,
        ),
        out_shape=[shape] * 3,
        compiler_params=pltpu.CompilerParams(vmem_limit_bytes=VMEM_BYTES),
    )(place, *current_parts, *right_side_parts, weights, right)


def mean_part(current, right_side, weights):
    slabs = slabs_of(right_side)
    return per_group(
        mean_kernel,
        right_side.shape[1] // GROUP,
        (current, right_side, weights),
        [slabs, slabs, whole(weights)],
        jax.ShapeDtypeStruct(right_side.shape, jnp.float32),
        slabs,
    )


def solve_flops(array, tables):
    nx, ny = tables[2].shape
    return array.shape[1] * 8 * 3 * nx * ny * (nx + ny) // 2


def step(current, base, coupled, tables, mode_count, slab_count, code_scale):
    nx, ny = tables[2].shape
    slabs = slabs_of(base)
    devices, modes, _ = coupled.shape
    state = (devices, modes, nx // devices * ny)
    return per_group(
        functools.partial(step_kernel, mode_count, slab_count, code_scale),
        modes // GROUP,
        (current, base, coupled, *tables),
        [slabs, slabs, strips_of(coupled.shape), *map(whole, tables)],
        [
            jax.ShapeDtypeStruct(base.shape, jnp.float32),
            jax.ShapeDtypeStruct(state, jnp.bfloat16),
        ],
        [slabs, strips_of(state)],
        [pltpu.VMEM((nx * GROUP, ny), jnp.float32)],
        solve_flops(base, tables),
    )


def last_residual(base, coupled, mode_count, slab_count, code_scale):
    slab, modes, rows, ny = base.shape
    slabs = pl.BlockSpec((slab, GROUP, rows, ny), lambda g, *_: (0, g, 0, 0))
    part = pl.BlockSpec((1, GROUP, rows, ny), lambda g, *_: (0, g, 0, 0))
    devices, _, cells = coupled.shape
    out, *parts = pl.pallas_call(
        functools.partial(residual_kernel, mode_count, slab_count, code_scale),
        grid_spec=pltpu.PrefetchScalarGridSpec(
            num_scalar_prefetch=1,
            grid=(modes // GROUP,),
            in_specs=[slabs, pl.BlockSpec((devices, GROUP, cells), lambda g, *_: (0, g, 0))],
            out_specs=[slabs] + [part] * slab,
            scratch_shapes=[pltpu.VMEM((slab * rows * GROUP, ny), jnp.float32)],
        ),
        out_shape=[jax.ShapeDtypeStruct(base.shape, jnp.float32)]
        + [jax.ShapeDtypeStruct((1, modes, rows, ny), jnp.bfloat16)] * slab,
        cost_estimate=pl.CostEstimate(
            flops=0, bytes_accessed=2 * base.size * 4, transcendentals=0
        ),
        compiler_params=pltpu.CompilerParams(vmem_limit_bytes=SHARED_VMEM_BYTES),
    )(lax.axis_index("slab").reshape(1), base, coupled)
    return out, parts


def correct(current, resid, tables, code_scale):
    slabs = slabs_of(resid)
    return per_group(
        functools.partial(correct_kernel, code_scale),
        resid.shape[1] // GROUP,
        (current, resid, *tables),
        [slabs, slabs, *map(whole, tables)],
        jax.ShapeDtypeStruct(resid.shape, jnp.bfloat16),
        slabs,
        (),
        solve_flops(resid, tables),
    )


def collect(parts, axis):
    count = lax.axis_size(axis)
    here = lax.axis_index(axis)
    out = jnp.zeros((count,) + parts[0].shape[1:], parts[0].dtype)
    for shift, part in enumerate(parts):
        source = lax.rem(here + count - shift, count)
        out = lax.dynamic_update_slice_in_dim(out, part, source, 0)
    return out


def onwards(part, axis, shift):
    count = lax.axis_size(axis)
    return lax.ppermute(part, axis, [(i, (i + shift) % count) for i in range(count)])


def parts_of(block, axis):
    count = lax.axis_size(axis)
    here = lax.axis_index(axis)
    return [
        lax.dynamic_index_in_dim(block, lax.rem(here + shift, count), 0) for shift in range(count)
    ]


def moved_parts(parts, axis):
    return [parts[0]] + [onwards(parts[i], axis, i) for i in range(1, len(parts))]


def local(guess, right_side, mean_coef, field_coef, coupling, coupling_list, pair_count):
    mode_count = lax.axis_size("mode")
    slab_count = lax.axis_size("slab")
    both = ("mode", "slab")
    modes, rows, cols = guess.shape
    fields = field_coef.shape[0]
    nx = rows * slab_count
    devices = mode_count * slab_count
    height = nx // devices
    share = modes // slab_count

    strips = pack_strips(guess, mode_count)
    coefs = jnp.concatenate([mean_coef[None], field_coef], 0)[None]
    state = lax.all_to_all(strips, "mode", 0, 0, tiled=True)
    state = state.reshape(mode_count * modes, height * cols)

    def to_slabs(block):
        flat = block.reshape(modes, rows, cols)
        return lax.all_to_all(flat, "slab", 0, 0, tiled=True)

    guess_parts = parts_of(guess.reshape(slab_count, share, rows, cols), "slab")
    guess_parts = [jnp.concatenate([part, coefs], axis=1) for part in guess_parts]
    guess_parts = moved_parts(guess_parts, "slab")
    right_parts = parts_of(right_side.reshape(slab_count, share, rows, cols), "slab")
    state, guess_parts, right_parts = lax.optimization_barrier((state, guess_parts, right_parts))
    right_parts = moved_parts(right_parts, "slab")

    slab = lax.axis_index("slab")
    place = jnp.stack([slab, slab * mode_count + lax.axis_index("mode")])
    strip_weights = strip_weights_of(guess_parts, place, fields + 1, height)
    mean_weights = mean_weights_of(guess_parts, place, fields + 1)
    matrix = dense_coupling(coupling, coupling_list, pair_count, fields)

    row_high, row_low = split_table(sine_table(nx))
    col_high, col_low = split_table(sine_table(cols))
    tables = (
        jnp.concatenate(
            [
                jnp.concatenate([col_high, col_low], 1),
                jnp.concatenate([col_high, jnp.zeros_like(col_low)], 1),
            ],
            0,
        ),
        jnp.concatenate(
            [
                jnp.concatenate([row_high, row_high], 1),
                jnp.concatenate([row_low, jnp.zeros_like(row_low)], 1),
            ],
            0,
        ),
        RELAXATION / eigen_table(nx, cols),
    )

    first_scale, sum_scale, solution_scale = code_scales(nx, cols, coupling.shape[1], modes)

    sums = coupled_sums(matrix, state, strip_weights, tables[0], True, first_scale, both)
    sums, right_parts = lax.optimization_barrier((sums, right_parts))
    sums = lax.all_to_all(sums, both, 0, 0, tiled=True).reshape(devices, share, -1)
    current, right_side, base = first_mean_part(
        place, guess_parts, right_parts, mean_weights, tables[0]
    )
    current, state = step(current, base, sums, tables, mode_count, slab_count, first_scale)
    state = state.reshape(devices * share, height * cols)
    state = lax.all_to_all(state, both, 0, 0, tiled=True)

    base = mean_part(current, right_side, mean_weights)
    sums = coupled_sums(matrix, state, strip_weights, tables[0], False, sum_scale, both)
    sums = lax.all_to_all(sums, both, 0, 0, tiled=True).reshape(devices, share, -1)
    resid, parts = last_residual(base, sums, mode_count, slab_count, sum_scale)
    moved = collect(moved_parts(parts, "slab"), "slab").reshape(modes, rows, cols)
    resid_out = decode(moved, SUM_POWER) * (1.0 / sum_scale)
    code = correct(current, resid, tables, solution_scale)
    return decode(to_slabs(code), SOLUTION_POWER) * (1.0 / solution_scale), resid_out


def solution(mesh):
    placed = (
        P("mode", "slab", None),
        P("mode", "slab", None),
        P("slab", None),
        P(None, "slab", None),
        P(),
        P(),
        P(),
    )
    return jax.shard_map(
        local,
        mesh=mesh,
        in_specs=placed,
        out_specs=(P("mode", "slab", None), P("mode", "slab", None)),
        check_vma=False,
    )
```

```python
import functools
import math

import jax
import jax.numpy as jnp
from jax import lax
from jax.experimental import pallas as pl
from jax.experimental.pallas import tpu as pltpu
from jax.sharding import PartitionSpec as P

RELAXATION = 0.6
VMEM_BYTES = 60 << 20
SHARED_VMEM_BYTES = 48 << 20
SMALL_VMEM_BYTES = 9 << 20
UNROLL = 4


def sine_table(length):
    counter = jnp.arange(length).astype(jnp.float32) + 1.0
    angle = math.pi * counter[:, None] * counter[None, :] / (length + 1)
    return math.sqrt(2.0 / (length + 1)) * jnp.sin(angle)


def eigen_table(first, second):
    along_first = 2.0 * jnp.cos(
        math.pi * (jnp.arange(first).astype(jnp.float32) + 1.0) / (first + 1)
    )
    along_second = 2.0 * jnp.cos(
        math.pi * (jnp.arange(second).astype(jnp.float32) + 1.0) / (second + 1)
    )
    return 4.0 - along_first[:, None] - along_second[None, :]


def stencil_weights(coef):
    nx, ny = coef.shape
    row = lax.broadcasted_iota(jnp.int32, (nx, ny), 0)
    col = lax.broadcasted_iota(jnp.int32, (nx, ny), 1)
    sides = (
        (pltpu.roll(coef, 1, 0), row == 0),
        (pltpu.roll(coef, nx - 1, 0), row == nx - 1),
        (pltpu.roll(coef, 1, 1), col == 0),
        (pltpu.roll(coef, ny - 1, 1), col == ny - 1),
    )
    centre = 0.0
    weights = []
    for other, outside in sides:
        weight = 0.5 * (coef + jnp.where(outside, coef, other))
        centre = centre + weight
        weights.append(jnp.where(outside, 0.0, weight))
    return [centre] + weights


def in_order(here, shift, count):
    return lax.rem(here + count - shift, count)


def in_order(here, shift, count):
    return lax.rem(here + count - shift, count)


MARGIN = 8


def strip_weights_kernel(slabs, height, place_ref, own_ref, low_ref, high_ref, out_ref, coef_ref):
    _, rows, ny = own_ref.shape
    nx = slabs * rows
    fields = out_ref.shape[0] // (5 * height)
    for f in range(1, fields + 1):
        coef_ref[f, MARGIN - 1 : MARGIN, :] = low_ref[f : f + 1, :]
        coef_ref[f, MARGIN : MARGIN + rows, :] = own_ref[f]
        coef_ref[f, MARGIN + rows : MARGIN + rows + 1, :] = high_ref[f : f + 1, :]
    offset = MARGIN - place_ref[0] * rows
    col = lax.broadcasted_iota(jnp.int32, (1, ny), 1)
    first = place_ref[1] * height
    for f in range(fields):
        lines = []
        for r in range(-1, height + 1):
            at = jnp.clip(first + r, 0, nx - 1)
            lines.append(coef_ref[f + 1, pl.ds(at + offset, 1), :])
        for r in range(height):
            here = lines[r + 1]
            up = 0.5 * (here + lines[r])
            down = 0.5 * (here + lines[r + 2])
            left = 0.5 * (here + jnp.where(col == 0, here, pltpu.roll(here, 1, 1)))
            right = 0.5 * (here + jnp.where(col == ny - 1, here, pltpu.roll(here, ny - 1, 1)))
            weights = (
                up + down + left + right,
                jnp.where(first + r == 0, 0.0, up),
                jnp.where(first + r == nx - 1, 0.0, down),
                jnp.where(col == 0, 0.0, left),
                jnp.where(col == ny - 1, 0.0, right),
            )
            for which, weight in enumerate(weights):
                at = (f * 5 + which) * height + r
                out_ref[at : at + 1, :] = weight


def mean_weights_kernel(slabs, place_ref, *refs):
    part_refs = refs[:slabs]
    out_ref, coef_ref = refs[slabs:]
    _, nx, ny = out_ref.shape
    for shift, part_ref in enumerate(part_refs):
        coef_ref[in_order(place_ref[0], shift, slabs)] = part_ref[0, 0]
    for which, weight in enumerate(stencil_weights(coef_ref[...].reshape(nx, ny))):
        out_ref[which] = weight


def strip_weights_of(own, low, high, place, slabs, height):
    coefs, rows, ny = own.shape
    out = ((coefs - 1) * 5 * height, ny)
    edge = pl.BlockSpec((coefs, ny), lambda i, *_: (0, 0))
    return pl.pallas_call(
        functools.partial(strip_weights_kernel, slabs, height),
        grid_spec=pltpu.PrefetchScalarGridSpec(
            num_scalar_prefetch=1,
            grid=(1,),
            in_specs=[pl.BlockSpec((coefs, rows, ny), lambda i, *_: (0, 0, 0)), edge, edge],
            out_specs=pl.BlockSpec(out, lambda i, *_: (0, 0)),
            scratch_shapes=[pltpu.VMEM((coefs, rows + 2 * MARGIN, ny), jnp.float32)],
        ),
        out_shape=jax.ShapeDtypeStruct(out, jnp.float32),
        compiler_params=pltpu.CompilerParams(vmem_limit_bytes=SMALL_VMEM_BYTES),
    )(place, own, low, high)


def mean_weights_of(parts, place, coefs):
    slabs = len(parts)
    _, entries, rows, ny = parts[0].shape
    last = entries // coefs - 1
    out = (5, slabs * rows, ny)
    return pl.pallas_call(
        functools.partial(mean_weights_kernel, slabs),
        grid_spec=pltpu.PrefetchScalarGridSpec(
            num_scalar_prefetch=1,
            grid=(1,),
            in_specs=[pl.BlockSpec((1, coefs, rows, ny), lambda i, *_: (0, last, 0, 0))] * slabs,
            out_specs=pl.BlockSpec(out, lambda i, *_: (0, 0, 0)),
            scratch_shapes=[pltpu.VMEM((slabs, rows, ny), jnp.float32)],
        ),
        out_shape=jax.ShapeDtypeStruct(out, jnp.float32),
        compiler_params=pltpu.CompilerParams(vmem_limit_bytes=SMALL_VMEM_BYTES),
    )(place, *parts)


def split(value):
    high = value.astype(jnp.bfloat16)
    low = (value - high.astype(jnp.float32)).astype(jnp.bfloat16)
    return high, low


def split_table(value):
    high = lax.reduce_precision(value, 8, 7)
    return high.astype(jnp.bfloat16), (value - high).astype(jnp.bfloat16)


LOW = 32
FIRST_POWER = 7
SUM_POWER = 5
SOLUTION_POWER = 4


def encode(value, power):
    square = value * value
    if power == 4:
        result = square * (value * jnp.abs(value))
    elif power == 5:
        result = square * square * value
    else:
        result = (square * square) * (square * value)
    return result.astype(jnp.bfloat16)


def decode(code, power):
    code = code.astype(jnp.float32)
    size = jnp.abs(code)
    value = jnp.exp(jnp.log(size) * (1.0 / power))
    value = jnp.where(size > 0.0, value, 0.0)
    return jnp.where(code < 0.0, -value, value)


def code_scales(nx, ny, entries, width):
    guess_max, mean_max, field_max, coupling_max = 6.0, 2.0, 2.5, 0.0625
    gain = 8.0 * field_max * entries * width * coupling_max * 1.01
    inverse = (min(nx, ny) + 1) ** 2 / 8.0

    def bound(iterate):
        return guess_max + (8.0 * mean_max + gain) * iterate

    change = RELAXATION * inverse * 1.01
    second = guess_max + change * bound(guess_max)
    third = second + change * bound(second)

    def scale(limit, power):
        return 0.8 * 2.0 ** (127.0 / power) / limit

    first = math.sqrt(2.0 * ny) * gain * guess_max
    return (
        min(1.0, scale(first, FIRST_POWER)),
        min(1.0, scale(bound(second), SUM_POWER)),
        min(1.0, scale(third, SOLUTION_POWER)),
    )


def pack_kernel(rows, height, x_ref, out_ref):
    strips, modes, cells = out_ref.shape
    cols = cells // height
    for strip in range(strips):
        for r in range(height):
            value = x_ref[pl.ds(strip * height + r, modes, stride=rows), :]
            out_ref[strip, :, r * cols : (r + 1) * cols] = value.astype(jnp.bfloat16)


def pack_strips(block, strips):
    modes, rows, cols = block.shape
    height = rows // strips
    return pl.pallas_call(
        functools.partial(pack_kernel, rows, height),
        grid=(2,),
        in_specs=[pl.BlockSpec((modes // 2 * rows, cols), lambda g: (g, 0))],
        out_specs=pl.BlockSpec((strips, modes // 2, height * cols), lambda g: (0, g, 0)),
        out_shape=jax.ShapeDtypeStruct((strips, modes, height * cols), jnp.bfloat16),
        compiler_params=pltpu.CompilerParams(vmem_limit_bytes=VMEM_BYTES),
    )(block.reshape(modes * rows, cols))


def dense_kernel(fields, entry_ref, count_ref, coupling_ref, out_ref):
    block = pl.program_id(0)
    width = coupling_ref.shape[-1]
    out_ref[...] = jnp.zeros_like(out_ref)

    def place(k, carry):
        entry = entry_ref[block, k]
        column = pl.multiple_of((entry // fields) * width, width)
        out_ref[0, entry % fields, :, pl.ds(column, width)] = coupling_ref[0, k]
        return carry

    lax.fori_loop(0, count_ref[block], place, 0)


def dense_coupling(coupling, coupling_list, pair_count, fields):
    blocks, entries, width, _ = coupling.shape
    moved = 2 * width * width * (entries + fields * blocks) * coupling.dtype.itemsize
    return pl.pallas_call(
        functools.partial(dense_kernel, fields),
        grid_spec=pltpu.PrefetchScalarGridSpec(
            num_scalar_prefetch=2,
            grid=(blocks,),
            in_specs=[pl.BlockSpec((1, entries, width, width), lambda i, *_: (i, 0, 0, 0))],
            out_specs=pl.BlockSpec(
                (1, fields, width, blocks * width), lambda i, *_: (i, 0, 0, 0)
            ),
        ),
        out_shape=jax.ShapeDtypeStruct((blocks, fields, width, blocks * width), coupling.dtype),
        compiler_params=pltpu.CompilerParams(vmem_limit_bytes=SMALL_VMEM_BYTES + moved),
    )(coupling_list, pair_count, coupling)


def low_tiles(height, cols):
    return -(-height * LOW // cols)


def along_cols(fields, right_ref):
    size, ny = fields[0].shape
    high, low = split(jnp.concatenate(fields, axis=0))
    both = jnp.dot(
        jnp.concatenate([high, low], axis=1), right_ref[...], preferred_element_type=jnp.float32
    )
    both = both[:, :ny] + both[:, ny:]
    return [both[i * size : (i + 1) * size] for i in range(len(fields))]


def along_rows(wide, left_ref):
    nx = wide.shape[0]
    high, low = split(wide)
    both = jnp.dot(
        left_ref[...], jnp.concatenate([high, low], axis=0), preferred_element_type=jnp.float32
    )
    return both[:nx] + both[nx:]


def weight_row(weight_ref, height, field, which, r):
    at = (field * 5 + which) * height + r
    return weight_ref[at : at + 1, :]


def inner_kernel(height, cols, matrix_ref, state_ref, weight_ref, out_ref, sums_ref):
    blocks, fields, width, depth = matrix_ref.shape
    sums_ref[...] = jnp.dot(
        matrix_ref[...].reshape(blocks * fields * width, depth),
        state_ref[...],
        preferred_element_type=jnp.float32,
    )
    for block in range(blocks):
        for r in range(height):
            total = 0.0
            from_left = 0.0
            from_right = 0.0
            for f in range(fields):

                def row(at):
                    start = (block * fields + f) * width
                    return sums_ref[start : start + width, at * cols : (at + 1) * cols]

                weight = functools.partial(weight_row, weight_ref, height, f)
                here = row(r)
                total = total + weight(0, r) * here
                if r > 0:
                    total = total - weight(1, r) * row(r - 1)
                if r < height - 1:
                    total = total - weight(2, r) * row(r + 1)
                from_left = from_left + weight(4, r) * here
                from_right = from_right + weight(3, r) * here
            total = total - pltpu.roll(from_left, 1, 1) - pltpu.roll(from_right, cols - 1, 1)
            out_ref[block * width : (block + 1) * width, r * cols : (r + 1) * cols] = total


def border_kernel(
    height,
    cols,
    first,
    scale,
    matrix_ref,
    above_ref,
    below_ref,
    weight_ref,
    inner_ref,
    right_ref,
    out_ref,
):
    blocks, fields, width, depth = matrix_ref.shape
    border = jnp.concatenate([above_ref[...], below_ref[...]], axis=1)
    low_col = lax.broadcasted_iota(jnp.int32, (width, cols), 1) < LOW
    matrix = matrix_ref[...].reshape(blocks * fields * width, depth)
    sums = jnp.dot(matrix, border, preferred_element_type=jnp.float32)
    for block in range(blocks):
        modes = slice(block * width, (block + 1) * width)
        rows = []
        for r in range(height):
            total = inner_ref[modes, r * cols : (r + 1) * cols]
            for f in range(fields):
                part = sums[(block * fields + f) * width : (block * fields + f + 1) * width]
                if r == 0:
                    total = total - weight_row(weight_ref, height, f, 1, r) * part[:, :cols]
                if r == height - 1:
                    total = total - weight_row(weight_ref, height, f, 2, r) * part[:, cols:]
            rows.append(total)
        if not first:
            for r in range(height):
                code = encode(rows[r] * scale, SUM_POWER)
                out_ref[modes, r * cols : (r + 1) * cols] = code
            continue
        rows = along_cols(rows, right_ref)
        for r in range(height):
            value = rows[r] * scale
            code = encode(value, FIRST_POWER)
            out_ref[modes, r * cols : (r + 1) * cols] = code
            rest = jnp.where(low_col, value - decode(code, FIRST_POWER), 0.0)
            place = r % (cols // LOW)
            rest = pltpu.roll(rest, place * LOW, 1) if place else rest
            packed = rest if place == 0 else packed + rest
            if place == cols // LOW - 1 or r == height - 1:
                at = (height + r // (cols // LOW)) * cols
                out_ref[modes, at : at + cols] = packed.astype(jnp.bfloat16)


def coupled_sums(matrix, state, borders, weights, right, first, scale, both):
    blocks, fields, width, depth = matrix.shape
    cells = state.shape[1]
    height = weights.shape[0] // (5 * fields)
    cols = cells // height
    mode_count = lax.axis_size("mode")
    slab_count = lax.axis_size("slab")
    place = [
        (t % mode_count) * slab_count + t // mode_count for t in range(mode_count * slab_count)
    ]
    onward = list(zip(place, place[1:] + place[:1]))
    above = lax.ppermute(borders[1], both, onward)
    below = lax.ppermute(borders[0], both, [(b, a) for a, b in onward])
    unroll = math.gcd(blocks, UNROLL)
    matrix_spec = pl.BlockSpec((unroll, fields, width, depth), lambda i: (i, 0, 0, 0))
    weight_spec = pl.BlockSpec(weights.shape, lambda i: (0, 0))
    sums_spec = pl.BlockSpec((unroll * width, cells), lambda i: (i, 0))
    moved = 2 * unroll * fields * width * depth * matrix.dtype.itemsize
    params = pltpu.CompilerParams(vmem_limit_bytes=2 * SMALL_VMEM_BYTES + moved)
    inner = pl.pallas_call(
        functools.partial(inner_kernel, height, cols),
        grid=(blocks // unroll,),
        in_specs=[matrix_spec, pl.BlockSpec((depth, cells), lambda i: (0, 0)), weight_spec],
        out_specs=sums_spec,
        out_shape=jax.ShapeDtypeStruct((blocks * width, cells), jnp.float32),
        scratch_shapes=[pltpu.VMEM((unroll * fields * width, cells), jnp.float32)],
        cost_estimate=pl.CostEstimate(
            flops=2 * matrix.size * cells, bytes_accessed=2 * matrix.size, transcendentals=0
        ),
        compiler_params=params,
    )(matrix, state, weights)
    border_spec = pl.BlockSpec((depth, cols), lambda i: (0, 0))
    sent = cells + (low_tiles(height, cols) * cols if first else 0)
    return pl.pallas_call(
        functools.partial(border_kernel, height, cols, first, scale),
        grid=(blocks // unroll,),
        in_specs=[
            matrix_spec,
            border_spec,
            border_spec,
            weight_spec,
            sums_spec,
            pl.BlockSpec(right.shape, lambda i: (0, 0)),
        ],
        out_specs=pl.BlockSpec((unroll * width, sent), lambda i: (i, 0)),
        out_shape=jax.ShapeDtypeStruct((blocks * width, sent), jnp.bfloat16),
        compiler_params=params,
    )(matrix, above, below, weights, inner, right)


TOGETHER = 16
MEAN_TOGETHER = 8
GROUP = 16


def solve(spectral, right_ref, left_ref, scale_ref):
    ny = spectral[0].shape[1]
    wide = along_rows(jnp.concatenate(spectral, axis=1), left_ref)
    wide = wide * jnp.concatenate([scale_ref[...]] * len(spectral), axis=1)
    wide = along_rows(wide, left_ref)
    return along_cols([wide[:, i * ny : (i + 1) * ny] for i in range(len(spectral))], right_ref)


def mean_fields(current_ref, right_side_ref, weight_ref, start):
    nx, ny = weight_ref.shape[1:]
    values = []
    for mode in range(start, start + MEAN_TOGETHER):
        here = current_ref[:, mode].reshape(nx, ny)
        mean = (
            weight_ref[0] * here
            - weight_ref[1] * pltpu.roll(here, 1, 0)
            - weight_ref[2] * pltpu.roll(here, nx - 1, 0)
            - pltpu.roll(weight_ref[4] * here, 1, 1)
            - pltpu.roll(weight_ref[3] * here, ny - 1, 1)
        )
        values.append(right_side_ref[:, mode].reshape(nx, ny) - mean)
    return values


def first_mean_kernel(slabs, place_ref, *refs):
    current_parts = refs[:slabs]
    right_side_parts = refs[slabs : 2 * slabs]
    weight_ref, right_ref, current_ref, right_side_ref, out_ref = refs[2 * slabs :]
    for shift in range(slabs):
        slab = in_order(place_ref[0], shift, slabs)
        current_ref[slab] = current_parts[shift][0]
        right_side_ref[slab] = right_side_parts[shift][0]
    shape = (slabs,) + out_ref.shape[2:]
    for start in range(0, out_ref.shape[1], MEAN_TOGETHER):
        values = mean_fields(current_ref, right_side_ref, weight_ref, start)
        for i, value in enumerate(along_cols(values, right_ref)):
            out_ref[:, start + i] = value.reshape(shape)


def mean_kernel(current_ref, right_side_ref, weight_ref, out_ref):
    shape = out_ref.shape[:1] + out_ref.shape[2:]
    for start in range(0, out_ref.shape[1], MEAN_TOGETHER):
        values = mean_fields(current_ref, right_side_ref, weight_ref, start)
        for i, value in enumerate(values):
            out_ref[:, start + i] = value.reshape(shape)


def turn_in(turned_ref, coupled_ref, mode_count, slab_count, height, first, scale):
    group = coupled_ref.shape[1]
    ny = turned_ref.shape[1]
    low_col = lax.broadcasted_iota(jnp.int32, (group, ny), 1) < LOW
    for source in range(mode_count * slab_count):
        start = ((source % slab_count) * mode_count + source // slab_count) * height
        for r in range(height):
            code = coupled_ref[source, :, r * ny : (r + 1) * ny]
            value = decode(code, FIRST_POWER if first else SUM_POWER)
            if first:
                at = (height + r // (ny // LOW)) * ny
                rest = coupled_ref[source, :, at : at + ny].astype(jnp.float32)
                place = r % (ny // LOW)
                rest = pltpu.roll(rest, ny - place * LOW, 1) if place else rest
                value = value + jnp.where(low_col, rest, 0.0)
            turned_ref[(start + r) * group : (start + r + 1) * group, :] = value * (1.0 / scale)


def step_kernel(
    mode_count,
    slab_count,
    code_scale,
    current_ref,
    base_ref,
    coupled_ref,
    right_ref,
    left_ref,
    scale_ref,
    solution_ref,
    state_ref,
    turned_ref,
):
    nx, ny = scale_ref.shape
    group = coupled_ref.shape[1]
    height = nx // (mode_count * slab_count)
    turn_in(turned_ref, coupled_ref, mode_count, slab_count, height, True, code_scale)

    def several(number, carry):
        start = number * TOGETHER
        resid = []
        for i in range(TOGETHER):
            coupled = turned_ref[pl.ds(start + i, nx, stride=group), :]
            resid.append(base_ref[:, start + i].reshape(nx, ny) - coupled)
        change = solve(resid, right_ref, left_ref, scale_ref)
        for i in range(TOGETHER):
            value = current_ref[:, start + i].reshape(nx, ny) + change[i]
            solution_ref[:, start + i] = value.reshape(slab_count, nx // slab_count, ny)
            turned_ref[pl.ds(start + i, nx, stride=group), :] = value
        return carry

    lax.fori_loop(0, group // TOGETHER, several, 0)

    for target in range(mode_count * slab_count):
        start = ((target % slab_count) * mode_count + target // slab_count) * height
        for r in range(height):
            row = start + r
            value = turned_ref[row * group : (row + 1) * group, :].astype(jnp.bfloat16)
            state_ref[target, :, r * ny : (r + 1) * ny] = value


def residual_kernel(
    mode_count, slab_count, code_scale, here_ref, base_ref, coupled_ref, out_ref, *refs
):
    *code_refs, turned_ref = refs
    group = coupled_ref.shape[1]
    ny = base_ref.shape[-1]
    nx = turned_ref.shape[0] // group
    height = nx // (mode_count * slab_count)
    turn_in(turned_ref, coupled_ref, mode_count, slab_count, height, False, code_scale)

    def one(mode, carry):
        coupled = turned_ref[pl.ds(mode, nx, stride=group), :]
        out_ref[:, mode] = base_ref[:, mode] - coupled.reshape(slab_count, nx // slab_count, ny)
        return carry

    lax.fori_loop(0, group, one, 0)
    for shift, code_ref in enumerate(code_refs):
        slab = lax.rem(here_ref[0] + shift, slab_count)
        code_ref[0] = encode(out_ref[slab] * code_scale, SUM_POWER)


def correct_kernel(code_scale, current_ref, resid_ref, right_ref, left_ref, scale_ref, out_ref):
    nx, ny = scale_ref.shape

    def several(number, carry):
        start = number * TOGETHER
        resid = [resid_ref[:, start + i].reshape(nx, ny) for i in range(TOGETHER)]
        change = solve(along_cols(resid, right_ref), right_ref, left_ref, scale_ref)
        for i in range(TOGETHER):
            shape = out_ref.shape[:1] + out_ref.shape[2:]
            value = current_ref[:, start + i] + change[i].reshape(shape)
            out_ref[:, start + i] = encode(value * code_scale, SOLUTION_POWER)
        return carry

    lax.fori_loop(0, out_ref.shape[1] // TOGETHER, several, 0)


def whole(array):
    return pl.BlockSpec(array.shape, lambda g: (0,) * array.ndim)


def slabs_of(array):
    slab_count, _, rows, ny = array.shape
    return pl.BlockSpec((slab_count, GROUP, rows, ny), lambda g: (0, g, 0, 0))


def strips_of(shape):
    return pl.BlockSpec((shape[0], GROUP, shape[2]), lambda g: (0, g, 0))


def per_group(
    kernel, groups, operands, in_specs, out_shape, out_specs, scratch=(), flops=0, vmem=SHARED_VMEM_BYTES
):
    moved = sum(a.size * a.dtype.itemsize for a in operands)
    return pl.pallas_call(
        kernel,
        grid=(groups,),
        in_specs=in_specs,
        out_specs=out_specs,
        out_shape=out_shape,
        scratch_shapes=scratch,
        cost_estimate=pl.CostEstimate(flops=flops, bytes_accessed=2 * moved, transcendentals=0),
        compiler_params=pltpu.CompilerParams(vmem_limit_bytes=vmem),
    )(*operands)


def first_mean_part(place, current_parts, right_side_parts, weights, right):
    slabs = len(right_side_parts)
    _, modes, rows, ny = right_side_parts[0].shape
    part = pl.BlockSpec((1, GROUP, rows, ny), lambda g, *_: (0, g, 0, 0))
    slab = pl.BlockSpec((slabs, GROUP, rows, ny), lambda g, *_: (0, g, 0, 0))
    shape = jax.ShapeDtypeStruct((slabs, modes, rows, ny), jnp.float32)
    return pl.pallas_call(
        functools.partial(first_mean_kernel, slabs),
        grid_spec=pltpu.PrefetchScalarGridSpec(
            num_scalar_prefetch=1,
            grid=(modes // GROUP,),
            in_specs=[part] * (2 * slabs)
            + [
                pl.BlockSpec(weights.shape, lambda g, *_: (0, 0, 0)),
                pl.BlockSpec(right.shape, lambda g, *_: (0, 0)),
            ],
            out_specs=[slab] * 3,
        ),
        out_shape=[shape] * 3,
        compiler_params=pltpu.CompilerParams(vmem_limit_bytes=VMEM_BYTES),
    )(place, *current_parts, *right_side_parts, weights, right)


def mean_part(current, right_side, weights):
    slabs = slabs_of(right_side)
    return per_group(
        mean_kernel,
        right_side.shape[1] // GROUP,
        (current, right_side, weights),
        [slabs, slabs, whole(weights)],
        jax.ShapeDtypeStruct(right_side.shape, jnp.float32),
        slabs,
    )


def solve_flops(array, tables):
    nx, ny = tables[2].shape
    return array.shape[1] * 8 * 3 * nx * ny * (nx + ny) // 2


def step(current, base, coupled, tables, mode_count, slab_count, code_scale):
    nx, ny = tables[2].shape
    slabs = slabs_of(base)
    devices, modes, _ = coupled.shape
    state = (devices, modes, nx // devices * ny)
    return per_group(
        functools.partial(step_kernel, mode_count, slab_count, code_scale),
        modes // GROUP,
        (current, base, coupled, *tables),
        [slabs, slabs, strips_of(coupled.shape), *map(whole, tables)],
        [
            jax.ShapeDtypeStruct(base.shape, jnp.float32),
            jax.ShapeDtypeStruct(state, jnp.bfloat16),
        ],
        [slabs, strips_of(state)],
        [pltpu.VMEM((nx * GROUP, ny), jnp.float32)],
        solve_flops(base, tables),
    )


def last_residual(base, coupled, mode_count, slab_count, code_scale):
    slab, modes, rows, ny = base.shape
    slabs = pl.BlockSpec((slab, GROUP, rows, ny), lambda g, *_: (0, g, 0, 0))
    part = pl.BlockSpec((1, GROUP, rows, ny), lambda g, *_: (0, g, 0, 0))
    devices, _, cells = coupled.shape
    out, *parts = pl.pallas_call(
        functools.partial(residual_kernel, mode_count, slab_count, code_scale),
        grid_spec=pltpu.PrefetchScalarGridSpec(
            num_scalar_prefetch=1,
            grid=(modes // GROUP,),
            in_specs=[slabs, pl.BlockSpec((devices, GROUP, cells), lambda g, *_: (0, g, 0))],
            out_specs=[slabs] + [part] * slab,
            scratch_shapes=[pltpu.VMEM((slab * rows * GROUP, ny), jnp.float32)],
        ),
        out_shape=[jax.ShapeDtypeStruct(base.shape, jnp.float32)]
        + [jax.ShapeDtypeStruct((1, modes, rows, ny), jnp.bfloat16)] * slab,
        cost_estimate=pl.CostEstimate(
            flops=0, bytes_accessed=2 * base.size * 4, transcendentals=0
        ),
        compiler_params=pltpu.CompilerParams(vmem_limit_bytes=SHARED_VMEM_BYTES),
    )(lax.axis_index("slab").reshape(1), base, coupled)
    return out, parts


def correct(current, resid, tables, code_scale):
    slabs = slabs_of(resid)
    return per_group(
        functools.partial(correct_kernel, code_scale),
        resid.shape[1] // GROUP,
        (current, resid, *tables),
        [slabs, slabs, *map(whole, tables)],
        jax.ShapeDtypeStruct(resid.shape, jnp.bfloat16),
        slabs,
        (),
        solve_flops(resid, tables),
    )


def collect(parts, axis):
    count = lax.axis_size(axis)
    here = lax.axis_index(axis)
    out = jnp.zeros((count,) + parts[0].shape[1:], parts[0].dtype)
    for shift, part in enumerate(parts):
        source = lax.rem(here + count - shift, count)
        out = lax.dynamic_update_slice_in_dim(out, part, source, 0)
    return out


def onwards(part, axis, shift):
    count = lax.axis_size(axis)
    return lax.ppermute(part, axis, [(i, (i + shift) % count) for i in range(count)])


def parts_of(block, axis):
    count = lax.axis_size(axis)
    here = lax.axis_index(axis)
    return [
        lax.dynamic_index_in_dim(block, lax.rem(here + shift, count), 0) for shift in range(count)
    ]


def moved_parts(parts, axis):
    return [parts[0]] + [onwards(parts[i], axis, i) for i in range(1, len(parts))]


def local(guess, right_side, mean_coef, field_coef, coupling, coupling_list, pair_count):
    mode_count = lax.axis_size("mode")
    slab_count = lax.axis_size("slab")
    both = ("mode", "slab")
    modes, rows, cols = guess.shape
    fields = field_coef.shape[0]
    nx = rows * slab_count
    devices = mode_count * slab_count
    height = nx // devices
    share = modes // slab_count

    strips = pack_strips(guess, mode_count)
    coefs = jnp.concatenate([mean_coef[None], field_coef], 0)[None]
    strips, coefs = lax.optimization_barrier((strips, coefs))
    state = lax.all_to_all(strips, "mode", 0, 0, tiled=True)
    state = state.reshape(mode_count * modes, height * cols)

    def to_slabs(block):
        flat = block.reshape(modes, rows, cols)
        return lax.all_to_all(flat, "slab", 0, 0, tiled=True)

    matrix = dense_coupling(coupling, coupling_list, pair_count, fields)

    slab = lax.axis_index("slab")
    place = jnp.stack([slab, slab * mode_count + lax.axis_index("mode")])
    forward = [(i, i + 1) for i in range(slab_count - 1)]
    low = lax.ppermute(coefs[0, :, -1], "slab", forward)
    high = lax.ppermute(coefs[0, :, 0], "slab", [(b, a) for a, b in forward])
    strip_weights = strip_weights_of(coefs[0], low, high, place, slab_count, height)

    guess_parts = parts_of(guess.reshape(slab_count, share, rows, cols), "slab")
    guess_parts = [jnp.concatenate([part, coefs], axis=1) for part in guess_parts]
    guess_parts = moved_parts(guess_parts, "slab")
    right_parts = parts_of(right_side.reshape(slab_count, share, rows, cols), "slab")
    state, guess_parts, right_parts, strip_weights = lax.optimization_barrier(
        (state, guess_parts, right_parts, strip_weights)
    )
    borders = (state[:, :cols], state[:, -cols:])
    right_parts = moved_parts(right_parts, "slab")
    mean_weights = mean_weights_of(guess_parts, place, fields + 1)

    row_high, row_low = split_table(sine_table(nx))
    col_high, col_low = split_table(sine_table(cols))
    tables = (
        jnp.concatenate(
            [
                jnp.concatenate([col_high, col_low], 1),
                jnp.concatenate([col_high, jnp.zeros_like(col_low)], 1),
            ],
            0,
        ),
        jnp.concatenate(
            [
                jnp.concatenate([row_high, row_high], 1),
                jnp.concatenate([row_low, jnp.zeros_like(row_low)], 1),
            ],
            0,
        ),
        RELAXATION / eigen_table(nx, cols),
    )

    first_scale, sum_scale, solution_scale = code_scales(nx, cols, coupling.shape[1], modes)

    sums = coupled_sums(
        matrix, state, borders, strip_weights, tables[0], True, first_scale, both
    )
    sums, right_parts = lax.optimization_barrier((sums, right_parts))
    sums = lax.all_to_all(sums, both, 0, 0, tiled=True).reshape(devices, share, -1)
    current, right_side, base = first_mean_part(
        place, guess_parts, right_parts, mean_weights, tables[0]
    )
    current, state = step(current, base, sums, tables, mode_count, slab_count, first_scale)
    state = state.reshape(devices * share, height * cols)
    state = lax.all_to_all(state, both, 0, 0, tiled=True)

    base = mean_part(current, right_side, mean_weights)
    borders = (state[:, :cols], state[:, -cols:])
    sums = coupled_sums(
        matrix, state, borders, strip_weights, tables[0], False, sum_scale, both
    )
    sums = lax.all_to_all(sums, both, 0, 0, tiled=True).reshape(devices, share, -1)
    resid, parts = last_residual(base, sums, mode_count, slab_count, sum_scale)
    moved = collect(moved_parts(parts, "slab"), "slab").reshape(modes, rows, cols)
    resid_out = decode(moved, SUM_POWER) * (1.0 / sum_scale)
    code = correct(current, resid, tables, solution_scale)
    return decode(to_slabs(code), SOLUTION_POWER) * (1.0 / solution_scale), resid_out


def solution(mesh):
    placed = (
        P("mode", "slab", None),
        P("mode", "slab", None),
        P("slab", None),
        P(None, "slab", None),
        P(),
        P(),
        P(),
    )
    return jax.shard_map(
        local,
        mesh=mesh,
        in_specs=placed,
        out_specs=(P("mode", "slab", None), P("mode", "slab", None)),
        check_vma=False,
    )
```

```python
import functools
import math

import jax
import jax.numpy as jnp
from jax import lax
from jax.experimental import pallas as pl
from jax.experimental.pallas import tpu as pltpu
from jax.sharding import PartitionSpec as P

RELAXATION = 0.6
VMEM_BYTES = 60 << 20
SHARED_VMEM_BYTES = 48 << 20
SMALL_VMEM_BYTES = 9 << 20
UNROLL = 2


def sine_table(length):
    counter = jnp.arange(length).astype(jnp.float32) + 1.0
    angle = math.pi * counter[:, None] * counter[None, :] / (length + 1)
    return math.sqrt(2.0 / (length + 1)) * jnp.sin(angle)


def eigen_table(first, second):
    along_first = 2.0 * jnp.cos(
        math.pi * (jnp.arange(first).astype(jnp.float32) + 1.0) / (first + 1)
    )
    along_second = 2.0 * jnp.cos(
        math.pi * (jnp.arange(second).astype(jnp.float32) + 1.0) / (second + 1)
    )
    return 4.0 - along_first[:, None] - along_second[None, :]


def stencil_weights(coef):
    nx, ny = coef.shape
    row = lax.broadcasted_iota(jnp.int32, (nx, ny), 0)
    col = lax.broadcasted_iota(jnp.int32, (nx, ny), 1)
    sides = (
        (pltpu.roll(coef, 1, 0), row == 0),
        (pltpu.roll(coef, nx - 1, 0), row == nx - 1),
        (pltpu.roll(coef, 1, 1), col == 0),
        (pltpu.roll(coef, ny - 1, 1), col == ny - 1),
    )
    centre = 0.0
    weights = []
    for other, outside in sides:
        weight = 0.5 * (coef + jnp.where(outside, coef, other))
        centre = centre + weight
        weights.append(jnp.where(outside, 0.0, weight))
    return [centre] + weights


def in_order(here, shift, count):
    return lax.rem(here + count - shift, count)


def in_order(here, shift, count):
    return lax.rem(here + count - shift, count)


def strip_weights_kernel(slabs, height, place_ref, *refs):
    part_refs = refs[:slabs]
    out_ref, coef_ref = refs[slabs:]
    _, nx, ny = coef_ref.shape
    rows = nx // slabs
    fields = out_ref.shape[0] // (5 * height)
    for shift, part_ref in enumerate(part_refs):
        start = in_order(place_ref[0], shift, slabs) * rows
        coef_ref[:, pl.ds(pl.multiple_of(start, rows), rows), :] = part_ref[0]
    col = lax.broadcasted_iota(jnp.int32, (1, ny), 1)
    first = place_ref[1] * height
    for f in range(fields):
        lines = []
        for r in range(-1, height + 1):
            at = jnp.clip(first + r, 0, nx - 1)
            lines.append(coef_ref[f + 1, pl.ds(at, 1), :])
        for r in range(height):
            here = lines[r + 1]
            up = 0.5 * (here + lines[r])
            down = 0.5 * (here + lines[r + 2])
            left = 0.5 * (here + jnp.where(col == 0, here, pltpu.roll(here, 1, 1)))
            right = 0.5 * (here + jnp.where(col == ny - 1, here, pltpu.roll(here, ny - 1, 1)))
            weights = (
                up + down + left + right,
                jnp.where(first + r == 0, 0.0, up),
                jnp.where(first + r == nx - 1, 0.0, down),
                jnp.where(col == 0, 0.0, left),
                jnp.where(col == ny - 1, 0.0, right),
            )
            for which, weight in enumerate(weights):
                at = (f * 5 + which) * height + r
                out_ref[at : at + 1, :] = weight


def mean_weights_kernel(slabs, place_ref, *refs):
    part_refs = refs[:slabs]
    out_ref, coef_ref = refs[slabs:]
    _, nx, ny = out_ref.shape
    for shift, part_ref in enumerate(part_refs):
        coef_ref[in_order(place_ref[0], shift, slabs)] = part_ref[0, 0]
    for which, weight in enumerate(stencil_weights(coef_ref[...].reshape(nx, ny))):
        out_ref[which] = weight


def weights_of(kernel, parts, place, coefs, out, scratch):
    _, entries, rows, ny = parts[0].shape
    last = entries // coefs - 1
    return pl.pallas_call(
        kernel,
        grid_spec=pltpu.PrefetchScalarGridSpec(
            num_scalar_prefetch=1,
            grid=(1,),
            in_specs=[pl.BlockSpec((1, coefs, rows, ny), lambda i, *_: (0, last, 0, 0))]
            * len(parts),
            out_specs=pl.BlockSpec(out, lambda i, *_: (0,) * len(out)),
            scratch_shapes=[pltpu.VMEM(scratch, jnp.float32)],
        ),
        out_shape=jax.ShapeDtypeStruct(out, jnp.float32),
        compiler_params=pltpu.CompilerParams(vmem_limit_bytes=SMALL_VMEM_BYTES),
    )(place, *parts)


def strip_weights_of(parts, place, coefs, height):
    slabs = len(parts)
    _, _, rows, ny = parts[0].shape
    kernel = functools.partial(strip_weights_kernel, slabs, height)
    out = ((coefs - 1) * 5 * height, ny)
    return weights_of(kernel, parts, place, coefs, out, (coefs, slabs * rows, ny))


def mean_weights_of(parts, place, coefs):
    slabs = len(parts)
    _, _, rows, ny = parts[0].shape
    kernel = functools.partial(mean_weights_kernel, slabs)
    return weights_of(kernel, parts, place, coefs, (5, slabs * rows, ny), (slabs, rows, ny))


def split(value):
    high = value.astype(jnp.bfloat16)
    low = (value - high.astype(jnp.float32)).astype(jnp.bfloat16)
    return high, low


def split_table(value):
    high = lax.reduce_precision(value, 8, 7)
    return high.astype(jnp.bfloat16), (value - high).astype(jnp.bfloat16)


LOW = 32
FIRST_POWER = 7
SUM_POWER = 5
SOLUTION_POWER = 4


def encode(value, power):
    square = value * value
    if power == 4:
        result = square * (value * jnp.abs(value))
    elif power == 5:
        result = square * square * value
    else:
        result = (square * square) * (square * value)
    return result.astype(jnp.bfloat16)


def decode(code, power):
    code = code.astype(jnp.float32)
    size = jnp.abs(code)
    value = jnp.exp(jnp.log(size) * (1.0 / power))
    value = jnp.where(size > 0.0, value, 0.0)
    return jnp.where(code < 0.0, -value, value)


def code_scales(nx, ny, entries, width):
    guess_max, mean_max, field_max, coupling_max = 6.0, 2.0, 2.5, 0.0625
    gain = 8.0 * field_max * entries * width * coupling_max * 1.01
    inverse = (min(nx, ny) + 1) ** 2 / 8.0

    def bound(iterate):
        return guess_max + (8.0 * mean_max + gain) * iterate

    change = RELAXATION * inverse * 1.01
    second = guess_max + change * bound(guess_max)
    third = second + change * bound(second)

    def scale(limit, power):
        return 0.8 * 2.0 ** (127.0 / power) / limit

    first = math.sqrt(2.0 * ny) * gain * guess_max
    return (
        min(1.0, scale(first, FIRST_POWER)),
        min(1.0, scale(bound(second), SUM_POWER)),
        min(1.0, scale(third, SOLUTION_POWER)),
    )


def pack_kernel(rows, height, x_ref, out_ref):
    strips, modes, cells = out_ref.shape
    cols = cells // height
    for strip in range(strips):
        for r in range(height):
            value = x_ref[pl.ds(strip * height + r, modes, stride=rows), :]
            out_ref[strip, :, r * cols : (r + 1) * cols] = value.astype(jnp.bfloat16)


def pack_strips(block, strips):
    modes, rows, cols = block.shape
    height = rows // strips
    return pl.pallas_call(
        functools.partial(pack_kernel, rows, height),
        grid=(2,),
        in_specs=[pl.BlockSpec((modes // 2 * rows, cols), lambda g: (g, 0))],
        out_specs=pl.BlockSpec((strips, modes // 2, height * cols), lambda g: (0, g, 0)),
        out_shape=jax.ShapeDtypeStruct((strips, modes, height * cols), jnp.bfloat16),
        compiler_params=pltpu.CompilerParams(vmem_limit_bytes=VMEM_BYTES),
    )(block.reshape(modes * rows, cols))


def dense_kernel(fields, entry_ref, count_ref, coupling_ref, out_ref):
    block = pl.program_id(0)
    width = coupling_ref.shape[-1]
    out_ref[...] = jnp.zeros_like(out_ref)

    def place(k, carry):
        entry = entry_ref[block, k]
        column = pl.multiple_of((entry // fields) * width, width)
        out_ref[0, entry % fields, :, pl.ds(column, width)] = coupling_ref[0, k]
        return carry

    lax.fori_loop(0, count_ref[block], place, 0)


def dense_coupling(coupling, coupling_list, pair_count, fields):
    blocks, entries, width, _ = coupling.shape
    moved = 2 * width * width * (entries + fields * blocks) * coupling.dtype.itemsize
    return pl.pallas_call(
        functools.partial(dense_kernel, fields),
        grid_spec=pltpu.PrefetchScalarGridSpec(
            num_scalar_prefetch=2,
            grid=(blocks,),
            in_specs=[pl.BlockSpec((1, entries, width, width), lambda i, *_: (i, 0, 0, 0))],
            out_specs=pl.BlockSpec(
                (1, fields, width, blocks * width), lambda i, *_: (i, 0, 0, 0)
            ),
        ),
        out_shape=jax.ShapeDtypeStruct((blocks, fields, width, blocks * width), coupling.dtype),
        compiler_params=pltpu.CompilerParams(vmem_limit_bytes=SMALL_VMEM_BYTES + moved),
    )(coupling_list, pair_count, coupling)


def low_tiles(height, cols):
    return -(-height * LOW // cols)


def along_cols(fields, right_ref):
    size, ny = fields[0].shape
    high, low = split(jnp.concatenate(fields, axis=0))
    both = jnp.dot(
        jnp.concatenate([high, low], axis=1), right_ref[...], preferred_element_type=jnp.float32
    )
    both = both[:, :ny] + both[:, ny:]
    return [both[i * size : (i + 1) * size] for i in range(len(fields))]


def along_rows(wide, left_ref):
    nx = wide.shape[0]
    high, low = split(wide)
    both = jnp.dot(
        left_ref[...], jnp.concatenate([high, low], axis=0), preferred_element_type=jnp.float32
    )
    return both[:nx] + both[nx:]


def weight_row(weight_ref, height, field, which, r):
    at = (field * 5 + which) * height + r
    return weight_ref[at : at + 1, :]


def inner_kernel(height, cols, matrix_ref, state_ref, weight_ref, out_ref, sums_ref):
    blocks, fields, width, depth = matrix_ref.shape
    sums_ref[...] = jnp.dot(
        matrix_ref[...].reshape(blocks * fields * width, depth),
        state_ref[...],
        preferred_element_type=jnp.float32,
    )
    for block in range(blocks):
        for r in range(height):
            total = 0.0
            from_left = 0.0
            from_right = 0.0
            for f in range(fields):

                def row(at):
                    start = (block * fields + f) * width
                    return sums_ref[start : start + width, at * cols : (at + 1) * cols]

                weight = functools.partial(weight_row, weight_ref, height, f)
                here = row(r)
                total = total + weight(0, r) * here
                if r > 0:
                    total = total - weight(1, r) * row(r - 1)
                if r < height - 1:
                    total = total - weight(2, r) * row(r + 1)
                from_left = from_left + weight(4, r) * here
                from_right = from_right + weight(3, r) * here
            total = total - pltpu.roll(from_left, 1, 1) - pltpu.roll(from_right, cols - 1, 1)
            out_ref[block * width : (block + 1) * width, r * cols : (r + 1) * cols] = total


def border_kernel(
    height,
    cols,
    first,
    scale,
    matrix_ref,
    above_ref,
    below_ref,
    weight_ref,
    inner_ref,
    right_ref,
    out_ref,
):
    blocks, fields, width, depth = matrix_ref.shape
    border = jnp.concatenate([above_ref[...], below_ref[...]], axis=1)
    low_col = lax.broadcasted_iota(jnp.int32, (width, cols), 1) < LOW
    matrix = matrix_ref[...].reshape(blocks * fields * width, depth)
    sums = jnp.dot(matrix, border, preferred_element_type=jnp.float32)
    for block in range(blocks):
        modes = slice(block * width, (block + 1) * width)
        rows = []
        for r in range(height):
            total = inner_ref[modes, r * cols : (r + 1) * cols]
            for f in range(fields):
                part = sums[(block * fields + f) * width : (block * fields + f + 1) * width]
                if r == 0:
                    total = total - weight_row(weight_ref, height, f, 1, r) * part[:, :cols]
                if r == height - 1:
                    total = total - weight_row(weight_ref, height, f, 2, r) * part[:, cols:]
            rows.append(total)
        if not first:
            for r in range(height):
                code = encode(rows[r] * scale, SUM_POWER)
                out_ref[modes, r * cols : (r + 1) * cols] = code
            continue
        rows = along_cols(rows, right_ref)
        for r in range(height):
            value = rows[r] * scale
            code = encode(value, FIRST_POWER)
            out_ref[modes, r * cols : (r + 1) * cols] = code
            rest = jnp.where(low_col, value - decode(code, FIRST_POWER), 0.0)
            place = r % (cols // LOW)
            rest = pltpu.roll(rest, place * LOW, 1) if place else rest
            packed = rest if place == 0 else packed + rest
            if place == cols // LOW - 1 or r == height - 1:
                at = (height + r // (cols // LOW)) * cols
                out_ref[modes, at : at + cols] = packed.astype(jnp.bfloat16)


def coupled_sums(matrix, state, weights, right, first, scale, both):
    blocks, fields, width, depth = matrix.shape
    cells = state.shape[1]
    height = weights.shape[0] // (5 * fields)
    cols = cells // height
    mode_count = lax.axis_size("mode")
    slab_count = lax.axis_size("slab")
    place = [
        (t % mode_count) * slab_count + t // mode_count for t in range(mode_count * slab_count)
    ]
    onward = list(zip(place, place[1:] + place[:1]))
    above = lax.ppermute(state[:, -cols:], both, onward)
    below = lax.ppermute(state[:, :cols], both, [(b, a) for a, b in onward])
    unroll = math.gcd(blocks, UNROLL)
    matrix_spec = pl.BlockSpec((unroll, fields, width, depth), lambda i: (i, 0, 0, 0))
    weight_spec = pl.BlockSpec(weights.shape, lambda i: (0, 0))
    sums_spec = pl.BlockSpec((unroll * width, cells), lambda i: (i, 0))
    moved = 2 * unroll * fields * width * depth * matrix.dtype.itemsize
    params = pltpu.CompilerParams(vmem_limit_bytes=2 * SMALL_VMEM_BYTES + moved)
    inner = pl.pallas_call(
        functools.partial(inner_kernel, height, cols),
        grid=(blocks // unroll,),
        in_specs=[matrix_spec, pl.BlockSpec((depth, cells), lambda i: (0, 0)), weight_spec],
        out_specs=sums_spec,
        out_shape=jax.ShapeDtypeStruct((blocks * width, cells), jnp.float32),
        scratch_shapes=[pltpu.VMEM((unroll * fields * width, cells), jnp.float32)],
        cost_estimate=pl.CostEstimate(
            flops=2 * matrix.size * cells, bytes_accessed=2 * matrix.size, transcendentals=0
        ),
        compiler_params=params,
    )(matrix, state, weights)
    border_spec = pl.BlockSpec((depth, cols), lambda i: (0, 0))
    sent = cells + (low_tiles(height, cols) * cols if first else 0)
    return pl.pallas_call(
        functools.partial(border_kernel, height, cols, first, scale),
        grid=(blocks // unroll,),
        in_specs=[
            matrix_spec,
            border_spec,
            border_spec,
            weight_spec,
            sums_spec,
            pl.BlockSpec(right.shape, lambda i: (0, 0)),
        ],
        out_specs=pl.BlockSpec((unroll * width, sent), lambda i: (i, 0)),
        out_shape=jax.ShapeDtypeStruct((blocks * width, sent), jnp.bfloat16),
        compiler_params=params,
    )(matrix, above, below, weights, inner, right)


TOGETHER = 16
MEAN_TOGETHER = 8
GROUP = 16


def solve(spectral, right_ref, left_ref, scale_ref):
    ny = spectral[0].shape[1]
    wide = along_rows(jnp.concatenate(spectral, axis=1), left_ref)
    wide = wide * jnp.concatenate([scale_ref[...]] * len(spectral), axis=1)
    wide = along_rows(wide, left_ref)
    return along_cols([wide[:, i * ny : (i + 1) * ny] for i in range(len(spectral))], right_ref)


def mean_fields(current_ref, right_side_ref, weight_ref, start):
    nx, ny = weight_ref.shape[1:]
    values = []
    for mode in range(start, start + MEAN_TOGETHER):
        here = current_ref[:, mode].reshape(nx, ny)
        mean = (
            weight_ref[0] * here
            - weight_ref[1] * pltpu.roll(here, 1, 0)
            - weight_ref[2] * pltpu.roll(here, nx - 1, 0)
            - pltpu.roll(weight_ref[4] * here, 1, 1)
            - pltpu.roll(weight_ref[3] * here, ny - 1, 1)
        )
        values.append(right_side_ref[:, mode].reshape(nx, ny) - mean)
    return values


def first_mean_kernel(slabs, place_ref, *refs):
    current_parts = refs[:slabs]
    right_side_parts = refs[slabs : 2 * slabs]
    weight_ref, right_ref, current_ref, right_side_ref, out_ref = refs[2 * slabs :]
    for shift in range(slabs):
        slab = in_order(place_ref[0], shift, slabs)
        current_ref[slab] = current_parts[shift][0]
        right_side_ref[slab] = right_side_parts[shift][0]
    shape = (slabs,) + out_ref.shape[2:]
    for start in range(0, out_ref.shape[1], MEAN_TOGETHER):
        values = mean_fields(current_ref, right_side_ref, weight_ref, start)
        for i, value in enumerate(along_cols(values, right_ref)):
            out_ref[:, start + i] = value.reshape(shape)


def mean_kernel(current_ref, right_side_ref, weight_ref, out_ref):
    shape = out_ref.shape[:1] + out_ref.shape[2:]
    for start in range(0, out_ref.shape[1], MEAN_TOGETHER):
        values = mean_fields(current_ref, right_side_ref, weight_ref, start)
        for i, value in enumerate(values):
            out_ref[:, start + i] = value.reshape(shape)


def turn_in(turned_ref, coupled_ref, mode_count, slab_count, height, first, scale):
    group = coupled_ref.shape[1]
    ny = turned_ref.shape[1]
    low_col = lax.broadcasted_iota(jnp.int32, (group, ny), 1) < LOW
    for source in range(mode_count * slab_count):
        start = ((source % slab_count) * mode_count + source // slab_count) * height
        for r in range(height):
            code = coupled_ref[source, :, r * ny : (r + 1) * ny]
            value = decode(code, FIRST_POWER if first else SUM_POWER)
            if first:
                at = (height + r // (ny // LOW)) * ny
                rest = coupled_ref[source, :, at : at + ny].astype(jnp.float32)
                place = r % (ny // LOW)
                rest = pltpu.roll(rest, ny - place * LOW, 1) if place else rest
                value = value + jnp.where(low_col, rest, 0.0)
            turned_ref[(start + r) * group : (start + r + 1) * group, :] = value * (1.0 / scale)


def step_kernel(
    mode_count,
    slab_count,
    code_scale,
    current_ref,
    base_ref,
    coupled_ref,
    right_ref,
    left_ref,
    scale_ref,
    solution_ref,
    state_ref,
    turned_ref,
):
    nx, ny = scale_ref.shape
    group = coupled_ref.shape[1]
    height = nx // (mode_count * slab_count)
    turn_in(turned_ref, coupled_ref, mode_count, slab_count, height, True, code_scale)

    def several(number, carry):
        start = number * TOGETHER
        resid = []
        for i in range(TOGETHER):
            coupled = turned_ref[pl.ds(start + i, nx, stride=group), :]
            resid.append(base_ref[:, start + i].reshape(nx, ny) - coupled)
        change = solve(resid, right_ref, left_ref, scale_ref)
        for i in range(TOGETHER):
            value = current_ref[:, start + i].reshape(nx, ny) + change[i]
            solution_ref[:, start + i] = value.reshape(slab_count, nx // slab_count, ny)
            turned_ref[pl.ds(start + i, nx, stride=group), :] = value
        return carry

    lax.fori_loop(0, group // TOGETHER, several, 0)

    for target in range(mode_count * slab_count):
        start = ((target % slab_count) * mode_count + target // slab_count) * height
        for r in range(height):
            row = start + r
            value = turned_ref[row * group : (row + 1) * group, :].astype(jnp.bfloat16)
            state_ref[target, :, r * ny : (r + 1) * ny] = value


def residual_kernel(
    mode_count, slab_count, code_scale, here_ref, base_ref, coupled_ref, out_ref, *refs
):
    *code_refs, turned_ref = refs
    group = coupled_ref.shape[1]
    ny = base_ref.shape[-1]
    nx = turned_ref.shape[0] // group
    height = nx // (mode_count * slab_count)
    turn_in(turned_ref, coupled_ref, mode_count, slab_count, height, False, code_scale)

    def one(mode, carry):
        coupled = turned_ref[pl.ds(mode, nx, stride=group), :]
        out_ref[:, mode] = base_ref[:, mode] - coupled.reshape(slab_count, nx // slab_count, ny)
        return carry

    lax.fori_loop(0, group, one, 0)
    for shift, code_ref in enumerate(code_refs):
        slab = lax.rem(here_ref[0] + shift, slab_count)
        code_ref[0] = encode(out_ref[slab] * code_scale, SUM_POWER)


def correct_kernel(code_scale, current_ref, resid_ref, right_ref, left_ref, scale_ref, out_ref):
    nx, ny = scale_ref.shape

    def several(number, carry):
        start = number * TOGETHER
        resid = [resid_ref[:, start + i].reshape(nx, ny) for i in range(TOGETHER)]
        change = solve(along_cols(resid, right_ref), right_ref, left_ref, scale_ref)
        for i in range(TOGETHER):
            shape = out_ref.shape[:1] + out_ref.shape[2:]
            value = current_ref[:, start + i] + change[i].reshape(shape)
            out_ref[:, start + i] = encode(value * code_scale, SOLUTION_POWER)
        return carry

    lax.fori_loop(0, out_ref.shape[1] // TOGETHER, several, 0)


def whole(array):
    return pl.BlockSpec(array.shape, lambda g: (0,) * array.ndim)


def slabs_of(array):
    slab_count, _, rows, ny = array.shape
    return pl.BlockSpec((slab_count, GROUP, rows, ny), lambda g: (0, g, 0, 0))


def strips_of(shape):
    return pl.BlockSpec((shape[0], GROUP, shape[2]), lambda g: (0, g, 0))


def per_group(
    kernel, groups, operands, in_specs, out_shape, out_specs, scratch=(), flops=0, vmem=SHARED_VMEM_BYTES
):
    moved = sum(a.size * a.dtype.itemsize for a in operands)
    return pl.pallas_call(
        kernel,
        grid=(groups,),
        in_specs=in_specs,
        out_specs=out_specs,
        out_shape=out_shape,
        scratch_shapes=scratch,
        cost_estimate=pl.CostEstimate(flops=flops, bytes_accessed=2 * moved, transcendentals=0),
        compiler_params=pltpu.CompilerParams(vmem_limit_bytes=vmem),
    )(*operands)


def first_mean_part(place, current_parts, right_side_parts, weights, right):
    slabs = len(right_side_parts)
    _, modes, rows, ny = right_side_parts[0].shape
    part = pl.BlockSpec((1, GROUP, rows, ny), lambda g, *_: (0, g, 0, 0))
    slab = pl.BlockSpec((slabs, GROUP, rows, ny), lambda g, *_: (0, g, 0, 0))
    shape = jax.ShapeDtypeStruct((slabs, modes, rows, ny), jnp.float32)
    return pl.pallas_call(
        functools.partial(first_mean_kernel, slabs),
        grid_spec=pltpu.PrefetchScalarGridSpec(
            num_scalar_prefetch=1,
            grid=(modes // GROUP,),
            in_specs=[part] * (2 * slabs)
            + [
                pl.BlockSpec(weights.shape, lambda g, *_: (0, 0, 0)),
                pl.BlockSpec(right.shape, lambda g, *_: (0, 0)),
            ],
            out_specs=[slab] * 3,
        ),
        out_shape=[shape] * 3,
        compiler_params=pltpu.CompilerParams(vmem_limit_bytes=VMEM_BYTES),
    )(place, *current_parts, *right_side_parts, weights, right)


def mean_part(current, right_side, weights):
    slabs = slabs_of(right_side)
    return per_group(
        mean_kernel,
        right_side.shape[1] // GROUP,
        (current, right_side, weights),
        [slabs, slabs, whole(weights)],
        jax.ShapeDtypeStruct(right_side.shape, jnp.float32),
        slabs,
    )


def solve_flops(array, tables):
    nx, ny = tables[2].shape
    return array.shape[1] * 8 * 3 * nx * ny * (nx + ny) // 2


def step(current, base, coupled, tables, mode_count, slab_count, code_scale):
    nx, ny = tables[2].shape
    slabs = slabs_of(base)
    devices, modes, _ = coupled.shape
    state = (devices, modes, nx // devices * ny)
    return per_group(
        functools.partial(step_kernel, mode_count, slab_count, code_scale),
        modes // GROUP,
        (current, base, coupled, *tables),
        [slabs, slabs, strips_of(coupled.shape), *map(whole, tables)],
        [
            jax.ShapeDtypeStruct(base.shape, jnp.float32),
            jax.ShapeDtypeStruct(state, jnp.bfloat16),
        ],
        [slabs, strips_of(state)],
        [pltpu.VMEM((nx * GROUP, ny), jnp.float32)],
        solve_flops(base, tables),
    )


def last_residual(base, coupled, mode_count, slab_count, code_scale):
    slab, modes, rows, ny = base.shape
    slabs = pl.BlockSpec((slab, GROUP, rows, ny), lambda g, *_: (0, g, 0, 0))
    part = pl.BlockSpec((1, GROUP, rows, ny), lambda g, *_: (0, g, 0, 0))
    devices, _, cells = coupled.shape
    out, *parts = pl.pallas_call(
        functools.partial(residual_kernel, mode_count, slab_count, code_scale),
        grid_spec=pltpu.PrefetchScalarGridSpec(
            num_scalar_prefetch=1,
            grid=(modes // GROUP,),
            in_specs=[slabs, pl.BlockSpec((devices, GROUP, cells), lambda g, *_: (0, g, 0))],
            out_specs=[slabs] + [part] * slab,
            scratch_shapes=[pltpu.VMEM((slab * rows * GROUP, ny), jnp.float32)],
        ),
        out_shape=[jax.ShapeDtypeStruct(base.shape, jnp.float32)]
        + [jax.ShapeDtypeStruct((1, modes, rows, ny), jnp.bfloat16)] * slab,
        cost_estimate=pl.CostEstimate(
            flops=0, bytes_accessed=2 * base.size * 4, transcendentals=0
        ),
        compiler_params=pltpu.CompilerParams(vmem_limit_bytes=SHARED_VMEM_BYTES),
    )(lax.axis_index("slab").reshape(1), base, coupled)
    return out, parts


def correct(current, resid, tables, code_scale):
    slabs = slabs_of(resid)
    return per_group(
        functools.partial(correct_kernel, code_scale),
        resid.shape[1] // GROUP,
        (current, resid, *tables),
        [slabs, slabs, *map(whole, tables)],
        jax.ShapeDtypeStruct(resid.shape, jnp.bfloat16),
        slabs,
        (),
        solve_flops(resid, tables),
    )


def collect(parts, axis):
    count = lax.axis_size(axis)
    here = lax.axis_index(axis)
    out = jnp.zeros((count,) + parts[0].shape[1:], parts[0].dtype)
    for shift, part in enumerate(parts):
        source = lax.rem(here + count - shift, count)
        out = lax.dynamic_update_slice_in_dim(out, part, source, 0)
    return out


def onwards(part, axis, shift):
    count = lax.axis_size(axis)
    return lax.ppermute(part, axis, [(i, (i + shift) % count) for i in range(count)])


def parts_of(block, axis):
    count = lax.axis_size(axis)
    here = lax.axis_index(axis)
    return [
        lax.dynamic_index_in_dim(block, lax.rem(here + shift, count), 0) for shift in range(count)
    ]


def moved_parts(parts, axis):
    return [parts[0]] + [onwards(parts[i], axis, i) for i in range(1, len(parts))]


def local(guess, right_side, mean_coef, field_coef, coupling, coupling_list, pair_count):
    mode_count = lax.axis_size("mode")
    slab_count = lax.axis_size("slab")
    both = ("mode", "slab")
    modes, rows, cols = guess.shape
    fields = field_coef.shape[0]
    nx = rows * slab_count
    devices = mode_count * slab_count
    height = nx // devices
    share = modes // slab_count

    strips = pack_strips(guess, mode_count)
    coefs = jnp.concatenate([mean_coef[None], field_coef], 0)[None]
    state = lax.all_to_all(strips, "mode", 0, 0, tiled=True)
    state = state.reshape(mode_count * modes, height * cols)

    def to_slabs(block):
        flat = block.reshape(modes, rows, cols)
        return lax.all_to_all(flat, "slab", 0, 0, tiled=True)

    guess_parts = parts_of(guess.reshape(slab_count, share, rows, cols), "slab")
    guess_parts = [jnp.concatenate([part, coefs], axis=1) for part in guess_parts]
    guess_parts = moved_parts(guess_parts, "slab")
    right_parts = parts_of(right_side.reshape(slab_count, share, rows, cols), "slab")
    state, guess_parts, right_parts = lax.optimization_barrier((state, guess_parts, right_parts))
    right_parts = moved_parts(right_parts, "slab")

    slab = lax.axis_index("slab")
    place = jnp.stack([slab, slab * mode_count + lax.axis_index("mode")])
    strip_weights = strip_weights_of(guess_parts, place, fields + 1, height)
    mean_weights = mean_weights_of(guess_parts, place, fields + 1)
    matrix = dense_coupling(coupling, coupling_list, pair_count, fields)

    row_high, row_low = split_table(sine_table(nx))
    col_high, col_low = split_table(sine_table(cols))
    tables = (
        jnp.concatenate(
            [
                jnp.concatenate([col_high, col_low], 1),
                jnp.concatenate([col_high, jnp.zeros_like(col_low)], 1),
            ],
            0,
        ),
        jnp.concatenate(
            [
                jnp.concatenate([row_high, row_high], 1),
                jnp.concatenate([row_low, jnp.zeros_like(row_low)], 1),
            ],
            0,
        ),
        RELAXATION / eigen_table(nx, cols),
    )

    first_scale, sum_scale, solution_scale = code_scales(nx, cols, coupling.shape[1], modes)

    sums = coupled_sums(matrix, state, strip_weights, tables[0], True, first_scale, both)
    sums, right_parts = lax.optimization_barrier((sums, right_parts))
    sums = lax.all_to_all(sums, both, 0, 0, tiled=True).reshape(devices, share, -1)
    current, right_side, base = first_mean_part(
        place, guess_parts, right_parts, mean_weights, tables[0]
    )
    current, state = step(current, base, sums, tables, mode_count, slab_count, first_scale)
    state = state.reshape(devices * share, height * cols)
    state = lax.all_to_all(state, both, 0, 0, tiled=True)

    base = mean_part(current, right_side, mean_weights)
    sums = coupled_sums(matrix, state, strip_weights, tables[0], False, sum_scale, both)
    sums = lax.all_to_all(sums, both, 0, 0, tiled=True).reshape(devices, share, -1)
    resid, parts = last_residual(base, sums, mode_count, slab_count, sum_scale)
    moved = collect(moved_parts(parts, "slab"), "slab").reshape(modes, rows, cols)
    resid_out = decode(moved, SUM_POWER) * (1.0 / sum_scale)
    code = correct(current, resid, tables, solution_scale)
    return decode(to_slabs(code), SOLUTION_POWER) * (1.0 / solution_scale), resid_out


def solution(mesh):
    placed = (
        P("mode", "slab", None),
        P("mode", "slab", None),
        P("slab", None),
        P(None, "slab", None),
        P(),
        P(),
        P(),
    )
    return jax.shard_map(
        local,
        mesh=mesh,
        in_specs=placed,
        out_specs=(P("mode", "slab", None), P("mode", "slab", None)),
        check_vma=False,
    )
```
